32 devices in a mesh: ctx: 16 (over z, y, core), wsh: 2 (over x).
Axes of the slice: x: 2, y: 2, z: 4, core: 2. Of those that a mesh axis runs over, the one named last changes fastest.
Arguments:
- tokens: bfloat16 [4, 2048, 1024], P('wsh', 'ctx'), may hold values from -6 to 6
- cotangent: bfloat16 [4, 2048, 1024], P('wsh', 'ctx'), may hold values from -6 to 6
- lengths: int32 [4, 4], P('wsh'), may hold values from 1 to 1536, as said below
- dealing: int32 [4, 16], P('wsh'), may hold values from 0 to 15, as said below
- gain_one: bfloat16 [1024], P('wsh'), may hold values from 0.099609375 to 1.8984375
- bias_one: bfloat16 [1024], P('wsh'), may hold values from -3 to 3
- gain_two: bfloat16 [1024], P('wsh'), may hold values from 0.099609375 to 1.8984375
- bias_two: bfloat16 [1024], P('wsh'), may hold values from -3 to 3
- w_qkv: bfloat16 [1024, 3072], P('wsh'), may hold values from -0.1875 to 0.1875
- w_out: bfloat16 [1024, 1024], P('wsh'), may hold values from -1.5 to 1.5
- w_up: bfloat16 [1024, 4096], P('wsh'), may hold values from -0.1875 to 0.1875
- w_down: bfloat16 [4096, 1024], P('wsh'), may hold values from -0.09375 to 0.09375
Outputs:
- out: bfloat16 [4, 2048, 1024], P('wsh', 'ctx')
- grad_tokens: float32 [4, 2048, 1024], P('wsh', 'ctx')
- grad_gain_one: float32 [1024], P(('ctx', 'wsh'))
- grad_bias_one: float32 [1024], P(('ctx', 'wsh'))
- grad_gain_two: float32 [1024], P(('ctx', 'wsh'))
- grad_bias_two: float32 [1024], P(('ctx', 'wsh'))
- grad_qkv: float32 [1024, 3072], P(('ctx', 'wsh'))
- grad_out: float32 [1024, 1024], P(('ctx', 'wsh'))
- grad_up: float32 [1024, 4096], P(('ctx', 'wsh'))
- grad_down: float32 [4096, 1024], P(('ctx', 'wsh'))
The draws below stay inside these ranges and needn't reach their ends.
Inputs may be any that keep to these rules, and one draw needn't show every extreme that they name: Each row holds 4 lengths in packed order that sum to 2048; one of them is exactly 1536. Each row is a permutation of 0 to 15: dealt block j (dealt tokens j * 128 to (j + 1) * 128 - 1) holds packed block dealing[g, j].
All inputs are finite; a program needn't handle non-finite values.
Results may differ from the reference program's by a relative error of at most 0.015.
Values may be sent and summed in bfloat16 or wider, within the bound.
A program may use at most 512 MiB of HBM per device.

```python
import jax
import jax.numpy as jnp
from jax import lax

D = 1024
H = 16
HD = 64
ROT = 16
FF = 4096
BLK = 128
GROUPS = 4
GROUP = 2048
NB = 16
LONGEST = 1536


def dealt_group(key):
    key_cut, key_other, key_roll, key_perm = jax.random.split(key, 4)
    remain = GROUP - LONGEST
    cut_low = jax.random.randint(key_cut, (), 1, remain // 2, dtype=jnp.int32)
    cut_high = jax.random.randint(key_other, (), remain // 2 + 1, remain, dtype=jnp.int32)
    pieces = jnp.stack([jnp.array(LONGEST, dtype=jnp.int32), cut_low, cut_high - cut_low, jnp.array(remain, dtype=jnp.int32) - cut_high]).astype(jnp.int32)
    shift_by = jax.random.randint(key_roll, (), 0, 4, dtype=jnp.int32)
    lengths_row = jnp.roll(pieces, shift_by).astype(jnp.int32)
    openings = (jnp.cumsum(lengths_row) - lengths_row).astype(jnp.int32)
    long_start = openings[shift_by]
    first_full = (long_start + BLK - 1) // BLK
    dealing_row = jax.random.permutation(key_perm, NB).astype(jnp.int32)
    for target, step_add in ((0, 0), (NB // 2, 1), (NB - 1, 2)):
        wanted = (first_full + step_add).astype(jnp.int32)
        where_now = jnp.argmax(dealing_row == wanted).astype(jnp.int32)
        moved_value = dealing_row[target]
        dealing_row = dealing_row.at[where_now].set(moved_value).at[target].set(wanted)
    return (lengths_row, dealing_row)


def both_rows(key):
    group_keys = jax.random.split(key, GROUPS)
    return jax.vmap(dealt_group)(group_keys)


def draw_lengths(key, part):
    shared = both_rows(key)
    return shared[0]


def draw_dealing(key, part):
    shared = both_rows(key)
    return shared[1]


def block_scale(stream_key, dims, cuts, smallest, largest):
    factor_of, own = 1.0, jax.random.fold_in(stream_key, 6)
    for dim, parts in cuts:
        steps = jnp.exp(jax.random.uniform(jax.random.fold_in(own, dim), (parts,), jnp.float32, smallest / len(cuts), largest / len(cuts)))
        factor_of = factor_of * jnp.repeat(steps, dims[dim] // parts).reshape([-1 if axis == dim else 1 for axis in range(len(dims))])
    return factor_of


def scatter_about(key, extent, width, bound, cuts=(), held_as=jnp.bfloat16):
    drawn = jax.random.normal(key, extent, jnp.float32) * width
    if len(cuts) > 0:
        drawn = block_scale(key, extent, cuts, -0.22, 0.18) * drawn
    return jnp.clip(drawn, min=-bound, max=bound).astype(held_as)


def setup_inputs(seed: int = 0) -> dict:
    seeds = jax.random.split(jax.random.key(seed), 13)
    return {
        "tokens": scatter_about(seeds[0], (GROUPS, GROUP, D), 1.0, 6.0, ((0, 2), (1, 16))),
        "cotangent": scatter_about(seeds[1], (GROUPS, GROUP, D), 1.0, 6.0, ((0, 2), (1, 16))),
        "lengths": draw_lengths(jax.random.fold_in(seeds[12], 71), 0),
        "dealing": draw_dealing(jax.random.fold_in(seeds[12], 71), 0),
        "gain_one": jnp.clip(1.0 + 0.18 * jax.random.normal(seeds[4], (D,), jnp.float32), 0.099609375, 1.8984375).astype(jnp.bfloat16),
        "bias_one": scatter_about(seeds[5], (D,), 0.5, 3.0, ((0, 2),)),
        "gain_two": jnp.clip(1.0 + 0.18 * jax.random.normal(seeds[6], (D,), jnp.float32), 0.099609375, 1.8984375).astype(jnp.bfloat16),
        "bias_two": scatter_about(seeds[7], (D,), 0.5, 3.0, ((0, 2),)),
        "w_qkv": scatter_about(seeds[8], (D, 3 * D), D ** -0.5, 0.1875, ((0, 2),)),
        "w_out": scatter_about(seeds[9], (D, D), (D // 64) ** -0.5, 1.5, ((0, 2),)),
        "w_up": scatter_about(seeds[10], (D, FF), D ** -0.5, 0.1875, ((0, 2),)),
        "w_down": scatter_about(seeds[11], (FF, D), FF ** -0.5, 0.09375, ((0, 2),)),
    }


@jax.custom_vjp
def low(v):
    return lax.optimization_barrier(v.astype(jnp.bfloat16)).astype(jnp.float32)

@jax.custom_vjp
def low_back(v):
    return v

def low_keep(v):
    return (low(v), None)

def low_pass(kept, grad):
    return (grad,)

def back_keep(v):
    return (v, None)

def back_low(kept, grad):
    return (low(grad),)
low.defvjp(low_keep, low_pass)
low_back.defvjp(back_keep, back_low)
HIGHEST = lax.Precision.HIGHEST
EPSILON = 1e-05
MASKED = -1e+30

def norm_layer(values_in, scale_by, shift_by):
    average = lax.optimization_barrier(jnp.mean(values_in, axis=-1, keepdims=True))
    centred = values_in - average
    variance = lax.optimization_barrier(jnp.mean(centred * centred, axis=-1, keepdims=True))
    return centred * lax.rsqrt(variance + EPSILON) * scale_by + shift_by

def rotate(values_in, places):
    split_at = ROT // 2
    frequency = 10000.0 ** (-2.0 * jnp.arange(split_at, dtype=jnp.float32) / ROT)
    angles = places.astype(jnp.float32)[:, None] * frequency[None, :]
    cosine_table = jnp.cos(angles)[:, None, :]
    sine_table = jnp.sin(angles)[:, None, :]
    first_half = values_in[..., :split_at]
    second_half = values_in[..., split_at:ROT]
    return jnp.concatenate([first_half * cosine_table - second_half * sine_table, second_half * cosine_table + first_half * sine_table, values_in[..., ROT:]], axis=-1)

def positions(lengths_row, dealing_row):
    ordinal = jnp.arange(GROUP, dtype=jnp.int32)
    natural = (dealing_row[ordinal // BLK] * BLK + ordinal % BLK).astype(jnp.int32)
    openings = (jnp.cumsum(lengths_row) - lengths_row).astype(jnp.int32)
    opening = lax.optimization_barrier(jnp.max(jnp.where(openings[None, :] <= natural[:, None], openings[None, :], 0), axis=1)).astype(jnp.int32)
    return (natural, opening)

def attention(queries, keys_all, values_all, natural, opening):
    block_count = GROUP // 512
    scale_factor = HD ** (-0.5)

    def one_block(block_item):
        block_queries, block_natural, block_opening = block_item
        scores = low_back(jnp.einsum('qhd,khd->hqk', block_queries, keys_all, precision=HIGHEST) * scale_factor)
        allowed = (natural[None, :] <= block_natural[:, None]) & (natural[None, :] >= block_opening[:, None])
        scores = jnp.where(allowed[None], scores, MASKED)
        soft_probs = low(jax.nn.softmax(scores, axis=-1))
        return jnp.einsum('hqk,khd->qhd', soft_probs, values_all, precision=HIGHEST)
    stacked = (queries.reshape(block_count, 512, H, HD), natural.reshape(block_count, 512), opening.reshape(block_count, 512))
    return lax.map(jax.checkpoint(one_block), stacked).reshape(GROUP, H, HD)

def group_layer(tokens_g, cotangent_g, lengths_row, dealing_row, params):
    natural, opening = positions(lengths_row, dealing_row)
    places = natural - opening

    def forward(tokens_in, scale_one, shift_one, scale_two, shift_two, w_qkv, w_out, w_up, w_down):
        normed_one = low(norm_layer(tokens_in, scale_one, shift_one))
        normed_two = low(norm_layer(tokens_in, scale_two, shift_two))
        mixed = low_back(jnp.dot(normed_one, w_qkv, precision=HIGHEST)).reshape(GROUP, 3, H, HD)
        queries = low(rotate(mixed[:, 0], places))
        keys_all = low(rotate(mixed[:, 1], places))
        values_all = low(mixed[:, 2])
        attended = low(low_back(attention(queries, keys_all, values_all, natural, opening))).reshape(GROUP, D)
        hidden = low_back(jnp.dot(normed_two, w_up, precision=HIGHEST))
        activated = low(jax.nn.gelu(hidden, approximate=False))
        return tokens_in + jnp.dot(attended, w_out, precision=HIGHEST) + jnp.dot(activated, w_down, precision=HIGHEST)
    result, backward = jax.vjp(forward, tokens_g, *params)
    return (result, backward(cotangent_g))

def reference(tokens, cotangent, lengths, dealing, gain_one, bias_one, gain_two, bias_two, w_qkv, w_out, w_up, w_down):
    params = tuple((member.astype(jnp.float32) for member in (gain_one, bias_one, gain_two, bias_two, w_qkv, w_out, w_up, w_down)))
    totals = tuple((jnp.zeros_like(member) for member in params))
    out_rows = []
    grad_rows = []
    for group_index in range(GROUPS):
        result, gradients = group_layer(tokens[group_index].astype(jnp.float32), cotangent[group_index].astype(jnp.float32), lengths[group_index], dealing[group_index], params)
        out_rows.append(result.astype(jnp.bfloat16))
        grad_rows.append(gradients[0])
        totals = tuple((total_now + added for total_now, added in zip(totals, gradients[1:])))
    return (jnp.stack(out_rows), jnp.stack(grad_rows), totals[0], totals[1], totals[2], totals[3], totals[4], totals[5], totals[6], totals[7])
```

```python
import functools

import jax
import jax.numpy as jnp
from jax import lax
from jax.experimental import pallas as pl
from jax.experimental.pallas import tpu as pltpu
from jax.sharding import PartitionSpec as P

D = 1024
H = 16
HD = 64
ROT = 16
BLK = 128


EPSILON = 1e-05
MASKED = -1e30
WIDE = jnp.float32
NARROW = jnp.bfloat16


def norm_layer(values_in, scale_by, shift_by):
    average = jnp.mean(values_in, axis=-1, keepdims=True)
    centred = values_in - average
    variance = jnp.mean(centred * centred, axis=-1, keepdims=True)
    return centred * lax.rsqrt(variance + EPSILON) * scale_by + shift_by


def rotate(values_in, places):
    split_at = ROT // 2
    frequency = 10000.0 ** (-2.0 * jnp.arange(split_at, dtype=WIDE) / ROT)
    angles = places.astype(WIDE)[:, None] * frequency[None, :]
    cosine_table = jnp.cos(angles)[:, None, :]
    sine_table = jnp.sin(angles)[:, None, :]
    first_half = values_in[..., :split_at]
    second_half = values_in[..., split_at:ROT]
    return jnp.concatenate(
        [
            first_half * cosine_table - second_half * sine_table,
            second_half * cosine_table + first_half * sine_table,
            values_in[..., ROT:],
        ],
        axis=-1,
    )


def natural_rows(dealing_row, offset_row, row_count):
    ordinal = offset_row + jnp.arange(row_count, dtype=jnp.int32)
    table_ids = jnp.arange(dealing_row.shape[0], dtype=jnp.int32)
    picked = jnp.sum(
        jnp.where((ordinal // BLK)[:, None] == table_ids[None, :], dealing_row[None, :], 0), axis=1
    )
    return picked * BLK + ordinal % BLK


def sequence_openings(natural, lengths_row):
    openings = jnp.cumsum(lengths_row) - lengths_row
    return jnp.max(jnp.where(openings[None, :] <= natural[:, None], openings[None, :], 0), axis=1)


def score_block(queries, block_keys, offset_row, natural_q, opening_q, dealing_row):
    row_count = block_keys.shape[0]
    key_natural = natural_rows(dealing_row, offset_row, row_count)
    scores = jnp.einsum(
        "qhd,khd->hqk", queries, block_keys.reshape(row_count, H, HD), preferred_element_type=WIDE
    ) * HD ** (-0.5)
    allowed = (key_natural[None, :] <= natural_q[:, None]) & (
        key_natural[None, :] >= opening_q[:, None]
    )
    return (scores, allowed[None])


def fold_blocks(step_fn, state_in, arrays):
    row_count = arrays[0].shape[0]
    block_width = 1024
    stacked = tuple(
        (
            member.reshape((row_count // block_width, block_width) + member.shape[1:])
            for member in arrays
        )
    )
    offsets = jnp.arange(row_count // block_width, dtype=jnp.int32) * block_width

    def inner_step(state_now, block_item):
        return (step_fn(state_now, block_item[0], block_item[1]), None)

    state_out, _ = lax.scan(inner_step, state_in, (stacked, offsets))
    return state_out


def project(tokens_f, weights, places):
    w_qkv, w_out, w_up, w_down, gain_one, bias_one, gain_two, bias_two = weights
    all_rows = tokens_f.shape[0]
    normed_one = norm_layer(tokens_f, gain_one.astype(WIDE), bias_one.astype(WIDE)).astype(NARROW)
    normed_two = norm_layer(tokens_f, gain_two.astype(WIDE), bias_two.astype(WIDE)).astype(NARROW)
    mixed = jnp.dot(normed_one, w_qkv, preferred_element_type=WIDE).reshape(all_rows, 3, H, HD)
    queries = rotate(mixed[:, 0], places).astype(NARROW)
    keys_here = rotate(mixed[:, 1], places).astype(NARROW).reshape(all_rows, D)
    values_here = mixed[:, 2].astype(NARROW).reshape(all_rows, D)
    hidden = jnp.dot(normed_two, w_up, preferred_element_type=WIDE)
    activated = jax.nn.gelu(hidden, approximate=False).astype(NARROW)
    return (normed_one, normed_two, queries, keys_here, values_here, hidden, activated)


def attend(queries, keys_here, values_here, natural_q, opening_q, dealing_row):
    local_rows = queries.shape[0]

    def max_step(state_in, block_arrays, offset_row):
        row_top, row_total = state_in
        scores, allowed = score_block(
            queries, block_arrays[0], offset_row, natural_q, opening_q, dealing_row
        )
        new_top = jnp.maximum(row_top, jnp.max(jnp.where(allowed, scores, MASKED), axis=-1))
        kept_terms = jnp.where(allowed, jnp.exp(scores - new_top[..., None]), 0.0)
        return (new_top, row_total * jnp.exp(row_top - new_top) + jnp.sum(kept_terms, axis=-1))

    start_state = (jnp.full((H, local_rows), MASKED, WIDE), jnp.zeros((H, local_rows), WIDE))
    row_top, row_total = fold_blocks(
        max_step, start_state, (lax.all_gather(keys_here, "ctx", axis=0, tiled=True),)
    )
    log_total = row_top + jnp.log(row_total)

    def value_step(state_in, block_arrays, offset_row):
        scores, allowed = score_block(
            queries, block_arrays[0], offset_row, natural_q, opening_q, dealing_row
        )
        soft_probs = jnp.where(allowed, jnp.exp(scores - log_total[..., None]), 0.0).astype(NARROW)
        row_count = block_arrays[1].shape[0]
        return state_in + jnp.einsum(
            "hqk,khd->qhd",
            soft_probs,
            block_arrays[1].reshape(row_count, H, HD),
            preferred_element_type=WIDE,
        )

    attended = fold_blocks(
        value_step,
        jnp.zeros((local_rows, H, HD), WIDE),
        (
            lax.all_gather(keys_here, "ctx", axis=0, tiled=True),
            lax.all_gather(values_here, "ctx", axis=0, tiled=True),
        ),
    )
    return (attended, log_total)


def attention_back(
    queries,
    keys_here,
    values_here,
    g_attended,
    row_dot,
    log_total,
    natural_q,
    opening_q,
    dealing_row,
):
    local_rows = queries.shape[0]
    scale_factor = HD ** (-0.5)
    gathered_keys, gathered_values = (
        lax.all_gather(keys_here, "ctx", axis=0, tiled=True),
        lax.all_gather(values_here, "ctx", axis=0, tiled=True),
    )
    group_rows = gathered_keys.shape[0]
    key_span = 1024

    def key_block(state_in, block_item):
        block_keys, block_values, offset_row = block_item
        scores, allowed = score_block(
            queries, block_keys, offset_row, natural_q, opening_q, dealing_row
        )
        soft_probs = jnp.where(allowed, jnp.exp(scores - log_total[..., None]), 0.0)
        g_probs = jnp.einsum(
            "qhd,khd->hqk",
            g_attended,
            block_values.reshape(key_span, H, HD),
            preferred_element_type=WIDE,
        )
        g_scores = (soft_probs * (g_probs - row_dot[..., None])).astype(NARROW)
        state_out = (
            state_in
            + jnp.einsum(
                "hqk,khd->qhd",
                g_scores,
                block_keys.reshape(key_span, H, HD),
                preferred_element_type=WIDE,
            )
            * scale_factor
        )
        key_terms = (
            jnp.einsum("hqk,qhd->khd", g_scores, queries, preferred_element_type=WIDE)
            * scale_factor
        )
        value_terms = jnp.einsum(
            "hqk,qhd->khd", soft_probs.astype(NARROW), g_attended, preferred_element_type=WIDE
        )
        return (
            state_out,
            jnp.concatenate(
                [key_terms.reshape(key_span, D), value_terms.reshape(key_span, D)], axis=1
            ),
        )

    block_total = group_rows // key_span
    block_starts = jnp.arange(block_total, dtype=jnp.int32) * key_span
    stacked_blocks = (
        gathered_keys.reshape(block_total, key_span, D),
        gathered_values.reshape(block_total, key_span, D),
        block_starts,
    )
    g_queries, stacked_terms = lax.scan(
        key_block, jnp.zeros((local_rows, H, HD), WIDE), stacked_blocks
    )
    g_pairs = lax.psum_scatter(
        stacked_terms.reshape(group_rows, 2 * D), "ctx", scatter_dimension=0, tiled=True
    )
    g_keys = g_pairs[:, :D].reshape(local_rows, H, HD)
    g_values = g_pairs[:, D:].reshape(local_rows, H, HD)
    return (g_queries, g_keys, g_values)


def shards(
    tokens,
    cotangent,
    lengths,
    dealing,
    gain_one,
    bias_one,
    gain_two,
    bias_two,
    w_qkv,
    w_out,
    w_up,
    w_down,
):
    group_count = tokens.shape[0]
    local_rows = tokens.shape[1]
    all_rows = group_count * local_rows
    tokens_f = tokens.reshape(all_rows, D).astype(WIDE)
    first_row = lax.axis_index("ctx") * local_rows
    natural_list = [
        natural_rows(dealing[member], first_row, local_rows) for member in range(group_count)
    ]
    opening_list = [
        sequence_openings(natural_list[member], lengths[member]) for member in range(group_count)
    ]
    places = jnp.concatenate(
        [natural_list[member] - opening_list[member] for member in range(group_count)], axis=0
    )

    def forward():
        weights = (
            lax.all_gather(w_qkv, "wsh", axis=0, tiled=True),
            lax.all_gather(w_out, "wsh", axis=0, tiled=True),
            lax.all_gather(w_up, "wsh", axis=0, tiled=True),
            lax.all_gather(w_down, "wsh", axis=0, tiled=True),
            lax.all_gather(gain_one, "wsh", axis=0, tiled=True),
            lax.all_gather(bias_one, "wsh", axis=0, tiled=True),
            lax.all_gather(gain_two, "wsh", axis=0, tiled=True),
            lax.all_gather(bias_two, "wsh", axis=0, tiled=True),
        )
        local_parts = project(tokens_f, weights, places)
        attended_list = []
        total_list = []
        for member in range(group_count):
            rows_from = member * local_rows
            attended_one, total_one = attend(
                local_parts[2][rows_from : rows_from + local_rows],
                local_parts[3][rows_from : rows_from + local_rows],
                local_parts[4][rows_from : rows_from + local_rows],
                natural_list[member],
                opening_list[member],
                dealing[member],
            )
            attended_list.append(attended_one)
            total_list.append(total_one)
        return (weights, local_parts, jnp.concatenate(attended_list, axis=0), total_list)

    weights, local_parts, attended, total_list = forward()
    attended_low = attended.reshape(all_rows, D).astype(NARROW)
    mixed_out = (
        tokens_f
        + jnp.dot(attended_low, weights[1], preferred_element_type=WIDE)
        + jnp.dot(local_parts[6], weights[3], preferred_element_type=WIDE)
    )
    out = mixed_out.astype(NARROW)
    weights, local_parts, attended, total_list = forward()
    attended_low = attended.reshape(all_rows, D).astype(NARROW)
    w_qkv_all, w_out_all, w_up_all, w_down_all = (weights[0], weights[1], weights[2], weights[3])
    normed_one, normed_two, queries, keys_here, values_here, hidden, activated = local_parts
    grad_rows = cotangent.reshape(all_rows, D)
    grad_f = grad_rows.astype(WIDE)
    g_down = jnp.einsum("tf,td->fd", activated, grad_rows, preferred_element_type=WIDE)
    g_activated = jnp.einsum("td,fd->tf", grad_rows, w_down_all, preferred_element_type=WIDE)
    _, gelu_back = jax.vjp(lambda pre_act: jax.nn.gelu(pre_act, approximate=False), hidden)
    g_hidden = gelu_back(g_activated)[0].astype(NARROW)
    g_up = jnp.einsum("td,tf->df", normed_two, g_hidden, preferred_element_type=WIDE)
    g_normed_two = jnp.einsum("tf,df->td", g_hidden, w_up_all, preferred_element_type=WIDE)
    g_weight_out = jnp.einsum("te,td->ed", attended_low, grad_rows, preferred_element_type=WIDE)
    g_attended = (
        jnp.einsum("td,ed->te", grad_rows, w_out_all, preferred_element_type=WIDE)
        .astype(NARROW)
        .reshape(all_rows, H, HD)
    )
    row_dot = jnp.einsum("qhd,qhd->hq", g_attended.astype(WIDE), attended)
    query_grads = []
    key_grads = []
    value_grads = []
    for member in range(group_count):
        rows_from = member * local_rows
        rows_to = rows_from + local_rows
        g_q, g_k, g_v = attention_back(
            queries[rows_from:rows_to],
            keys_here[rows_from:rows_to],
            values_here[rows_from:rows_to],
            g_attended[rows_from:rows_to],
            row_dot[:, rows_from:rows_to],
            total_list[member],
            natural_list[member],
            opening_list[member],
            dealing[member],
        )
        query_grads.append(g_q)
        key_grads.append(g_k)
        value_grads.append(g_v)
    g_queries = jnp.concatenate(query_grads, axis=0)
    g_keys = jnp.concatenate(key_grads, axis=0)
    g_values = jnp.concatenate(value_grads, axis=0)
    _, rotate_back = jax.vjp(
        lambda pre_rot: rotate(pre_rot, places), jnp.zeros((all_rows, H, HD), WIDE)
    )
    g_queries_pre = rotate_back(g_queries)[0]
    g_keys_pre = rotate_back(g_keys)[0]
    g_mixed = (
        jnp.stack([g_queries_pre, g_keys_pre, g_values], axis=1)
        .reshape(all_rows, 3 * D)
        .astype(NARROW)
    )
    g_qkv = jnp.einsum("td,te->de", normed_one, g_mixed, preferred_element_type=WIDE)
    g_normed_one = jnp.einsum("te,de->td", g_mixed, w_qkv_all, preferred_element_type=WIDE)

    def both_norms(tokens_in, scale_one, shift_one, scale_two, shift_two):
        return (
            norm_layer(tokens_in, scale_one, shift_one),
            norm_layer(tokens_in, scale_two, shift_two),
        )

    _, norm_back = jax.vjp(
        both_norms,
        tokens_f,
        weights[4].astype(WIDE),
        weights[5].astype(WIDE),
        weights[6].astype(WIDE),
        weights[7].astype(WIDE),
    )
    g_tokens, g_scale_one, g_shift_one, g_scale_two, g_shift_two = norm_back(
        (g_normed_one, g_normed_two)
    )
    grad_tokens = g_tokens + grad_f
    summed = (
        lax.psum_scatter(g_qkv, ("ctx", "wsh"), scatter_dimension=0, tiled=True),
        lax.psum_scatter(g_weight_out, ("ctx", "wsh"), scatter_dimension=0, tiled=True),
        lax.psum_scatter(g_up, ("ctx", "wsh"), scatter_dimension=0, tiled=True),
        lax.psum_scatter(g_down, ("ctx", "wsh"), scatter_dimension=0, tiled=True),
        lax.psum_scatter(g_scale_one, ("ctx", "wsh"), scatter_dimension=0, tiled=True),
        lax.psum_scatter(g_shift_one, ("ctx", "wsh"), scatter_dimension=0, tiled=True),
        lax.psum_scatter(g_scale_two, ("ctx", "wsh"), scatter_dimension=0, tiled=True),
        lax.psum_scatter(g_shift_two, ("ctx", "wsh"), scatter_dimension=0, tiled=True),
    )
    return (
        out.reshape(group_count, local_rows, D),
        grad_tokens.reshape(group_count, local_rows, D),
        summed[4],
        summed[5],
        summed[6],
        summed[7],
        summed[0],
        summed[1],
        summed[2],
        summed[3],
    )


MESH = pl.DeviceIdType.MESH
NT = (((1,), (1,)), ((), ()))
TN = (((0,), (0,)), ((), ()))
VMEM_LIMIT = 60 * 1024 * 1024


def dot(a, b, dims=(((1,), (0,)), ((), ()))):
    return lax.dot_general(a, b, dims, preferred_element_type=WIDE)


def pick(index, table):
    result = jnp.int32(table[0])
    for at in range(1, len(table)):
        result = jnp.where(index == at, jnp.int32(table[at]), result)
    return result


def near_first(depth):
    return [sorted(range(depth), key=lambda to, z=z: (abs(to - z), to)) for z in range(depth)]


def pick2(row, column, table):
    result = pick(column, table[0])
    for at in range(1, len(table)):
        result = jnp.where(row == at, pick(column, table[at]), result)
    return result


class Place:
    def __init__(self, depth):
        self.depth = depth
        self.c = lax.axis_index("ctx")
        self.x = lax.axis_index("wsh")
        self.core = lax.rem(self.c, 2)
        self.y = lax.rem(self.c // 2, 2)
        self.z = self.c // 4
        self.beside = (self.at(self.z, 1 - self.y, self.core), self.x)
        self.twin = (self.at(self.z, self.y, 1 - self.core), self.x)
        self.above = (self.at(self.z + 1, self.y, self.core), self.x)
        self.below = (self.at(self.z - 1, self.y, self.core), self.x)
        self.across = (self.c, 1 - self.x)
        self.has_above = self.z < depth - 1
        self.has_below = self.z > 0

    def at(self, z, y, core):
        return (z * 2 + y) * 2 + core

    def greet(self):
        barrier = pltpu.get_barrier_semaphore()

        def hail(device):
            pl.semaphore_signal(barrier, inc=1, device_id=device, device_id_type=MESH)

        hail(self.beside)
        hail(self.twin)
        hail(self.across)

        @pl.when(self.has_above)
        def _():
            hail(self.above)

        @pl.when(self.has_below)
        def _():
            hail(self.below)

        pl.semaphore_wait(
            barrier, 3 + self.has_above.astype(jnp.int32) + self.has_below.astype(jnp.int32)
        )


def gather_kernel(
    depth,
    tok_ref,
    cot_ref,
    prm_ref,
    turn_ref,
    wqkv_ref,
    wout_ref,
    wup_ref,
    wdown_ref,
    heads_out,
    units_out,
    xhat_out,
    cot_out,
    g_up,
    g_down,
    g_sum,
    wqkv_t,
    wup_all,
    wdown_part,
    wout_part,
    prm_all,
    both,
    xhat_all,
    heads_buf,
    units_buf,
    wq_buf,
    prm_buf,
    in_sem,
    w_sem,
    wsend_sem,
    wrecv_sem,
    send_sem,
    recv_sem,
    out_sem,
):
    here = Place(depth)
    c, x, y, z, core = here.c, here.x, here.y, here.z, here.core
    count = depth * 4
    rows = tok_ref.shape[0]
    units = wup_all.shape[1]
    half = prm_ref.shape[1]
    order = near_first(depth)

    own_in = (
        pltpu.make_async_copy(tok_ref, both.at[c, pl.ds(0, rows)], in_sem.at[0]),
        pltpu.make_async_copy(cot_ref, both.at[c, pl.ds(rows, rows)], in_sem.at[1]),
    )
    for copy in own_in:
        copy.start()

    pair = c // 2
    per_half = count // 2
    owner = c // per_half
    inside = lax.rem(c, per_half)
    shared = []
    for part in range(3):
        shared.append(
            (
                wqkv_ref.at[:, pl.ds(pl.multiple_of(part * D + pair * 128, 128), 128)],
                wq_buf.at[x, part],
            )
        )
    shared.append(
        (
            wup_ref.at[:, pl.ds(pl.multiple_of(c * units, 128), units)],
            wup_all.at[pl.ds(pl.multiple_of(x * half, 128), half)],
        )
    )
    shared.append((prm_ref, prm_buf.at[x]))
    held = (
        (wdown_ref.at[pl.ds(pl.multiple_of(inside * units, 128), units)], wdown_part),
        (wout_ref.at[pl.ds(pl.multiple_of(inside * HD, HD), HD)], wout_part),
    )
    is_owner = owner == x
    for at, (source, place) in enumerate(shared):
        pltpu.make_async_copy(source, place, w_sem.at[at]).start()

    @pl.when(is_owner)
    def _():
        for at, (source, place) in enumerate(held):
            pltpu.make_async_copy(source, place, w_sem.at[5 + at]).start()

    here.greet()

    def remote(source, place, at):
        return pltpu.make_async_remote_copy(
            source,
            place,
            wsend_sem.at[at],
            wrecv_sem.at[at],
            device_id=here.across,
            device_id_type=MESH,
        )

    for at, (source, place) in enumerate(shared):
        remote(source, place, at).start()

    @pl.when(is_owner)
    def _():
        for at, (source, place) in enumerate(held):
            remote(source, place, 5 + at).start()

    def passing(shard, way):
        device = (here.beside, here.twin, here.above, here.below)[way]
        return pltpu.make_async_remote_copy(
            both.at[shard],
            both.at[shard],
            send_sem.at[way, shard],
            recv_sem.at[shard],
            device_id=device,
            device_id_type=MESH,
        )

    for copy in own_in:
        copy.wait()

    def onward(shard, from_z):
        passing(shard, 0).start()

        @pl.when(jnp.logical_and(from_z <= z, here.has_above))
        def _():
            passing(shard, 2).start()

        @pl.when(jnp.logical_and(from_z >= z, here.has_below))
        def _():
            passing(shard, 3).start()

        passing(shard, 1).start()

    onward(c, z)

    for at, (source, place) in enumerate(shared):
        pltpu.make_async_copy(source, place, w_sem.at[at]).wait()
        remote(source, place, at).wait_recv()

    @pl.when(is_owner)
    def _():
        for at, (source, place) in enumerate(held):
            pltpu.make_async_copy(source, place, w_sem.at[5 + at]).wait()

    @pl.when(jnp.logical_not(is_owner))
    def _():
        for at, (source, place) in enumerate(held):
            remote(source, place, 5 + at).wait_recv()

    odd = lax.rem(c, 2) == 1
    for side in range(2):
        prm_all[:, side * half : (side + 1) * half] = prm_buf[side]
        for part in range(3):
            turned = wq_buf[side, part].astype(WIDE).T
            chosen = jnp.where(odd, turned[HD:], turned[:HD])
            wqkv_t[part * HD : (part + 1) * HD, side * half : (side + 1) * half] = chosen.astype(
                NARROW
            )
    g_up[...] = jnp.zeros_like(g_up)
    g_down[...] = jnp.zeros_like(g_down)
    g_sum[...] = jnp.zeros_like(g_sum)

    def compute(shard):
        tokens = both[shard, 0:rows, :].astype(WIDE)
        average = jnp.mean(tokens, axis=-1, keepdims=True)
        centred = tokens - average
        variance = jnp.mean(centred * centred, axis=-1, keepdims=True)
        xhat = centred * lax.rsqrt(variance + EPSILON)
        xhat_low = xhat.astype(NARROW)
        xhat_all[shard] = xhat_low
        n_one = (xhat * prm_all[0:1, :] + prm_all[1:2, :]).astype(NARROW)
        n_two = (xhat * prm_all[2:3, :] + prm_all[3:4, :]).astype(NARROW)
        cotangent = both[shard, rows : 2 * rows, :]
        mixed = dot(wqkv_t[...], n_one, NT)
        turn = turn_ref[shard]
        cosine, sine = turn[0:8], turn[8:16]
        pieces = []
        for base in (0, HD):
            first, second = mixed[base : base + 8], mixed[base + 8 : base + 16]
            pieces += [
                first * cosine - second * sine,
                second * cosine + first * sine,
                mixed[base + 16 : base + HD],
            ]
        pieces.append(mixed[2 * HD : 3 * HD])
        pieces.append(dot(wout_part[...], cotangent, NT))
        heads_buf[shard] = jnp.concatenate(pieces, axis=0).astype(NARROW)
        hidden = dot(n_two, wup_all[...])
        spread = 0.5 * (1.0 + lax.erf(hidden * (0.5**0.5)))
        activated = (hidden * spread).astype(NARROW)
        slope = spread + hidden * (jnp.exp(hidden * hidden * -0.5) * 0.3989422804014327)
        g_hidden_f = dot(cotangent, wdown_part[...], NT) * slope
        g_hidden = g_hidden_f.astype(NARROW)
        units_buf[shard, :, 0:units] = activated
        units_buf[shard, :, units : 2 * units] = g_hidden
        g_up[...] += dot(g_hidden, xhat_low, TN)
        g_down[...] += dot(activated, cotangent, TN)
        g_sum[...] += jnp.sum(g_hidden.astype(WIDE).reshape(rows // 8, 8, units), axis=0)
        pltpu.make_async_copy(xhat_all.at[shard], xhat_out.at[shard], out_sem.at[0, shard]).start()
        pltpu.make_async_copy(
            both.at[shard, pl.ds(rows, rows)], cot_out.at[shard], out_sem.at[1, shard]
        ).start()
        pltpu.make_async_copy(
            heads_buf.at[shard], heads_out.at[shard], out_sem.at[2, shard]
        ).start()
        pltpu.make_async_copy(
            units_buf.at[shard], units_out.at[shard], out_sem.at[3, shard]
        ).start()

    inner = jnp.logical_and(here.has_above, here.has_below)

    def step(at, carry):
        turn_no = at // 4
        kind = lax.rem(at, 4)
        behind = jnp.where(kind >= 2, turn_no - 1, turn_no)
        from_z = pick2(z, jnp.clip(behind, 0, depth - 1), order)
        next_z = pick2(z, jnp.clip(turn_no + 1, 0, depth - 1), order)
        shard_y = jnp.where(kind >= 2, 1 - y, y)
        shard_core = jnp.where(lax.rem(kind, 2) == 1, 1 - core, core)
        shard = here.at(from_z, shard_y, shard_core)
        live = jnp.logical_and(behind >= 0, behind < depth)

        early = jnp.logical_and(inner, turn_no == 2)
        is_own = jnp.logical_and(kind == 0, turn_no == 0)

        @pl.when(jnp.logical_and(live, jnp.logical_not(jnp.logical_or(is_own, jnp.logical_and(kind == 0, early)))))
        def _():
            passing(shard, 1).wait_recv()

        @pl.when(
            jnp.logical_and(
                jnp.logical_and(kind == 0, live),
                jnp.logical_not(jnp.logical_or(turn_no == 0, early)),
            )
        )
        def _():
            onward(shard, from_z)

        @pl.when(jnp.logical_and(kind == 2, live))
        def _():
            passing(shard, 1).start()

        @pl.when(jnp.logical_and(jnp.logical_and(kind == 1, turn_no == 1), inner))
        def _():
            following = here.at(next_z, y, core)
            passing(following, 1).wait_recv()
            onward(following, next_z)

        @pl.when(live)
        def _():
            compute(shard)

        return carry

    lax.fori_loop(0, 4 * depth + 4, step, 0)

    def finish(shard, carry):
        shard_z = shard // 4
        mine = lax.rem(shard, 2) == core
        column = lax.rem(shard // 2, 2) == y

        @pl.when(mine)
        def _():
            passing(shard, 1).wait_send()

        @pl.when(jnp.logical_and(mine, column))
        def _():
            passing(shard, 0).wait_send()

            @pl.when(jnp.logical_and(shard_z <= z, here.has_above))
            def _():
                passing(shard, 2).wait_send()

            @pl.when(jnp.logical_and(shard_z >= z, here.has_below))
            def _():
                passing(shard, 3).wait_send()

        pltpu.make_async_copy(xhat_all.at[shard], xhat_out.at[shard], out_sem.at[0, shard]).wait()
        pltpu.make_async_copy(
            both.at[shard, pl.ds(rows, rows)], cot_out.at[shard], out_sem.at[1, shard]
        ).wait()
        pltpu.make_async_copy(heads_buf.at[shard], heads_out.at[shard], out_sem.at[2, shard]).wait()
        pltpu.make_async_copy(units_buf.at[shard], units_out.at[shard], out_sem.at[3, shard]).wait()
        return carry

    lax.fori_loop(0, count, finish, 0)
    for at, (source, place) in enumerate(shared):
        remote(source, place, at).wait_send()

    @pl.when(is_owner)
    def _():
        for at, (source, place) in enumerate(held):
            remote(source, place, 5 + at).wait_send()


def gather_call(depth, tok, cot, prm, turn, w_qkv, w_out, w_up, w_down):
    count = depth * 4
    rows = tok.shape[0]
    units = w_up.shape[1] // count
    any_spec = pl.BlockSpec(memory_space=pl.ANY)
    vmem = pl.BlockSpec(memory_space=pltpu.VMEM)
    shape = jax.ShapeDtypeStruct
    return pl.pallas_call(
        functools.partial(gather_kernel, depth),
        out_shape=(
            shape((count, 4 * HD, rows), NARROW),
            shape((count, rows, 2 * units), NARROW),
            shape((count, rows, D), NARROW),
            shape((count, rows, D), NARROW),
            shape((units, D), WIDE),
            shape((units, D), WIDE),
            shape((8, units), WIDE),
            shape((3 * HD, D), NARROW),
            shape((D, units), NARROW),
            shape((units, D), NARROW),
            shape((HD, D), NARROW),
            shape((8, D), WIDE),
        ),
        in_specs=[any_spec, any_spec, any_spec, vmem] + [any_spec] * 4,
        out_specs=(any_spec,) * 4 + (vmem,) * 8,
        scratch_shapes=[
            pltpu.VMEM((count, 2 * rows, D), NARROW),
            pltpu.VMEM((count, rows, D), NARROW),
            pltpu.VMEM((count, 4 * HD, rows), NARROW),
            pltpu.VMEM((count, rows, 2 * units), NARROW),
            pltpu.VMEM((2, 3, D // 2, 128), NARROW),
            pltpu.VMEM((2, 8, D // 2), WIDE),
            pltpu.SemaphoreType.DMA((2,)),
            pltpu.SemaphoreType.DMA((7,)),
            pltpu.SemaphoreType.DMA((7,)),
            pltpu.SemaphoreType.DMA((7,)),
            pltpu.SemaphoreType.DMA((4, count)),
            pltpu.SemaphoreType.DMA((count,)),
            pltpu.SemaphoreType.DMA((4, count)),
        ],
        name="gather_and_units",
        compiler_params=pltpu.CompilerParams(
            collective_id=1, has_side_effects=True, vmem_limit_bytes=VMEM_LIMIT
        ),
    )(tok, cot, prm, turn, w_qkv, w_out, w_up, w_down)


def attention_kernel(
    lengths_ref,
    dealing_ref,
    heads_ref,
    turn_ref,
    turned_out,
    tokens_out,
    wide,
    q_rows,
    k_rows,
    v_rows,
    g_rows,
    scores,
    probs,
    g_query,
    attended,
    g_key,
    g_value,
    turn_wide,
    found,
):
    blocks = heads_ref.shape[0]
    groups = heads_ref.shape[2] // BLK
    spans = blocks // 2
    span = 2 * BLK
    scale = HD ** (-0.5)

    for group in range(groups):
        lanes = slice(group * BLK, (group + 1) * BLK)

        def note(block, carry):
            found[dealing_ref[group, block]] = block
            return carry

        lax.fori_loop(0, blocks, note, 0)
        starts = [jnp.int32(0)]
        for piece in range(lengths_ref.shape[1] - 1):
            starts.append(starts[-1] + lengths_ref[group, piece])

        def bring(at, carry):
            for side in range(2):
                source = found[2 * at + side]
                part = heads_ref[source, :, lanes]
                to = slice(side * BLK, (side + 1) * BLK)
                wide[at, :, to] = part
                turn_wide[at, :, to] = turn_ref[source, :, lanes]
                part = part.astype(WIDE)
                row = pl.ds(pl.multiple_of(side * BLK, BLK), BLK)
                q_rows[at, row, :] = part[0:HD].T.astype(NARROW)
                k_rows[at, row, :] = part[HD : 2 * HD].T.astype(NARROW)
                v_rows[at, row, :] = part[2 * HD : 3 * HD].T.astype(NARROW)
                g_rows[at, row, :] = part[3 * HD : 4 * HD].T.astype(NARROW)
            g_key[at] = jnp.zeros((span, HD), WIDE)
            g_value[at] = jnp.zeros((span, HD), WIDE)
            return carry

        lax.fori_loop(0, spans, bring, 0)

        def one_span(at, carry):
            natural = at * span + lax.broadcasted_iota(jnp.int32, (1, span), 1)
            opening = jnp.zeros((1, span), jnp.int32)
            first = jnp.int32(0)
            for start in starts[1:]:
                opening = jnp.where(natural >= start, start, opening)
                first = jnp.where(at * span >= start, start, first)
            low = first // span
            queries_t = wide[at, 0:HD, :]
            g_attended_t = wide[at, 3 * HD : 4 * HD, :]
            key_in = lax.broadcasted_iota(jnp.int32, (span, span), 0)

            def score(keys_at, top):
                raw = dot(k_rows[keys_at], queries_t) * scale
                place = key_in + keys_at * span
                allowed = jnp.logical_and(place <= natural, place >= opening)
                kept = jnp.where(allowed, raw, MASKED)
                scores[keys_at] = kept
                return jnp.maximum(top, jnp.max(kept.reshape(span // 8, 8, span), axis=0))

            top = lax.fori_loop(low, at + 1, score, jnp.full((8, span), MASKED, WIDE))
            top = jnp.max(top, axis=0, keepdims=True)

            def power(keys_at, total):
                risen = jnp.exp(scores[keys_at] - top)
                scores[keys_at] = risen
                return total + jnp.sum(risen.reshape(span // 8, 8, span), axis=0)

            total = lax.fori_loop(low, at + 1, power, jnp.zeros((8, span), WIDE))
            share = 1.0 / jnp.sum(total, axis=0, keepdims=True)
            attended[...] = jnp.zeros_like(attended)
            g_query[...] = jnp.zeros_like(g_query)

            def weigh(keys_at, carry):
                part = scores[keys_at] * share
                scores[keys_at] = part
                low_part = part.astype(NARROW)
                probs[keys_at] = low_part
                attended[...] += dot(wide[keys_at, 2 * HD : 3 * HD, :], low_part)
                return carry

            lax.fori_loop(low, at + 1, weigh, 0)
            row_dot = jnp.sum(attended[...] * g_attended_t.astype(WIDE), axis=0, keepdims=True)

            def back(keys_at, carry):
                g_probs = dot(v_rows[keys_at], g_attended_t)
                g_scores = (scores[keys_at] * (g_probs - row_dot)).astype(NARROW)
                g_query[...] += dot(wide[keys_at, HD : 2 * HD, :], g_scores)
                g_key[keys_at] += dot(g_scores, q_rows[at])
                g_value[keys_at] += dot(probs[keys_at], g_rows[at])
                return carry

            lax.fori_loop(low, at + 1, back, 0)
            wide[at, 0:HD, :] = (unturn(g_query[...] * scale, turn_wide[at])).astype(NARROW)
            wide[at, 3 * HD : 4 * HD, :] = attended[...].astype(NARROW)
            return carry

        lax.fori_loop(0, spans, one_span, 0)

        def give(at, carry):
            keys_t = unturn(g_key[at].T * scale, turn_wide[at]).astype(NARROW)
            values_t = g_value[at].T.astype(NARROW)
            whole = jnp.concatenate(
                [wide[at, 3 * HD : 4 * HD, :], wide[at, 0:HD, :], keys_t, values_t], axis=0
            )
            for side in range(2):
                to = found[2 * at + side]
                part = whole[:, side * BLK : (side + 1) * BLK]
                turned_out[to, :, lanes] = part
                tokens_out[to, lanes, :] = part.astype(WIDE).T.astype(NARROW)
            return carry

        lax.fori_loop(0, spans, give, 0)


def unturn(rows, turn):
    cosine, sine = turn[0:8], turn[8:16]
    first, second = rows[0:8], rows[8:16]
    return jnp.concatenate(
        [first * cosine + second * sine, second * cosine - first * sine, rows[16:]], axis=0
    )


def attention_call(lengths, dealing, heads, turn):
    blocks, _, rows = heads.shape
    spans, span = blocks // 2, 2 * BLK
    vmem = pl.BlockSpec(memory_space=pltpu.VMEM)
    smem = pl.BlockSpec(memory_space=pltpu.SMEM)
    shape = jax.ShapeDtypeStruct
    return pl.pallas_call(
        attention_kernel,
        out_shape=(
            shape((blocks, 4 * HD, rows), NARROW),
            shape((blocks, rows, 4 * HD), NARROW),
        ),
        in_specs=[smem, smem, vmem, vmem],
        out_specs=(vmem, vmem),
        scratch_shapes=[
            pltpu.VMEM((spans, 4 * HD, span), NARROW),
            pltpu.VMEM((spans, span, HD), NARROW),
            pltpu.VMEM((spans, span, HD), NARROW),
            pltpu.VMEM((spans, span, HD), NARROW),
            pltpu.VMEM((spans, span, HD), NARROW),
            pltpu.VMEM((spans, span, span), WIDE),
            pltpu.VMEM((spans, span, span), NARROW),
            pltpu.VMEM((HD, span), WIDE),
            pltpu.VMEM((HD, span), WIDE),
            pltpu.VMEM((spans, span, HD), WIDE),
            pltpu.VMEM((spans, span, HD), WIDE),
            pltpu.VMEM((spans, 16, span), WIDE),
            pltpu.SMEM((blocks,), jnp.int32),
        ],
        name="head_attention",
        compiler_params=pltpu.CompilerParams(vmem_limit_bytes=VMEM_LIMIT),
    )(lengths, dealing, heads, turn)


def far_first(depth):
    return [list(reversed(row)) for row in near_first(depth)]


def reduce_kernel(
    depth,
    tokens_in,
    units_in,
    tok_ref,
    cot_ref,
    prm_all,
    wqkv_t,
    wup_all,
    wdown_part,
    wout_part,
    out_ref,
    grad_ref,
    w_heads_out,
    w_heads_back,
    give_buf,
    sum_buf,
    beside_buf,
    under_buf,
    over_buf,
    send_sem,
    recv_twin,
    recv_beside,
    recv_z,
):
    here = Place(depth)
    x, y, z, core = here.x, here.y, here.z, here.core
    rows = tok_ref.shape[0]
    units = wup_all.shape[1]
    order = far_first(depth)
    here.greet()
    w_heads_out[0:HD, :] = wout_part[...]
    w_heads_out[HD:, :] = jnp.zeros((3 * HD, D), NARROW)
    w_heads_back[0:HD, :] = jnp.zeros((HD, D), NARROW)
    w_heads_back[HD:, :] = wqkv_t[...]

    def partial(shard):
        heads = tokens_in[shard]
        activated = units_in[shard, :, 0:units]
        g_hidden = units_in[shard, :, units : 2 * units]
        part_out = dot(heads, w_heads_out[...]) + dot(activated, wdown_part[...])
        part_back = dot(heads, w_heads_back[...]) * prm_all[0:1, :] + dot(
            g_hidden, wup_all[...], NT
        ) * prm_all[2:3, :]
        return part_out, part_back

    def to_twin(slot):
        return pltpu.make_async_remote_copy(
            give_buf.at[slot],
            sum_buf.at[slot],
            send_sem.at[0, slot],
            recv_twin.at[slot],
            device_id=here.twin,
            device_id_type=MESH,
        )

    def to_beside(to_z):
        return pltpu.make_async_remote_copy(
            sum_buf.at[to_z],
            beside_buf.at[to_z],
            send_sem.at[1, to_z],
            recv_beside.at[to_z],
            device_id=here.beside,
            device_id_type=MESH,
        )

    def to_above(to_z):
        return pltpu.make_async_remote_copy(
            sum_buf.at[depth + to_z],
            under_buf.at[to_z],
            send_sem.at[2, to_z],
            recv_z.at[0, to_z],
            device_id=here.above,
            device_id_type=MESH,
        )

    def to_below(to_z):
        return pltpu.make_async_remote_copy(
            sum_buf.at[depth + to_z],
            over_buf.at[to_z],
            send_sem.at[2, to_z],
            recv_z.at[1, to_z],
            device_id=here.below,
            device_id_type=MESH,
        )

    def produce(at, carry):
        to_z = pick2(z, at // 4, order)
        kind = lax.rem(at, 4)
        home = lax.rem(kind, 2)
        to_y = jnp.where(home == 1, y, 1 - y)
        slot = home * depth + to_z
        to_core = jnp.where(kind < 2, 1 - core, core)
        part_out, part_back = partial(here.at(to_z, to_y, to_core))

        @pl.when(kind < 2)
        def _():
            give_buf[slot, 0:rows, :] = part_out.astype(NARROW)
            give_buf[slot, rows : 2 * rows, :] = part_back.astype(NARROW)
            to_twin(slot).start()

        @pl.when(kind >= 2)
        def _():
            to_twin(slot).wait_recv()
            sum_buf[slot, 0:rows, :] = (
                part_out + sum_buf[slot, 0:rows, :].astype(WIDE)
            ).astype(NARROW)
            sum_buf[slot, rows : 2 * rows, :] = (
                part_back + sum_buf[slot, rows : 2 * rows, :].astype(WIDE)
            ).astype(NARROW)

        @pl.when(kind == 2)
        def _():
            to_beside(to_z).start()

        return carry

    lax.fori_loop(0, 4 * depth, produce, 0)

    def chain(at, carry):
        to_z = pick2(z, at, order)
        slot = depth + to_z
        to_beside(to_z).wait_recv()

        def add(incoming):
            for part in range(4):
                span = slice(part * rows // 2, (part + 1) * rows // 2)
                total = sum_buf[slot, span, :].astype(WIDE) + beside_buf[to_z, span, :].astype(WIDE)
                if incoming is not None:
                    total = total + incoming[to_z, span, :].astype(WIDE)
                sum_buf[slot, span, :] = total.astype(NARROW)

        @pl.when(to_z > z)
        def _():
            @pl.when(here.has_below)
            def _():
                to_above(to_z).wait_recv()
                add(under_buf)

            @pl.when(jnp.logical_not(here.has_below))
            def _():
                add(None)

            to_above(to_z).start()

        @pl.when(to_z < z)
        def _():
            @pl.when(here.has_above)
            def _():
                to_below(to_z).wait_recv()
                add(over_buf)

            @pl.when(jnp.logical_not(here.has_above))
            def _():
                add(None)

            to_below(to_z).start()

        return carry

    lax.fori_loop(0, depth, chain, 0)

    @pl.when(here.has_below)
    def _():
        to_above(z).wait_recv()

    @pl.when(jnp.logical_not(here.has_below))
    def _():
        under_buf[z] = jnp.zeros((2 * rows, D), NARROW)

    @pl.when(here.has_above)
    def _():
        to_below(z).wait_recv()

    @pl.when(jnp.logical_not(here.has_above))
    def _():
        over_buf[z] = jnp.zeros((2 * rows, D), NARROW)

    def total(span):
        return (
            sum_buf[depth + z, span, :].astype(WIDE)
            + beside_buf[z, span, :].astype(WIDE)
            + under_buf[z, span, :].astype(WIDE)
            + over_buf[z, span, :].astype(WIDE)
        )

    tokens = tok_ref[...].astype(WIDE)
    out_ref[...] = (tokens + total(slice(0, rows))).astype(NARROW)
    average = jnp.mean(tokens, axis=-1, keepdims=True)
    centred = tokens - average
    variance = jnp.mean(centred * centred, axis=-1, keepdims=True)
    rise = lax.rsqrt(variance + EPSILON)
    xhat = centred * rise
    g_xhat = total(slice(rows, 2 * rows))
    along = jnp.mean(g_xhat * xhat, axis=-1, keepdims=True)
    level = jnp.mean(g_xhat, axis=-1, keepdims=True)
    grad_ref[...] = cot_ref[...].astype(WIDE) + rise * (g_xhat - level - xhat * along)

    def finish(to_z, carry):
        to_twin(to_z).wait_send()
        to_twin(depth + to_z).wait_send()
        to_beside(to_z).wait_send()

        @pl.when(to_z > z)
        def _():
            to_above(to_z).wait_send()

        @pl.when(to_z < z)
        def _():
            to_below(to_z).wait_send()

        return carry

    lax.fori_loop(0, depth, finish, 0)


def reduce_call(depth, tokens_in, units_in, tok, cot, prm_all, wqkv_t, wup_all, wdown_part, wout_part):
    rows = tok.shape[0]
    vmem = pl.BlockSpec(memory_space=pltpu.VMEM)
    shape = jax.ShapeDtypeStruct
    message = (2 * rows, D)
    return pl.pallas_call(
        functools.partial(reduce_kernel, depth),
        out_shape=(shape((rows, D), NARROW), shape((rows, D), WIDE)),
        in_specs=[vmem] * 9,
        out_specs=(vmem, vmem),
        scratch_shapes=[
            pltpu.VMEM((4 * HD, D), NARROW),
            pltpu.VMEM((4 * HD, D), NARROW),
            pltpu.VMEM((2 * depth,) + message, NARROW),
            pltpu.VMEM((2 * depth,) + message, NARROW),
            pltpu.VMEM((depth,) + message, NARROW),
            pltpu.VMEM((depth,) + message, NARROW),
            pltpu.VMEM((depth,) + message, NARROW),
            pltpu.SemaphoreType.DMA((3, 2 * depth)),
            pltpu.SemaphoreType.DMA((2 * depth,)),
            pltpu.SemaphoreType.DMA((depth,)),
            pltpu.SemaphoreType.DMA((2, depth)),
        ],
        name="reduce_rows",
        compiler_params=pltpu.CompilerParams(
            collective_id=2, has_side_effects=True, vmem_limit_bytes=VMEM_LIMIT
        ),
    )(tokens_in, units_in, tok, cot, prm_all, wqkv_t, wup_all, wdown_part, wout_part)


def fast_shards(depth, *arguments):
    (tokens, cotangent, lengths, dealing, gain_one, bias_one, gain_two, bias_two) = arguments[:8]
    w_qkv, w_out, w_up, w_down = arguments[8:]
    groups, local_rows, _ = tokens.shape
    rows = groups * local_rows
    count = depth * 4
    tok = tokens.reshape(rows, D)
    cot = cotangent.reshape(rows, D)
    prm = jnp.stack([gain_one, bias_one, gain_two, bias_two] * 2).astype(WIDE)

    openings = jnp.cumsum(lengths, axis=1) - lengths
    natural = (dealing.T[:, :, None] * BLK + jnp.arange(BLK, dtype=jnp.int32)[None, None, :]).reshape(
        count, rows
    )
    start_rows = jnp.repeat(openings.T, BLK, axis=1)[:, None, :]
    opening = jnp.max(jnp.where(start_rows <= natural[None], start_rows, 0), axis=0)
    place = (natural - opening).astype(WIDE)
    frequency = 10000.0 ** (-2.0 * jnp.arange(ROT // 2, dtype=WIDE) / ROT)
    angles = place[:, None, :] * frequency[None, :, None]
    turn = jnp.concatenate([jnp.cos(angles), jnp.sin(angles)], axis=1)

    (heads, units, xhat, cot_all, g_up, g_down, g_sum, wqkv_t, wup_all, wdown_part, wout_part, prm_all) = (
        gather_call(depth, tok, cot, prm, turn, w_qkv, w_out, w_up, w_down)
    )
    turned, by_token = attention_call(lengths, dealing, heads, turn)
    out, grad_tokens = reduce_call(
        depth, by_token, units, tok, cot, prm_all, wqkv_t, wup_all, wdown_part, wout_part
    )

    g_out = jnp.einsum("ser,srd->ed", turned[:, :HD], cot_all, preferred_element_type=WIDE)
    g_one = jnp.einsum("ser,srd->ed", turned[:, HD:], xhat, preferred_element_type=WIDE)
    sum_one = jnp.sum(turned[:, HD:].astype(WIDE), axis=(0, 2))[:, None]
    sum_two = jnp.sum(g_sum, axis=0)[:, None]
    gain_a, bias_a, gain_b, bias_b = prm_all[0:1], prm_all[1:2], prm_all[2:3], prm_all[3:4]
    wide_qkv = wqkv_t.astype(WIDE)
    wide_up = wup_all.astype(WIDE).T
    vectors = jnp.stack(
        [
            jnp.sum(wide_qkv * g_one, axis=0),
            jnp.sum(wide_qkv * sum_one, axis=0),
            jnp.sum(wide_up * g_up, axis=0),
            jnp.sum(wide_up * sum_two, axis=0),
        ]
    )
    columns = jnp.concatenate(
        [g_one * gain_a + bias_a * sum_one, g_up * gain_b + bias_b * sum_two, vectors], axis=0
    )
    width = columns.shape[0]
    piece = D // (2 * count)
    split = columns.reshape(width, count, 2, piece).transpose(2, 1, 0, 3)
    split = lax.psum_scatter(split, "wsh", scatter_dimension=0, tiled=False)
    split = lax.all_to_all(split, "ctx", split_axis=0, concat_axis=0, tiled=True)
    units_count = g_up.shape[0]
    qkv_part = split[:, : 3 * HD].reshape(count, 3, HD, piece).transpose(3, 1, 0, 2).reshape(piece, 3 * D)
    up_part = split[:, 3 * HD : 3 * HD + units_count].transpose(2, 0, 1).reshape(piece, count * units_count)
    vector_part = jnp.sum(split[:, 3 * HD + units_count :], axis=0)
    out_part = lax.psum_scatter(g_out, "wsh", scatter_dimension=0, tiled=True)
    down_part = lax.psum_scatter(g_down, "wsh", scatter_dimension=0, tiled=True)
    return (
        out.reshape(tokens.shape),
        grad_tokens.reshape(tokens.shape),
        vector_part[0],
        vector_part[1],
        vector_part[2],
        vector_part[3],
        qkv_part,
        out_part,
        up_part,
        down_part,
    )


def solution(mesh):
    placed = (
        P("wsh", "ctx", None),
        P("wsh", "ctx", None),
        P("wsh", None),
        P("wsh", None),
        P("wsh"),
        P("wsh"),
        P("wsh"),
        P("wsh"),
        P("wsh", None),
        P("wsh", None),
        P("wsh", None),
        P("wsh", None),
    )
    ctx_size = mesh.shape["ctx"]
    by_heads = ctx_size == H and mesh.shape["wsh"] == 2
    body = functools.partial(fast_shards, ctx_size // 4) if by_heads else shards
    return jax.shard_map(
        body,
        mesh=mesh,
        in_specs=placed,
        out_specs=(
            P("wsh", "ctx", None),
            P("wsh", "ctx", None),
            P(("ctx", "wsh")),
            P(("ctx", "wsh")),
            P(("ctx", "wsh")),
            P(("ctx", "wsh")),
            P(("ctx", "wsh"), None),
            P(("ctx", "wsh"), None),
            P(("ctx", "wsh"), None),
            P(("ctx", "wsh"), None),
        ),
        check_vma=False,
    )
```

```python
import functools

import jax
import jax.numpy as jnp
from jax import lax
from jax.experimental import pallas as pl
from jax.experimental.pallas import tpu as pltpu
from jax.sharding import PartitionSpec as P

D = 1024
H = 16
HD = 64
ROT = 16
BLK = 128


EPSILON = 1e-05
MASKED = -1e30
WIDE = jnp.float32
NARROW = jnp.bfloat16


def norm_layer(values_in, scale_by, shift_by):
    average = jnp.mean(values_in, axis=-1, keepdims=True)
    centred = values_in - average
    variance = jnp.mean(centred * centred, axis=-1, keepdims=True)
    return centred * lax.rsqrt(variance + EPSILON) * scale_by + shift_by


def rotate(values_in, places):
    split_at = ROT // 2
    frequency = 10000.0 ** (-2.0 * jnp.arange(split_at, dtype=WIDE) / ROT)
    angles = places.astype(WIDE)[:, None] * frequency[None, :]
    cosine_table = jnp.cos(angles)[:, None, :]
    sine_table = jnp.sin(angles)[:, None, :]
    first_half = values_in[..., :split_at]
    second_half = values_in[..., split_at:ROT]
    return jnp.concatenate(
        [
            first_half * cosine_table - second_half * sine_table,
            second_half * cosine_table + first_half * sine_table,
            values_in[..., ROT:],
        ],
        axis=-1,
    )


def natural_rows(dealing_row, offset_row, row_count):
    ordinal = offset_row + jnp.arange(row_count, dtype=jnp.int32)
    table_ids = jnp.arange(dealing_row.shape[0], dtype=jnp.int32)
    picked = jnp.sum(
        jnp.where((ordinal // BLK)[:, None] == table_ids[None, :], dealing_row[None, :], 0), axis=1
    )
    return picked * BLK + ordinal % BLK


def sequence_openings(natural, lengths_row):
    openings = jnp.cumsum(lengths_row) - lengths_row
    return jnp.max(jnp.where(openings[None, :] <= natural[:, None], openings[None, :], 0), axis=1)


def score_block(queries, block_keys, offset_row, natural_q, opening_q, dealing_row):
    row_count = block_keys.shape[0]
    key_natural = natural_rows(dealing_row, offset_row, row_count)
    scores = jnp.einsum(
        "qhd,khd->hqk", queries, block_keys.reshape(row_count, H, HD), preferred_element_type=WIDE
    ) * HD ** (-0.5)
    allowed = (key_natural[None, :] <= natural_q[:, None]) & (
        key_natural[None, :] >= opening_q[:, None]
    )
    return (scores, allowed[None])


def fold_blocks(step_fn, state_in, arrays):
    row_count = arrays[0].shape[0]
    block_width = 1024
    stacked = tuple(
        (
            member.reshape((row_count // block_width, block_width) + member.shape[1:])
            for member in arrays
        )
    )
    offsets = jnp.arange(row_count // block_width, dtype=jnp.int32) * block_width

    def inner_step(state_now, block_item):
        return (step_fn(state_now, block_item[0], block_item[1]), None)

    state_out, _ = lax.scan(inner_step, state_in, (stacked, offsets))
    return state_out


def project(tokens_f, weights, places):
    w_qkv, w_out, w_up, w_down, gain_one, bias_one, gain_two, bias_two = weights
    all_rows = tokens_f.shape[0]
    normed_one = norm_layer(tokens_f, gain_one.astype(WIDE), bias_one.astype(WIDE)).astype(NARROW)
    normed_two = norm_layer(tokens_f, gain_two.astype(WIDE), bias_two.astype(WIDE)).astype(NARROW)
    mixed = jnp.dot(normed_one, w_qkv, preferred_element_type=WIDE).reshape(all_rows, 3, H, HD)
    queries = rotate(mixed[:, 0], places).astype(NARROW)
    keys_here = rotate(mixed[:, 1], places).astype(NARROW).reshape(all_rows, D)
    values_here = mixed[:, 2].astype(NARROW).reshape(all_rows, D)
    hidden = jnp.dot(normed_two, w_up, preferred_element_type=WIDE)
    activated = jax.nn.gelu(hidden, approximate=False).astype(NARROW)
    return (normed_one, normed_two, queries, keys_here, values_here, hidden, activated)


def attend(queries, keys_here, values_here, natural_q, opening_q, dealing_row):
    local_rows = queries.shape[0]

    def max_step(state_in, block_arrays, offset_row):
        row_top, row_total = state_in
        scores, allowed = score_block(
            queries, block_arrays[0], offset_row, natural_q, opening_q, dealing_row
        )
        new_top = jnp.maximum(row_top, jnp.max(jnp.where(allowed, scores, MASKED), axis=-1))
        kept_terms = jnp.where(allowed, jnp.exp(scores - new_top[..., None]), 0.0)
        return (new_top, row_total * jnp.exp(row_top - new_top) + jnp.sum(kept_terms, axis=-1))

    start_state = (jnp.full((H, local_rows), MASKED, WIDE), jnp.zeros((H, local_rows), WIDE))
    row_top, row_total = fold_blocks(
        max_step, start_state, (lax.all_gather(keys_here, "ctx", axis=0, tiled=True),)
    )
    log_total = row_top + jnp.log(row_total)

    def value_step(state_in, block_arrays, offset_row):
        scores, allowed = score_block(
            queries, block_arrays[0], offset_row, natural_q, opening_q, dealing_row
        )
        soft_probs = jnp.where(allowed, jnp.exp(scores - log_total[..., None]), 0.0).astype(NARROW)
        row_count = block_arrays[1].shape[0]
        return state_in + jnp.einsum(
            "hqk,khd->qhd",
            soft_probs,
            block_arrays[1].reshape(row_count, H, HD),
            preferred_element_type=WIDE,
        )

    attended = fold_blocks(
        value_step,
        jnp.zeros((local_rows, H, HD), WIDE),
        (
            lax.all_gather(keys_here, "ctx", axis=0, tiled=True),
            lax.all_gather(values_here, "ctx", axis=0, tiled=True),
        ),
    )
    return (attended, log_total)


def attention_back(
    queries,
    keys_here,
    values_here,
    g_attended,
    row_dot,
    log_total,
    natural_q,
    opening_q,
    dealing_row,
):
    local_rows = queries.shape[0]
    scale_factor = HD ** (-0.5)
    gathered_keys, gathered_values = (
        lax.all_gather(keys_here, "ctx", axis=0, tiled=True),
        lax.all_gather(values_here, "ctx", axis=0, tiled=True),
    )
    group_rows = gathered_keys.shape[0]
    key_span = 1024

    def key_block(state_in, block_item):
        block_keys, block_values, offset_row = block_item
        scores, allowed = score_block(
            queries, block_keys, offset_row, natural_q, opening_q, dealing_row
        )
        soft_probs = jnp.where(allowed, jnp.exp(scores - log_total[..., None]), 0.0)
        g_probs = jnp.einsum(
            "qhd,khd->hqk",
            g_attended,
            block_values.reshape(key_span, H, HD),
            preferred_element_type=WIDE,
        )
        g_scores = (soft_probs * (g_probs - row_dot[..., None])).astype(NARROW)
        state_out = (
            state_in
            + jnp.einsum(
                "hqk,khd->qhd",
                g_scores,
                block_keys.reshape(key_span, H, HD),
                preferred_element_type=WIDE,
            )
            * scale_factor
        )
        key_terms = (
            jnp.einsum("hqk,qhd->khd", g_scores, queries, preferred_element_type=WIDE)
            * scale_factor
        )
        value_terms = jnp.einsum(
            "hqk,qhd->khd", soft_probs.astype(NARROW), g_attended, preferred_element_type=WIDE
        )
        return (
            state_out,
            jnp.concatenate(
                [key_terms.reshape(key_span, D), value_terms.reshape(key_span, D)], axis=1
            ),
        )

    block_total = group_rows // key_span
    block_starts = jnp.arange(block_total, dtype=jnp.int32) * key_span
    stacked_blocks = (
        gathered_keys.reshape(block_total, key_span, D),
        gathered_values.reshape(block_total, key_span, D),
        block_starts,
    )
    g_queries, stacked_terms = lax.scan(
        key_block, jnp.zeros((local_rows, H, HD), WIDE), stacked_blocks
    )
    g_pairs = lax.psum_scatter(
        stacked_terms.reshape(group_rows, 2 * D), "ctx", scatter_dimension=0, tiled=True
    )
    g_keys = g_pairs[:, :D].reshape(local_rows, H, HD)
    g_values = g_pairs[:, D:].reshape(local_rows, H, HD)
    return (g_queries, g_keys, g_values)


def shards(
    tokens,
    cotangent,
    lengths,
    dealing,
    gain_one,
    bias_one,
    gain_two,
    bias_two,
    w_qkv,
    w_out,
    w_up,
    w_down,
):
    group_count = tokens.shape[0]
    local_rows = tokens.shape[1]
    all_rows = group_count * local_rows
    tokens_f = tokens.reshape(all_rows, D).astype(WIDE)
    first_row = lax.axis_index("ctx") * local_rows
    natural_list = [
        natural_rows(dealing[member], first_row, local_rows) for member in range(group_count)
    ]
    opening_list = [
        sequence_openings(natural_list[member], lengths[member]) for member in range(group_count)
    ]
    places = jnp.concatenate(
        [natural_list[member] - opening_list[member] for member in range(group_count)], axis=0
    )

    def forward():
        weights = (
            lax.all_gather(w_qkv, "wsh", axis=0, tiled=True),
            lax.all_gather(w_out, "wsh", axis=0, tiled=True),
            lax.all_gather(w_up, "wsh", axis=0, tiled=True),
            lax.all_gather(w_down, "wsh", axis=0, tiled=True),
            lax.all_gather(gain_one, "wsh", axis=0, tiled=True),
            lax.all_gather(bias_one, "wsh", axis=0, tiled=True),
            lax.all_gather(gain_two, "wsh", axis=0, tiled=True),
            lax.all_gather(bias_two, "wsh", axis=0, tiled=True),
        )
        local_parts = project(tokens_f, weights, places)
        attended_list = []
        total_list = []
        for member in range(group_count):
            rows_from = member * local_rows
            attended_one, total_one = attend(
                local_parts[2][rows_from : rows_from + local_rows],
                local_parts[3][rows_from : rows_from + local_rows],
                local_parts[4][rows_from : rows_from + local_rows],
                natural_list[member],
                opening_list[member],
                dealing[member],
            )
            attended_list.append(attended_one)
            total_list.append(total_one)
        return (weights, local_parts, jnp.concatenate(attended_list, axis=0), total_list)

    weights, local_parts, attended, total_list = forward()
    attended_low = attended.reshape(all_rows, D).astype(NARROW)
    mixed_out = (
        tokens_f
        + jnp.dot(attended_low, weights[1], preferred_element_type=WIDE)
        + jnp.dot(local_parts[6], weights[3], preferred_element_type=WIDE)
    )
    out = mixed_out.astype(NARROW)
    weights, local_parts, attended, total_list = forward()
    attended_low = attended.reshape(all_rows, D).astype(NARROW)
    w_qkv_all, w_out_all, w_up_all, w_down_all = (weights[0], weights[1], weights[2], weights[3])
    normed_one, normed_two, queries, keys_here, values_here, hidden, activated = local_parts
    grad_rows = cotangent.reshape(all_rows, D)
    grad_f = grad_rows.astype(WIDE)
    g_down = jnp.einsum("tf,td->fd", activated, grad_rows, preferred_element_type=WIDE)
    g_activated = jnp.einsum("td,fd->tf", grad_rows, w_down_all, preferred_element_type=WIDE)
    _, gelu_back = jax.vjp(lambda pre_act: jax.nn.gelu(pre_act, approximate=False), hidden)
    g_hidden = gelu_back(g_activated)[0].astype(NARROW)
    g_up = jnp.einsum("td,tf->df", normed_two, g_hidden, preferred_element_type=WIDE)
    g_normed_two = jnp.einsum("tf,df->td", g_hidden, w_up_all, preferred_element_type=WIDE)
    g_weight_out = jnp.einsum("te,td->ed", attended_low, grad_rows, preferred_element_type=WIDE)
    g_attended = (
        jnp.einsum("td,ed->te", grad_rows, w_out_all, preferred_element_type=WIDE)
        .astype(NARROW)
        .reshape(all_rows, H, HD)
    )
    row_dot = jnp.einsum("qhd,qhd->hq", g_attended.astype(WIDE), attended)
    query_grads = []
    key_grads = []
    value_grads = []
    for member in range(group_count):
        rows_from = member * local_rows
        rows_to = rows_from + local_rows
        g_q, g_k, g_v = attention_back(
            queries[rows_from:rows_to],
            keys_here[rows_from:rows_to],
            values_here[rows_from:rows_to],
            g_attended[rows_from:rows_to],
            row_dot[:, rows_from:rows_to],
            total_list[member],
            natural_list[member],
            opening_list[member],
            dealing[member],
        )
        query_grads.append(g_q)
        key_grads.append(g_k)
        value_grads.append(g_v)
    g_queries = jnp.concatenate(query_grads, axis=0)
    g_keys = jnp.concatenate(key_grads, axis=0)
    g_values = jnp.concatenate(value_grads, axis=0)
    _, rotate_back = jax.vjp(
        lambda pre_rot: rotate(pre_rot, places), jnp.zeros((all_rows, H, HD), WIDE)
    )
    g_queries_pre = rotate_back(g_queries)[0]
    g_keys_pre = rotate_back(g_keys)[0]
    g_mixed = (
        jnp.stack([g_queries_pre, g_keys_pre, g_values], axis=1)
        .reshape(all_rows, 3 * D)
        .astype(NARROW)
    )
    g_qkv = jnp.einsum("td,te->de", normed_one, g_mixed, preferred_element_type=WIDE)
    g_normed_one = jnp.einsum("te,de->td", g_mixed, w_qkv_all, preferred_element_type=WIDE)

    def both_norms(tokens_in, scale_one, shift_one, scale_two, shift_two):
        return (
            norm_layer(tokens_in, scale_one, shift_one),
            norm_layer(tokens_in, scale_two, shift_two),
        )

    _, norm_back = jax.vjp(
        both_norms,
        tokens_f,
        weights[4].astype(WIDE),
        weights[5].astype(WIDE),
        weights[6].astype(WIDE),
        weights[7].astype(WIDE),
    )
    g_tokens, g_scale_one, g_shift_one, g_scale_two, g_shift_two = norm_back(
        (g_normed_one, g_normed_two)
    )
    grad_tokens = g_tokens + grad_f
    summed = (
        lax.psum_scatter(g_qkv, ("ctx", "wsh"), scatter_dimension=0, tiled=True),
        lax.psum_scatter(g_weight_out, ("ctx", "wsh"), scatter_dimension=0, tiled=True),
        lax.psum_scatter(g_up, ("ctx", "wsh"), scatter_dimension=0, tiled=True),
        lax.psum_scatter(g_down, ("ctx", "wsh"), scatter_dimension=0, tiled=True),
        lax.psum_scatter(g_scale_one, ("ctx", "wsh"), scatter_dimension=0, tiled=True),
        lax.psum_scatter(g_shift_one, ("ctx", "wsh"), scatter_dimension=0, tiled=True),
        lax.psum_scatter(g_scale_two, ("ctx", "wsh"), scatter_dimension=0, tiled=True),
        lax.psum_scatter(g_shift_two, ("ctx", "wsh"), scatter_dimension=0, tiled=True),
    )
    return (
        out.reshape(group_count, local_rows, D),
        grad_tokens.reshape(group_count, local_rows, D),
        summed[4],
        summed[5],
        summed[6],
        summed[7],
        summed[0],
        summed[1],
        summed[2],
        summed[3],
    )


MESH = pl.DeviceIdType.MESH
NT = (((1,), (1,)), ((), ()))
TN = (((0,), (0,)), ((), ()))
VMEM_LIMIT = 60 * 1024 * 1024


def dot(a, b, dims=(((1,), (0,)), ((), ()))):
    return lax.dot_general(a, b, dims, preferred_element_type=WIDE)


def pick(index, table):
    result = jnp.int32(table[0])
    for at in range(1, len(table)):
        result = jnp.where(index == at, jnp.int32(table[at]), result)
    return result


def near_first(depth):
    return [sorted(range(depth), key=lambda to, z=z: (abs(to - z), to)) for z in range(depth)]


def pick2(row, column, table):
    result = pick(column, table[0])
    for at in range(1, len(table)):
        result = jnp.where(row == at, pick(column, table[at]), result)
    return result


class Place:
    def __init__(self, depth):
        self.depth = depth
        self.c = lax.axis_index("ctx")
        self.x = lax.axis_index("wsh")
        self.core = lax.rem(self.c, 2)
        self.y = lax.rem(self.c // 2, 2)
        self.z = self.c // 4
        self.beside = (self.at(self.z, 1 - self.y, self.core), self.x)
        self.twin = (self.at(self.z, self.y, 1 - self.core), self.x)
        self.above = (self.at(self.z + 1, self.y, self.core), self.x)
        self.below = (self.at(self.z - 1, self.y, self.core), self.x)
        self.across = (self.c, 1 - self.x)
        self.has_above = self.z < depth - 1
        self.has_below = self.z > 0

    def at(self, z, y, core):
        return (z * 2 + y) * 2 + core

    def greet(self):
        barrier = pltpu.get_barrier_semaphore()

        def hail(device):
            pl.semaphore_signal(barrier, inc=1, device_id=device, device_id_type=MESH)

        hail(self.beside)
        hail(self.twin)
        hail(self.across)

        @pl.when(self.has_above)
        def _():
            hail(self.above)

        @pl.when(self.has_below)
        def _():
            hail(self.below)

        pl.semaphore_wait(
            barrier, 3 + self.has_above.astype(jnp.int32) + self.has_below.astype(jnp.int32)
        )


    def greet_all(self):
        barrier = pltpu.get_barrier_semaphore()
        count = 4 * self.depth
        pl.semaphore_signal(barrier, inc=1, device_id=self.across, device_id_type=MESH)

        def hail(offset, carry):
            device = (lax.rem(self.c + offset, count), self.x)
            pl.semaphore_signal(barrier, inc=1, device_id=device, device_id_type=MESH)
            return carry

        lax.fori_loop(1, count, hail, 0)
        pl.semaphore_wait(barrier, count)


def gather_kernel(
    depth,
    tok_ref,
    cot_ref,
    prm_ref,
    turn_ref,
    wqkv_ref,
    wout_ref,
    wup_ref,
    wdown_ref,
    heads_out,
    units_out,
    xhat_out,
    cot_out,
    g_up,
    g_down,
    g_sum,
    wqkv_t,
    wup_all,
    wdown_part,
    wout_part,
    prm_all,
    both,
    xhat_all,
    heads_buf,
    units_buf,
    wq_buf,
    prm_buf,
    in_sem,
    w_sem,
    wsend_sem,
    wrecv_sem,
    send_sem,
    recv_sem,
    out_sem,
):
    here = Place(depth)
    c, x, y, z, core = here.c, here.x, here.y, here.z, here.core
    count = depth * 4
    rows = tok_ref.shape[0]
    units = wup_all.shape[1]
    half = prm_ref.shape[1]
    order = near_first(depth)

    own_in = (
        pltpu.make_async_copy(tok_ref, both.at[c, pl.ds(0, rows)], in_sem.at[0]),
        pltpu.make_async_copy(cot_ref, both.at[c, pl.ds(rows, rows)], in_sem.at[1]),
    )
    for copy in own_in:
        copy.start()

    pair = c // 2
    per_half = count // 2
    owner = c // per_half
    inside = lax.rem(c, per_half)
    shared = []
    for part in range(3):
        shared.append(
            (
                wqkv_ref.at[:, pl.ds(pl.multiple_of(part * D + pair * 128, 128), 128)],
                wq_buf.at[x, part],
            )
        )
    shared.append(
        (
            wup_ref.at[:, pl.ds(pl.multiple_of(c * units, 128), units)],
            wup_all.at[pl.ds(pl.multiple_of(x * half, 128), half)],
        )
    )
    shared.append((prm_ref, prm_buf.at[x]))
    held = (
        (wdown_ref.at[pl.ds(pl.multiple_of(inside * units, 128), units)], wdown_part),
        (wout_ref.at[pl.ds(pl.multiple_of(inside * HD, HD), HD)], wout_part),
    )
    is_owner = owner == x
    for at, (source, place) in enumerate(shared):
        pltpu.make_async_copy(source, place, w_sem.at[at]).start()

    @pl.when(is_owner)
    def _():
        for at, (source, place) in enumerate(held):
            pltpu.make_async_copy(source, place, w_sem.at[5 + at]).start()

    here.greet()

    def remote(source, place, at):
        return pltpu.make_async_remote_copy(
            source,
            place,
            wsend_sem.at[at],
            wrecv_sem.at[at],
            device_id=here.across,
            device_id_type=MESH,
        )

    for at, (source, place) in enumerate(shared):
        remote(source, place, at).start()

    @pl.when(is_owner)
    def _():
        for at, (source, place) in enumerate(held):
            remote(source, place, 5 + at).start()

    def passing(shard, way):
        device = (here.beside, here.twin, here.above, here.below)[way]
        return pltpu.make_async_remote_copy(
            both.at[shard],
            both.at[shard],
            send_sem.at[way, shard],
            recv_sem.at[shard],
            device_id=device,
            device_id_type=MESH,
        )

    for copy in own_in:
        copy.wait()

    def onward(shard, from_z):
        passing(shard, 0).start()

        @pl.when(jnp.logical_and(from_z <= z, here.has_above))
        def _():
            passing(shard, 2).start()

        @pl.when(jnp.logical_and(from_z >= z, here.has_below))
        def _():
            passing(shard, 3).start()

        passing(shard, 1).start()

    onward(c, z)

    for at, (source, place) in enumerate(shared):
        pltpu.make_async_copy(source, place, w_sem.at[at]).wait()
        remote(source, place, at).wait_recv()

    @pl.when(is_owner)
    def _():
        for at, (source, place) in enumerate(held):
            pltpu.make_async_copy(source, place, w_sem.at[5 + at]).wait()

    @pl.when(jnp.logical_not(is_owner))
    def _():
        for at, (source, place) in enumerate(held):
            remote(source, place, 5 + at).wait_recv()

    odd = lax.rem(c, 2) == 1
    for side in range(2):
        prm_all[:, side * half : (side + 1) * half] = prm_buf[side]
        for part in range(3):
            turned = wq_buf[side, part].astype(WIDE).T
            chosen = jnp.where(odd, turned[HD:], turned[:HD])
            wqkv_t[part * HD : (part + 1) * HD, side * half : (side + 1) * half] = chosen.astype(
                NARROW
            )
    g_up[...] = jnp.zeros_like(g_up)
    g_down[...] = jnp.zeros_like(g_down)
    g_sum[...] = jnp.zeros_like(g_sum)

    def compute(shard):
        tokens = both[shard, 0:rows, :].astype(WIDE)
        average = jnp.mean(tokens, axis=-1, keepdims=True)
        centred = tokens - average
        variance = jnp.mean(centred * centred, axis=-1, keepdims=True)
        xhat = centred * lax.rsqrt(variance + EPSILON)
        xhat_low = xhat.astype(NARROW)
        xhat_all[shard] = xhat_low
        n_one = (xhat * prm_all[0:1, :] + prm_all[1:2, :]).astype(NARROW)
        n_two = (xhat * prm_all[2:3, :] + prm_all[3:4, :]).astype(NARROW)
        cotangent = both[shard, rows : 2 * rows, :]
        mixed = dot(wqkv_t[...], n_one, NT)
        turn = turn_ref[shard]
        cosine, sine = turn[0:8], turn[8:16]
        pieces = []
        for base in (0, HD):
            first, second = mixed[base : base + 8], mixed[base + 8 : base + 16]
            pieces += [
                first * cosine - second * sine,
                second * cosine + first * sine,
                mixed[base + 16 : base + HD],
            ]
        pieces.append(mixed[2 * HD : 3 * HD])
        pieces.append(dot(wout_part[...], cotangent, NT))
        heads_buf[shard] = jnp.concatenate(pieces, axis=0).astype(NARROW)
        hidden = dot(n_two, wup_all[...])
        spread = 0.5 * (1.0 + lax.erf(hidden * (0.5**0.5)))
        activated = (hidden * spread).astype(NARROW)
        slope = spread + hidden * (jnp.exp(hidden * hidden * -0.5) * 0.3989422804014327)
        g_hidden_f = dot(cotangent, wdown_part[...], NT) * slope
        g_hidden = g_hidden_f.astype(NARROW)
        units_buf[shard, :, 0:units] = activated
        units_buf[shard, :, units : 2 * units] = g_hidden
        g_up[...] += dot(g_hidden, xhat_low, TN)
        g_down[...] += dot(activated, cotangent, TN)
        g_sum[...] += jnp.sum(g_hidden.astype(WIDE).reshape(rows // 8, 8, units), axis=0)
        pltpu.make_async_copy(xhat_all.at[shard], xhat_out.at[shard], out_sem.at[0, shard]).start()
        pltpu.make_async_copy(
            both.at[shard, pl.ds(rows, rows)], cot_out.at[shard], out_sem.at[1, shard]
        ).start()
        pltpu.make_async_copy(
            heads_buf.at[shard], heads_out.at[shard], out_sem.at[2, shard]
        ).start()
        pltpu.make_async_copy(
            units_buf.at[shard], units_out.at[shard], out_sem.at[3, shard]
        ).start()

    inner = jnp.logical_and(here.has_above, here.has_below)

    def step(at, carry):
        turn_no = at // 4
        kind = lax.rem(at, 4)
        behind = jnp.where(kind >= 2, turn_no - 1, turn_no)
        from_z = pick2(z, jnp.clip(behind, 0, depth - 1), order)
        next_z = pick2(z, jnp.clip(turn_no + 1, 0, depth - 1), order)
        shard_y = jnp.where(kind >= 2, 1 - y, y)
        shard_core = jnp.where(lax.rem(kind, 2) == 1, 1 - core, core)
        shard = here.at(from_z, shard_y, shard_core)
        live = jnp.logical_and(behind >= 0, behind < depth)

        early = jnp.logical_and(inner, turn_no == 2)
        is_own = jnp.logical_and(kind == 0, turn_no == 0)

        @pl.when(jnp.logical_and(live, jnp.logical_not(jnp.logical_or(is_own, jnp.logical_and(kind == 0, early)))))
        def _():
            passing(shard, 1).wait_recv()

        @pl.when(
            jnp.logical_and(
                jnp.logical_and(kind == 0, live),
                jnp.logical_not(jnp.logical_or(turn_no == 0, early)),
            )
        )
        def _():
            onward(shard, from_z)

        @pl.when(jnp.logical_and(kind == 2, live))
        def _():
            passing(shard, 1).start()

        @pl.when(jnp.logical_and(jnp.logical_and(kind == 1, turn_no == 1), inner))
        def _():
            following = here.at(next_z, y, core)
            passing(following, 1).wait_recv()
            onward(following, next_z)

        @pl.when(live)
        def _():
            compute(shard)

        return carry

    lax.fori_loop(0, 4 * depth + 4, step, 0)

    def finish(shard, carry):
        shard_z = shard // 4
        mine = lax.rem(shard, 2) == core
        column = lax.rem(shard // 2, 2) == y

        @pl.when(mine)
        def _():
            passing(shard, 1).wait_send()

        @pl.when(jnp.logical_and(mine, column))
        def _():
            passing(shard, 0).wait_send()

            @pl.when(jnp.logical_and(shard_z <= z, here.has_above))
            def _():
                passing(shard, 2).wait_send()

            @pl.when(jnp.logical_and(shard_z >= z, here.has_below))
            def _():
                passing(shard, 3).wait_send()

        pltpu.make_async_copy(xhat_all.at[shard], xhat_out.at[shard], out_sem.at[0, shard]).wait()
        pltpu.make_async_copy(
            both.at[shard, pl.ds(rows, rows)], cot_out.at[shard], out_sem.at[1, shard]
        ).wait()
        pltpu.make_async_copy(heads_buf.at[shard], heads_out.at[shard], out_sem.at[2, shard]).wait()
        pltpu.make_async_copy(units_buf.at[shard], units_out.at[shard], out_sem.at[3, shard]).wait()
        return carry

    lax.fori_loop(0, count, finish, 0)
    for at, (source, place) in enumerate(shared):
        remote(source, place, at).wait_send()

    @pl.when(is_owner)
    def _():
        for at, (source, place) in enumerate(held):
            remote(source, place, 5 + at).wait_send()


def gather_call(depth, tok, cot, prm, turn, w_qkv, w_out, w_up, w_down):
    count = depth * 4
    rows = tok.shape[0]
    units = w_up.shape[1] // count
    any_spec = pl.BlockSpec(memory_space=pl.ANY)
    vmem = pl.BlockSpec(memory_space=pltpu.VMEM)
    shape = jax.ShapeDtypeStruct
    return pl.pallas_call(
        functools.partial(gather_kernel, depth),
        out_shape=(
            shape((count, 4 * HD, rows), NARROW),
            shape((count, rows, 2 * units), NARROW),
            shape((count, rows, D), NARROW),
            shape((count, rows, D), NARROW),
            shape((units, D), WIDE),
            shape((units, D), WIDE),
            shape((8, units), WIDE),
            shape((3 * HD, D), NARROW),
            shape((D, units), NARROW),
            shape((units, D), NARROW),
            shape((HD, D), NARROW),
            shape((8, D), WIDE),
        ),
        in_specs=[any_spec, any_spec, any_spec, vmem] + [any_spec] * 4,
        out_specs=(any_spec,) * 4 + (vmem,) * 8,
        scratch_shapes=[
            pltpu.VMEM((count, 2 * rows, D), NARROW),
            pltpu.VMEM((count, rows, D), NARROW),
            pltpu.VMEM((count, 4 * HD, rows), NARROW),
            pltpu.VMEM((count, rows, 2 * units), NARROW),
            pltpu.VMEM((2, 3, D // 2, 128), NARROW),
            pltpu.VMEM((2, 8, D // 2), WIDE),
            pltpu.SemaphoreType.DMA((2,)),
            pltpu.SemaphoreType.DMA((7,)),
            pltpu.SemaphoreType.DMA((7,)),
            pltpu.SemaphoreType.DMA((7,)),
            pltpu.SemaphoreType.DMA((4, count)),
            pltpu.SemaphoreType.DMA((count,)),
            pltpu.SemaphoreType.DMA((4, count)),
        ],
        name="gather_and_units",
        compiler_params=pltpu.CompilerParams(
            collective_id=1, has_side_effects=True, vmem_limit_bytes=VMEM_LIMIT
        ),
    )(tok, cot, prm, turn, w_qkv, w_out, w_up, w_down)


def attention_kernel(
    lengths_ref,
    dealing_ref,
    heads_ref,
    turn_ref,
    turned_out,
    tokens_out,
    wide,
    q_rows,
    k_rows,
    v_rows,
    g_rows,
    scores,
    probs,
    g_query,
    attended,
    g_key,
    g_value,
    turn_wide,
    found,
):
    blocks = heads_ref.shape[0]
    groups = heads_ref.shape[2] // BLK
    spans = blocks // 2
    span = 2 * BLK
    scale = HD ** (-0.5)

    for group in range(groups):
        lanes = slice(group * BLK, (group + 1) * BLK)

        def note(block, carry):
            found[dealing_ref[group, block]] = block
            return carry

        lax.fori_loop(0, blocks, note, 0)
        starts = [jnp.int32(0)]
        for piece in range(lengths_ref.shape[1] - 1):
            starts.append(starts[-1] + lengths_ref[group, piece])

        def bring(at, carry):
            for side in range(2):
                source = found[2 * at + side]
                part = heads_ref[source, :, lanes]
                to = slice(side * BLK, (side + 1) * BLK)
                wide[at, :, to] = part
                turn_wide[at, :, to] = turn_ref[source, :, lanes]
                part = part.astype(WIDE)
                row = pl.ds(pl.multiple_of(side * BLK, BLK), BLK)
                q_rows[at, row, :] = part[0:HD].T.astype(NARROW)
                k_rows[at, row, :] = part[HD : 2 * HD].T.astype(NARROW)
                v_rows[at, row, :] = part[2 * HD : 3 * HD].T.astype(NARROW)
                g_rows[at, row, :] = part[3 * HD : 4 * HD].T.astype(NARROW)
            g_key[at] = jnp.zeros((span, HD), WIDE)
            g_value[at] = jnp.zeros((span, HD), WIDE)
            return carry

        lax.fori_loop(0, spans, bring, 0)

        def one_span(at, carry):
            natural = at * span + lax.broadcasted_iota(jnp.int32, (1, span), 1)
            opening = jnp.zeros((1, span), jnp.int32)
            first = jnp.int32(0)
            for start in starts[1:]:
                opening = jnp.where(natural >= start, start, opening)
                first = jnp.where(at * span >= start, start, first)
            low = first // span
            queries_t = wide[at, 0:HD, :]
            g_attended_t = wide[at, 3 * HD : 4 * HD, :]
            key_in = lax.broadcasted_iota(jnp.int32, (span, span), 0)

            def score(keys_at, top):
                raw = dot(k_rows[keys_at], queries_t) * scale
                place = key_in + keys_at * span
                allowed = jnp.logical_and(place <= natural, place >= opening)
                kept = jnp.where(allowed, raw, MASKED)
                scores[keys_at] = kept
                return jnp.maximum(top, jnp.max(kept.reshape(span // 8, 8, span), axis=0))

            top = lax.fori_loop(low, at + 1, score, jnp.full((8, span), MASKED, WIDE))
            top = jnp.max(top, axis=0, keepdims=True)

            def power(keys_at, total):
                risen = jnp.exp(scores[keys_at] - top)
                scores[keys_at] = risen
                return total + jnp.sum(risen.reshape(span // 8, 8, span), axis=0)

            total = lax.fori_loop(low, at + 1, power, jnp.zeros((8, span), WIDE))
            share = 1.0 / jnp.sum(total, axis=0, keepdims=True)
            attended[...] = jnp.zeros_like(attended)
            g_query[...] = jnp.zeros_like(g_query)

            def weigh(keys_at, carry):
                part = scores[keys_at] * share
                scores[keys_at] = part
                low_part = part.astype(NARROW)
                probs[keys_at] = low_part
                attended[...] += dot(wide[keys_at, 2 * HD : 3 * HD, :], low_part)
                return carry

            lax.fori_loop(low, at + 1, weigh, 0)
            row_dot = jnp.sum(attended[...] * g_attended_t.astype(WIDE), axis=0, keepdims=True)

            def back(keys_at, carry):
                g_probs = dot(v_rows[keys_at], g_attended_t)
                g_scores = (scores[keys_at] * (g_probs - row_dot)).astype(NARROW)
                g_query[...] += dot(wide[keys_at, HD : 2 * HD, :], g_scores)
                g_key[keys_at] += dot(g_scores, q_rows[at])
                g_value[keys_at] += dot(probs[keys_at], g_rows[at])
                return carry

            lax.fori_loop(low, at + 1, back, 0)
            wide[at, 0:HD, :] = (unturn(g_query[...] * scale, turn_wide[at])).astype(NARROW)
            wide[at, 3 * HD : 4 * HD, :] = attended[...].astype(NARROW)
            return carry

        lax.fori_loop(0, spans, one_span, 0)

        def give(at, carry):
            keys_t = unturn(g_key[at].T * scale, turn_wide[at]).astype(NARROW)
            values_t = g_value[at].T.astype(NARROW)
            whole = jnp.concatenate(
                [wide[at, 3 * HD : 4 * HD, :], wide[at, 0:HD, :], keys_t, values_t], axis=0
            )
            for side in range(2):
                to = found[2 * at + side]
                part = whole[:, side * BLK : (side + 1) * BLK]
                turned_out[to, :, lanes] = part
                tokens_out[to, lanes, :] = part.astype(WIDE).T.astype(NARROW)
            return carry

        lax.fori_loop(0, spans, give, 0)


def unturn(rows, turn):
    cosine, sine = turn[0:8], turn[8:16]
    first, second = rows[0:8], rows[8:16]
    return jnp.concatenate(
        [first * cosine + second * sine, second * cosine - first * sine, rows[16:]], axis=0
    )


def attention_call(lengths, dealing, heads, turn):
    blocks, _, rows = heads.shape
    spans, span = blocks // 2, 2 * BLK
    vmem = pl.BlockSpec(memory_space=pltpu.VMEM)
    smem = pl.BlockSpec(memory_space=pltpu.SMEM)
    shape = jax.ShapeDtypeStruct
    return pl.pallas_call(
        attention_kernel,
        out_shape=(
            shape((blocks, 4 * HD, rows), NARROW),
            shape((blocks, rows, 4 * HD), NARROW),
        ),
        in_specs=[smem, smem, vmem, vmem],
        out_specs=(vmem, vmem),
        scratch_shapes=[
            pltpu.VMEM((spans, 4 * HD, span), NARROW),
            pltpu.VMEM((spans, span, HD), NARROW),
            pltpu.VMEM((spans, span, HD), NARROW),
            pltpu.VMEM((spans, span, HD), NARROW),
            pltpu.VMEM((spans, span, HD), NARROW),
            pltpu.VMEM((spans, span, span), WIDE),
            pltpu.VMEM((spans, span, span), NARROW),
            pltpu.VMEM((HD, span), WIDE),
            pltpu.VMEM((HD, span), WIDE),
            pltpu.VMEM((spans, span, HD), WIDE),
            pltpu.VMEM((spans, span, HD), WIDE),
            pltpu.VMEM((spans, 16, span), WIDE),
            pltpu.SMEM((blocks,), jnp.int32),
        ],
        name="head_attention",
        compiler_params=pltpu.CompilerParams(vmem_limit_bytes=VMEM_LIMIT),
    )(lengths, dealing, heads, turn)


def far_first(depth):
    return [list(reversed(row)) for row in near_first(depth)]


def reduce_kernel(
    depth,
    tokens_in,
    turned_in,
    units_in,
    tok_ref,
    cot_ref,
    prm_all,
    wqkv_t,
    wup_all,
    wdown_part,
    wout_part,
    g_up,
    g_down,
    g_sum,
    xhat_in,
    cot_in,
    out_ref,
    grad_ref,
    qkv_ref,
    wout_ref,
    up_ref,
    down_ref,
    vec_ref,
    w_heads_out,
    w_heads_back,
    give_buf,
    sum_buf,
    beside_buf,
    line_buf,
    stream,
    g_heads,
    g_wout,
    sum_heads,
    vectors,
    grads,
    grads_in,
    mail,
    inbox,
    wout_in,
    down_in,
    send_sem,
    recv_twin,
    recv_beside,
    recv_z,
    stream_sem,
    across_send,
    across_recv,
    mail_send,
    mail_recv,
):
    here = Place(depth)
    c, x, y, z, core = here.c, here.x, here.y, here.z, here.core
    rows = tok_ref.shape[0]
    units = wup_all.shape[1]
    count = 4 * depth
    piece = D // (2 * count)
    order = far_first(depth)

    def shard_of(at):
        kind = lax.rem(at, 4)
        to_y = jnp.where(lax.rem(kind, 2) == 1, y, 1 - y)
        to_core = jnp.where(kind < 2, 1 - core, core)
        return here.at(pick2(z, at // 4, order), to_y, to_core)

    def load(at):
        shard, slot = shard_of(at), lax.rem(at, 2)
        return (
            pltpu.make_async_copy(xhat_in.at[shard], stream.at[0, slot], stream_sem.at[0, slot]),
            pltpu.make_async_copy(cot_in.at[shard], stream.at[1, slot], stream_sem.at[1, slot]),
        )

    for copy in load(0):
        copy.start()
    here.greet_all()

    def crossing(source, place, at):
        return pltpu.make_async_remote_copy(
            source,
            place,
            across_send.at[at],
            across_recv.at[at],
            device_id=here.across,
            device_id_type=MESH,
        )

    half_down = g_down.shape[0] // 2
    half_wout = HD // 2
    send_down = crossing(g_down.at[pl.ds((1 - x) * half_down, half_down)], down_in, 0)
    send_wout = crossing(g_wout.at[pl.ds((1 - x) * half_wout, half_wout)], wout_in, 1)
    send_grads = [crossing(grads.at[part, 1 - x], grads_in.at[part], 2 + part) for part in range(2)]
    send_down.start()

    w_heads_out[0:HD, :] = wout_part[...]
    w_heads_out[HD:, :] = jnp.zeros((3 * HD, D), NARROW)
    w_heads_back[0:HD, :] = jnp.zeros((HD, D), NARROW)
    w_heads_back[HD:, :] = wqkv_t[...]
    g_heads[...] = jnp.zeros_like(g_heads)
    g_wout[...] = jnp.zeros_like(g_wout)
    sum_heads[...] = jnp.zeros_like(sum_heads)
    sum_units = jnp.sum(g_sum[...], axis=0, keepdims=True)

    def settle(chunk, part, raw, weights, sums, column):
        scaled = raw * column[:, 2 - 2 * part : 3 - 2 * part] + sums * column[:, 3 - 2 * part : 4 - 2 * part]
        gain_sum = jnp.sum(weights * raw, axis=1, keepdims=True)
        bias_sum = jnp.sum(weights * sums, axis=1, keepdims=True)
        row = pl.ds(pl.multiple_of(chunk * 128, 128), 128)
        if part == 0:
            vectors[row, 0:1] = gain_sum
            vectors[row, 1:2] = bias_sum
        else:
            lane = lax.broadcasted_iota(jnp.int32, scaled.shape, 1)
            scaled = jnp.where(lane == 0, gain_sum, scaled)
            scaled = jnp.where(lane == 1, bias_sum, scaled)
            scaled = jnp.where(lane == 2, vectors[row, 0:1], scaled)
            scaled = jnp.where(lane == 3, vectors[row, 1:2], scaled)
        per = 128 // piece
        for at in range(per):
            grads[part, at % 2, chunk * (per // 2) + at // 2] = scaled[at * piece : (at + 1) * piece]

    def settle_up(chunk, carry):
        lanes = pl.ds(pl.multiple_of(chunk * 128, 128), 128)
        weights = wup_all[lanes, :].astype(WIDE)
        settle(chunk, 0, g_up[:, lanes].T, weights, sum_units, prm_all[:, lanes].T)
        return carry

    lax.fori_loop(0, D // 128, settle_up, 0)
    send_grads[0].start()

    def partial(at):
        shard, slot = shard_of(at), lax.rem(at, 2)
        heads = tokens_in[shard]
        activated = units_in[shard, :, 0:units]
        g_hidden = units_in[shard, :, units : 2 * units]
        part_out = dot(heads, w_heads_out[...]) + dot(activated, wdown_part[...])
        part_back = dot(heads, w_heads_back[...]) * prm_all[0:1, :] + dot(
            g_hidden, wup_all[...], NT
        ) * prm_all[2:3, :]

        @pl.when(at + 1 < count)
        def _():
            for copy in load(at + 1):
                copy.start()

        for copy in load(at):
            copy.wait()
        g_wout[...] += dot(turned_in[shard, 0:HD, :], stream[1, slot])
        g_heads[HD:, :] += dot(turned_in[shard, HD:, :], stream[0, slot])
        sum_heads[...] += jnp.sum(heads.astype(WIDE).reshape(rows // 8, 8, 4 * HD), axis=0)
        return part_out, part_back

    def to_twin(slot):
        return pltpu.make_async_remote_copy(
            give_buf.at[slot],
            sum_buf.at[slot],
            send_sem.at[0, slot],
            recv_twin.at[slot],
            device_id=here.twin,
            device_id_type=MESH,
        )

    def to_beside(to_z):
        return pltpu.make_async_remote_copy(
            sum_buf.at[to_z],
            beside_buf.at[to_z],
            send_sem.at[1, to_z],
            recv_beside.at[to_z],
            device_id=here.beside,
            device_id_type=MESH,
        )

    def to_above(to_z):
        return pltpu.make_async_remote_copy(
            sum_buf.at[depth + to_z],
            line_buf.at[to_z],
            send_sem.at[2, to_z],
            recv_z.at[to_z],
            device_id=here.above,
            device_id_type=MESH,
        )

    def over_slot(to_z, at_z):
        return jnp.where(to_z == at_z, depth, to_z)

    def to_below(to_z):
        return pltpu.make_async_remote_copy(
            sum_buf.at[depth + to_z],
            line_buf.at[over_slot(to_z, z - 1)],
            send_sem.at[2, to_z],
            recv_z.at[over_slot(to_z, z - 1)],
            device_id=here.below,
            device_id_type=MESH,
        )

    def from_above(to_z):
        slot = over_slot(to_z, z)
        return pltpu.make_async_remote_copy(
            sum_buf.at[depth + to_z],
            line_buf.at[slot],
            send_sem.at[2, to_z],
            recv_z.at[slot],
            device_id=here.above,
            device_id_type=MESH,
        )

    def produce(at, carry):
        to_z = pick2(z, at // 4, order)
        kind = lax.rem(at, 4)
        home = lax.rem(kind, 2)
        slot = home * depth + to_z
        part_out, part_back = partial(at)

        @pl.when(kind < 2)
        def _():
            give_buf[slot, 0:rows, :] = part_out.astype(NARROW)
            give_buf[slot, rows : 2 * rows, :] = part_back.astype(NARROW)
            to_twin(slot).start()

        @pl.when(kind >= 2)
        def _():
            to_twin(slot).wait_recv()
            sum_buf[slot, 0:rows, :] = (
                part_out + sum_buf[slot, 0:rows, :].astype(WIDE)
            ).astype(NARROW)
            sum_buf[slot, rows : 2 * rows, :] = (
                part_back + sum_buf[slot, rows : 2 * rows, :].astype(WIDE)
            ).astype(NARROW)

        @pl.when(kind == 2)
        def _():
            to_beside(to_z).start()

        return carry

    lax.fori_loop(0, 4 * depth, produce, 0)
    send_wout.start()
    sum_row = jnp.sum(sum_heads[...], axis=0, keepdims=True)

    def settle_qkv(chunk, carry):
        lanes = pl.ds(pl.multiple_of(chunk * 128, 128), 128)
        weights = w_heads_back[:, lanes].astype(WIDE).T
        settle(chunk, 1, g_heads[:, lanes].T, weights, sum_row, prm_all[:, lanes].T)
        return carry

    lax.fori_loop(0, D // 128, settle_qkv, 0)
    send_grads[1].start()

    def post(part, to_c):
        return pltpu.make_async_remote_copy(
            mail.at[part, to_c],
            inbox.at[part, c],
            mail_send.at[part, to_c],
            mail_recv.at[part, c],
            device_id=(to_c, x),
            device_id_type=MESH,
        )

    def collect(part, from_c):
        return pltpu.make_async_remote_copy(
            mail.at[part, from_c],
            inbox.at[part, from_c],
            mail_send.at[part, from_c],
            mail_recv.at[part, from_c],
            device_id=(from_c, x),
            device_id_type=MESH,
        )

    def mail_out(part):
        send_grads[part].wait_recv()

        def fold(to_c, carry):
            mail[part, to_c] = (grads[part, x, to_c] + grads_in[part, to_c]).astype(NARROW)
            return carry

        lax.fori_loop(0, count, fold, 0)

        def start(offset, carry):
            post(part, lax.rem(c + offset, count)).start()
            return carry

        lax.fori_loop(1, count, start, 0)
        inbox[part, c] = mail[part, c]

    mail_out(0)

    def chain(at, carry):
        to_z = pick2(z, at, order)
        slot = depth + to_z
        to_beside(to_z).wait_recv()

        def add(incoming):
            for part in range(4):
                span = slice(part * rows // 2, (part + 1) * rows // 2)
                total = sum_buf[slot, span, :].astype(WIDE) + beside_buf[to_z, span, :].astype(WIDE)
                if incoming:
                    total = total + line_buf[to_z, span, :].astype(WIDE)
                sum_buf[slot, span, :] = total.astype(NARROW)

        @pl.when(to_z > z)
        def _():
            @pl.when(here.has_below)
            def _():
                to_above(to_z).wait_recv()
                add(True)

            @pl.when(jnp.logical_not(here.has_below))
            def _():
                add(False)

            to_above(to_z).start()

        @pl.when(to_z < z)
        def _():
            @pl.when(here.has_above)
            def _():
                from_above(to_z).wait_recv()
                add(True)

            @pl.when(jnp.logical_not(here.has_above))
            def _():
                add(False)

            to_below(to_z).start()

        return carry

    lax.fori_loop(0, 1, chain, 0)
    mail_out(1)
    lax.fori_loop(1, depth, chain, 0)

    @pl.when(here.has_below)
    def _():
        to_above(z).wait_recv()

    @pl.when(jnp.logical_not(here.has_below))
    def _():
        line_buf[z] = jnp.zeros((2 * rows, D), NARROW)

    @pl.when(here.has_above)
    def _():
        from_above(z).wait_recv()

    @pl.when(jnp.logical_not(here.has_above))
    def _():
        line_buf[depth] = jnp.zeros((2 * rows, D), NARROW)

    def total(span):
        return (
            sum_buf[depth + z, span, :].astype(WIDE)
            + beside_buf[z, span, :].astype(WIDE)
            + line_buf[z, span, :].astype(WIDE)
            + line_buf[depth, span, :].astype(WIDE)
        )

    tokens = tok_ref[...].astype(WIDE)
    out_ref[...] = (tokens + total(slice(0, rows))).astype(NARROW)
    average = jnp.mean(tokens, axis=-1, keepdims=True)
    centred = tokens - average
    variance = jnp.mean(centred * centred, axis=-1, keepdims=True)
    rise = lax.rsqrt(variance + EPSILON)
    xhat = centred * rise
    g_xhat = total(slice(rows, 2 * rows))
    along = jnp.mean(g_xhat * xhat, axis=-1, keepdims=True)
    level = jnp.mean(g_xhat, axis=-1, keepdims=True)
    grad_ref[...] = cot_ref[...].astype(WIDE) + rise * (g_xhat - level - xhat * along)

    def finish(to_z, carry):
        to_twin(to_z).wait_send()
        to_twin(depth + to_z).wait_send()
        to_beside(to_z).wait_send()

        @pl.when(to_z > z)
        def _():
            to_above(to_z).wait_send()

        @pl.when(to_z < z)
        def _():
            to_below(to_z).wait_send()

        return carry

    lax.fori_loop(0, depth, finish, 0)

    send_down.wait()
    down_ref[...] = g_down[pl.ds(x * half_down, half_down), :] + down_in[...]
    send_wout.wait()
    wout_ref[...] = g_wout[pl.ds(x * half_wout, half_wout), :] + wout_in[...]

    def close(offset, carry):
        other = lax.rem(c + offset, count)
        for part in range(2):
            collect(part, other).wait_recv()
            post(part, other).wait_send()
        return carry

    lax.fori_loop(1, count, close, 0)
    for part in range(2):
        send_grads[part].wait_send()
    together = jnp.zeros((piece, 128), WIDE)
    for from_c in range(count):
        up_ref[:, from_c * units : (from_c + 1) * units] = inbox[0, from_c].astype(WIDE)
        together = together + inbox[1, from_c, :, 0:128].astype(WIDE)
    vec_ref[...] = together.T[0:8]
    for pair in range(count // 2):
        left = inbox[1, 2 * pair].astype(WIDE)
        right = inbox[1, 2 * pair + 1].astype(WIDE)
        for part in range(3):
            lanes = slice((part + 1) * HD, (part + 2) * HD)
            to = part * D + pair * 128
            qkv_ref[:, to : to + 128] = jnp.concatenate([left[:, lanes], right[:, lanes]], axis=1)


def reduce_call(depth, tokens_in, turned_in, units_in, tok, cot, rest, xhat, cot_all):
    rows = tok.shape[0]
    count = depth * 4
    piece = D // (2 * count)
    units = rest[2].shape[1]
    vmem = pl.BlockSpec(memory_space=pltpu.VMEM)
    any_spec = pl.BlockSpec(memory_space=pl.ANY)
    shape = jax.ShapeDtypeStruct
    message = (2 * rows, D)
    return pl.pallas_call(
        functools.partial(reduce_kernel, depth),
        out_shape=(
            shape((rows, D), NARROW),
            shape((rows, D), WIDE),
            shape((piece, 3 * D), WIDE),
            shape((HD // 2, D), WIDE),
            shape((piece, count * units), WIDE),
            shape((units // 2, D), WIDE),
            shape((8, piece), WIDE),
        ),
        in_specs=[vmem] * 13 + [any_spec] * 2,
        out_specs=(vmem,) * 7,
        scratch_shapes=[
            pltpu.VMEM((4 * HD, D), NARROW),
            pltpu.VMEM((4 * HD, D), NARROW),
            pltpu.VMEM((2 * depth,) + message, NARROW),
            pltpu.VMEM((2 * depth,) + message, NARROW),
            pltpu.VMEM((depth,) + message, NARROW),
            pltpu.VMEM((depth + 1,) + message, NARROW),
            pltpu.VMEM((2, 2, rows, D), NARROW),
            pltpu.VMEM((4 * HD, D), WIDE),
            pltpu.VMEM((HD, D), WIDE),
            pltpu.VMEM((8, 4 * HD), WIDE),
            pltpu.VMEM((D, 128), WIDE),
            pltpu.VMEM((2, 2, count, piece, 256), WIDE),
            pltpu.VMEM((2, count, piece, 256), WIDE),
            pltpu.VMEM((2, count, piece, 256), NARROW),
            pltpu.VMEM((2, count, piece, 256), NARROW),
            pltpu.VMEM((HD // 2, D), WIDE),
            pltpu.VMEM((units // 2, D), WIDE),
            pltpu.SemaphoreType.DMA((3, 2 * depth)),
            pltpu.SemaphoreType.DMA((2 * depth,)),
            pltpu.SemaphoreType.DMA((depth,)),
            pltpu.SemaphoreType.DMA((depth + 1,)),
            pltpu.SemaphoreType.DMA((2, 2)),
            pltpu.SemaphoreType.DMA((4,)),
            pltpu.SemaphoreType.DMA((4,)),
            pltpu.SemaphoreType.DMA((2, count)),
            pltpu.SemaphoreType.DMA((2, count)),
        ],
        name="reduce_rows",
        compiler_params=pltpu.CompilerParams(
            collective_id=2, has_side_effects=True, vmem_limit_bytes=VMEM_LIMIT
        ),
    )(tokens_in, turned_in, units_in, tok, cot, *rest, xhat, cot_all)


def fast_shards(depth, *arguments):
    (tokens, cotangent, lengths, dealing, gain_one, bias_one, gain_two, bias_two) = arguments[:8]
    w_qkv, w_out, w_up, w_down = arguments[8:]
    groups, local_rows, _ = tokens.shape
    rows = groups * local_rows
    count = depth * 4
    tok = tokens.reshape(rows, D)
    cot = cotangent.reshape(rows, D)
    prm = jnp.stack([gain_one, bias_one, gain_two, bias_two] * 2).astype(WIDE)

    openings = jnp.cumsum(lengths, axis=1) - lengths
    natural = (dealing.T[:, :, None] * BLK + jnp.arange(BLK, dtype=jnp.int32)[None, None, :]).reshape(
        count, rows
    )
    start_rows = jnp.repeat(openings.T, BLK, axis=1)[:, None, :]
    opening = jnp.max(jnp.where(start_rows <= natural[None], start_rows, 0), axis=0)
    place = (natural - opening).astype(WIDE)
    frequency = 10000.0 ** (-2.0 * jnp.arange(ROT // 2, dtype=WIDE) / ROT)
    angles = place[:, None, :] * frequency[None, :, None]
    turn = jnp.concatenate([jnp.cos(angles), jnp.sin(angles)], axis=1)

    (heads, units, xhat, cot_all, g_up, g_down, g_sum, wqkv_t, wup_all, wdown_part, wout_part, prm_all) = (
        gather_call(depth, tok, cot, prm, turn, w_qkv, w_out, w_up, w_down)
    )
    turned, by_token = attention_call(lengths, dealing, heads, turn)
    rest = (prm_all, wqkv_t, wup_all, wdown_part, wout_part, g_up, g_down, g_sum)
    out, grad_tokens, qkv_part, out_part, up_part, down_part, vector_part = reduce_call(
        depth, by_token, turned, units, tok, cot, rest, xhat, cot_all
    )
    return (
        out.reshape(tokens.shape),
        grad_tokens.reshape(tokens.shape),
        vector_part[0],
        vector_part[1],
        vector_part[2],
        vector_part[3],
        qkv_part,
        out_part,
        up_part,
        down_part,
    )


def solution(mesh):
    placed = (
        P("wsh", "ctx", None),
        P("wsh", "ctx", None),
        P("wsh", None),
        P("wsh", None),
        P("wsh"),
        P("wsh"),
        P("wsh"),
        P("wsh"),
        P("wsh", None),
        P("wsh", None),
        P("wsh", None),
        P("wsh", None),
    )
    ctx_size = mesh.shape["ctx"]
    by_heads = ctx_size == H and mesh.shape["wsh"] == 2
    body = functools.partial(fast_shards, ctx_size // 4) if by_heads else shards
    return jax.shard_map(
        body,
        mesh=mesh,
        in_specs=placed,
        out_specs=(
            P("wsh", "ctx", None),
            P("wsh", "ctx", None),
            P(("ctx", "wsh")),
            P(("ctx", "wsh")),
            P(("ctx", "wsh")),
            P(("ctx", "wsh")),
            P(("ctx", "wsh"), None),
            P(("ctx", "wsh"), None),
            P(("ctx", "wsh"), None),
            P(("ctx", "wsh"), None),
        ),
        check_vma=False,
    )
```

```python
import functools

import jax
import jax.numpy as jnp
from jax import lax
from jax.experimental import pallas as pl
from jax.experimental.pallas import tpu as pltpu
from jax.sharding import PartitionSpec as P

D = 1024
H = 16
HD = 64
ROT = 16
BLK = 128


EPSILON = 1e-05
MASKED = -1e30
WIDE = jnp.float32
NARROW = jnp.bfloat16


def norm_layer(values_in, scale_by, shift_by):
    average = jnp.mean(values_in, axis=-1, keepdims=True)
    centred = values_in - average
    variance = jnp.mean(centred * centred, axis=-1, keepdims=True)
    return centred * lax.rsqrt(variance + EPSILON) * scale_by + shift_by


def rotate(values_in, places):
    split_at = ROT // 2
    frequency = 10000.0 ** (-2.0 * jnp.arange(split_at, dtype=WIDE) / ROT)
    angles = places.astype(WIDE)[:, None] * frequency[None, :]
    cosine_table = jnp.cos(angles)[:, None, :]
    sine_table = jnp.sin(angles)[:, None, :]
    first_half = values_in[..., :split_at]
    second_half = values_in[..., split_at:ROT]
    return jnp.concatenate(
        [
            first_half * cosine_table - second_half * sine_table,
            second_half * cosine_table + first_half * sine_table,
            values_in[..., ROT:],
        ],
        axis=-1,
    )


def natural_rows(dealing_row, offset_row, row_count):
    ordinal = offset_row + jnp.arange(row_count, dtype=jnp.int32)
    table_ids = jnp.arange(dealing_row.shape[0], dtype=jnp.int32)
    picked = jnp.sum(
        jnp.where((ordinal // BLK)[:, None] == table_ids[None, :], dealing_row[None, :], 0), axis=1
    )
    return picked * BLK + ordinal % BLK


def sequence_openings(natural, lengths_row):
    openings = jnp.cumsum(lengths_row) - lengths_row
    return jnp.max(jnp.where(openings[None, :] <= natural[:, None], openings[None, :], 0), axis=1)


def score_block(queries, block_keys, offset_row, natural_q, opening_q, dealing_row):
    row_count = block_keys.shape[0]
    key_natural = natural_rows(dealing_row, offset_row, row_count)
    scores = jnp.einsum(
        "qhd,khd->hqk", queries, block_keys.reshape(row_count, H, HD), preferred_element_type=WIDE
    ) * HD ** (-0.5)
    allowed = (key_natural[None, :] <= natural_q[:, None]) & (
        key_natural[None, :] >= opening_q[:, None]
    )
    return (scores, allowed[None])


def fold_blocks(step_fn, state_in, arrays):
    row_count = arrays[0].shape[0]
    block_width = 1024
    stacked = tuple(
        (
            member.reshape((row_count // block_width, block_width) + member.shape[1:])
            for member in arrays
        )
    )
    offsets = jnp.arange(row_count // block_width, dtype=jnp.int32) * block_width

    def inner_step(state_now, block_item):
        return (step_fn(state_now, block_item[0], block_item[1]), None)

    state_out, _ = lax.scan(inner_step, state_in, (stacked, offsets))
    return state_out


def project(tokens_f, weights, places):
    w_qkv, w_out, w_up, w_down, gain_one, bias_one, gain_two, bias_two = weights
    all_rows = tokens_f.shape[0]
    normed_one = norm_layer(tokens_f, gain_one.astype(WIDE), bias_one.astype(WIDE)).astype(NARROW)
    normed_two = norm_layer(tokens_f, gain_two.astype(WIDE), bias_two.astype(WIDE)).astype(NARROW)
    mixed = jnp.dot(normed_one, w_qkv, preferred_element_type=WIDE).reshape(all_rows, 3, H, HD)
    queries = rotate(mixed[:, 0], places).astype(NARROW)
    keys_here = rotate(mixed[:, 1], places).astype(NARROW).reshape(all_rows, D)
    values_here = mixed[:, 2].astype(NARROW).reshape(all_rows, D)
    hidden = jnp.dot(normed_two, w_up, preferred_element_type=WIDE)
    activated = jax.nn.gelu(hidden, approximate=False).astype(NARROW)
    return (normed_one, normed_two, queries, keys_here, values_here, hidden, activated)


def attend(queries, keys_here, values_here, natural_q, opening_q, dealing_row):
    local_rows = queries.shape[0]

    def max_step(state_in, block_arrays, offset_row):
        row_top, row_total = state_in
        scores, allowed = score_block(
            queries, block_arrays[0], offset_row, natural_q, opening_q, dealing_row
        )
        new_top = jnp.maximum(row_top, jnp.max(jnp.where(allowed, scores, MASKED), axis=-1))
        kept_terms = jnp.where(allowed, jnp.exp(scores - new_top[..., None]), 0.0)
        return (new_top, row_total * jnp.exp(row_top - new_top) + jnp.sum(kept_terms, axis=-1))

    start_state = (jnp.full((H, local_rows), MASKED, WIDE), jnp.zeros((H, local_rows), WIDE))
    row_top, row_total = fold_blocks(
        max_step, start_state, (lax.all_gather(keys_here, "ctx", axis=0, tiled=True),)
    )
    log_total = row_top + jnp.log(row_total)

    def value_step(state_in, block_arrays, offset_row):
        scores, allowed = score_block(
            queries, block_arrays[0], offset_row, natural_q, opening_q, dealing_row
        )
        soft_probs = jnp.where(allowed, jnp.exp(scores - log_total[..., None]), 0.0).astype(NARROW)
        row_count = block_arrays[1].shape[0]
        return state_in + jnp.einsum(
            "hqk,khd->qhd",
            soft_probs,
            block_arrays[1].reshape(row_count, H, HD),
            preferred_element_type=WIDE,
        )

    attended = fold_blocks(
        value_step,
        jnp.zeros((local_rows, H, HD), WIDE),
        (
            lax.all_gather(keys_here, "ctx", axis=0, tiled=True),
            lax.all_gather(values_here, "ctx", axis=0, tiled=True),
        ),
    )
    return (attended, log_total)


def attention_back(
    queries,
    keys_here,
    values_here,
    g_attended,
    row_dot,
    log_total,
    natural_q,
    opening_q,
    dealing_row,
):
    local_rows = queries.shape[0]
    scale_factor = HD ** (-0.5)
    gathered_keys, gathered_values = (
        lax.all_gather(keys_here, "ctx", axis=0, tiled=True),
        lax.all_gather(values_here, "ctx", axis=0, tiled=True),
    )
    group_rows = gathered_keys.shape[0]
    key_span = 1024

    def key_block(state_in, block_item):
        block_keys, block_values, offset_row = block_item
        scores, allowed = score_block(
            queries, block_keys, offset_row, natural_q, opening_q, dealing_row
        )
        soft_probs = jnp.where(allowed, jnp.exp(scores - log_total[..., None]), 0.0)
        g_probs = jnp.einsum(
            "qhd,khd->hqk",
            g_attended,
            block_values.reshape(key_span, H, HD),
            preferred_element_type=WIDE,
        )
        g_scores = (soft_probs * (g_probs - row_dot[..., None])).astype(NARROW)
        state_out = (
            state_in
            + jnp.einsum(
                "hqk,khd->qhd",
                g_scores,
                block_keys.reshape(key_span, H, HD),
                preferred_element_type=WIDE,
            )
            * scale_factor
        )
        key_terms = (
            jnp.einsum("hqk,qhd->khd", g_scores, queries, preferred_element_type=WIDE)
            * scale_factor
        )
        value_terms = jnp.einsum(
            "hqk,qhd->khd", soft_probs.astype(NARROW), g_attended, preferred_element_type=WIDE
        )
        return (
            state_out,
            jnp.concatenate(
                [key_terms.reshape(key_span, D), value_terms.reshape(key_span, D)], axis=1
            ),
        )

    block_total = group_rows // key_span
    block_starts = jnp.arange(block_total, dtype=jnp.int32) * key_span
    stacked_blocks = (
        gathered_keys.reshape(block_total, key_span, D),
        gathered_values.reshape(block_total, key_span, D),
        block_starts,
    )
    g_queries, stacked_terms = lax.scan(
        key_block, jnp.zeros((local_rows, H, HD), WIDE), stacked_blocks
    )
    g_pairs = lax.psum_scatter(
        stacked_terms.reshape(group_rows, 2 * D), "ctx", scatter_dimension=0, tiled=True
    )
    g_keys = g_pairs[:, :D].reshape(local_rows, H, HD)
    g_values = g_pairs[:, D:].reshape(local_rows, H, HD)
    return (g_queries, g_keys, g_values)


def shards(
    tokens,
    cotangent,
    lengths,
    dealing,
    gain_one,
    bias_one,
    gain_two,
    bias_two,
    w_qkv,
    w_out,
    w_up,
    w_down,
):
    group_count = tokens.shape[0]
    local_rows = tokens.shape[1]
    all_rows = group_count * local_rows
    tokens_f = tokens.reshape(all_rows, D).astype(WIDE)
    first_row = lax.axis_index("ctx") * local_rows
    natural_list = [
        natural_rows(dealing[member], first_row, local_rows) for member in range(group_count)
    ]
    opening_list = [
        sequence_openings(natural_list[member], lengths[member]) for member in range(group_count)
    ]
    places = jnp.concatenate(
        [natural_list[member] - opening_list[member] for member in range(group_count)], axis=0
    )

    def forward():
        weights = (
            lax.all_gather(w_qkv, "wsh", axis=0, tiled=True),
            lax.all_gather(w_out, "wsh", axis=0, tiled=True),
            lax.all_gather(w_up, "wsh", axis=0, tiled=True),
            lax.all_gather(w_down, "wsh", axis=0, tiled=True),
            lax.all_gather(gain_one, "wsh", axis=0, tiled=True),
            lax.all_gather(bias_one, "wsh", axis=0, tiled=True),
            lax.all_gather(gain_two, "wsh", axis=0, tiled=True),
            lax.all_gather(bias_two, "wsh", axis=0, tiled=True),
        )
        local_parts = project(tokens_f, weights, places)
        attended_list = []
        total_list = []
        for member in range(group_count):
            rows_from = member * local_rows
            attended_one, total_one = attend(
                local_parts[2][rows_from : rows_from + local_rows],
                local_parts[3][rows_from : rows_from + local_rows],
                local_parts[4][rows_from : rows_from + local_rows],
                natural_list[member],
                opening_list[member],
                dealing[member],
            )
            attended_list.append(attended_one)
            total_list.append(total_one)
        return (weights, local_parts, jnp.concatenate(attended_list, axis=0), total_list)

    weights, local_parts, attended, total_list = forward()
    attended_low = attended.reshape(all_rows, D).astype(NARROW)
    mixed_out = (
        tokens_f
        + jnp.dot(attended_low, weights[1], preferred_element_type=WIDE)
        + jnp.dot(local_parts[6], weights[3], preferred_element_type=WIDE)
    )
    out = mixed_out.astype(NARROW)
    weights, local_parts, attended, total_list = forward()
    attended_low = attended.reshape(all_rows, D).astype(NARROW)
    w_qkv_all, w_out_all, w_up_all, w_down_all = (weights[0], weights[1], weights[2], weights[3])
    normed_one, normed_two, queries, keys_here, values_here, hidden, activated = local_parts
    grad_rows = cotangent.reshape(all_rows, D)
    grad_f = grad_rows.astype(WIDE)
    g_down = jnp.einsum("tf,td->fd", activated, grad_rows, preferred_element_type=WIDE)
    g_activated = jnp.einsum("td,fd->tf", grad_rows, w_down_all, preferred_element_type=WIDE)
    _, gelu_back = jax.vjp(lambda pre_act: jax.nn.gelu(pre_act, approximate=False), hidden)
    g_hidden = gelu_back(g_activated)[0].astype(NARROW)
    g_up = jnp.einsum("td,tf->df", normed_two, g_hidden, preferred_element_type=WIDE)
    g_normed_two = jnp.einsum("tf,df->td", g_hidden, w_up_all, preferred_element_type=WIDE)
    g_weight_out = jnp.einsum("te,td->ed", attended_low, grad_rows, preferred_element_type=WIDE)
    g_attended = (
        jnp.einsum("td,ed->te", grad_rows, w_out_all, preferred_element_type=WIDE)
        .astype(NARROW)
        .reshape(all_rows, H, HD)
    )
    row_dot = jnp.einsum("qhd,qhd->hq", g_attended.astype(WIDE), attended)
    query_grads = []
    key_grads = []
    value_grads = []
    for member in range(group_count):
        rows_from = member * local_rows
        rows_to = rows_from + local_rows
        g_q, g_k, g_v = attention_back(
            queries[rows_from:rows_to],
            keys_here[rows_from:rows_to],
            values_here[rows_from:rows_to],
            g_attended[rows_from:rows_to],
            row_dot[:, rows_from:rows_to],
            total_list[member],
            natural_list[member],
            opening_list[member],
            dealing[member],
        )
        query_grads.append(g_q)
        key_grads.append(g_k)
        value_grads.append(g_v)
    g_queries = jnp.concatenate(query_grads, axis=0)
    g_keys = jnp.concatenate(key_grads, axis=0)
    g_values = jnp.concatenate(value_grads, axis=0)
    _, rotate_back = jax.vjp(
        lambda pre_rot: rotate(pre_rot, places), jnp.zeros((all_rows, H, HD), WIDE)
    )
    g_queries_pre = rotate_back(g_queries)[0]
    g_keys_pre = rotate_back(g_keys)[0]
    g_mixed = (
        jnp.stack([g_queries_pre, g_keys_pre, g_values], axis=1)
        .reshape(all_rows, 3 * D)
        .astype(NARROW)
    )
    g_qkv = jnp.einsum("td,te->de", normed_one, g_mixed, preferred_element_type=WIDE)
    g_normed_one = jnp.einsum("te,de->td", g_mixed, w_qkv_all, preferred_element_type=WIDE)

    def both_norms(tokens_in, scale_one, shift_one, scale_two, shift_two):
        return (
            norm_layer(tokens_in, scale_one, shift_one),
            norm_layer(tokens_in, scale_two, shift_two),
        )

    _, norm_back = jax.vjp(
        both_norms,
        tokens_f,
        weights[4].astype(WIDE),
        weights[5].astype(WIDE),
        weights[6].astype(WIDE),
        weights[7].astype(WIDE),
    )
    g_tokens, g_scale_one, g_shift_one, g_scale_two, g_shift_two = norm_back(
        (g_normed_one, g_normed_two)
    )
    grad_tokens = g_tokens + grad_f
    summed = (
        lax.psum_scatter(g_qkv, ("ctx", "wsh"), scatter_dimension=0, tiled=True),
        lax.psum_scatter(g_weight_out, ("ctx", "wsh"), scatter_dimension=0, tiled=True),
        lax.psum_scatter(g_up, ("ctx", "wsh"), scatter_dimension=0, tiled=True),
        lax.psum_scatter(g_down, ("ctx", "wsh"), scatter_dimension=0, tiled=True),
        lax.psum_scatter(g_scale_one, ("ctx", "wsh"), scatter_dimension=0, tiled=True),
        lax.psum_scatter(g_shift_one, ("ctx", "wsh"), scatter_dimension=0, tiled=True),
        lax.psum_scatter(g_scale_two, ("ctx", "wsh"), scatter_dimension=0, tiled=True),
        lax.psum_scatter(g_shift_two, ("ctx", "wsh"), scatter_dimension=0, tiled=True),
    )
    return (
        out.reshape(group_count, local_rows, D),
        grad_tokens.reshape(group_count, local_rows, D),
        summed[4],
        summed[5],
        summed[6],
        summed[7],
        summed[0],
        summed[1],
        summed[2],
        summed[3],
    )


MESH = pl.DeviceIdType.MESH
NT = (((1,), (1,)), ((), ()))
TN = (((0,), (0,)), ((), ()))
VMEM_LIMIT = 60 * 1024 * 1024


def dot(a, b, dims=(((1,), (0,)), ((), ()))):
    return lax.dot_general(a, b, dims, preferred_element_type=WIDE)


def pick(index, table):
    result = jnp.int32(table[0])
    for at in range(1, len(table)):
        result = jnp.where(index == at, jnp.int32(table[at]), result)
    return result


def near_first(depth):
    return [sorted(range(depth), key=lambda to, z=z: (abs(to - z), to)) for z in range(depth)]


def pick2(row, column, table):
    result = pick(column, table[0])
    for at in range(1, len(table)):
        result = jnp.where(row == at, pick(column, table[at]), result)
    return result


class Place:
    def __init__(self, depth):
        self.depth = depth
        self.c = lax.axis_index("ctx")
        self.x = lax.axis_index("wsh")
        self.core = lax.rem(self.c, 2)
        self.y = lax.rem(self.c // 2, 2)
        self.z = self.c // 4
        self.beside = (self.at(self.z, 1 - self.y, self.core), self.x)
        self.twin = (self.at(self.z, self.y, 1 - self.core), self.x)
        self.above = (self.at(self.z + 1, self.y, self.core), self.x)
        self.below = (self.at(self.z - 1, self.y, self.core), self.x)
        self.across = (self.c, 1 - self.x)
        self.has_above = self.z < depth - 1
        self.has_below = self.z > 0

    def at(self, z, y, core):
        return (z * 2 + y) * 2 + core

    def greet(self):
        barrier = pltpu.get_barrier_semaphore()

        def hail(device):
            pl.semaphore_signal(barrier, inc=1, device_id=device, device_id_type=MESH)

        hail(self.beside)
        hail(self.twin)
        hail(self.across)

        @pl.when(self.has_above)
        def _():
            hail(self.above)

        @pl.when(self.has_below)
        def _():
            hail(self.below)

        pl.semaphore_wait(
            barrier, 3 + self.has_above.astype(jnp.int32) + self.has_below.astype(jnp.int32)
        )


    def greet_all(self):
        barrier = pltpu.get_barrier_semaphore()
        count = 4 * self.depth
        pl.semaphore_signal(barrier, inc=1, device_id=self.across, device_id_type=MESH)

        def hail(offset, carry):
            device = (lax.rem(self.c + offset, count), self.x)
            pl.semaphore_signal(barrier, inc=1, device_id=device, device_id_type=MESH)
            return carry

        lax.fori_loop(1, count, hail, 0)
        pl.semaphore_wait(barrier, count)


FREQUENCY = tuple(10000.0 ** (-2.0 * i / ROT) for i in range(ROT // 2))


def turning(place):
    row = lax.broadcasted_iota(jnp.int32, (ROT // 2, 1), 0)
    frequency = jnp.full((ROT // 2, 1), FREQUENCY[0], WIDE)
    for at in range(1, ROT // 2):
        frequency = jnp.where(row == at, FREQUENCY[at], frequency)
    angles = place.astype(WIDE) * frequency
    return jnp.cos(angles), jnp.sin(angles)


def starts_of(lengths_ref, group):
    starts = []
    so_far = jnp.int32(0)
    for piece in range(lengths_ref.shape[1] - 1):
        so_far = so_far + lengths_ref[group, piece]
        starts.append(so_far)
    return starts


def opening_of(natural, starts):
    opening = jnp.zeros(natural.shape, jnp.int32)
    for start in starts:
        opening = jnp.where(natural >= start, start, opening)
    return opening


def find_blocks(dealing_ref, found):
    groups, blocks = dealing_ref.shape
    for group in range(groups):

        def look(block, carry):
            where = jnp.int32(0)
            for at in range(blocks):
                where = jnp.where(dealing_ref[group, at] == block, jnp.int32(at), where)
            found[group, block] = where
            return carry

        lax.fori_loop(0, blocks, look, 0)


def gather_kernel(
    depth,
    lengths_ref,
    dealing_ref,
    tok_ref,
    cot_ref,
    gain_one_ref,
    bias_one_ref,
    gain_two_ref,
    bias_two_ref,
    wqkv_ref,
    wout_ref,
    wup_ref,
    wdown_ref,
    heads_out,
    units_out,
    xhat_out,
    cot_out,
    attended_out,
    total_out,
    g_up,
    g_down,
    g_sum,
    wqkv_t,
    wup_all,
    wdown_part,
    wout_part,
    prm_all,
    both,
    xhat_all,
    heads_buf,
    units_buf,
    slope_buf,
    wide,
    k_rows,
    wq_buf,
    prm_buf,
    found,
    in_sem,
    w_sem,
    wsend_sem,
    wrecv_sem,
    send_sem,
    recv_sem,
    out_sem,
):
    here = Place(depth)
    c, x, y, z, core = here.c, here.x, here.y, here.z, here.core
    count = depth * 4
    rows = tok_ref.shape[0]
    groups = dealing_ref.shape[0]
    units = wup_all.shape[1]
    half = prm_buf.shape[2]
    order = near_first(depth)

    own_in = (
        pltpu.make_async_copy(tok_ref, both.at[0, c], in_sem.at[0]),
        pltpu.make_async_copy(cot_ref, both.at[1, c], in_sem.at[1]),
    )
    for copy in own_in:
        copy.start()
    prm_rows = [
        ref[...].astype(WIDE) for ref in (gain_one_ref, bias_one_ref, gain_two_ref, bias_two_ref)
    ]
    prm_buf[x] = jnp.concatenate(prm_rows + prm_rows, axis=0)

    pair = c // 2
    per_half = count // 2
    owner = c // per_half
    inside = lax.rem(c, per_half)
    shared = []
    for part in range(3):
        shared.append(
            (
                wqkv_ref.at[:, pl.ds(pl.multiple_of(part * D + pair * 128, 128), 128)],
                wq_buf.at[x, part],
            )
        )
    shared.append(
        (
            wup_ref.at[:, pl.ds(pl.multiple_of(c * units, 128), units)],
            wup_all.at[pl.ds(pl.multiple_of(x * half, 128), half)],
        )
    )
    held = (
        (wdown_ref.at[pl.ds(pl.multiple_of(inside * units, 128), units)], wdown_part),
        (wout_ref.at[pl.ds(pl.multiple_of(inside * HD, HD), HD)], wout_part),
    )
    is_owner = owner == x
    for at, (source, place) in enumerate(shared):
        pltpu.make_async_copy(source, place, w_sem.at[at]).start()

    @pl.when(is_owner)
    def _():
        for at, (source, place) in enumerate(held):
            pltpu.make_async_copy(source, place, w_sem.at[5 + at]).start()

    here.greet()

    def remote(source, place, at):
        return pltpu.make_async_remote_copy(
            source,
            place,
            wsend_sem.at[at],
            wrecv_sem.at[at],
            device_id=here.across,
            device_id_type=MESH,
        )

    prm_copy = remote(prm_buf.at[x], prm_buf.at[x], 4)
    prm_copy.start()
    for at, (source, place) in enumerate(shared):
        remote(source, place, at).start()

    @pl.when(is_owner)
    def _():
        for at, (source, place) in enumerate(held):
            remote(source, place, 5 + at).start()

    def passing(what, shard, way):
        device = (here.beside, here.twin, here.above, here.below)[way]
        return pltpu.make_async_remote_copy(
            both.at[what, shard],
            both.at[what, shard],
            send_sem.at[what, way, shard],
            recv_sem.at[what, shard],
            device_id=device,
            device_id_type=MESH,
        )

    def onward(what, shard, from_z):
        passing(what, shard, 0).start()

        @pl.when(jnp.logical_and(from_z <= z, here.has_above))
        def _():
            passing(what, shard, 2).start()

        @pl.when(jnp.logical_and(from_z >= z, here.has_below))
        def _():
            passing(what, shard, 3).start()

        passing(what, shard, 1).start()

    own_in[0].wait()
    onward(0, c, z)
    own_in[1].wait()
    find_blocks(dealing_ref, found)

    for at, (source, place) in enumerate(shared):
        pltpu.make_async_copy(source, place, w_sem.at[at]).wait()
        remote(source, place, at).wait_recv()
    prm_copy.wait_recv()

    @pl.when(is_owner)
    def _():
        for at, (source, place) in enumerate(held):
            pltpu.make_async_copy(source, place, w_sem.at[5 + at]).wait()

    @pl.when(jnp.logical_not(is_owner))
    def _():
        for at, (source, place) in enumerate(held):
            remote(source, place, 5 + at).wait_recv()

    odd = lax.rem(c, 2) == 1
    for side in range(2):
        prm_all[:, side * half : (side + 1) * half] = prm_buf[side]
        for part in range(3):
            turned = wq_buf[side, part].astype(WIDE).T
            chosen = jnp.where(odd, turned[HD:], turned[:HD])
            wqkv_t[part * HD : (part + 1) * HD, side * half : (side + 1) * half] = chosen.astype(
                NARROW
            )
    g_up[...] = jnp.zeros_like(g_up)
    g_down[...] = jnp.zeros_like(g_down)
    g_sum[...] = jnp.zeros_like(g_sum)

    kept = (
        (xhat_all, xhat_out),
        (both.at[1], cot_out),
        (heads_buf, heads_out),
        (units_buf, units_out),
    )

    def copy_out(at, shard):
        source, place = kept[at]
        return pltpu.make_async_copy(source.at[shard], place.at[shard], out_sem.at[at, shard])

    def ahead(shard):
        tokens = both[0, shard].astype(WIDE)
        average = jnp.mean(tokens, axis=-1, keepdims=True)
        centred = tokens - average
        variance = jnp.mean(centred * centred, axis=-1, keepdims=True)
        xhat = centred * lax.rsqrt(variance + EPSILON)
        xhat_all[shard] = xhat.astype(NARROW)
        n_one = (xhat * prm_all[0:1, :] + prm_all[1:2, :]).astype(NARROW)
        n_two = (xhat * prm_all[2:3, :] + prm_all[3:4, :]).astype(NARROW)
        mixed = dot(wqkv_t[...], n_one, NT)
        places = []
        for group in range(groups):
            natural = dealing_ref[group, shard] * BLK + lax.broadcasted_iota(jnp.int32, (1, BLK), 1)
            places.append(natural - opening_of(natural, starts_of(lengths_ref, group)))
        cosine, sine = turning(jnp.concatenate(places, axis=1))
        pieces = []
        for base in (0, HD):
            first, second = mixed[base : base + 8], mixed[base + 8 : base + 16]
            pieces += [
                first * cosine - second * sine,
                second * cosine + first * sine,
                mixed[base + 16 : base + HD],
            ]
        pieces.append(mixed[2 * HD : 3 * HD])
        heads_buf[shard, 0 : 3 * HD, :] = jnp.concatenate(pieces, axis=0).astype(NARROW)
        hidden = dot(n_two, wup_all[...])
        spread = 0.5 * (1.0 + lax.erf(hidden * (0.5**0.5)))
        units_buf[shard, :, 0:units] = (hidden * spread).astype(NARROW)
        slope_buf[shard] = spread + hidden * (jnp.exp(hidden * hidden * -0.5) * 0.3989422804014327)
        copy_out(0, shard).start()

    def behind(shard):
        cotangent = both[1, shard]
        heads_buf[shard, 3 * HD : 4 * HD, :] = dot(wout_part[...], cotangent, NT).astype(NARROW)
        g_hidden = (dot(cotangent, wdown_part[...], NT) * slope_buf[shard]).astype(NARROW)
        units_buf[shard, :, units : 2 * units] = g_hidden
        g_up[...] += dot(g_hidden, xhat_all[shard], TN)
        g_down[...] += dot(units_buf[shard, :, 0:units], cotangent, TN)
        g_sum[...] += jnp.sum(g_hidden.astype(WIDE).reshape(rows // 8, 8, units), axis=0)
        for at in (1, 2, 3):
            copy_out(at, shard).start()

    inner = jnp.logical_and(here.has_above, here.has_below)

    def sweep(what, work, beside_work):
        def step(at, carry):
            turn_no = at // 4
            kind = lax.rem(at, 4)
            late = jnp.where(kind >= 2, turn_no - 1, turn_no)
            from_z = pick2(z, jnp.clip(late, 0, depth - 1), order)
            next_z = pick2(z, jnp.clip(turn_no + 1, 0, depth - 1), order)
            shard_y = jnp.where(kind >= 2, 1 - y, y)
            shard_core = jnp.where(lax.rem(kind, 2) == 1, 1 - core, core)
            shard = here.at(from_z, shard_y, shard_core)
            live = jnp.logical_and(late >= 0, late < depth)

            early = jnp.logical_and(inner, turn_no == 2)
            is_own = jnp.logical_and(kind == 0, turn_no == 0)
            done = jnp.logical_or(is_own, jnp.logical_and(kind == 0, early))

            @pl.when(jnp.logical_and(live, jnp.logical_not(done)))
            def _():
                passing(what, shard, 1).wait_recv()

            @pl.when(jnp.logical_and(jnp.logical_and(kind == 0, live), jnp.logical_not(done)))
            def _():
                onward(what, shard, from_z)

            @pl.when(jnp.logical_and(kind == 2, live))
            def _():
                passing(what, shard, 1).start()

            @pl.when(jnp.logical_and(jnp.logical_and(kind == 1, turn_no == 1), inner))
            def _():
                following = here.at(next_z, y, core)
                passing(what, following, 1).wait_recv()
                onward(what, following, next_z)

            beside_work(at)

            @pl.when(live)
            def _():
                work(shard)

            return carry

        lax.fori_loop(0, 4 * depth + 4, step, 0)

    def cotangent_too(at):
        @pl.when(at == 4 * (depth - 1) + 1)
        def _():
            onward(1, c, z)

    sweep(0, ahead, cotangent_too)

    spans = count // 2
    span = 2 * BLK

    def bring(at, carry):
        for group in range(groups):
            lanes = slice(group * BLK, (group + 1) * BLK)
            for side in range(2):
                source = found[group, 2 * at + side]
                part = heads_buf[source, 0 : 3 * HD, lanes]
                to = slice(side * BLK, (side + 1) * BLK)
                wide[group, at, 0:HD, to] = (part[0:HD].astype(WIDE) * HD ** (-0.5)).astype(NARROW)
                wide[group, at, HD : 2 * HD, to] = part[2 * HD : 3 * HD]
                k_rows[group, at, to, :] = part[HD : 2 * HD].astype(WIDE).T.astype(NARROW)
        return carry

    lax.fori_loop(0, spans, bring, 0)
    openings = [starts_of(lengths_ref, group) for group in range(groups)]

    def attend(at):
        group = lax.rem(at, groups)
        turn_no = at // groups
        mine = jnp.where(lax.rem(turn_no, 2) == 0, spans - 1 - turn_no // 2, turn_no // 2)
        natural = mine * span + lax.broadcasted_iota(jnp.int32, (1, span), 1)
        opening = opening_of(natural, [jnp.where(group == 0, *pair) for pair in zip(*openings)])
        key_in = lax.broadcasted_iota(jnp.int32, (span, span), 0)
        queries = wide[group, mine, 0:HD, :]

        def add(keys_at, state, allowed):
            top, total, so_far = state
            raw = jnp.where(allowed, dot(k_rows[group, keys_at], queries), MASKED)
            new_top = jnp.maximum(top, jnp.max(raw, axis=0, keepdims=True))
            risen = jnp.exp(raw - new_top)
            fade = jnp.exp(top - new_top)
            total = total * fade + jnp.sum(risen, axis=0, keepdims=True)
            values = wide[group, keys_at, HD : 2 * HD, :]
            return new_top, total, so_far * fade + dot(values, risen.astype(NARROW))

        state = (
            jnp.full((1, span), MASKED, WIDE),
            jnp.zeros((1, span), WIDE),
            jnp.zeros((HD, span), WIDE),
        )
        place = key_in + mine * span
        state = add(mine, state, jnp.logical_and(place <= natural, place >= opening))

        def earlier(back, state):
            keys_at = mine - 1 - back
            return add(keys_at, state, key_in >= opening - keys_at * span)

        top, total, so_far = lax.fori_loop(0, mine, earlier, state)
        attended = so_far / total
        for side in range(2):
            attended_out[group, 2 * mine + side] = attended[:, side * BLK : (side + 1) * BLK]
        total_out[group, mine] = jnp.broadcast_to(top + jnp.log(total), (8, span))

    def attend_too(at):
        @pl.when(at < groups * spans)
        def _():
            attend(at)

    sweep(1, behind, attend_too)

    def finish(shard, carry):
        shard_z = shard // 4
        mine = lax.rem(shard, 2) == core
        column = lax.rem(shard // 2, 2) == y
        for what in range(2):

            @pl.when(mine)
            def _():
                passing(what, shard, 1).wait_send()

            @pl.when(jnp.logical_and(mine, column))
            def _():
                passing(what, shard, 0).wait_send()

                @pl.when(jnp.logical_and(shard_z <= z, here.has_above))
                def _():
                    passing(what, shard, 2).wait_send()

                @pl.when(jnp.logical_and(shard_z >= z, here.has_below))
                def _():
                    passing(what, shard, 3).wait_send()

        for at in range(4):
            copy_out(at, shard).wait()
        return carry

    lax.fori_loop(0, count, finish, 0)
    for at, (source, place) in enumerate(shared):
        remote(source, place, at).wait_send()
    prm_copy.wait_send()

    @pl.when(is_owner)
    def _():
        for at, (source, place) in enumerate(held):
            remote(source, place, 5 + at).wait_send()


def gather_call(depth, lengths, dealing, tok, cot, gains, w_qkv, w_out, w_up, w_down):
    count = depth * 4
    rows = tok.shape[0]
    groups = dealing.shape[0]
    spans, span = count // 2, 2 * BLK
    units = w_up.shape[1] // count
    any_spec = pl.BlockSpec(memory_space=pl.ANY)
    vmem = pl.BlockSpec(memory_space=pltpu.VMEM)
    smem = pl.BlockSpec(memory_space=pltpu.SMEM)
    shape = jax.ShapeDtypeStruct
    return pl.pallas_call(
        functools.partial(gather_kernel, depth),
        out_shape=(
            shape((count, 4 * HD, rows), NARROW),
            shape((count, rows, 2 * units), NARROW),
            shape((count, rows, D), NARROW),
            shape((count, rows, D), NARROW),
            shape((groups, count, HD, BLK), WIDE),
            shape((groups, spans, 8, span), WIDE),
            shape((units, D), WIDE),
            shape((units, D), WIDE),
            shape((8, units), WIDE),
            shape((3 * HD, D), NARROW),
            shape((D, units), NARROW),
            shape((units, D), NARROW),
            shape((HD, D), NARROW),
            shape((8, D), WIDE),
        ),
        in_specs=[smem, smem, any_spec, any_spec] + [vmem] * 4 + [any_spec] * 4,
        out_specs=(any_spec,) * 4 + (vmem,) * 10,
        scratch_shapes=[
            pltpu.VMEM((2, count, rows, D), NARROW),
            pltpu.VMEM((count, rows, D), NARROW),
            pltpu.VMEM((count, 4 * HD, rows), NARROW),
            pltpu.VMEM((count, rows, 2 * units), NARROW),
            pltpu.VMEM((count, rows, units), WIDE),
            pltpu.VMEM((groups, spans, 2 * HD, span), NARROW),
            pltpu.VMEM((groups, spans, span, HD), NARROW),
            pltpu.VMEM((2, 3, D // 2, 128), NARROW),
            pltpu.VMEM((2, 8, D // 2), WIDE),
            pltpu.SMEM((groups, count), jnp.int32),
            pltpu.SemaphoreType.DMA((2,)),
            pltpu.SemaphoreType.DMA((7,)),
            pltpu.SemaphoreType.DMA((7,)),
            pltpu.SemaphoreType.DMA((7,)),
            pltpu.SemaphoreType.DMA((2, 4, count)),
            pltpu.SemaphoreType.DMA((2, count)),
            pltpu.SemaphoreType.DMA((4, count)),
        ],
        name="gather_and_forward",
        compiler_params=pltpu.CompilerParams(
            collective_id=1, has_side_effects=True, vmem_limit_bytes=VMEM_LIMIT
        ),
    )(lengths, dealing, tok, cot, *gains, w_qkv, w_out, w_up, w_down)


def far_first(depth):
    return [list(reversed(row)) for row in near_first(depth)]


def unturn(rows, cosine, sine):
    first, second = rows[0:8], rows[8:16]
    return jnp.concatenate(
        [first * cosine + second * sine, second * cosine - first * sine, rows[16:]], axis=0
    )


def reduce_kernel(
    depth,
    lengths_ref,
    dealing_ref,
    heads_in,
    units_in,
    attended_in,
    total_in,
    tok_ref,
    cot_ref,
    prm_all,
    wqkv_t,
    wup_all,
    wdown_part,
    wout_part,
    g_up,
    g_down,
    g_sum,
    xhat_in,
    cot_in,
    out_ref,
    grad_ref,
    qkv_ref,
    wout_ref,
    up_ref,
    down_ref,
    vec_ref,
    w_heads_back,
    give_buf,
    sum_buf,
    beside_buf,
    line_buf,
    wide,
    q_rows,
    k_rows,
    v_rows,
    g_rows,
    g_key,
    g_value,
    turned_all,
    by_token,
    stream,
    g_heads,
    g_wout,
    sum_heads,
    vectors,
    grads,
    grads_in,
    mail,
    inbox,
    wout_in,
    down_in,
    found,
    send_sem,
    recv_twin,
    recv_beside,
    recv_z,
    stream_sem,
    across_send,
    across_recv,
    mail_send,
    mail_recv,
):
    here = Place(depth)
    c, x, y, z, core = here.c, here.x, here.y, here.z, here.core
    rows = tok_ref.shape[0]
    units = wup_all.shape[1]
    groups = dealing_ref.shape[0]
    count = 4 * depth
    spans, span = count // 2, 2 * BLK
    scale = HD ** (-0.5)
    piece = D // (2 * count)
    order = far_first(depth)

    def shard_of(at):
        kind = lax.rem(at, 4)
        to_y = jnp.where(lax.rem(kind, 2) == 1, y, 1 - y)
        to_core = jnp.where(kind < 2, 1 - core, core)
        return here.at(pick2(z, at // 4, order), to_y, to_core)

    def load(at):
        shard, slot = shard_of(at), lax.rem(at, 2)
        return (
            pltpu.make_async_copy(xhat_in.at[shard], stream.at[0, slot], stream_sem.at[0, slot]),
            pltpu.make_async_copy(cot_in.at[shard], stream.at[1, slot], stream_sem.at[1, slot]),
        )

    here.greet_all()

    def crossing(source, place, at):
        return pltpu.make_async_remote_copy(
            source,
            place,
            across_send.at[at],
            across_recv.at[at],
            device_id=here.across,
            device_id_type=MESH,
        )

    half_down = g_down.shape[0] // 2
    half_wout = HD // 2
    send_down = crossing(g_down.at[pl.ds((1 - x) * half_down, half_down)], down_in, 0)
    send_wout = crossing(g_wout.at[pl.ds((1 - x) * half_wout, half_wout)], wout_in, 1)
    send_grads = [crossing(grads.at[part, 1 - x], grads_in.at[part], 2 + part) for part in range(2)]
    send_down.start()

    def to_twin(what, slot):
        return pltpu.make_async_remote_copy(
            give_buf.at[slot],
            sum_buf.at[what, slot],
            send_sem.at[what, 0, slot],
            recv_twin.at[what, slot],
            device_id=here.twin,
            device_id_type=MESH,
        )

    def to_beside(what, to_z):
        return pltpu.make_async_remote_copy(
            sum_buf.at[what, to_z],
            beside_buf.at[what, to_z],
            send_sem.at[what, 1, to_z],
            recv_beside.at[what, to_z],
            device_id=here.beside,
            device_id_type=MESH,
        )

    def to_above(what, to_z):
        return pltpu.make_async_remote_copy(
            sum_buf.at[what, depth + to_z],
            line_buf.at[what, to_z],
            send_sem.at[what, 2, to_z],
            recv_z.at[what, to_z],
            device_id=here.above,
            device_id_type=MESH,
        )

    def over_slot(to_z, at_z):
        return jnp.where(to_z == at_z, depth, to_z)

    def to_below(what, to_z):
        slot = over_slot(to_z, z - 1)
        return pltpu.make_async_remote_copy(
            sum_buf.at[what, depth + to_z],
            line_buf.at[what, slot],
            send_sem.at[what, 2, to_z],
            recv_z.at[what, slot],
            device_id=here.below,
            device_id_type=MESH,
        )

    def from_above(what, to_z):
        slot = over_slot(to_z, z)
        return pltpu.make_async_remote_copy(
            sum_buf.at[what, depth + to_z],
            line_buf.at[what, slot],
            send_sem.at[what, 2, to_z],
            recv_z.at[what, slot],
            device_id=here.above,
            device_id_type=MESH,
        )

    def pass_on(what, at, part):
        to_z = pick2(z, at // 4, order)
        kind = lax.rem(at, 4)
        slot = lax.rem(kind, 2) * depth + to_z

        @pl.when(kind < 2)
        def _():
            if what == 1:
                to_twin(0, slot).wait_send()
            give_buf[slot] = part.astype(NARROW)
            to_twin(what, slot).start()

        @pl.when(kind >= 2)
        def _():
            to_twin(what, slot).wait_recv()
            sum_buf[what, slot] = (part + sum_buf[what, slot].astype(WIDE)).astype(NARROW)

        @pl.when(kind == 2)
        def _():
            to_beside(what, to_z).start()

    def chain(what, at):
        to_z = pick2(z, at, order)
        slot = depth + to_z
        to_beside(what, to_z).wait_recv()

        def add(incoming):
            for part in range(2):
                half = slice(part * rows // 2, (part + 1) * rows // 2)
                total = sum_buf[what, slot, half, :].astype(WIDE)
                total = total + beside_buf[what, to_z, half, :].astype(WIDE)
                if incoming:
                    total = total + line_buf[what, to_z, half, :].astype(WIDE)
                sum_buf[what, slot, half, :] = total.astype(NARROW)

        @pl.when(to_z > z)
        def _():
            @pl.when(here.has_below)
            def _():
                to_above(what, to_z).wait_recv()
                add(True)

            @pl.when(jnp.logical_not(here.has_below))
            def _():
                add(False)

            to_above(what, to_z).start()

        @pl.when(to_z < z)
        def _():
            @pl.when(here.has_above)
            def _():
                from_above(what, to_z).wait_recv()
                add(True)

            @pl.when(jnp.logical_not(here.has_above))
            def _():
                add(False)

            to_below(what, to_z).start()

    def gather_total(what):
        @pl.when(here.has_below)
        def _():
            to_above(what, z).wait_recv()

        @pl.when(jnp.logical_not(here.has_below))
        def _():
            line_buf[what, z] = jnp.zeros((rows, D), NARROW)

        @pl.when(here.has_above)
        def _():
            from_above(what, z).wait_recv()

        @pl.when(jnp.logical_not(here.has_above))
        def _():
            line_buf[what, depth] = jnp.zeros((rows, D), NARROW)

        return (
            sum_buf[what, depth + z].astype(WIDE)
            + beside_buf[what, z].astype(WIDE)
            + line_buf[what, z].astype(WIDE)
            + line_buf[what, depth].astype(WIDE)
        )

    def give_out(at, carry):
        shard = shard_of(at)
        parts = []
        for group in range(groups):
            attended = attended_in[group, dealing_ref[group, shard]].astype(NARROW)
            parts.append(dot(attended, wout_part[...], TN))
        part = jnp.concatenate(parts, axis=0) + dot(units_in[shard, :, 0:units], wdown_part[...])
        pass_on(0, at, part)
        return carry

    lax.fori_loop(0, count, give_out, 0)

    def settle(chunk, part, raw, weights, sums, column):
        scaled = raw * column[:, 2 - 2 * part : 3 - 2 * part] + sums * column[:, 3 - 2 * part : 4 - 2 * part]
        gain_sum = jnp.sum(weights * raw, axis=1, keepdims=True)
        bias_sum = jnp.sum(weights * sums, axis=1, keepdims=True)
        row = pl.ds(pl.multiple_of(chunk * 128, 128), 128)
        if part == 0:
            vectors[row, 0:1] = gain_sum
            vectors[row, 1:2] = bias_sum
        else:
            lane = lax.broadcasted_iota(jnp.int32, scaled.shape, 1)
            scaled = jnp.where(lane == 0, gain_sum, scaled)
            scaled = jnp.where(lane == 1, bias_sum, scaled)
            scaled = jnp.where(lane == 2, vectors[row, 0:1], scaled)
            scaled = jnp.where(lane == 3, vectors[row, 1:2], scaled)
        per = 128 // piece
        for at in range(per):
            grads[part, at % 2, chunk * (per // 2) + at // 2] = scaled[at * piece : (at + 1) * piece]

    sum_units = jnp.sum(g_sum[...], axis=0, keepdims=True)

    def settle_up(chunk, carry):
        lanes = pl.ds(pl.multiple_of(chunk * 128, 128), 128)
        weights = wup_all[lanes, :].astype(WIDE)
        settle(chunk, 0, g_up[:, lanes].T, weights, sum_units, prm_all[:, lanes].T)
        return carry

    lax.fori_loop(0, D // 128, settle_up, 0)
    send_grads[0].start()
    find_blocks(dealing_ref, found)
    w_heads_back[0:HD, :] = jnp.zeros((HD, D), NARROW)
    w_heads_back[HD:, :] = wqkv_t[...]
    g_heads[...] = jnp.zeros_like(g_heads)
    g_wout[...] = jnp.zeros_like(g_wout)
    sum_heads[...] = jnp.zeros_like(sum_heads)

    for group in range(groups):
        lanes = slice(group * BLK, (group + 1) * BLK)
        starts = starts_of(lengths_ref, group)

        def bring(at, carry, group=group, lanes=lanes):
            for side in range(2):
                source = found[group, 2 * at + side]
                part = heads_in[source, :, lanes]
                to = slice(side * BLK, (side + 1) * BLK)
                queries = part[0:HD].astype(WIDE) * scale
                keys = part[HD : 2 * HD]
                grads_part = part[3 * HD : 4 * HD]
                wide[at, 0:HD, to] = queries.astype(NARROW)
                wide[at, HD : 2 * HD, to] = keys
                wide[at, 2 * HD : 3 * HD, to] = grads_part
                q_rows[at, to, :] = queries.T.astype(NARROW)
                k_rows[at, to, :] = keys.astype(WIDE).T.astype(NARROW)
                v_rows[at, to, :] = part[2 * HD : 3 * HD].astype(WIDE).T.astype(NARROW)
                g_rows[at, to, :] = grads_part.astype(WIDE).T.astype(NARROW)
            g_key[at] = jnp.zeros((span, HD), WIDE)
            g_value[at] = jnp.zeros((span, HD), WIDE)
            return carry

        lax.fori_loop(0, spans, bring, 0)
        chain(0, 2 * group)

        def one_span(at, carry, group=group, starts=starts):
            natural = at * span + lax.broadcasted_iota(jnp.int32, (1, span), 1)
            opening = opening_of(natural, starts)
            key_in = lax.broadcasted_iota(jnp.int32, (span, span), 0)
            queries = wide[at, 0:HD, :]
            g_attended = wide[at, 2 * HD : 3 * HD, :]
            attended = jnp.concatenate(
                [attended_in[group, 2 * at], attended_in[group, 2 * at + 1]], axis=1
            )
            row_dot = jnp.sum(attended * g_attended.astype(WIDE), axis=0, keepdims=True)
            log_total = total_in[group, at, 0:1, :]

            def add(keys_at, so_far, allowed):
                scores = dot(k_rows[keys_at], queries)
                probs = jnp.where(allowed, jnp.exp(scores - log_total), 0.0)
                g_probs = dot(v_rows[keys_at], g_attended)
                g_scores = (probs * (g_probs - row_dot)).astype(NARROW)
                g_key[keys_at] += dot(g_scores, q_rows[at])
                g_value[keys_at] += dot(probs.astype(NARROW), g_rows[at])
                return so_far + dot(wide[keys_at, HD : 2 * HD, :], g_scores)

            def earlier(keys_at, so_far):
                return add(keys_at, so_far, key_in >= opening - keys_at * span)

            so_far = lax.fori_loop(0, at, earlier, jnp.zeros((HD, span), WIDE))
            place = key_in + at * span
            so_far = add(at, so_far, jnp.logical_and(place <= natural, place >= opening))
            cosine, sine = turning(natural - opening)
            turned = jnp.concatenate([attended, unturn(so_far * scale, cosine, sine)], axis=0)
            for side in range(2):
                part = turned[:, side * BLK : (side + 1) * BLK]
                turned_all[group, 2 * at + side, 0 : 2 * HD, :] = part.astype(NARROW)
            return carry

        lax.fori_loop(0, spans, one_span, 0)
        chain(0, 2 * group + 1)

        def give(at, carry, group=group, starts=starts):
            natural = at * span + lax.broadcasted_iota(jnp.int32, (1, span), 1)
            cosine, sine = turning(natural - opening_of(natural, starts))
            keys = unturn(g_key[at].T, cosine, sine)
            turned = jnp.concatenate([keys, g_value[at].T], axis=0)
            for side in range(2):
                part = turned[:, side * BLK : (side + 1) * BLK]
                turned_all[group, 2 * at + side, 2 * HD : 4 * HD, :] = part.astype(NARROW)
                whole = turned_all[group, 2 * at + side].astype(WIDE)
                by_token[group, 2 * at + side] = whole.T.astype(NARROW)
            return carry

        lax.fori_loop(0, spans, give, 0)

    for copy in load(0):
        copy.start()

    def give_back(at, carry):
        shard, slot = shard_of(at), lax.rem(at, 2)
        blocks = [dealing_ref[group, shard] for group in range(groups)]
        heads = jnp.concatenate([by_token[group, blocks[group]] for group in range(groups)], axis=0)
        g_hidden = units_in[shard, :, units : 2 * units]
        part = dot(heads, w_heads_back[...]) * prm_all[0:1, :] + dot(
            g_hidden, wup_all[...], NT
        ) * prm_all[2:3, :]
        pass_on(1, at, part)

        @pl.when(at + 1 < count)
        def _():
            for copy in load(at + 1):
                copy.start()

        for copy in load(at):
            copy.wait()
        turned = jnp.concatenate([turned_all[group, blocks[group]] for group in range(groups)], axis=1)
        g_wout[...] += dot(turned[0:HD], stream[1, slot])
        g_heads[HD:, :] += dot(turned[HD:], stream[0, slot])
        sum_heads[...] += jnp.sum(heads.astype(WIDE).reshape(rows // 8, 8, 4 * HD), axis=0)
        return carry

    lax.fori_loop(0, count, give_back, 0)
    send_wout.start()
    sum_row = jnp.sum(sum_heads[...], axis=0, keepdims=True)

    def settle_qkv(chunk, carry):
        lanes = pl.ds(pl.multiple_of(chunk * 128, 128), 128)
        weights = w_heads_back[:, lanes].astype(WIDE).T
        settle(chunk, 1, g_heads[:, lanes].T, weights, sum_row, prm_all[:, lanes].T)
        return carry

    lax.fori_loop(0, D // 128, settle_qkv, 0)
    send_grads[1].start()

    def post(part, to_c):
        return pltpu.make_async_remote_copy(
            mail.at[part, to_c],
            inbox.at[part, c],
            mail_send.at[part, to_c],
            mail_recv.at[part, c],
            device_id=(to_c, x),
            device_id_type=MESH,
        )

    def collect(part, from_c):
        return pltpu.make_async_remote_copy(
            mail.at[part, from_c],
            inbox.at[part, from_c],
            mail_send.at[part, from_c],
            mail_recv.at[part, from_c],
            device_id=(from_c, x),
            device_id_type=MESH,
        )

    def mail_out(part):
        send_grads[part].wait_recv()

        def fold(to_c, carry):
            mail[part, to_c] = (grads[part, x, to_c] + grads_in[part, to_c]).astype(NARROW)
            return carry

        lax.fori_loop(0, count, fold, 0)

        def start(offset, carry):
            post(part, lax.rem(c + offset, count)).start()
            return carry

        lax.fori_loop(1, count, start, 0)
        inbox[part, c] = mail[part, c]

    mail_out(0)
    chain(1, 0)
    mail_out(1)

    def rest(at, carry):
        chain(1, at)
        return carry

    lax.fori_loop(1, depth, rest, 0)

    out_ref[...] = (tok_ref[...].astype(WIDE) + gather_total(0)).astype(NARROW)
    send_down.wait()
    down_ref[...] = g_down[pl.ds(x * half_down, half_down), :] + down_in[...]
    send_wout.wait()
    wout_ref[...] = g_wout[pl.ds(x * half_wout, half_wout), :] + wout_in[...]

    def close(offset, carry):
        other = lax.rem(c + offset, count)
        for part in range(2):
            collect(part, other).wait_recv()
            post(part, other).wait_send()
        return carry

    lax.fori_loop(1, count, close, 0)
    for part in range(2):
        send_grads[part].wait_send()
    together = jnp.zeros((piece, 128), WIDE)
    for from_c in range(count):
        up_ref[:, from_c * units : (from_c + 1) * units] = inbox[0, from_c].astype(WIDE)
        together = together + inbox[1, from_c, :, 0:128].astype(WIDE)
    vec_ref[...] = together.T[0:8]
    for pair in range(count // 2):
        left = inbox[1, 2 * pair].astype(WIDE)
        right = inbox[1, 2 * pair + 1].astype(WIDE)
        for part in range(3):
            lanes = slice((part + 1) * HD, (part + 2) * HD)
            to = part * D + pair * 128
            qkv_ref[:, to : to + 128] = jnp.concatenate([left[:, lanes], right[:, lanes]], axis=1)

    tokens = tok_ref[...].astype(WIDE)
    average = jnp.mean(tokens, axis=-1, keepdims=True)
    centred = tokens - average
    variance = jnp.mean(centred * centred, axis=-1, keepdims=True)
    rise = lax.rsqrt(variance + EPSILON)
    xhat = centred * rise
    g_xhat = gather_total(1)
    along = jnp.mean(g_xhat * xhat, axis=-1, keepdims=True)
    level = jnp.mean(g_xhat, axis=-1, keepdims=True)
    grad_ref[...] = cot_ref[...].astype(WIDE) + rise * (g_xhat - level - xhat * along)

    def finish(to_z, carry):
        to_twin(1, to_z).wait_send()
        to_twin(1, depth + to_z).wait_send()
        for what in range(2):
            to_beside(what, to_z).wait_send()

            @pl.when(to_z > z)
            def _():
                to_above(what, to_z).wait_send()

            @pl.when(to_z < z)
            def _():
                to_below(what, to_z).wait_send()

        return carry

    lax.fori_loop(0, depth, finish, 0)


def reduce_call(depth, lengths, dealing, heads, units_in, attended, total, tok, cot, rest, xhat, cot_all):
    rows = tok.shape[0]
    count = depth * 4
    groups = dealing.shape[0]
    spans, span = count // 2, 2 * BLK
    piece = D // (2 * count)
    units = rest[2].shape[1]
    vmem = pl.BlockSpec(memory_space=pltpu.VMEM)
    smem = pl.BlockSpec(memory_space=pltpu.SMEM)
    any_spec = pl.BlockSpec(memory_space=pl.ANY)
    shape = jax.ShapeDtypeStruct
    message = (rows, D)
    row_form = pltpu.VMEM((spans, span, HD), NARROW)
    return pl.pallas_call(
        functools.partial(reduce_kernel, depth),
        out_shape=(
            shape((rows, D), NARROW),
            shape((rows, D), WIDE),
            shape((piece, 3 * D), WIDE),
            shape((HD // 2, D), WIDE),
            shape((piece, count * units), WIDE),
            shape((units // 2, D), WIDE),
            shape((8, piece), WIDE),
        ),
        in_specs=[smem] * 2 + [vmem] * 14 + [any_spec] * 2,
        out_specs=(vmem,) * 7,
        scratch_shapes=[
            pltpu.VMEM((4 * HD, D), NARROW),
            pltpu.VMEM((2 * depth,) + message, NARROW),
            pltpu.VMEM((2, 2 * depth) + message, NARROW),
            pltpu.VMEM((2, depth) + message, NARROW),
            pltpu.VMEM((2, depth + 1) + message, NARROW),
            pltpu.VMEM((spans, 3 * HD, span), NARROW),
            row_form,
            row_form,
            row_form,
            row_form,
            pltpu.VMEM((spans, span, HD), WIDE),
            pltpu.VMEM((spans, span, HD), WIDE),
            pltpu.VMEM((groups, count, 4 * HD, BLK), NARROW),
            pltpu.VMEM((groups, count, BLK, 4 * HD), NARROW),
            pltpu.VMEM((2, 2, rows, D), NARROW),
            pltpu.VMEM((4 * HD, D), WIDE),
            pltpu.VMEM((HD, D), WIDE),
            pltpu.VMEM((8, 4 * HD), WIDE),
            pltpu.VMEM((D, 128), WIDE),
            pltpu.VMEM((2, 2, count, piece, 256), WIDE),
            pltpu.VMEM((2, count, piece, 256), WIDE),
            pltpu.VMEM((2, count, piece, 256), NARROW),
            pltpu.VMEM((2, count, piece, 256), NARROW),
            pltpu.VMEM((HD // 2, D), WIDE),
            pltpu.VMEM((units // 2, D), WIDE),
            pltpu.SMEM((groups, count), jnp.int32),
            pltpu.SemaphoreType.DMA((2, 3, 2 * depth)),
            pltpu.SemaphoreType.DMA((2, 2 * depth)),
            pltpu.SemaphoreType.DMA((2, depth)),
            pltpu.SemaphoreType.DMA((2, depth + 1)),
            pltpu.SemaphoreType.DMA((2, 2)),
            pltpu.SemaphoreType.DMA((4,)),
            pltpu.SemaphoreType.DMA((4,)),
            pltpu.SemaphoreType.DMA((2, count)),
            pltpu.SemaphoreType.DMA((2, count)),
        ],
        name="backward_and_reduce",
        compiler_params=pltpu.CompilerParams(
            collective_id=2, has_side_effects=True, vmem_limit_bytes=VMEM_LIMIT
        ),
    )(lengths, dealing, heads, units_in, attended, total, tok, cot, *rest, xhat, cot_all)


def fast_shards(depth, *arguments):
    tokens, cotangent, lengths, dealing = arguments[:4]
    gains = [vector.reshape(1, -1) for vector in arguments[4:8]]
    rows = tokens.shape[0] * tokens.shape[1]
    tok = tokens.reshape(rows, D)
    cot = cotangent.reshape(rows, D)
    forward = gather_call(depth, lengths, dealing, tok, cot, gains, *arguments[8:])
    heads, units, xhat, cot_all, attended, total, g_up, g_down, g_sum = forward[:9]
    wqkv_t, wup_all, wdown_part, wout_part, prm_all = forward[9:]
    rest = (prm_all, wqkv_t, wup_all, wdown_part, wout_part, g_up, g_down, g_sum)
    out, grad_tokens, qkv_part, out_part, up_part, down_part, vector_part = reduce_call(
        depth, lengths, dealing, heads, units, attended, total, tok, cot, rest, xhat, cot_all
    )
    return (
        out.reshape(tokens.shape),
        grad_tokens.reshape(tokens.shape),
        vector_part[0],
        vector_part[1],
        vector_part[2],
        vector_part[3],
        qkv_part,
        out_part,
        up_part,
        down_part,
    )


def solution(mesh):
    placed = (
        P("wsh", "ctx", None),
        P("wsh", "ctx", None),
        P("wsh", None),
        P("wsh", None),
        P("wsh"),
        P("wsh"),
        P("wsh"),
        P("wsh"),
        P("wsh", None),
        P("wsh", None),
        P("wsh", None),
        P("wsh", None),
    )
    ctx_size = mesh.shape["ctx"]
    by_heads = ctx_size == H and mesh.shape["wsh"] == 2
    body = functools.partial(fast_shards, ctx_size // 4) if by_heads else shards
    return jax.shard_map(
        body,
        mesh=mesh,
        in_specs=placed,
        out_specs=(
            P("wsh", "ctx", None),
            P("wsh", "ctx", None),
            P(("ctx", "wsh")),
            P(("ctx", "wsh")),
            P(("ctx", "wsh")),
            P(("ctx", "wsh")),
            P(("ctx", "wsh"), None),
            P(("ctx", "wsh"), None),
            P(("ctx", "wsh"), None),
            P(("ctx", "wsh"), None),
        ),
        check_vma=False,
    )
```

```python
import functools

import jax
import jax.numpy as jnp
from jax import lax
from jax.experimental import pallas as pl
from jax.experimental.pallas import tpu as pltpu
from jax.sharding import PartitionSpec as P

D = 1024
H = 16
HD = 64
ROT = 16
BLK = 128


EPSILON = 1e-05
MASKED = -1e30
WIDE = jnp.float32
NARROW = jnp.bfloat16


def norm_layer(values_in, scale_by, shift_by):
    average = jnp.mean(values_in, axis=-1, keepdims=True)
    centred = values_in - average
    variance = jnp.mean(centred * centred, axis=-1, keepdims=True)
    return centred * lax.rsqrt(variance + EPSILON) * scale_by + shift_by


def rotate(values_in, places):
    split_at = ROT // 2
    frequency = 10000.0 ** (-2.0 * jnp.arange(split_at, dtype=WIDE) / ROT)
    angles = places.astype(WIDE)[:, None] * frequency[None, :]
    cosine_table = jnp.cos(angles)[:, None, :]
    sine_table = jnp.sin(angles)[:, None, :]
    first_half = values_in[..., :split_at]
    second_half = values_in[..., split_at:ROT]
    return jnp.concatenate(
        [
            first_half * cosine_table - second_half * sine_table,
            second_half * cosine_table + first_half * sine_table,
            values_in[..., ROT:],
        ],
        axis=-1,
    )


def natural_rows(dealing_row, offset_row, row_count):
    ordinal = offset_row + jnp.arange(row_count, dtype=jnp.int32)
    table_ids = jnp.arange(dealing_row.shape[0], dtype=jnp.int32)
    picked = jnp.sum(
        jnp.where((ordinal // BLK)[:, None] == table_ids[None, :], dealing_row[None, :], 0), axis=1
    )
    return picked * BLK + ordinal % BLK


def sequence_openings(natural, lengths_row):
    openings = jnp.cumsum(lengths_row) - lengths_row
    return jnp.max(jnp.where(openings[None, :] <= natural[:, None], openings[None, :], 0), axis=1)


def score_block(queries, block_keys, offset_row, natural_q, opening_q, dealing_row):
    row_count = block_keys.shape[0]
    key_natural = natural_rows(dealing_row, offset_row, row_count)
    scores = jnp.einsum(
        "qhd,khd->hqk", queries, block_keys.reshape(row_count, H, HD), preferred_element_type=WIDE
    ) * HD ** (-0.5)
    allowed = (key_natural[None, :] <= natural_q[:, None]) & (
        key_natural[None, :] >= opening_q[:, None]
    )
    return (scores, allowed[None])


def fold_blocks(step_fn, state_in, arrays):
    row_count = arrays[0].shape[0]
    block_width = 1024
    stacked = tuple(
        (
            member.reshape((row_count // block_width, block_width) + member.shape[1:])
            for member in arrays
        )
    )
    offsets = jnp.arange(row_count // block_width, dtype=jnp.int32) * block_width

    def inner_step(state_now, block_item):
        return (step_fn(state_now, block_item[0], block_item[1]), None)

    state_out, _ = lax.scan(inner_step, state_in, (stacked, offsets))
    return state_out


def project(tokens_f, weights, places):
    w_qkv, w_out, w_up, w_down, gain_one, bias_one, gain_two, bias_two = weights
    all_rows = tokens_f.shape[0]
    normed_one = norm_layer(tokens_f, gain_one.astype(WIDE), bias_one.astype(WIDE)).astype(NARROW)
    normed_two = norm_layer(tokens_f, gain_two.astype(WIDE), bias_two.astype(WIDE)).astype(NARROW)
    mixed = jnp.dot(normed_one, w_qkv, preferred_element_type=WIDE).reshape(all_rows, 3, H, HD)
    queries = rotate(mixed[:, 0], places).astype(NARROW)
    keys_here = rotate(mixed[:, 1], places).astype(NARROW).reshape(all_rows, D)
    values_here = mixed[:, 2].astype(NARROW).reshape(all_rows, D)
    hidden = jnp.dot(normed_two, w_up, preferred_element_type=WIDE)
    activated = jax.nn.gelu(hidden, approximate=False).astype(NARROW)
    return (normed_one, normed_two, queries, keys_here, values_here, hidden, activated)


def attend(queries, keys_here, values_here, natural_q, opening_q, dealing_row):
    local_rows = queries.shape[0]

    def max_step(state_in, block_arrays, offset_row):
        row_top, row_total = state_in
        scores, allowed = score_block(
            queries, block_arrays[0], offset_row, natural_q, opening_q, dealing_row
        )
        new_top = jnp.maximum(row_top, jnp.max(jnp.where(allowed, scores, MASKED), axis=-1))
        kept_terms = jnp.where(allowed, jnp.exp(scores - new_top[..., None]), 0.0)
        return (new_top, row_total * jnp.exp(row_top - new_top) + jnp.sum(kept_terms, axis=-1))

    start_state = (jnp.full((H, local_rows), MASKED, WIDE), jnp.zeros((H, local_rows), WIDE))
    row_top, row_total = fold_blocks(
        max_step, start_state, (lax.all_gather(keys_here, "ctx", axis=0, tiled=True),)
    )
    log_total = row_top + jnp.log(row_total)

    def value_step(state_in, block_arrays, offset_row):
        scores, allowed = score_block(
            queries, block_arrays[0], offset_row, natural_q, opening_q, dealing_row
        )
        soft_probs = jnp.where(allowed, jnp.exp(scores - log_total[..., None]), 0.0).astype(NARROW)
        row_count = block_arrays[1].shape[0]
        return state_in + jnp.einsum(
            "hqk,khd->qhd",
            soft_probs,
            block_arrays[1].reshape(row_count, H, HD),
            preferred_element_type=WIDE,
        )

    attended = fold_blocks(
        value_step,
        jnp.zeros((local_rows, H, HD), WIDE),
        (
            lax.all_gather(keys_here, "ctx", axis=0, tiled=True),
            lax.all_gather(values_here, "ctx", axis=0, tiled=True),
        ),
    )
    return (attended, log_total)


def attention_back(
    queries,
    keys_here,
    values_here,
    g_attended,
    row_dot,
    log_total,
    natural_q,
    opening_q,
    dealing_row,
):
    local_rows = queries.shape[0]
    scale_factor = HD ** (-0.5)
    gathered_keys, gathered_values = (
        lax.all_gather(keys_here, "ctx", axis=0, tiled=True),
        lax.all_gather(values_here, "ctx", axis=0, tiled=True),
    )
    group_rows = gathered_keys.shape[0]
    key_span = 1024

    def key_block(state_in, block_item):
        block_keys, block_values, offset_row = block_item
        scores, allowed = score_block(
            queries, block_keys, offset_row, natural_q, opening_q, dealing_row
        )
        soft_probs = jnp.where(allowed, jnp.exp(scores - log_total[..., None]), 0.0)
        g_probs = jnp.einsum(
            "qhd,khd->hqk",
            g_attended,
            block_values.reshape(key_span, H, HD),
            preferred_element_type=WIDE,
        )
        g_scores = (soft_probs * (g_probs - row_dot[..., None])).astype(NARROW)
        state_out = (
            state_in
            + jnp.einsum(
                "hqk,khd->qhd",
                g_scores,
                block_keys.reshape(key_span, H, HD),
                preferred_element_type=WIDE,
            )
            * scale_factor
        )
        key_terms = (
            jnp.einsum("hqk,qhd->khd", g_scores, queries, preferred_element_type=WIDE)
            * scale_factor
        )
        value_terms = jnp.einsum(
            "hqk,qhd->khd", soft_probs.astype(NARROW), g_attended, preferred_element_type=WIDE
        )
        return (
            state_out,
            jnp.concatenate(
                [key_terms.reshape(key_span, D), value_terms.reshape(key_span, D)], axis=1
            ),
        )

    block_total = group_rows // key_span
    block_starts = jnp.arange(block_total, dtype=jnp.int32) * key_span
    stacked_blocks = (
        gathered_keys.reshape(block_total, key_span, D),
        gathered_values.reshape(block_total, key_span, D),
        block_starts,
    )
    g_queries, stacked_terms = lax.scan(
        key_block, jnp.zeros((local_rows, H, HD), WIDE), stacked_blocks
    )
    g_pairs = lax.psum_scatter(
        stacked_terms.reshape(group_rows, 2 * D), "ctx", scatter_dimension=0, tiled=True
    )
    g_keys = g_pairs[:, :D].reshape(local_rows, H, HD)
    g_values = g_pairs[:, D:].reshape(local_rows, H, HD)
    return (g_queries, g_keys, g_values)


def shards(
    tokens,
    cotangent,
    lengths,
    dealing,
    gain_one,
    bias_one,
    gain_two,
    bias_two,
    w_qkv,
    w_out,
    w_up,
    w_down,
):
    group_count = tokens.shape[0]
    local_rows = tokens.shape[1]
    all_rows = group_count * local_rows
    tokens_f = tokens.reshape(all_rows, D).astype(WIDE)
    first_row = lax.axis_index("ctx") * local_rows
    natural_list = [
        natural_rows(dealing[member], first_row, local_rows) for member in range(group_count)
    ]
    opening_list = [
        sequence_openings(natural_list[member], lengths[member]) for member in range(group_count)
    ]
    places = jnp.concatenate(
        [natural_list[member] - opening_list[member] for member in range(group_count)], axis=0
    )

    def forward():
        weights = (
            lax.all_gather(w_qkv, "wsh", axis=0, tiled=True),
            lax.all_gather(w_out, "wsh", axis=0, tiled=True),
            lax.all_gather(w_up, "wsh", axis=0, tiled=True),
            lax.all_gather(w_down, "wsh", axis=0, tiled=True),
            lax.all_gather(gain_one, "wsh", axis=0, tiled=True),
            lax.all_gather(bias_one, "wsh", axis=0, tiled=True),
            lax.all_gather(gain_two, "wsh", axis=0, tiled=True),
            lax.all_gather(bias_two, "wsh", axis=0, tiled=True),
        )
        local_parts = project(tokens_f, weights, places)
        attended_list = []
        total_list = []
        for member in range(group_count):
            rows_from = member * local_rows
            attended_one, total_one = attend(
                local_parts[2][rows_from : rows_from + local_rows],
                local_parts[3][rows_from : rows_from + local_rows],
                local_parts[4][rows_from : rows_from + local_rows],
                natural_list[member],
                opening_list[member],
                dealing[member],
            )
            attended_list.append(attended_one)
            total_list.append(total_one)
        return (weights, local_parts, jnp.concatenate(attended_list, axis=0), total_list)

    weights, local_parts, attended, total_list = forward()
    attended_low = attended.reshape(all_rows, D).astype(NARROW)
    mixed_out = (
        tokens_f
        + jnp.dot(attended_low, weights[1], preferred_element_type=WIDE)
        + jnp.dot(local_parts[6], weights[3], preferred_element_type=WIDE)
    )
    out = mixed_out.astype(NARROW)
    weights, local_parts, attended, total_list = forward()
    attended_low = attended.reshape(all_rows, D).astype(NARROW)
    w_qkv_all, w_out_all, w_up_all, w_down_all = (weights[0], weights[1], weights[2], weights[3])
    normed_one, normed_two, queries, keys_here, values_here, hidden, activated = local_parts
    grad_rows = cotangent.reshape(all_rows, D)
    grad_f = grad_rows.astype(WIDE)
    g_down = jnp.einsum("tf,td->fd", activated, grad_rows, preferred_element_type=WIDE)
    g_activated = jnp.einsum("td,fd->tf", grad_rows, w_down_all, preferred_element_type=WIDE)
    _, gelu_back = jax.vjp(lambda pre_act: jax.nn.gelu(pre_act, approximate=False), hidden)
    g_hidden = gelu_back(g_activated)[0].astype(NARROW)
    g_up = jnp.einsum("td,tf->df", normed_two, g_hidden, preferred_element_type=WIDE)
    g_normed_two = jnp.einsum("tf,df->td", g_hidden, w_up_all, preferred_element_type=WIDE)
    g_weight_out = jnp.einsum("te,td->ed", attended_low, grad_rows, preferred_element_type=WIDE)
    g_attended = (
        jnp.einsum("td,ed->te", grad_rows, w_out_all, preferred_element_type=WIDE)
        .astype(NARROW)
        .reshape(all_rows, H, HD)
    )
    row_dot = jnp.einsum("qhd,qhd->hq", g_attended.astype(WIDE), attended)
    query_grads = []
    key_grads = []
    value_grads = []
    for member in range(group_count):
        rows_from = member * local_rows
        rows_to = rows_from + local_rows
        g_q, g_k, g_v = attention_back(
            queries[rows_from:rows_to],
            keys_here[rows_from:rows_to],
            values_here[rows_from:rows_to],
            g_attended[rows_from:rows_to],
            row_dot[:, rows_from:rows_to],
            total_list[member],
            natural_list[member],
            opening_list[member],
            dealing[member],
        )
        query_grads.append(g_q)
        key_grads.append(g_k)
        value_grads.append(g_v)
    g_queries = jnp.concatenate(query_grads, axis=0)
    g_keys = jnp.concatenate(key_grads, axis=0)
    g_values = jnp.concatenate(value_grads, axis=0)
    _, rotate_back = jax.vjp(
        lambda pre_rot: rotate(pre_rot, places), jnp.zeros((all_rows, H, HD), WIDE)
    )
    g_queries_pre = rotate_back(g_queries)[0]
    g_keys_pre = rotate_back(g_keys)[0]
    g_mixed = (
        jnp.stack([g_queries_pre, g_keys_pre, g_values], axis=1)
        .reshape(all_rows, 3 * D)
        .astype(NARROW)
    )
    g_qkv = jnp.einsum("td,te->de", normed_one, g_mixed, preferred_element_type=WIDE)
    g_normed_one = jnp.einsum("te,de->td", g_mixed, w_qkv_all, preferred_element_type=WIDE)

    def both_norms(tokens_in, scale_one, shift_one, scale_two, shift_two):
        return (
            norm_layer(tokens_in, scale_one, shift_one),
            norm_layer(tokens_in, scale_two, shift_two),
        )

    _, norm_back = jax.vjp(
        both_norms,
        tokens_f,
        weights[4].astype(WIDE),
        weights[5].astype(WIDE),
        weights[6].astype(WIDE),
        weights[7].astype(WIDE),
    )
    g_tokens, g_scale_one, g_shift_one, g_scale_two, g_shift_two = norm_back(
        (g_normed_one, g_normed_two)
    )
    grad_tokens = g_tokens + grad_f
    summed = (
        lax.psum_scatter(g_qkv, ("ctx", "wsh"), scatter_dimension=0, tiled=True),
        lax.psum_scatter(g_weight_out, ("ctx", "wsh"), scatter_dimension=0, tiled=True),
        lax.psum_scatter(g_up, ("ctx", "wsh"), scatter_dimension=0, tiled=True),
        lax.psum_scatter(g_down, ("ctx", "wsh"), scatter_dimension=0, tiled=True),
        lax.psum_scatter(g_scale_one, ("ctx", "wsh"), scatter_dimension=0, tiled=True),
        lax.psum_scatter(g_shift_one, ("ctx", "wsh"), scatter_dimension=0, tiled=True),
        lax.psum_scatter(g_scale_two, ("ctx", "wsh"), scatter_dimension=0, tiled=True),
        lax.psum_scatter(g_shift_two, ("ctx", "wsh"), scatter_dimension=0, tiled=True),
    )
    return (
        out.reshape(group_count, local_rows, D),
        grad_tokens.reshape(group_count, local_rows, D),
        summed[4],
        summed[5],
        summed[6],
        summed[7],
        summed[0],
        summed[1],
        summed[2],
        summed[3],
    )


MESH = pl.DeviceIdType.MESH
NT = (((1,), (1,)), ((), ()))
TN = (((0,), (0,)), ((), ()))
VMEM_LIMIT = 60 * 1024 * 1024


def dot(a, b, dims=(((1,), (0,)), ((), ()))):
    return lax.dot_general(a, b, dims, preferred_element_type=WIDE)


def pick(index, table):
    result = jnp.int32(table[0])
    for at in range(1, len(table)):
        result = jnp.where(index == at, jnp.int32(table[at]), result)
    return result


def near_first(depth):
    return [sorted(range(depth), key=lambda to, z=z: (abs(to - z), to)) for z in range(depth)]


def pick2(row, column, table):
    result = pick(column, table[0])
    for at in range(1, len(table)):
        result = jnp.where(row == at, pick(column, table[at]), result)
    return result


class Place:
    def __init__(self, depth):
        self.depth = depth
        self.c = lax.axis_index("ctx")
        self.x = lax.axis_index("wsh")
        self.core = lax.rem(self.c, 2)
        self.y = lax.rem(self.c // 2, 2)
        self.z = self.c // 4
        self.beside = (self.at(self.z, 1 - self.y, self.core), self.x)
        self.twin = (self.at(self.z, self.y, 1 - self.core), self.x)
        self.above = (self.at(self.z + 1, self.y, self.core), self.x)
        self.below = (self.at(self.z - 1, self.y, self.core), self.x)
        self.across = (self.c, 1 - self.x)
        self.has_above = self.z < depth - 1
        self.has_below = self.z > 0

    def at(self, z, y, core):
        return (z * 2 + y) * 2 + core

    def greet(self):
        barrier = pltpu.get_barrier_semaphore()

        def hail(device):
            pl.semaphore_signal(barrier, inc=1, device_id=device, device_id_type=MESH)

        hail(self.beside)
        hail(self.twin)
        hail(self.across)

        @pl.when(self.has_above)
        def _():
            hail(self.above)

        @pl.when(self.has_below)
        def _():
            hail(self.below)

        pl.semaphore_wait(
            barrier, 3 + self.has_above.astype(jnp.int32) + self.has_below.astype(jnp.int32)
        )


    def greet_all(self):
        barrier = pltpu.get_barrier_semaphore()
        count = 4 * self.depth
        pl.semaphore_signal(barrier, inc=1, device_id=self.across, device_id_type=MESH)

        def hail(offset, carry):
            device = (lax.rem(self.c + offset, count), self.x)
            pl.semaphore_signal(barrier, inc=1, device_id=device, device_id_type=MESH)
            return carry

        lax.fori_loop(1, count, hail, 0)
        pl.semaphore_wait(barrier, count)


FREQUENCY = tuple(10000.0 ** (-2.0 * i / ROT) for i in range(ROT // 2))


def turning(place):
    row = lax.broadcasted_iota(jnp.int32, (ROT // 2, 1), 0)
    frequency = jnp.full((ROT // 2, 1), FREQUENCY[0], WIDE)
    for at in range(1, ROT // 2):
        frequency = jnp.where(row == at, FREQUENCY[at], frequency)
    angles = place.astype(WIDE) * frequency
    return jnp.cos(angles), jnp.sin(angles)


def starts_of(lengths_ref, group):
    starts = []
    so_far = jnp.int32(0)
    for piece in range(lengths_ref.shape[1] - 1):
        so_far = so_far + lengths_ref[group, piece]
        starts.append(so_far)
    return starts


def opening_of(natural, starts):
    opening = jnp.zeros(natural.shape, jnp.int32)
    for start in starts:
        opening = jnp.where(natural >= start, start, opening)
    return opening


def find_blocks(dealing_ref, found):
    groups, blocks = dealing_ref.shape
    for group in range(groups):

        def look(block, carry):
            where = jnp.int32(0)
            for at in range(blocks):
                where = jnp.where(dealing_ref[group, at] == block, jnp.int32(at), where)
            found[group, block] = where
            return carry

        lax.fori_loop(0, blocks, look, 0)


def gather_kernel(
    depth,
    lengths_ref,
    dealing_ref,
    tok_ref,
    cot_ref,
    gain_one_ref,
    bias_one_ref,
    gain_two_ref,
    bias_two_ref,
    wqkv_ref,
    wout_ref,
    wup_ref,
    wdown_ref,
    heads_out,
    units_out,
    xhat_out,
    cot_out,
    attended_out,
    total_out,
    g_up,
    g_down,
    g_sum,
    wqkv_t,
    wup_all,
    wdown_part,
    wout_part,
    prm_all,
    both,
    xhat_all,
    heads_buf,
    units_buf,
    slope_buf,
    wide,
    k_rows,
    wq_buf,
    prm_buf,
    found,
    in_sem,
    w_sem,
    wsend_sem,
    wrecv_sem,
    send_sem,
    recv_sem,
    out_sem,
):
    here = Place(depth)
    c, x, y, z, core = here.c, here.x, here.y, here.z, here.core
    count = depth * 4
    rows = tok_ref.shape[0]
    groups = dealing_ref.shape[0]
    units = wup_all.shape[1]
    half = prm_buf.shape[2]
    order = near_first(depth)

    own_in = (
        pltpu.make_async_copy(tok_ref, both.at[0, c], in_sem.at[0]),
        pltpu.make_async_copy(cot_ref, both.at[1, c], in_sem.at[1]),
    )
    for copy in own_in:
        copy.start()
    prm_rows = [
        ref[...].astype(WIDE).reshape(1, half) for ref in (gain_one_ref, bias_one_ref, gain_two_ref, bias_two_ref)
    ]
    prm_buf[x] = jnp.concatenate(prm_rows + prm_rows, axis=0)

    pair = c // 2
    per_half = count // 2
    owner = c // per_half
    inside = lax.rem(c, per_half)
    shared = []
    for part in range(3):
        shared.append(
            (
                wqkv_ref.at[:, pl.ds(pl.multiple_of(part * D + pair * 128, 128), 128)],
                wq_buf.at[x, part],
            )
        )
    shared.append(
        (
            wup_ref.at[:, pl.ds(pl.multiple_of(c * units, 128), units)],
            wup_all.at[pl.ds(pl.multiple_of(x * half, 128), half)],
        )
    )
    held = (
        (wdown_ref.at[pl.ds(pl.multiple_of(inside * units, 128), units)], wdown_part),
        (wout_ref.at[pl.ds(pl.multiple_of(inside * HD, HD), HD)], wout_part),
    )
    is_owner = owner == x
    for at, (source, place) in enumerate(shared):
        pltpu.make_async_copy(source, place, w_sem.at[at]).start()

    @pl.when(is_owner)
    def _():
        for at, (source, place) in enumerate(held):
            pltpu.make_async_copy(source, place, w_sem.at[5 + at]).start()

    here.greet()

    def remote(source, place, at):
        return pltpu.make_async_remote_copy(
            source,
            place,
            wsend_sem.at[at],
            wrecv_sem.at[at],
            device_id=here.across,
            device_id_type=MESH,
        )

    prm_copy = remote(prm_buf.at[x], prm_buf.at[x], 4)
    prm_copy.start()
    for at, (source, place) in enumerate(shared):
        remote(source, place, at).start()

    def passing(what, shard, way):
        device = (here.beside, here.twin, here.above, here.below)[way]
        return pltpu.make_async_remote_copy(
            both.at[what, shard],
            both.at[what, shard],
            send_sem.at[what, way, shard],
            recv_sem.at[what, shard],
            device_id=device,
            device_id_type=MESH,
        )

    def onward(what, shard, from_z):
        passing(what, shard, 0).start()

        @pl.when(jnp.logical_and(from_z <= z, here.has_above))
        def _():
            passing(what, shard, 2).start()

        @pl.when(jnp.logical_and(from_z >= z, here.has_below))
        def _():
            passing(what, shard, 3).start()

        passing(what, shard, 1).start()

    own_in[0].wait()
    onward(0, c, z)
    own_in[1].wait()
    onward(1, c, z)
    find_blocks(dealing_ref, found)

    for at, (source, place) in enumerate(shared):
        pltpu.make_async_copy(source, place, w_sem.at[at]).wait()
        remote(source, place, at).wait_recv()
    prm_copy.wait_recv()

    @pl.when(is_owner)
    def _():
        for at, (source, place) in enumerate(held):
            remote(source, place, 5 + at).start()

    odd = lax.rem(c, 2) == 1
    for side in range(2):
        prm_all[:, side * half : (side + 1) * half] = prm_buf[side]
        for part in range(3):
            turned = wq_buf[side, part].astype(WIDE).T
            chosen = jnp.where(odd, turned[HD:], turned[:HD])
            wqkv_t[part * HD : (part + 1) * HD, side * half : (side + 1) * half] = chosen.astype(
                NARROW
            )
    g_up[...] = jnp.zeros_like(g_up)
    g_down[...] = jnp.zeros_like(g_down)
    g_sum[...] = jnp.zeros_like(g_sum)

    kept = (
        (xhat_all, xhat_out),
        (both.at[1], cot_out),
        (heads_buf, heads_out),
        (units_buf, units_out),
    )

    def copy_out(at, shard):
        source, place = kept[at]
        return pltpu.make_async_copy(source.at[shard], place.at[shard], out_sem.at[at, shard])

    def ahead(shard):
        tokens = both[0, shard].astype(WIDE)
        average = jnp.mean(tokens, axis=-1, keepdims=True)
        centred = tokens - average
        variance = jnp.mean(centred * centred, axis=-1, keepdims=True)
        xhat = centred * lax.rsqrt(variance + EPSILON)
        xhat_all[shard] = xhat.astype(NARROW)
        n_one = (xhat * prm_all[0:1, :] + prm_all[1:2, :]).astype(NARROW)
        n_two = (xhat * prm_all[2:3, :] + prm_all[3:4, :]).astype(NARROW)
        mixed = dot(wqkv_t[...], n_one, NT)
        places = []
        for group in range(groups):
            natural = dealing_ref[group, shard] * BLK + lax.broadcasted_iota(jnp.int32, (1, BLK), 1)
            places.append(natural - opening_of(natural, starts_of(lengths_ref, group)))
        cosine, sine = turning(jnp.concatenate(places, axis=1))
        pieces = []
        for base in (0, HD):
            first, second = mixed[base : base + 8], mixed[base + 8 : base + 16]
            pieces += [
                first * cosine - second * sine,
                second * cosine + first * sine,
                mixed[base + 16 : base + HD],
            ]
        pieces.append(mixed[2 * HD : 3 * HD])
        heads_buf[shard, 0 : 3 * HD, :] = jnp.concatenate(pieces, axis=0).astype(NARROW)
        hidden = dot(n_two, wup_all[...])
        spread = 0.5 * (1.0 + lax.erf(hidden * (0.5**0.5)))
        units_buf[shard, :, 0:units] = (hidden * spread).astype(NARROW)
        slope_buf[shard] = spread + hidden * (jnp.exp(hidden * hidden * -0.5) * 0.3989422804014327)
        copy_out(0, shard).start()

    def behind(shard):
        cotangent = both[1, shard]
        heads_buf[shard, 3 * HD : 4 * HD, :] = dot(wout_part[...], cotangent, NT).astype(NARROW)
        g_hidden = (dot(cotangent, wdown_part[...], NT) * slope_buf[shard]).astype(NARROW)
        units_buf[shard, :, units : 2 * units] = g_hidden
        g_up[...] += dot(g_hidden, xhat_all[shard], TN)
        g_down[...] += dot(units_buf[shard, :, 0:units], cotangent, TN)
        g_sum[...] += jnp.sum(g_hidden.astype(WIDE).reshape(rows // 8, 8, units), axis=0)
        for at in (1, 2, 3):
            copy_out(at, shard).start()

    inner = jnp.logical_and(here.has_above, here.has_below)

    def sweep(what, work, beside_work):
        def step(at, carry):
            turn_no = at // 4
            kind = lax.rem(at, 4)
            late = jnp.where(kind >= 2, turn_no - 1, turn_no)
            from_z = pick2(z, jnp.clip(late, 0, depth - 1), order)
            next_z = pick2(z, jnp.clip(turn_no + 1, 0, depth - 1), order)
            shard_y = jnp.where(kind >= 2, 1 - y, y)
            shard_core = jnp.where(lax.rem(kind, 2) == 1, 1 - core, core)
            shard = here.at(from_z, shard_y, shard_core)
            live = jnp.logical_and(late >= 0, late < depth)

            early = jnp.logical_and(inner, turn_no == 2)
            is_own = jnp.logical_and(kind == 0, turn_no == 0)
            done = jnp.logical_or(is_own, jnp.logical_and(kind == 0, early))

            @pl.when(jnp.logical_and(live, jnp.logical_not(done)))
            def _():
                passing(what, shard, 1).wait_recv()

            @pl.when(jnp.logical_and(jnp.logical_and(kind == 0, live), jnp.logical_not(done)))
            def _():
                onward(what, shard, from_z)

            @pl.when(jnp.logical_and(kind == 2, live))
            def _():
                passing(what, shard, 1).start()

            @pl.when(jnp.logical_and(jnp.logical_and(kind == 1, turn_no == 1), inner))
            def _():
                following = here.at(next_z, y, core)
                passing(what, following, 1).wait_recv()
                onward(what, following, next_z)

            beside_work(at)

            @pl.when(live)
            def _():
                work(shard)

            return carry

        lax.fori_loop(0, 4 * depth + 4, step, 0)

    sweep(0, ahead, lambda at: None)

    @pl.when(is_owner)
    def _():
        for at, (source, place) in enumerate(held):
            pltpu.make_async_copy(source, place, w_sem.at[5 + at]).wait()

    @pl.when(jnp.logical_not(is_owner))
    def _():
        for at, (source, place) in enumerate(held):
            remote(source, place, 5 + at).wait_recv()

    spans = count // 2
    span = 2 * BLK

    def bring(at, carry):
        for group in range(groups):
            lanes = slice(group * BLK, (group + 1) * BLK)
            for side in range(2):
                source = found[group, 2 * at + side]
                part = heads_buf[source, 0 : 3 * HD, lanes]
                to = slice(side * BLK, (side + 1) * BLK)
                wide[group, at, 0:HD, to] = (part[0:HD].astype(WIDE) * HD ** (-0.5)).astype(NARROW)
                wide[group, at, HD : 2 * HD, to] = part[2 * HD : 3 * HD]
                k_rows[group, at, to, :] = part[HD : 2 * HD].astype(WIDE).T.astype(NARROW)
        return carry

    lax.fori_loop(0, spans, bring, 0)
    openings = [starts_of(lengths_ref, group) for group in range(groups)]

    def attend(at):
        group = lax.rem(at, groups)
        turn_no = at // groups
        mine = jnp.where(lax.rem(turn_no, 2) == 0, spans - 1 - turn_no // 2, turn_no // 2)
        natural = mine * span + lax.broadcasted_iota(jnp.int32, (1, span), 1)
        opening = opening_of(natural, [jnp.where(group == 0, *pair) for pair in zip(*openings)])
        key_in = lax.broadcasted_iota(jnp.int32, (2 * span, span), 0)
        queries = wide[group, mine, 0:HD, :]

        def add(keys_at, state, allowed):
            top, total, so_far = state
            keys = k_rows[group, pl.ds(2 * keys_at, 2)].reshape(2 * span, HD)
            raw = jnp.where(allowed, dot(keys, queries), MASKED)
            new_top = jnp.maximum(top, jnp.max(raw, axis=0, keepdims=True))
            risen = jnp.exp(raw - new_top)
            fade = jnp.exp(top - new_top)
            total = total * fade + jnp.sum(risen, axis=0, keepdims=True)
            values = jnp.concatenate(
                [wide[group, 2 * keys_at + side, HD : 2 * HD, :] for side in range(2)], axis=1
            )
            return new_top, total, so_far * fade + dot(values, risen.astype(NARROW))

        state = (
            jnp.full((1, span), MASKED, WIDE),
            jnp.zeros((1, span), WIDE),
            jnp.zeros((HD, span), WIDE),
        )
        last = mine // 2
        place = key_in + last * (2 * span)
        state = add(last, state, jnp.logical_and(place <= natural, place >= opening))

        def earlier(back, state):
            keys_at = last - 1 - back
            return add(keys_at, state, key_in >= opening - keys_at * (2 * span))

        top, total, so_far = lax.fori_loop(0, last, earlier, state)
        attended = so_far / total
        for side in range(2):
            attended_out[group, 2 * mine + side] = attended[:, side * BLK : (side + 1) * BLK]
        total_out[group, mine] = jnp.broadcast_to(top + jnp.log(total), (8, span))

    def attend_too(at):
        @pl.when(at < groups * spans)
        def _():
            attend(at)

    sweep(1, behind, attend_too)

    def finish(shard, carry):
        shard_z = shard // 4
        mine = lax.rem(shard, 2) == core
        column = lax.rem(shard // 2, 2) == y
        for what in range(2):

            @pl.when(mine)
            def _():
                passing(what, shard, 1).wait_send()

            @pl.when(jnp.logical_and(mine, column))
            def _():
                passing(what, shard, 0).wait_send()

                @pl.when(jnp.logical_and(shard_z <= z, here.has_above))
                def _():
                    passing(what, shard, 2).wait_send()

                @pl.when(jnp.logical_and(shard_z >= z, here.has_below))
                def _():
                    passing(what, shard, 3).wait_send()

        for at in range(4):
            copy_out(at, shard).wait()
        return carry

    lax.fori_loop(0, count, finish, 0)
    for at, (source, place) in enumerate(shared):
        remote(source, place, at).wait_send()
    prm_copy.wait_send()

    @pl.when(is_owner)
    def _():
        for at, (source, place) in enumerate(held):
            remote(source, place, 5 + at).wait_send()


def gather_call(depth, lengths, dealing, tok, cot, gains, w_qkv, w_out, w_up, w_down):
    count = depth * 4
    rows = tok.shape[0]
    groups = dealing.shape[0]
    spans, span = count // 2, 2 * BLK
    units = w_up.shape[1] // count
    any_spec = pl.BlockSpec(memory_space=pl.ANY)
    vmem = pl.BlockSpec(memory_space=pltpu.VMEM)
    smem = pl.BlockSpec(memory_space=pltpu.SMEM)
    shape = jax.ShapeDtypeStruct
    return pl.pallas_call(
        functools.partial(gather_kernel, depth),
        out_shape=(
            shape((count, 4 * HD, rows), NARROW),
            shape((count, rows, 2 * units), NARROW),
            shape((count, rows, D), NARROW),
            shape((count, rows, D), NARROW),
            shape((groups, count, HD, BLK), WIDE),
            shape((groups, spans, 8, span), WIDE),
            shape((units, D), WIDE),
            shape((units, D), WIDE),
            shape((8, units), WIDE),
            shape((3 * HD, D), NARROW),
            shape((D, units), NARROW),
            shape((units, D), NARROW),
            shape((HD, D), NARROW),
            shape((8, D), WIDE),
        ),
        in_specs=[smem, smem, any_spec, any_spec] + [vmem] * 4 + [any_spec] * 4,
        out_specs=(any_spec,) * 4 + (vmem,) * 10,
        scratch_shapes=[
            pltpu.VMEM((2, count, rows, D), NARROW),
            pltpu.VMEM((count, rows, D), NARROW),
            pltpu.VMEM((count, 4 * HD, rows), NARROW),
            pltpu.VMEM((count, rows, 2 * units), NARROW),
            pltpu.VMEM((count, rows, units), WIDE),
            pltpu.VMEM((groups, spans, 2 * HD, span), NARROW),
            pltpu.VMEM((groups, spans, span, HD), NARROW),
            pltpu.VMEM((2, 3, D // 2, 128), NARROW),
            pltpu.VMEM((2, 8, D // 2), WIDE),
            pltpu.SMEM((groups, count), jnp.int32),
            pltpu.SemaphoreType.DMA((2,)),
            pltpu.SemaphoreType.DMA((7,)),
            pltpu.SemaphoreType.DMA((7,)),
            pltpu.SemaphoreType.DMA((7,)),
            pltpu.SemaphoreType.DMA((2, 4, count)),
            pltpu.SemaphoreType.DMA((2, count)),
            pltpu.SemaphoreType.DMA((4, count)),
        ],
        name="gather_and_forward",
        compiler_params=pltpu.CompilerParams(
            collective_id=1, has_side_effects=True, vmem_limit_bytes=VMEM_LIMIT
        ),
    )(lengths, dealing, tok, cot, *gains, w_qkv, w_out, w_up, w_down)


def far_first(depth):
    return [list(reversed(row)) for row in near_first(depth)]


def unturn(rows, cosine, sine):
    first, second = rows[0:8], rows[8:16]
    return jnp.concatenate(
        [first * cosine + second * sine, second * cosine - first * sine, rows[16:]], axis=0
    )


def reduce_kernel(
    depth,
    lengths_ref,
    dealing_ref,
    total_in,
    prm_all,
    g_sum,
    attended_hbm,
    wout_hbm,
    wdown_hbm,
    units_hbm,
    g_up_hbm,
    wup_hbm,
    wqkv_hbm,
    g_down_hbm,
    heads_hbm,
    xhat_in,
    cot_in,
    sum_out,
    sum_back,
    inbox,
    wout_ref,
    down_ref,
    vec_ref,
    attended_in,
    wout_part,
    wdown_part,
    units_in,
    g_up,
    wup_all,
    wqkv_t,
    g_down,
    heads_in,
    w_heads_back,
    give_buf,
    sum_buf,
    beside_buf,
    line_buf,
    wide,
    q_rows,
    k_rows,
    v_rows,
    g_rows,
    g_key,
    g_value,
    turned_all,
    by_token,
    stream,
    g_heads,
    g_wout,
    sum_heads,
    vectors,
    grads,
    grads_in,
    mail,
    wout_in,
    down_in,
    found,
    first_sem,
    send_sem,
    recv_twin,
    recv_beside,
    recv_z,
    stream_sem,
    across_send,
    across_recv,
    mail_send,
    mail_recv,
):
    here = Place(depth)
    c, x, y, z, core = here.c, here.x, here.y, here.z, here.core
    rows = sum_out.shape[0]
    units = wup_all.shape[1]
    groups = dealing_ref.shape[0]
    count = 4 * depth
    brought = [
        pltpu.make_async_copy(source, place, first_sem.at[at])
        for at, (source, place) in enumerate(
            (
                (attended_hbm, attended_in),
                (wout_hbm, wout_part),
                (wdown_hbm, wdown_part),
                (units_hbm, units_in),
                (g_up_hbm, g_up),
                (wup_hbm, wup_all),
                (wqkv_hbm, wqkv_t),
                (g_down_hbm, g_down),
                (heads_hbm, heads_in),
            )
        )
    ]
    for copy in brought:
        copy.start()
    spans, span = count // 2, 2 * BLK
    scale = HD ** (-0.5)
    piece = D // (2 * count)
    order = far_first(depth)

    def shard_of(at):
        kind = lax.rem(at, 4)
        to_y = jnp.where(lax.rem(kind, 2) == 1, y, 1 - y)
        to_core = jnp.where(kind < 2, 1 - core, core)
        return here.at(pick2(z, at // 4, order), to_y, to_core)

    def load(at):
        shard, slot = shard_of(at), lax.rem(at, 2)
        return (
            pltpu.make_async_copy(xhat_in.at[shard], stream.at[0, slot], stream_sem.at[0, slot]),
            pltpu.make_async_copy(cot_in.at[shard], stream.at[1, slot], stream_sem.at[1, slot]),
        )

    here.greet_all()

    def crossing(source, place, at):
        return pltpu.make_async_remote_copy(
            source,
            place,
            across_send.at[at],
            across_recv.at[at],
            device_id=here.across,
            device_id_type=MESH,
        )

    half_down = g_down.shape[0] // 2
    half_wout = HD // 2
    send_down = crossing(g_down.at[pl.ds((1 - x) * half_down, half_down)], down_in, 0)
    send_wout = crossing(g_wout.at[pl.ds((1 - x) * half_wout, half_wout)], wout_in, 1)
    send_grads = [crossing(grads.at[part, 1 - x], grads_in.at[part], 2 + part) for part in range(2)]

    def to_twin(what, slot):
        return pltpu.make_async_remote_copy(
            give_buf.at[slot],
            sum_buf.at[what, slot],
            send_sem.at[what, 0, slot],
            recv_twin.at[what, slot],
            device_id=here.twin,
            device_id_type=MESH,
        )

    def to_beside(what, to_z):
        return pltpu.make_async_remote_copy(
            sum_buf.at[what, to_z],
            beside_buf.at[what, to_z],
            send_sem.at[what, 1, to_z],
            recv_beside.at[what, to_z],
            device_id=here.beside,
            device_id_type=MESH,
        )

    def to_above(what, to_z):
        return pltpu.make_async_remote_copy(
            sum_buf.at[what, depth + to_z],
            line_buf.at[what, to_z],
            send_sem.at[what, 2, to_z],
            recv_z.at[what, to_z],
            device_id=here.above,
            device_id_type=MESH,
        )

    def over_slot(to_z, at_z):
        return jnp.where(to_z == at_z, depth, to_z)

    def to_below(what, to_z):
        slot = over_slot(to_z, z - 1)
        return pltpu.make_async_remote_copy(
            sum_buf.at[what, depth + to_z],
            line_buf.at[what, slot],
            send_sem.at[what, 2, to_z],
            recv_z.at[what, slot],
            device_id=here.below,
            device_id_type=MESH,
        )

    def from_above(what, to_z):
        slot = over_slot(to_z, z)
        return pltpu.make_async_remote_copy(
            sum_buf.at[what, depth + to_z],
            line_buf.at[what, slot],
            send_sem.at[what, 2, to_z],
            recv_z.at[what, slot],
            device_id=here.above,
            device_id_type=MESH,
        )

    def pass_on(what, at, part):
        to_z = pick2(z, at // 4, order)
        kind = lax.rem(at, 4)
        slot = lax.rem(kind, 2) * depth + to_z

        @pl.when(kind < 2)
        def _():
            if what == 1:
                to_twin(0, slot).wait_send()
            give_buf[slot] = part.astype(NARROW)
            to_twin(what, slot).start()

        @pl.when(kind >= 2)
        def _():
            to_twin(what, slot).wait_recv()
            sum_buf[what, slot] = (part + sum_buf[what, slot].astype(WIDE)).astype(NARROW)

        @pl.when(kind == 2)
        def _():
            to_beside(what, to_z).start()

    def chain(what, at):
        to_z = pick2(z, at, order)
        slot = depth + to_z
        to_beside(what, to_z).wait_recv()

        def add(incoming):
            for part in range(2):
                half = slice(part * rows // 2, (part + 1) * rows // 2)
                total = sum_buf[what, slot, half, :].astype(WIDE)
                total = total + beside_buf[what, to_z, half, :].astype(WIDE)
                if incoming:
                    total = total + line_buf[what, to_z, half, :].astype(WIDE)
                sum_buf[what, slot, half, :] = total.astype(NARROW)

        @pl.when(to_z > z)
        def _():
            @pl.when(here.has_below)
            def _():
                to_above(what, to_z).wait_recv()
                add(True)

            @pl.when(jnp.logical_not(here.has_below))
            def _():
                add(False)

            to_above(what, to_z).start()

        @pl.when(to_z < z)
        def _():
            @pl.when(here.has_above)
            def _():
                from_above(what, to_z).wait_recv()
                add(True)

            @pl.when(jnp.logical_not(here.has_above))
            def _():
                add(False)

            to_below(what, to_z).start()

    def gather_total(what):
        @pl.when(here.has_below)
        def _():
            to_above(what, z).wait_recv()

        @pl.when(jnp.logical_not(here.has_below))
        def _():
            line_buf[what, z] = jnp.zeros((rows, D), NARROW)

        @pl.when(here.has_above)
        def _():
            from_above(what, z).wait_recv()

        @pl.when(jnp.logical_not(here.has_above))
        def _():
            line_buf[what, depth] = jnp.zeros((rows, D), NARROW)

        return (
            sum_buf[what, depth + z].astype(WIDE)
            + beside_buf[what, z].astype(WIDE)
            + line_buf[what, z].astype(WIDE)
            + line_buf[what, depth].astype(WIDE)
        )

    def give_out(at, carry):
        shard = shard_of(at)
        parts = []
        for group in range(groups):
            attended = attended_in[group, dealing_ref[group, shard]].astype(NARROW)
            parts.append(dot(attended, wout_part[...], TN))
        part = jnp.concatenate(parts, axis=0) + dot(units_in[shard, :, 0:units], wdown_part[...])
        pass_on(0, at, part)
        return carry

    for copy in brought[:4]:
        copy.wait()
    lax.fori_loop(0, count, give_out, 0)
    for copy in brought[4:]:
        copy.wait()
    send_down.start()

    def settle(chunk, part, raw, weights, sums, column):
        scaled = raw * column[:, 2 - 2 * part : 3 - 2 * part] + sums * column[:, 3 - 2 * part : 4 - 2 * part]
        gain_sum = jnp.sum(weights * raw, axis=1, keepdims=True)
        bias_sum = jnp.sum(weights * sums, axis=1, keepdims=True)
        row = pl.ds(pl.multiple_of(chunk * 128, 128), 128)
        if part == 0:
            vectors[row, 0:1] = gain_sum
            vectors[row, 1:2] = bias_sum
        else:
            lane = lax.broadcasted_iota(jnp.int32, scaled.shape, 1)
            scaled = jnp.where(lane == 0, gain_sum, scaled)
            scaled = jnp.where(lane == 1, bias_sum, scaled)
            scaled = jnp.where(lane == 2, vectors[row, 0:1], scaled)
            scaled = jnp.where(lane == 3, vectors[row, 1:2], scaled)
        per = 128 // piece
        for at in range(per):
            grads[part, at % 2, chunk * (per // 2) + at // 2] = scaled[at * piece : (at + 1) * piece]

    sum_units = jnp.sum(g_sum[...], axis=0, keepdims=True)

    def settle_up(chunk, carry):
        lanes = pl.ds(pl.multiple_of(chunk * 128, 128), 128)
        weights = wup_all[lanes, :].astype(WIDE)
        settle(chunk, 0, g_up[:, lanes].T, weights, sum_units, prm_all[:, lanes].T)
        return carry

    lax.fori_loop(0, D // 128, settle_up, 0)
    send_grads[0].start()
    find_blocks(dealing_ref, found)
    w_heads_back[0:HD, :] = jnp.zeros((HD, D), NARROW)
    w_heads_back[HD:, :] = wqkv_t[...]
    g_heads[...] = jnp.zeros_like(g_heads)
    g_wout[...] = jnp.zeros_like(g_wout)
    sum_heads[...] = jnp.zeros_like(sum_heads)

    for group in range(groups):
        lanes = slice(group * BLK, (group + 1) * BLK)
        starts = starts_of(lengths_ref, group)

        def bring(at, carry, group=group, lanes=lanes):
            for side in range(2):
                source = found[group, 2 * at + side]
                part = heads_in[source, :, lanes]
                to = slice(side * BLK, (side + 1) * BLK)
                queries = part[0:HD].astype(WIDE) * scale
                keys = part[HD : 2 * HD]
                grads_part = part[3 * HD : 4 * HD]
                wide[at, 0:HD, to] = queries.astype(NARROW)
                wide[at, HD : 2 * HD, to] = keys
                wide[at, 2 * HD : 3 * HD, to] = grads_part
                q_rows[at, to, :] = queries.T.astype(NARROW)
                k_rows[at, to, :] = keys.astype(WIDE).T.astype(NARROW)
                v_rows[at, to, :] = part[2 * HD : 3 * HD].astype(WIDE).T.astype(NARROW)
                g_rows[at, to, :] = grads_part.astype(WIDE).T.astype(NARROW)
            g_key[at] = jnp.zeros((span, HD), WIDE)
            g_value[at] = jnp.zeros((span, HD), WIDE)
            return carry

        lax.fori_loop(0, spans, bring, 0)
        chain(0, 2 * group)

        def one_span(at, carry, group=group, starts=starts):
            natural = at * span + lax.broadcasted_iota(jnp.int32, (1, span), 1)
            opening = opening_of(natural, starts)
            key_in = lax.broadcasted_iota(jnp.int32, (2 * span, span), 0)
            queries = wide[at, 0:HD, :]
            g_attended = wide[at, 2 * HD : 3 * HD, :]
            attended = jnp.concatenate(
                [attended_in[group, 2 * at], attended_in[group, 2 * at + 1]], axis=1
            )
            row_dot = jnp.sum(attended * g_attended.astype(WIDE), axis=0, keepdims=True)
            log_total = total_in[group, at, 0:1, :]

            def add(pair, so_far, allowed):
                two = pl.ds(2 * pair, 2)
                keys = k_rows[two].reshape(2 * span, HD)
                values = v_rows[two].reshape(2 * span, HD)
                scores = dot(keys, queries)
                probs = jnp.where(allowed, jnp.exp(scores - log_total), 0.0)
                g_scores = (probs * (dot(values, g_attended) - row_dot)).astype(NARROW)
                g_key[two] += dot(g_scores, q_rows[at]).reshape(2, span, HD)
                g_value[two] += dot(probs.astype(NARROW), g_rows[at]).reshape(2, span, HD)
                keys_t = jnp.concatenate(
                    [wide[2 * pair + side, HD : 2 * HD, :] for side in range(2)], axis=1
                )
                return so_far + dot(keys_t, g_scores)

            def earlier(pair, so_far):
                return add(pair, so_far, key_in >= opening - pair * (2 * span))

            last = at // 2
            so_far = lax.fori_loop(0, last, earlier, jnp.zeros((HD, span), WIDE))
            place = key_in + last * (2 * span)
            so_far = add(last, so_far, jnp.logical_and(place <= natural, place >= opening))
            cosine, sine = turning(natural - opening)
            turned = jnp.concatenate([attended, unturn(so_far * scale, cosine, sine)], axis=0)
            for side in range(2):
                part = turned[:, side * BLK : (side + 1) * BLK]
                turned_all[group, 2 * at + side, 0 : 2 * HD, :] = part.astype(NARROW)
            return carry

        lax.fori_loop(0, spans, one_span, 0)
        chain(0, 2 * group + 1)

        def give(at, carry, group=group, starts=starts):
            natural = at * span + lax.broadcasted_iota(jnp.int32, (1, span), 1)
            cosine, sine = turning(natural - opening_of(natural, starts))
            keys = unturn(g_key[at].T, cosine, sine)
            turned = jnp.concatenate([keys, g_value[at].T], axis=0)
            for side in range(2):
                part = turned[:, side * BLK : (side + 1) * BLK]
                turned_all[group, 2 * at + side, 2 * HD : 4 * HD, :] = part.astype(NARROW)
                whole = turned_all[group, 2 * at + side].astype(WIDE)
                by_token[group, 2 * at + side] = whole.T.astype(NARROW)
            return carry

        lax.fori_loop(0, spans, give, 0)

    for copy in load(0):
        copy.start()

    def give_back(at, carry):
        shard, slot = shard_of(at), lax.rem(at, 2)
        blocks = [dealing_ref[group, shard] for group in range(groups)]
        heads = jnp.concatenate([by_token[group, blocks[group]] for group in range(groups)], axis=0)
        g_hidden = units_in[shard, :, units : 2 * units]
        part = dot(heads, w_heads_back[...]) * prm_all[0:1, :] + dot(
            g_hidden, wup_all[...], NT
        ) * prm_all[2:3, :]
        pass_on(1, at, part)

        @pl.when(at + 1 < count)
        def _():
            for copy in load(at + 1):
                copy.start()

        for copy in load(at):
            copy.wait()
        turned = jnp.concatenate([turned_all[group, blocks[group]] for group in range(groups)], axis=1)
        g_wout[...] += dot(turned[0:HD], stream[1, slot])
        g_heads[HD:, :] += dot(turned[HD:], stream[0, slot])
        sum_heads[...] += jnp.sum(heads.astype(WIDE).reshape(rows // 8, 8, 4 * HD), axis=0)

        @pl.when(at == count - 4)
        def _():
            chain(1, 0)

        return carry

    lax.fori_loop(0, count, give_back, 0)
    send_wout.start()
    sum_row = jnp.sum(sum_heads[...], axis=0, keepdims=True)

    def settle_qkv(chunk, carry):
        lanes = pl.ds(pl.multiple_of(chunk * 128, 128), 128)
        weights = w_heads_back[:, lanes].astype(WIDE).T
        settle(chunk, 1, g_heads[:, lanes].T, weights, sum_row, prm_all[:, lanes].T)
        return carry

    lax.fori_loop(0, D // 128, settle_qkv, 0)
    send_grads[1].start()

    def post(part, to_c):
        return pltpu.make_async_remote_copy(
            mail.at[part, to_c],
            inbox.at[part, c],
            mail_send.at[part, to_c],
            mail_recv.at[part, c],
            device_id=(to_c, x),
            device_id_type=MESH,
        )

    def collect(part, from_c):
        return pltpu.make_async_remote_copy(
            mail.at[part, from_c],
            inbox.at[part, from_c],
            mail_send.at[part, from_c],
            mail_recv.at[part, from_c],
            device_id=(from_c, x),
            device_id_type=MESH,
        )

    def mail_out(part):
        send_grads[part].wait_recv()

        def fold(to_c, carry):
            mail[part, to_c] = (grads[part, x, to_c] + grads_in[part, to_c]).astype(NARROW)
            return carry

        lax.fori_loop(0, count, fold, 0)

        def start(offset, carry):
            post(part, lax.rem(c + offset, count)).start()
            return carry

        lax.fori_loop(1, count, start, 0)
        inbox[part, c] = mail[part, c]

    mail_out(0)
    chain(1, 1)
    mail_out(1)

    def rest(at, carry):
        chain(1, at)
        return carry

    lax.fori_loop(2, depth, rest, 0)

    sum_out[...] = gather_total(0)
    send_down.wait()
    down_ref[...] = g_down[pl.ds(x * half_down, half_down), :] + down_in[...]
    send_wout.wait()
    wout_ref[...] = g_wout[pl.ds(x * half_wout, half_wout), :] + wout_in[...]

    def close(offset, carry):
        other = lax.rem(c + offset, count)
        for part in range(2):
            collect(part, other).wait_recv()
            post(part, other).wait_send()
        return carry

    lax.fori_loop(1, count, close, 0)
    for part in range(2):
        send_grads[part].wait_send()
    together = jnp.zeros((piece, 128), WIDE)
    for from_c in range(count):
        together = together + inbox[1, from_c, :, 0:128].astype(WIDE)
    vec_ref[...] = together.T[0:8]
    sum_back[...] = gather_total(1)

    def finish(to_z, carry):
        to_twin(1, to_z).wait_send()
        to_twin(1, depth + to_z).wait_send()
        for what in range(2):
            to_beside(what, to_z).wait_send()

            @pl.when(to_z > z)
            def _():
                to_above(what, to_z).wait_send()

            @pl.when(to_z < z)
            def _():
                to_below(what, to_z).wait_send()

        return carry

    lax.fori_loop(0, depth, finish, 0)


def reduce_call(depth, scalars, small, large, rows):
    count = depth * 4
    groups = scalars[0].shape[0]
    spans, span = count // 2, 2 * BLK
    piece = D // (2 * count)
    units = large[5].shape[1]
    vmem = pl.BlockSpec(memory_space=pltpu.VMEM)
    smem = pl.BlockSpec(memory_space=pltpu.SMEM)
    any_spec = pl.BlockSpec(memory_space=pl.ANY)
    shape = jax.ShapeDtypeStruct
    message = (rows, D)
    row_form = pltpu.VMEM((spans, span, HD), NARROW)
    return pl.pallas_call(
        functools.partial(reduce_kernel, depth),
        out_shape=(
            shape((rows, D), WIDE),
            shape((rows, D), WIDE),
            shape((2, count, piece, 256), NARROW),
            shape((HD // 2, D), WIDE),
            shape((units // 2, D), WIDE),
            shape((8, piece), WIDE),
        ),
        in_specs=[smem] * 2 + [vmem] * 3 + [any_spec] * 11,
        out_specs=(vmem,) * 6,
        scratch_shapes=[pltpu.VMEM(array.shape, array.dtype) for array in large[:9]]
        + [
            pltpu.VMEM((4 * HD, D), NARROW),
            pltpu.VMEM((2 * depth,) + message, NARROW),
            pltpu.VMEM((2, 2 * depth) + message, NARROW),
            pltpu.VMEM((2, depth) + message, NARROW),
            pltpu.VMEM((2, depth + 1) + message, NARROW),
            pltpu.VMEM((spans, 3 * HD, span), NARROW),
            row_form,
            row_form,
            row_form,
            row_form,
            pltpu.VMEM((spans, span, HD), WIDE),
            pltpu.VMEM((spans, span, HD), WIDE),
            pltpu.VMEM((groups, count, 4 * HD, BLK), NARROW),
            pltpu.VMEM((groups, count, BLK, 4 * HD), NARROW),
            pltpu.VMEM((2, 2, rows, D), NARROW),
            pltpu.VMEM((4 * HD, D), WIDE),
            pltpu.VMEM((HD, D), WIDE),
            pltpu.VMEM((8, 4 * HD), WIDE),
            pltpu.VMEM((D, 128), WIDE),
            pltpu.VMEM((2, 2, count, piece, 256), WIDE),
            pltpu.VMEM((2, count, piece, 256), WIDE),
            pltpu.VMEM((2, count, piece, 256), NARROW),
            pltpu.VMEM((HD // 2, D), WIDE),
            pltpu.VMEM((units // 2, D), WIDE),
            pltpu.SMEM((groups, count), jnp.int32),
            pltpu.SemaphoreType.DMA((9,)),
            pltpu.SemaphoreType.DMA((2, 3, 2 * depth)),
            pltpu.SemaphoreType.DMA((2, 2 * depth)),
            pltpu.SemaphoreType.DMA((2, depth)),
            pltpu.SemaphoreType.DMA((2, depth + 1)),
            pltpu.SemaphoreType.DMA((2, 2)),
            pltpu.SemaphoreType.DMA((4,)),
            pltpu.SemaphoreType.DMA((4,)),
            pltpu.SemaphoreType.DMA((2, count)),
            pltpu.SemaphoreType.DMA((2, count)),
        ],
        name="backward_and_reduce",
        compiler_params=pltpu.CompilerParams(
            collective_id=2, has_side_effects=True, vmem_limit_bytes=VMEM_LIMIT
        ),
    )(*scalars, *small, *large)


def last_kernel(
    tok_ref,
    cot_ref,
    sum_out,
    sum_back,
    inbox,
    wout_in,
    down_in,
    vec_in,
    out_ref,
    grad_ref,
    qkv_ref,
    wout_ref,
    up_ref,
    down_ref,
    vec_a,
    vec_b,
    vec_c,
    vec_d,
):
    tokens = tok_ref[...].astype(WIDE)
    out_ref[...] = (tokens + sum_out[...]).astype(NARROW)
    average = jnp.mean(tokens, axis=-1, keepdims=True)
    centred = tokens - average
    variance = jnp.mean(centred * centred, axis=-1, keepdims=True)
    rise = lax.rsqrt(variance + EPSILON)
    xhat = centred * rise
    g_xhat = sum_back[...]
    along = jnp.mean(g_xhat * xhat, axis=-1, keepdims=True)
    level = jnp.mean(g_xhat, axis=-1, keepdims=True)
    grad_ref[...] = cot_ref[...].astype(WIDE) + rise * (g_xhat - level - xhat * along)
    count = inbox.shape[1]
    units = up_ref.shape[1] // count
    for from_c in range(count):
        up_ref[:, from_c * units : (from_c + 1) * units] = inbox[0, from_c].astype(WIDE)
    for pair in range(count // 2):
        left = inbox[1, 2 * pair].astype(WIDE)
        right = inbox[1, 2 * pair + 1].astype(WIDE)
        for part in range(3):
            lanes = slice((part + 1) * HD, (part + 2) * HD)
            to = part * D + pair * 128
            qkv_ref[:, to : to + 128] = jnp.concatenate([left[:, lanes], right[:, lanes]], axis=1)
    wout_ref[...] = wout_in[...]
    down_ref[...] = down_in[...]
    for at, ref in enumerate((vec_a, vec_b, vec_c, vec_d)):
        ref[...] = vec_in[at]


def last_call(tok, cot, sum_out, sum_back, inbox, wout_in, down_in, vec_in):
    rows = tok.shape[0]
    _, count, piece, units = inbox.shape
    shape = jax.ShapeDtypeStruct
    steps = 2

    def cut(array_shape):
        return pl.BlockSpec((array_shape[0] // steps,) + array_shape[1:], lambda at: (at, 0))

    whole = pl.BlockSpec((8, piece), lambda at: (0, 0))
    vector = pl.BlockSpec((piece,), lambda at: (0,))
    letters = pl.BlockSpec((2, count, piece // steps, units), lambda at: (0, 0, at, 0))
    outs = (
        shape((rows, D), NARROW),
        shape((rows, D), WIDE),
        shape((piece, 3 * D), WIDE),
        shape(wout_in.shape, WIDE),
        shape((piece, count * units), WIDE),
        shape(down_in.shape, WIDE),
    )
    return pl.pallas_call(
        last_kernel,
        grid=(steps,),
        out_shape=outs + (shape((piece,), WIDE),) * 4,
        in_specs=[cut(array.shape) for array in (tok, cot, sum_out, sum_back)]
        + [letters, cut(wout_in.shape), cut(down_in.shape), whole],
        out_specs=tuple(cut(array.shape) for array in outs) + (vector,) * 4,
        name="last_rows",
        compiler_params=pltpu.CompilerParams(vmem_limit_bytes=VMEM_LIMIT),
    )(tok, cot, sum_out, sum_back, inbox, wout_in, down_in, vec_in)


def fast_shards(depth, *arguments):
    tokens, cotangent, lengths, dealing = arguments[:4]
    gains = arguments[4:8]
    rows = tokens.shape[0] * tokens.shape[1]
    tok = tokens.reshape(rows, D)
    cot = cotangent.reshape(rows, D)
    forward = gather_call(depth, lengths, dealing, tok, cot, gains, *arguments[8:])
    heads, units, xhat, cot_all, attended, total, g_up, g_down, g_sum = forward[:9]
    wqkv_t, wup_all, wdown_part, wout_part, prm_all = forward[9:]
    small = (total, prm_all, g_sum)
    large = (
        attended, wout_part, wdown_part, units, g_up, wup_all, wqkv_t, g_down, heads, xhat, cot_all
    )
    out, grad_tokens, qkv_part, out_part, up_part, down_part, *vectors = last_call(
        tok, cot, *reduce_call(depth, (lengths, dealing), small, large, rows)
    )
    return (
        out.reshape(tokens.shape),
        grad_tokens.reshape(tokens.shape),
        *vectors,
        qkv_part,
        out_part,
        up_part,
        down_part,
    )


def solution(mesh):
    placed = (
        P("wsh", "ctx", None),
        P("wsh", "ctx", None),
        P("wsh", None),
        P("wsh", None),
        P("wsh"),
        P("wsh"),
        P("wsh"),
        P("wsh"),
        P("wsh", None),
        P("wsh", None),
        P("wsh", None),
        P("wsh", None),
    )
    ctx_size = mesh.shape["ctx"]
    by_heads = ctx_size == H and mesh.shape["wsh"] == 2
    body = functools.partial(fast_shards, ctx_size // 4) if by_heads else shards
    return jax.shard_map(
        body,
        mesh=mesh,
        in_specs=placed,
        out_specs=(
            P("wsh", "ctx", None),
            P("wsh", "ctx", None),
            P(("ctx", "wsh")),
            P(("ctx", "wsh")),
            P(("ctx", "wsh")),
            P(("ctx", "wsh")),
            P(("ctx", "wsh"), None),
            P(("ctx", "wsh"), None),
            P(("ctx", "wsh"), None),
            P(("ctx", "wsh"), None),
        ),
        check_vma=False,
    )
```

```python
import functools

import jax
import jax.numpy as jnp
from jax import lax
from jax.experimental import pallas as pl
from jax.experimental.pallas import tpu as pltpu
from jax.sharding import PartitionSpec as P

D = 1024
H = 16
HD = 64
ROT = 16
BLK = 128


EPSILON = 1e-05
MASKED = -1e30
WIDE = jnp.float32
NARROW = jnp.bfloat16


def norm_layer(values_in, scale_by, shift_by):
    average = jnp.mean(values_in, axis=-1, keepdims=True)
    centred = values_in - average
    variance = jnp.mean(centred * centred, axis=-1, keepdims=True)
    return centred * lax.rsqrt(variance + EPSILON) * scale_by + shift_by


def rotate(values_in, places):
    split_at = ROT // 2
    frequency = 10000.0 ** (-2.0 * jnp.arange(split_at, dtype=WIDE) / ROT)
    angles = places.astype(WIDE)[:, None] * frequency[None, :]
    cosine_table = jnp.cos(angles)[:, None, :]
    sine_table = jnp.sin(angles)[:, None, :]
    first_half = values_in[..., :split_at]
    second_half = values_in[..., split_at:ROT]
    return jnp.concatenate(
        [
            first_half * cosine_table - second_half * sine_table,
            second_half * cosine_table + first_half * sine_table,
            values_in[..., ROT:],
        ],
        axis=-1,
    )


def natural_rows(dealing_row, offset_row, row_count):
    ordinal = offset_row + jnp.arange(row_count, dtype=jnp.int32)
    table_ids = jnp.arange(dealing_row.shape[0], dtype=jnp.int32)
    picked = jnp.sum(
        jnp.where((ordinal // BLK)[:, None] == table_ids[None, :], dealing_row[None, :], 0), axis=1
    )
    return picked * BLK + ordinal % BLK


def sequence_openings(natural, lengths_row):
    openings = jnp.cumsum(lengths_row) - lengths_row
    return jnp.max(jnp.where(openings[None, :] <= natural[:, None], openings[None, :], 0), axis=1)


def score_block(queries, block_keys, offset_row, natural_q, opening_q, dealing_row):
    row_count = block_keys.shape[0]
    key_natural = natural_rows(dealing_row, offset_row, row_count)
    scores = jnp.einsum(
        "qhd,khd->hqk", queries, block_keys.reshape(row_count, H, HD), preferred_element_type=WIDE
    ) * HD ** (-0.5)
    allowed = (key_natural[None, :] <= natural_q[:, None]) & (
        key_natural[None, :] >= opening_q[:, None]
    )
    return (scores, allowed[None])


def fold_blocks(step_fn, state_in, arrays):
    row_count = arrays[0].shape[0]
    block_width = 1024
    stacked = tuple(
        (
            member.reshape((row_count // block_width, block_width) + member.shape[1:])
            for member in arrays
        )
    )
    offsets = jnp.arange(row_count // block_width, dtype=jnp.int32) * block_width

    def inner_step(state_now, block_item):
        return (step_fn(state_now, block_item[0], block_item[1]), None)

    state_out, _ = lax.scan(inner_step, state_in, (stacked, offsets))
    return state_out


def project(tokens_f, weights, places):
    w_qkv, w_out, w_up, w_down, gain_one, bias_one, gain_two, bias_two = weights
    all_rows = tokens_f.shape[0]
    normed_one = norm_layer(tokens_f, gain_one.astype(WIDE), bias_one.astype(WIDE)).astype(NARROW)
    normed_two = norm_layer(tokens_f, gain_two.astype(WIDE), bias_two.astype(WIDE)).astype(NARROW)
    mixed = jnp.dot(normed_one, w_qkv, preferred_element_type=WIDE).reshape(all_rows, 3, H, HD)
    queries = rotate(mixed[:, 0], places).astype(NARROW)
    keys_here = rotate(mixed[:, 1], places).astype(NARROW).reshape(all_rows, D)
    values_here = mixed[:, 2].astype(NARROW).reshape(all_rows, D)
    hidden = jnp.dot(normed_two, w_up, preferred_element_type=WIDE)
    activated = jax.nn.gelu(hidden, approximate=False).astype(NARROW)
    return (normed_one, normed_two, queries, keys_here, values_here, hidden, activated)


def attend(queries, keys_here, values_here, natural_q, opening_q, dealing_row):
    local_rows = queries.shape[0]

    def max_step(state_in, block_arrays, offset_row):
        row_top, row_total = state_in
        scores, allowed = score_block(
            queries, block_arrays[0], offset_row, natural_q, opening_q, dealing_row
        )
        new_top = jnp.maximum(row_top, jnp.max(jnp.where(allowed, scores, MASKED), axis=-1))
        kept_terms = jnp.where(allowed, jnp.exp(scores - new_top[..., None]), 0.0)
        return (new_top, row_total * jnp.exp(row_top - new_top) + jnp.sum(kept_terms, axis=-1))

    start_state = (jnp.full((H, local_rows), MASKED, WIDE), jnp.zeros((H, local_rows), WIDE))
    row_top, row_total = fold_blocks(
        max_step, start_state, (lax.all_gather(keys_here, "ctx", axis=0, tiled=True),)
    )
    log_total = row_top + jnp.log(row_total)

    def value_step(state_in, block_arrays, offset_row):
        scores, allowed = score_block(
            queries, block_arrays[0], offset_row, natural_q, opening_q, dealing_row
        )
        soft_probs = jnp.where(allowed, jnp.exp(scores - log_total[..., None]), 0.0).astype(NARROW)
        row_count = block_arrays[1].shape[0]
        return state_in + jnp.einsum(
            "hqk,khd->qhd",
            soft_probs,
            block_arrays[1].reshape(row_count, H, HD),
            preferred_element_type=WIDE,
        )

    attended = fold_blocks(
        value_step,
        jnp.zeros((local_rows, H, HD), WIDE),
        (
            lax.all_gather(keys_here, "ctx", axis=0, tiled=True),
            lax.all_gather(values_here, "ctx", axis=0, tiled=True),
        ),
    )
    return (attended, log_total)


def attention_back(
    queries,
    keys_here,
    values_here,
    g_attended,
    row_dot,
    log_total,
    natural_q,
    opening_q,
    dealing_row,
):
    local_rows = queries.shape[0]
    scale_factor = HD ** (-0.5)
    gathered_keys, gathered_values = (
        lax.all_gather(keys_here, "ctx", axis=0, tiled=True),
        lax.all_gather(values_here, "ctx", axis=0, tiled=True),
    )
    group_rows = gathered_keys.shape[0]
    key_span = 1024

    def key_block(state_in, block_item):
        block_keys, block_values, offset_row = block_item
        scores, allowed = score_block(
            queries, block_keys, offset_row, natural_q, opening_q, dealing_row
        )
        soft_probs = jnp.where(allowed, jnp.exp(scores - log_total[..., None]), 0.0)
        g_probs = jnp.einsum(
            "qhd,khd->hqk",
            g_attended,
            block_values.reshape(key_span, H, HD),
            preferred_element_type=WIDE,
        )
        g_scores = (soft_probs * (g_probs - row_dot[..., None])).astype(NARROW)
        state_out = (
            state_in
            + jnp.einsum(
                "hqk,khd->qhd",
                g_scores,
                block_keys.reshape(key_span, H, HD),
                preferred_element_type=WIDE,
            )
            * scale_factor
        )
        key_terms = (
            jnp.einsum("hqk,qhd->khd", g_scores, queries, preferred_element_type=WIDE)
            * scale_factor
        )
        value_terms = jnp.einsum(
            "hqk,qhd->khd", soft_probs.astype(NARROW), g_attended, preferred_element_type=WIDE
        )
        return (
            state_out,
            jnp.concatenate(
                [key_terms.reshape(key_span, D), value_terms.reshape(key_span, D)], axis=1
            ),
        )

    block_total = group_rows // key_span
    block_starts = jnp.arange(block_total, dtype=jnp.int32) * key_span
    stacked_blocks = (
        gathered_keys.reshape(block_total, key_span, D),
        gathered_values.reshape(block_total, key_span, D),
        block_starts,
    )
    g_queries, stacked_terms = lax.scan(
        key_block, jnp.zeros((local_rows, H, HD), WIDE), stacked_blocks
    )
    g_pairs = lax.psum_scatter(
        stacked_terms.reshape(group_rows, 2 * D), "ctx", scatter_dimension=0, tiled=True
    )
    g_keys = g_pairs[:, :D].reshape(local_rows, H, HD)
    g_values = g_pairs[:, D:].reshape(local_rows, H, HD)
    return (g_queries, g_keys, g_values)


def shards(
    tokens,
    cotangent,
    lengths,
    dealing,
    gain_one,
    bias_one,
    gain_two,
    bias_two,
    w_qkv,
    w_out,
    w_up,
    w_down,
):
    group_count = tokens.shape[0]
    local_rows = tokens.shape[1]
    all_rows = group_count * local_rows
    tokens_f = tokens.reshape(all_rows, D).astype(WIDE)
    first_row = lax.axis_index("ctx") * local_rows
    natural_list = [
        natural_rows(dealing[member], first_row, local_rows) for member in range(group_count)
    ]
    opening_list = [
        sequence_openings(natural_list[member], lengths[member]) for member in range(group_count)
    ]
    places = jnp.concatenate(
        [natural_list[member] - opening_list[member] for member in range(group_count)], axis=0
    )

    def forward():
        weights = (
            lax.all_gather(w_qkv, "wsh", axis=0, tiled=True),
            lax.all_gather(w_out, "wsh", axis=0, tiled=True),
            lax.all_gather(w_up, "wsh", axis=0, tiled=True),
            lax.all_gather(w_down, "wsh", axis=0, tiled=True),
            lax.all_gather(gain_one, "wsh", axis=0, tiled=True),
            lax.all_gather(bias_one, "wsh", axis=0, tiled=True),
            lax.all_gather(gain_two, "wsh", axis=0, tiled=True),
            lax.all_gather(bias_two, "wsh", axis=0, tiled=True),
        )
        local_parts = project(tokens_f, weights, places)
        attended_list = []
        total_list = []
        for member in range(group_count):
            rows_from = member * local_rows
            attended_one, total_one = attend(
                local_parts[2][rows_from : rows_from + local_rows],
                local_parts[3][rows_from : rows_from + local_rows],
                local_parts[4][rows_from : rows_from + local_rows],
                natural_list[member],
                opening_list[member],
                dealing[member],
            )
            attended_list.append(attended_one)
            total_list.append(total_one)
        return (weights, local_parts, jnp.concatenate(attended_list, axis=0), total_list)

    weights, local_parts, attended, total_list = forward()
    attended_low = attended.reshape(all_rows, D).astype(NARROW)
    mixed_out = (
        tokens_f
        + jnp.dot(attended_low, weights[1], preferred_element_type=WIDE)
        + jnp.dot(local_parts[6], weights[3], preferred_element_type=WIDE)
    )
    out = mixed_out.astype(NARROW)
    weights, local_parts, attended, total_list = forward()
    attended_low = attended.reshape(all_rows, D).astype(NARROW)
    w_qkv_all, w_out_all, w_up_all, w_down_all = (weights[0], weights[1], weights[2], weights[3])
    normed_one, normed_two, queries, keys_here, values_here, hidden, activated = local_parts
    grad_rows = cotangent.reshape(all_rows, D)
    grad_f = grad_rows.astype(WIDE)
    g_down = jnp.einsum("tf,td->fd", activated, grad_rows, preferred_element_type=WIDE)
    g_activated = jnp.einsum("td,fd->tf", grad_rows, w_down_all, preferred_element_type=WIDE)
    _, gelu_back = jax.vjp(lambda pre_act: jax.nn.gelu(pre_act, approximate=False), hidden)
    g_hidden = gelu_back(g_activated)[0].astype(NARROW)
    g_up = jnp.einsum("td,tf->df", normed_two, g_hidden, preferred_element_type=WIDE)
    g_normed_two = jnp.einsum("tf,df->td", g_hidden, w_up_all, preferred_element_type=WIDE)
    g_weight_out = jnp.einsum("te,td->ed", attended_low, grad_rows, preferred_element_type=WIDE)
    g_attended = (
        jnp.einsum("td,ed->te", grad_rows, w_out_all, preferred_element_type=WIDE)
        .astype(NARROW)
        .reshape(all_rows, H, HD)
    )
    row_dot = jnp.einsum("qhd,qhd->hq", g_attended.astype(WIDE), attended)
    query_grads = []
    key_grads = []
    value_grads = []
    for member in range(group_count):
        rows_from = member * local_rows
        rows_to = rows_from + local_rows
        g_q, g_k, g_v = attention_back(
            queries[rows_from:rows_to],
            keys_here[rows_from:rows_to],
            values_here[rows_from:rows_to],
            g_attended[rows_from:rows_to],
            row_dot[:, rows_from:rows_to],
            total_list[member],
            natural_list[member],
            opening_list[member],
            dealing[member],
        )
        query_grads.append(g_q)
        key_grads.append(g_k)
        value_grads.append(g_v)
    g_queries = jnp.concatenate(query_grads, axis=0)
    g_keys = jnp.concatenate(key_grads, axis=0)
    g_values = jnp.concatenate(value_grads, axis=0)
    _, rotate_back = jax.vjp(
        lambda pre_rot: rotate(pre_rot, places), jnp.zeros((all_rows, H, HD), WIDE)
    )
    g_queries_pre = rotate_back(g_queries)[0]
    g_keys_pre = rotate_back(g_keys)[0]
    g_mixed = (
        jnp.stack([g_queries_pre, g_keys_pre, g_values], axis=1)
        .reshape(all_rows, 3 * D)
        .astype(NARROW)
    )
    g_qkv = jnp.einsum("td,te->de", normed_one, g_mixed, preferred_element_type=WIDE)
    g_normed_one = jnp.einsum("te,de->td", g_mixed, w_qkv_all, preferred_element_type=WIDE)

    def both_norms(tokens_in, scale_one, shift_one, scale_two, shift_two):
        return (
            norm_layer(tokens_in, scale_one, shift_one),
            norm_layer(tokens_in, scale_two, shift_two),
        )

    _, norm_back = jax.vjp(
        both_norms,
        tokens_f,
        weights[4].astype(WIDE),
        weights[5].astype(WIDE),
        weights[6].astype(WIDE),
        weights[7].astype(WIDE),
    )
    g_tokens, g_scale_one, g_shift_one, g_scale_two, g_shift_two = norm_back(
        (g_normed_one, g_normed_two)
    )
    grad_tokens = g_tokens + grad_f
    summed = (
        lax.psum_scatter(g_qkv, ("ctx", "wsh"), scatter_dimension=0, tiled=True),
        lax.psum_scatter(g_weight_out, ("ctx", "wsh"), scatter_dimension=0, tiled=True),
        lax.psum_scatter(g_up, ("ctx", "wsh"), scatter_dimension=0, tiled=True),
        lax.psum_scatter(g_down, ("ctx", "wsh"), scatter_dimension=0, tiled=True),
        lax.psum_scatter(g_scale_one, ("ctx", "wsh"), scatter_dimension=0, tiled=True),
        lax.psum_scatter(g_shift_one, ("ctx", "wsh"), scatter_dimension=0, tiled=True),
        lax.psum_scatter(g_scale_two, ("ctx", "wsh"), scatter_dimension=0, tiled=True),
        lax.psum_scatter(g_shift_two, ("ctx", "wsh"), scatter_dimension=0, tiled=True),
    )
    return (
        out.reshape(group_count, local_rows, D),
        grad_tokens.reshape(group_count, local_rows, D),
        summed[4],
        summed[5],
        summed[6],
        summed[7],
        summed[0],
        summed[1],
        summed[2],
        summed[3],
    )


MESH = pl.DeviceIdType.MESH
NT = (((1,), (1,)), ((), ()))
TN = (((0,), (0,)), ((), ()))
VMEM_LIMIT = 60 * 1024 * 1024


def dot(a, b, dims=(((1,), (0,)), ((), ()))):
    return lax.dot_general(a, b, dims, preferred_element_type=WIDE)


def pick(index, table):
    result = jnp.int32(table[0])
    for at in range(1, len(table)):
        result = jnp.where(index == at, jnp.int32(table[at]), result)
    return result


def near_first(depth):
    return [sorted(range(depth), key=lambda to, z=z: (abs(to - z), to)) for z in range(depth)]


def pick2(row, column, table):
    result = pick(column, table[0])
    for at in range(1, len(table)):
        result = jnp.where(row == at, pick(column, table[at]), result)
    return result


class Place:
    def __init__(self, depth):
        self.depth = depth
        self.c = lax.axis_index("ctx")
        self.x = lax.axis_index("wsh")
        self.core = lax.rem(self.c, 2)
        self.y = lax.rem(self.c // 2, 2)
        self.z = self.c // 4
        self.beside = (self.at(self.z, 1 - self.y, self.core), self.x)
        self.twin = (self.at(self.z, self.y, 1 - self.core), self.x)
        self.above = (self.at(self.z + 1, self.y, self.core), self.x)
        self.below = (self.at(self.z - 1, self.y, self.core), self.x)
        self.across = (self.c, 1 - self.x)
        self.has_above = self.z < depth - 1
        self.has_below = self.z > 0

    def at(self, z, y, core):
        return (z * 2 + y) * 2 + core

    def greet(self):
        barrier = pltpu.get_barrier_semaphore()

        def hail(device):
            pl.semaphore_signal(barrier, inc=1, device_id=device, device_id_type=MESH)

        hail(self.beside)
        hail(self.twin)
        hail(self.across)

        @pl.when(self.has_above)
        def _():
            hail(self.above)

        @pl.when(self.has_below)
        def _():
            hail(self.below)

        pl.semaphore_wait(
            barrier, 3 + self.has_above.astype(jnp.int32) + self.has_below.astype(jnp.int32)
        )


    def greet_all(self):
        barrier = pltpu.get_barrier_semaphore()
        count = 4 * self.depth
        pl.semaphore_signal(barrier, inc=1, device_id=self.across, device_id_type=MESH)

        def hail(offset, carry):
            device = (lax.rem(self.c + offset, count), self.x)
            pl.semaphore_signal(barrier, inc=1, device_id=device, device_id_type=MESH)
            return carry

        lax.fori_loop(1, count, hail, 0)
        pl.semaphore_wait(barrier, count)


FREQUENCY = tuple(10000.0 ** (-2.0 * i / ROT) for i in range(ROT // 2))


def turning(place):
    row = lax.broadcasted_iota(jnp.int32, (ROT // 2, 1), 0)
    frequency = jnp.full((ROT // 2, 1), FREQUENCY[0], WIDE)
    for at in range(1, ROT // 2):
        frequency = jnp.where(row == at, FREQUENCY[at], frequency)
    angles = place.astype(WIDE) * frequency
    return jnp.cos(angles), jnp.sin(angles)


ALONG = (16, 16)


def cut(rows, what, piece):
    rest = rows - ALONG[what]
    first = (rest // 2 + 15) // 16 * 16
    begin = (0, first, rest, rows)
    return pl.ds(begin[piece], begin[piece + 1] - begin[piece])


def starts_of(lengths_ref, group):
    starts = []
    so_far = jnp.int32(0)
    for piece in range(lengths_ref.shape[1] - 1):
        so_far = so_far + lengths_ref[group, piece]
        starts.append(so_far)
    return starts


def opening_of(natural, starts):
    opening = jnp.zeros(natural.shape, jnp.int32)
    for start in starts:
        opening = jnp.where(natural >= start, start, opening)
    return opening


def find_blocks(dealing_ref, found):
    groups, blocks = dealing_ref.shape
    for group in range(groups):

        def look(block, carry):
            where = jnp.int32(0)
            for at in range(blocks):
                where = jnp.where(dealing_ref[group, at] == block, jnp.int32(at), where)
            found[group, block] = where
            return carry

        lax.fori_loop(0, blocks, look, 0)


def gather_kernel(
    depth,
    lengths_ref,
    dealing_ref,
    tok_ref,
    cot_ref,
    gain_one_ref,
    bias_one_ref,
    gain_two_ref,
    bias_two_ref,
    wqkv_ref,
    wout_ref,
    wup_ref,
    wdown_ref,
    heads_out,
    units_out,
    xhat_out,
    cot_out,
    attended_out,
    total_out,
    g_up,
    g_down,
    g_sum,
    wqkv_t,
    wup_all,
    wdown_part,
    wout_part,
    prm_all,
    found,
    both,
    xhat_all,
    heads_buf,
    units_buf,
    slope_buf,
    wide,
    k_rows,
    wq_buf,
    prm_buf,
    in_sem,
    w_sem,
    wsend_sem,
    wrecv_sem,
    send_sem,
    recv_sem,
    out_sem,
):
    here = Place(depth)
    c, x, y, z, core = here.c, here.x, here.y, here.z, here.core
    count = depth * 4
    rows = tok_ref.shape[0]
    groups = dealing_ref.shape[0]
    units = wup_all.shape[1]
    half = prm_buf.shape[2]
    order = near_first(depth)

    own_in = (
        pltpu.make_async_copy(tok_ref, both.at[0, c], in_sem.at[0]),
        pltpu.make_async_copy(cot_ref, both.at[1, c], in_sem.at[1]),
    )
    for copy in own_in:
        copy.start()
    prm_rows = [
        ref[...].astype(WIDE).reshape(1, half) for ref in (gain_one_ref, bias_one_ref, gain_two_ref, bias_two_ref)
    ]
    prm_buf[x] = jnp.concatenate(prm_rows + prm_rows, axis=0)

    pair = c // 2
    per_half = count // 2
    owner = c // per_half
    inside = lax.rem(c, per_half)
    shared = []
    for part in range(3):
        shared.append(
            (
                wqkv_ref.at[:, pl.ds(pl.multiple_of(part * D + pair * 128, 128), 128)],
                wq_buf.at[x, part],
            )
        )
    shared.append(
        (
            wup_ref.at[:, pl.ds(pl.multiple_of(c * units, 128), units)],
            wup_all.at[pl.ds(pl.multiple_of(x * half, 128), half)],
        )
    )
    held = (
        (wdown_ref.at[pl.ds(pl.multiple_of(inside * units, 128), units)], wdown_part),
        (wout_ref.at[pl.ds(pl.multiple_of(inside * HD, HD), HD)], wout_part),
    )
    is_owner = owner == x
    for at, (source, place) in enumerate(shared):
        pltpu.make_async_copy(source, place, w_sem.at[at]).start()

    @pl.when(is_owner)
    def _():
        for at, (source, place) in enumerate(held):
            pltpu.make_async_copy(source, place, w_sem.at[5 + at]).start()

    here.greet()

    def remote(source, place, at):
        return pltpu.make_async_remote_copy(
            source,
            place,
            wsend_sem.at[at],
            wrecv_sem.at[at],
            device_id=here.across,
            device_id_type=MESH,
        )

    prm_copy = remote(prm_buf.at[x], prm_buf.at[x], 4)
    prm_copy.start()
    for at, (source, place) in enumerate(shared):
        remote(source, place, at).start()

    def passing(what, piece, shard, way):
        device = (here.beside, here.twin, here.above, here.below)[way]
        return pltpu.make_async_remote_copy(
            both.at[what, shard, cut(rows, what, piece)],
            both.at[what, shard, cut(rows, what, piece)],
            send_sem.at[what, piece, way, shard],
            recv_sem.at[what, piece, shard],
            device_id=device,
            device_id_type=MESH,
        )

    def onward(what, piece, shard, from_z, cross):
        if cross:
            passing(what, piece, shard, 0).start()

        @pl.when(jnp.logical_and(from_z <= z, here.has_above))
        def _():
            passing(what, piece, shard, 2).start()

        @pl.when(jnp.logical_and(from_z >= z, here.has_below))
        def _():
            passing(what, piece, shard, 3).start()

        passing(what, piece, shard, 1).start()

    def arrived(what, piece, shard):
        passing(what, piece, shard, 1).wait_recv()

    def relay(what, shard, from_z):
        for piece in range(3):
            arrived(what, piece, shard)
            onward(what, piece, shard, from_z, piece < 2)

    own_in[0].wait()
    for piece in range(3):
        onward(0, piece, c, z, True)
    own_in[1].wait()
    for piece in range(3):
        onward(1, piece, c, z, True)
    find_blocks(dealing_ref, found)

    for at, (source, place) in enumerate(shared):
        pltpu.make_async_copy(source, place, w_sem.at[at]).wait()
        remote(source, place, at).wait_recv()
    prm_copy.wait_recv()

    @pl.when(is_owner)
    def _():
        for at, (source, place) in enumerate(held):
            remote(source, place, 5 + at).start()

    odd = lax.rem(c, 2) == 1
    for side in range(2):
        prm_all[:, side * half : (side + 1) * half] = prm_buf[side]
        for part in range(3):
            turned = wq_buf[side, part].astype(WIDE).T
            chosen = jnp.where(odd, turned[HD:], turned[:HD])
            wqkv_t[part * HD : (part + 1) * HD, side * half : (side + 1) * half] = chosen.astype(
                NARROW
            )
    g_up[...] = jnp.zeros_like(g_up)
    g_down[...] = jnp.zeros_like(g_down)
    g_sum[...] = jnp.zeros_like(g_sum)

    kept = (
        (xhat_all, xhat_out),
        (both.at[1], cot_out),
        (heads_buf, heads_out),
        (units_buf, units_out),
    )

    def copy_out(at, shard):
        source, place = kept[at]
        return pltpu.make_async_copy(source.at[shard], place.at[shard], out_sem.at[at, shard])

    def ahead(shard):
        tokens = both[0, shard].astype(WIDE)
        average = jnp.mean(tokens, axis=-1, keepdims=True)
        centred = tokens - average
        variance = jnp.mean(centred * centred, axis=-1, keepdims=True)
        xhat = centred * lax.rsqrt(variance + EPSILON)
        xhat_all[shard] = xhat.astype(NARROW)
        n_one = (xhat * prm_all[0:1, :] + prm_all[1:2, :]).astype(NARROW)
        n_two = (xhat * prm_all[2:3, :] + prm_all[3:4, :]).astype(NARROW)
        mixed = dot(wqkv_t[...], n_one, NT)
        places = []
        for group in range(groups):
            natural = dealing_ref[group, shard] * BLK + lax.broadcasted_iota(jnp.int32, (1, BLK), 1)
            places.append(natural - opening_of(natural, starts_of(lengths_ref, group)))
        cosine, sine = turning(jnp.concatenate(places, axis=1))
        pieces = []
        for base in (0, HD):
            first, second = mixed[base : base + 8], mixed[base + 8 : base + 16]
            pieces += [
                first * cosine - second * sine,
                second * cosine + first * sine,
                mixed[base + 16 : base + HD],
            ]
        pieces.append(mixed[2 * HD : 3 * HD])
        heads_buf[shard, 0 : 3 * HD, :] = jnp.concatenate(pieces, axis=0).astype(NARROW)
        hidden = dot(n_two, wup_all[...])
        spread = 0.5 * (1.0 + lax.erf(hidden * (0.5**0.5)))
        units_buf[shard, :, 0:units] = (hidden * spread).astype(NARROW)
        slope_buf[shard] = spread + hidden * (jnp.exp(hidden * hidden * -0.5) * 0.3989422804014327)
        copy_out(0, shard).start()

    def behind(shard):
        cotangent = both[1, shard]
        heads_buf[shard, 3 * HD : 4 * HD, :] = dot(wout_part[...], cotangent, NT).astype(NARROW)
        g_hidden = (dot(cotangent, wdown_part[...], NT) * slope_buf[shard]).astype(NARROW)
        units_buf[shard, :, units : 2 * units] = g_hidden
        g_up[...] += dot(g_hidden, xhat_all[shard], TN)
        g_down[...] += dot(units_buf[shard, :, 0:units], cotangent, TN)
        g_sum[...] += jnp.sum(g_hidden.astype(WIDE).reshape(rows // 8, 8, units), axis=0)
        for at in (1, 2, 3):
            copy_out(at, shard).start()

    inner = jnp.logical_and(here.has_above, here.has_below)

    def sweep(what, work, beside_work, first=0):
        relays = what == 0

        def step(at, carry):
            turn_no = at // 4
            kind = lax.rem(at, 4)
            late = jnp.where(kind >= 2, turn_no - 1, turn_no)
            from_z = pick2(z, jnp.clip(late, 0, depth - 1), order)
            next_z = pick2(z, jnp.clip(turn_no + 1, 0, depth - 1), order)
            shard_y = jnp.where(kind >= 2, 1 - y, y)
            shard_core = jnp.where(lax.rem(kind, 2) == 1, 1 - core, core)
            shard = here.at(from_z, shard_y, shard_core)
            live = jnp.logical_and(late >= 0, late < depth)

            early = jnp.logical_and(inner, turn_no == 2)
            is_own = jnp.logical_and(kind == 0, turn_no == 0)
            done = jnp.logical_or(is_own, jnp.logical_and(kind == 0, early))

            @pl.when(jnp.logical_and(lax.rem(kind, 2) == 1, live))
            def _():
                for piece in range(3):
                    arrived(what, piece, shard)

            if relays:

                @pl.when(jnp.logical_and(jnp.logical_and(kind == 0, live), jnp.logical_not(done)))
                def _():
                    relay(what, shard, from_z)

            @pl.when(jnp.logical_and(kind == 2, live))
            def _():
                arrived(what, 2, shard)
                onward(what, 2, shard, from_z, False)
                for piece in range(2):
                    arrived(what, piece, shard)
                    passing(what, piece, shard, 1).start()

            if relays:

                @pl.when(jnp.logical_and(jnp.logical_and(kind == 1, turn_no == 1), inner))
                def _():
                    relay(what, here.at(next_z, y, core), next_z)

            beside_work(at)

            @pl.when(live)
            def _():
                work(shard)

            return carry

        lax.fori_loop(first, 4 * depth + 4, step, 0)

    def relay_next(at, wanted, index, which):
        @pl.when(jnp.logical_and(at == wanted, which))
        def _():
            from_z = pick2(z, jnp.int32(index), order)
            relay(1, here.at(from_z, y, core), from_z)

    outer = jnp.logical_not(inner)

    def late_weights():
        @pl.when(is_owner)
        def _():
            for at, (source, place) in enumerate(held):
                pltpu.make_async_copy(source, place, w_sem.at[5 + at]).wait()

        @pl.when(jnp.logical_not(is_owner))
        def _():
            for at, (source, place) in enumerate(held):
                remote(source, place, 5 + at).wait_recv()

    def cotangents_start(at):
        relay_next(at, 4 * depth, 1, at >= 0)
        relay_next(at, 4 * depth + 1, 2, inner)

        @pl.when(at == 4 * depth)
        def _():
            late_weights()
            behind(c)

        @pl.when(at == 4 * depth + 1)
        def _():
            twin = here.at(z, y, 1 - core)
            for piece in range(3):
                arrived(1, piece, twin)
            behind(twin)

    sweep(0, ahead, cotangents_start)

    spans = count // 2
    span = 2 * BLK

    def bring(at, carry):
        for group in range(groups):
            lanes = slice(group * BLK, (group + 1) * BLK)
            for side in range(2):
                source = found[group, 2 * at + side]
                part = heads_buf[source, 0 : 3 * HD, lanes]
                to = slice(side * BLK, (side + 1) * BLK)
                wide[group, at, 0:HD, to] = (part[0:HD].astype(WIDE) * HD ** (-0.5)).astype(NARROW)
                wide[group, at, HD : 2 * HD, to] = part[2 * HD : 3 * HD]
                k_rows[group, at, to, :] = part[HD : 2 * HD].astype(WIDE).T.astype(NARROW)
        return carry

    lax.fori_loop(0, spans, bring, 0)
    openings = [starts_of(lengths_ref, group) for group in range(groups)]

    def attend(at):
        group = lax.rem(at, groups)
        turn_no = at // groups
        mine = jnp.where(lax.rem(turn_no, 2) == 0, spans - 1 - turn_no // 2, turn_no // 2)
        natural = mine * span + lax.broadcasted_iota(jnp.int32, (1, span), 1)
        opening = opening_of(natural, [jnp.where(group == 0, *pair) for pair in zip(*openings)])
        key_in = lax.broadcasted_iota(jnp.int32, (2 * span, span), 0)
        queries = wide[group, mine, 0:HD, :]

        def add(keys_at, state, allowed):
            top, total, so_far = state
            keys = k_rows[group, pl.ds(2 * keys_at, 2)].reshape(2 * span, HD)
            raw = jnp.where(allowed, dot(keys, queries), MASKED)
            new_top = jnp.maximum(top, jnp.max(raw, axis=0, keepdims=True))
            risen = jnp.exp(raw - new_top)
            fade = jnp.exp(top - new_top)
            total = total * fade + jnp.sum(risen, axis=0, keepdims=True)
            values = jnp.concatenate(
                [wide[group, 2 * keys_at + side, HD : 2 * HD, :] for side in range(2)], axis=1
            )
            return new_top, total, so_far * fade + dot(values, risen.astype(NARROW))

        state = (
            jnp.full((1, span), MASKED, WIDE),
            jnp.zeros((1, span), WIDE),
            jnp.zeros((HD, span), WIDE),
        )
        last = mine // 2
        place = key_in + last * (2 * span)
        state = add(last, state, jnp.logical_and(place <= natural, place >= opening))

        def earlier(back, state):
            keys_at = last - 1 - back
            return add(keys_at, state, key_in >= opening - keys_at * (2 * span))

        top, total, so_far = lax.fori_loop(0, last, earlier, state)
        attended = so_far / total
        for side in range(2):
            attended_out[group, 2 * mine + side] = attended[:, side * BLK : (side + 1) * BLK]
        total_out[group, mine] = jnp.broadcast_to(top + jnp.log(total), (8, span))

    def attend_too(at):
        relay_next(at, 4, 2, outer)
        relay_next(at, 4, 3, inner)
        relay_next(at, 7, 3, outer)

        @pl.when(at < groups * spans + 4)
        def _():
            attend(at - 4)

    sweep(1, behind, attend_too, first=4)

    def finish(shard, carry):
        shard_z = shard // 4
        mine = lax.rem(shard, 2) == core
        column = lax.rem(shard // 2, 2) == y
        for what in range(2):

            @pl.when(mine)
            def _():
                for piece in range(3):
                    passing(what, piece, shard, 1).wait_send()

            for piece in range(3):
                along = mine if piece == 2 else jnp.logical_and(mine, column)

                @pl.when(jnp.logical_and(along, jnp.logical_and(shard_z <= z, here.has_above)))
                def _():
                    passing(what, piece, shard, 2).wait_send()

                @pl.when(jnp.logical_and(along, jnp.logical_and(shard_z >= z, here.has_below)))
                def _():
                    passing(what, piece, shard, 3).wait_send()

                crossed = shard == c if piece == 2 else jnp.logical_and(mine, column)

                @pl.when(crossed)
                def _():
                    passing(what, piece, shard, 0).wait_send()

        for at in range(4):
            copy_out(at, shard).wait()
        return carry

    lax.fori_loop(0, count, finish, 0)
    for at, (source, place) in enumerate(shared):
        remote(source, place, at).wait_send()
    prm_copy.wait_send()

    @pl.when(is_owner)
    def _():
        for at, (source, place) in enumerate(held):
            remote(source, place, 5 + at).wait_send()


def gather_call(depth, lengths, dealing, tok, cot, gains, w_qkv, w_out, w_up, w_down):
    count = depth * 4
    rows = tok.shape[0]
    groups = dealing.shape[0]
    spans, span = count // 2, 2 * BLK
    units = w_up.shape[1] // count
    any_spec = pl.BlockSpec(memory_space=pl.ANY)
    vmem = pl.BlockSpec(memory_space=pltpu.VMEM)
    smem = pl.BlockSpec(memory_space=pltpu.SMEM)
    shape = jax.ShapeDtypeStruct
    return pl.pallas_call(
        functools.partial(gather_kernel, depth),
        out_shape=(
            shape((count, 4 * HD, rows), NARROW),
            shape((count, rows, 2 * units), NARROW),
            shape((count, rows, D), NARROW),
            shape((count, rows, D), NARROW),
            shape((groups, count, HD, BLK), WIDE),
            shape((groups, spans, 8, span), WIDE),
            shape((units, D), WIDE),
            shape((units, D), WIDE),
            shape((8, units), WIDE),
            shape((3 * HD, D), NARROW),
            shape((D, units), NARROW),
            shape((units, D), NARROW),
            shape((HD, D), NARROW),
            shape((8, D), WIDE),
            shape((groups, count), jnp.int32),
        ),
        in_specs=[smem, smem, any_spec, any_spec] + [vmem] * 4 + [any_spec] * 4,
        out_specs=(any_spec,) * 4 + (vmem,) * 10 + (smem,),
        scratch_shapes=[
            pltpu.VMEM((2, count, rows, D), NARROW),
            pltpu.VMEM((count, rows, D), NARROW),
            pltpu.VMEM((count, 4 * HD, rows), NARROW),
            pltpu.VMEM((count, rows, 2 * units), NARROW),
            pltpu.VMEM((count, rows, units), WIDE),
            pltpu.VMEM((groups, spans, 2 * HD, span), NARROW),
            pltpu.VMEM((groups, spans, span, HD), NARROW),
            pltpu.VMEM((2, 3, D // 2, 128), NARROW),
            pltpu.VMEM((2, 8, D // 2), WIDE),
            pltpu.SemaphoreType.DMA((2,)),
            pltpu.SemaphoreType.DMA((7,)),
            pltpu.SemaphoreType.DMA((7,)),
            pltpu.SemaphoreType.DMA((7,)),
            pltpu.SemaphoreType.DMA((2, 3, 4, count)),
            pltpu.SemaphoreType.DMA((2, 3, count)),
            pltpu.SemaphoreType.DMA((4, count)),
        ],
        name="gather_and_forward",
        compiler_params=pltpu.CompilerParams(
            collective_id=1, has_side_effects=True, vmem_limit_bytes=VMEM_LIMIT
        ),
    )(lengths, dealing, tok, cot, *gains, w_qkv, w_out, w_up, w_down)


def far_first(depth):
    return [list(reversed(row)) for row in near_first(depth)]


def unturn(rows, cosine, sine):
    first, second = rows[0:8], rows[8:16]
    return jnp.concatenate(
        [first * cosine + second * sine, second * cosine - first * sine, rows[16:]], axis=0
    )


def reduce_kernel(
    depth,
    lengths_ref,
    dealing_ref,
    found,
    total_in,
    prm_all,
    g_sum,
    attended_hbm,
    wout_hbm,
    wdown_hbm,
    units_hbm,
    g_up_hbm,
    wup_hbm,
    wqkv_hbm,
    g_down_hbm,
    heads_hbm,
    xhat_in,
    cot_in,
    sum_out,
    sum_back,
    inbox,
    wout_ref,
    down_ref,
    vec_ref,
    attended_in,
    wout_part,
    wdown_part,
    units_in,
    g_up,
    wup_all,
    wqkv_t,
    g_down,
    heads_in,
    w_heads_back,
    give_buf,
    sum_buf,
    beside_buf,
    line_buf,
    other_line,
    wide,
    q_rows,
    k_rows,
    v_rows,
    g_rows,
    g_key,
    g_value,
    turned_all,
    by_token,
    stream,
    g_heads,
    g_wout,
    sum_heads,
    vectors,
    grads,
    grads_in,
    mail,
    wout_in,
    down_in,
    first_sem,
    send_twin,
    send_beside,
    recv_twin,
    recv_beside,
    recv_z,
    send_z,
    send_last,
    recv_last,
    stream_sem,
    across_send,
    across_recv,
    mail_send,
    mail_recv,
):
    here = Place(depth)
    c, x, y, z, core = here.c, here.x, here.y, here.z, here.core
    rows = sum_out.shape[0]
    units = wup_all.shape[1]
    groups = dealing_ref.shape[0]
    count = 4 * depth
    brought = [
        pltpu.make_async_copy(source, place, first_sem.at[at])
        for at, (source, place) in enumerate(
            (
                (attended_hbm, attended_in),
                (wout_hbm, wout_part),
                (wdown_hbm, wdown_part),
                (units_hbm, units_in),
                (g_up_hbm, g_up),
                (wup_hbm, wup_all),
                (wqkv_hbm, wqkv_t),
                (g_down_hbm, g_down),
                (heads_hbm, heads_in),
            )
        )
    ]
    for copy in brought:
        copy.start()
    spans, span = count // 2, 2 * BLK
    scale = HD ** (-0.5)
    piece = D // (2 * count)
    order = far_first(depth)

    def shard_of(at):
        kind = lax.rem(at, 4)
        to_y = jnp.where(lax.rem(kind, 2) == 1, y, 1 - y)
        to_core = jnp.where(kind < 2, 1 - core, core)
        return here.at(pick2(z, at // 4, order), to_y, to_core)

    def load(at):
        shard, slot = shard_of(at), lax.rem(at, 2)
        return (
            pltpu.make_async_copy(xhat_in.at[shard], stream.at[0, slot], stream_sem.at[0, slot]),
            pltpu.make_async_copy(cot_in.at[shard], stream.at[1, slot], stream_sem.at[1, slot]),
        )

    here.greet_all()

    def crossing(source, place, at):
        return pltpu.make_async_remote_copy(
            source,
            place,
            across_send.at[at],
            across_recv.at[at],
            device_id=here.across,
            device_id_type=MESH,
        )

    half_down = g_down.shape[0] // 2
    half_wout = HD // 2
    send_down = crossing(g_down.at[pl.ds((1 - x) * half_down, half_down)], down_in, 0)
    send_wout = crossing(g_wout.at[pl.ds((1 - x) * half_wout, half_wout)], wout_in, 1)
    send_grads = [crossing(grads.at[part, 1 - x], grads_in.at[part], 2 + part) for part in range(2)]

    def to_twin(what, slot):
        return pltpu.make_async_remote_copy(
            give_buf.at[slot],
            sum_buf.at[what, slot],
            send_twin.at[what, slot],
            recv_twin.at[what, slot],
            device_id=here.twin,
            device_id_type=MESH,
        )

    def to_beside(what, piece, to_z):
        return pltpu.make_async_remote_copy(
            sum_buf.at[what, to_z, cut(rows, what, piece)],
            beside_buf.at[what, to_z, cut(rows, what, piece)],
            send_beside.at[what, piece, to_z],
            recv_beside.at[what, piece, to_z],
            device_id=here.beside,
            device_id_type=MESH,
        )

    def over_slot(to_z, at_z):
        return jnp.where(to_z == at_z, depth, to_z)

    def along(what, piece, home, to_z, place, device):
        here_rows = cut(rows, what, piece)
        if piece == 2:
            target = other_line.at[what, place, pl.ds(0, ALONG[what])]
            if home == 1:
                target = line_buf.at[what, place, here_rows]
        else:
            target = line_buf.at[what, place, here_rows]
        lane = piece + (home if piece == 2 else 0)
        return pltpu.make_async_remote_copy(
            sum_buf.at[what, home * depth + to_z, here_rows],
            target,
            send_z.at[what, lane, to_z],
            recv_z.at[what, lane, place],
            device_id=device,
            device_id_type=MESH,
        )

    def to_above(what, piece, home, to_z):
        return along(what, piece, home, to_z, to_z, here.above)

    def to_below(what, piece, home, to_z):
        return along(what, piece, home, to_z, over_slot(to_z, z - 1), here.below)

    def from_above(what, piece, home, to_z):
        return along(what, piece, home, to_z, over_slot(to_z, z), here.above)

    def cross_last(what):
        here_rows = cut(rows, what, 2)
        return pltpu.make_async_remote_copy(
            sum_buf.at[what, z, here_rows],
            beside_buf.at[what, z, here_rows],
            send_last.at[what],
            recv_last.at[what],
            device_id=here.beside,
            device_id_type=MESH,
        )

    def pass_on(what, at, part):
        to_z = pick2(z, at // 4, order)
        kind = lax.rem(at, 4)
        slot = lax.rem(kind, 2) * depth + to_z

        @pl.when(kind < 2)
        def _():
            if what == 1:
                to_twin(0, slot).wait_send()
            give_buf[slot] = part.astype(NARROW)
            to_twin(what, slot).start()

        @pl.when(kind >= 2)
        def _():
            to_twin(what, slot).wait_recv()
            sum_buf[what, slot] = (part + sum_buf[what, slot].astype(WIDE)).astype(NARROW)

        @pl.when(kind == 2)
        def _():
            for piece in range(2):
                to_beside(what, piece, to_z).start()

    def chain_piece(what, at, piece, home):
        to_z = pick2(z, at, order)
        slot = home * depth + to_z
        here_rows = cut(rows, what, piece)
        if piece < 2:
            to_beside(what, piece, to_z).wait_recv()

        def add(incoming):
            total = sum_buf[what, slot, here_rows, :].astype(WIDE)
            if piece < 2:
                total = total + beside_buf[what, to_z, here_rows, :].astype(WIDE)
            if incoming:
                if piece == 2 and home == 0:
                    came = other_line[what, to_z, 0 : ALONG[what], :]
                else:
                    came = line_buf[what, to_z, here_rows, :]
                total = total + came.astype(WIDE)
            sum_buf[what, slot, here_rows, :] = total.astype(NARROW)

        @pl.when(to_z > z)
        def _():
            @pl.when(here.has_below)
            def _():
                to_above(what, piece, home, to_z).wait_recv()
                add(True)

            if piece < 2:

                @pl.when(jnp.logical_not(here.has_below))
                def _():
                    add(False)

            to_above(what, piece, home, to_z).start()

        @pl.when(to_z < z)
        def _():
            @pl.when(here.has_above)
            def _():
                from_above(what, piece, home, to_z).wait_recv()
                add(True)

            if piece < 2:

                @pl.when(jnp.logical_not(here.has_above))
                def _():
                    add(False)

            to_below(what, piece, home, to_z).start()

    def chain(what, at):
        for home in range(2):
            chain_piece(what, at, 2, home)
        for piece in range(2):
            chain_piece(what, at, piece, 1)

    def cross_over(what):
        here_rows = cut(rows, what, 2)
        came = slice(0, ALONG[what])

        @pl.when(here.has_below)
        def _():
            to_above(what, 2, 0, z).wait_recv()
            total = sum_buf[what, z, here_rows, :].astype(WIDE)
            total = total + other_line[what, z, came, :].astype(WIDE)
            sum_buf[what, z, here_rows, :] = total.astype(NARROW)

        @pl.when(here.has_above)
        def _():
            from_above(what, 2, 0, z).wait_recv()
            total = sum_buf[what, z, here_rows, :].astype(WIDE)
            total = total + other_line[what, depth, came, :].astype(WIDE)
            sum_buf[what, z, here_rows, :] = total.astype(NARROW)

        cross_last(what).start()

    def gather_total(what):
        for piece in range(2):
            to_beside(what, piece, z).wait_recv()
        cross_last(what).wait_recv()

        @pl.when(here.has_below)
        def _():
            for piece in range(3):
                to_above(what, piece, 1, z).wait_recv()

        @pl.when(jnp.logical_not(here.has_below))
        def _():
            line_buf[what, z] = jnp.zeros((rows, D), NARROW)

        @pl.when(here.has_above)
        def _():
            for piece in range(3):
                from_above(what, piece, 1, z).wait_recv()

        @pl.when(jnp.logical_not(here.has_above))
        def _():
            line_buf[what, depth] = jnp.zeros((rows, D), NARROW)

        return (
            sum_buf[what, depth + z].astype(WIDE)
            + beside_buf[what, z].astype(WIDE)
            + line_buf[what, z].astype(WIDE)
            + line_buf[what, depth].astype(WIDE)
        )

    def give_out(at, carry):
        shard = shard_of(at)
        parts = []
        for group in range(groups):
            attended = attended_in[group, dealing_ref[group, shard]].astype(NARROW)
            parts.append(dot(attended, wout_part[...], TN))
        part = jnp.concatenate(parts, axis=0) + dot(units_in[shard, :, 0:units], wdown_part[...])
        pass_on(0, at, part)
        return carry

    for copy in brought[:4]:
        copy.wait()
    lax.fori_loop(0, count, give_out, 0)
    for copy in brought[4:]:
        copy.wait()
    send_down.start()

    def settle(chunk, part, raw, weights, sums, column):
        scaled = raw * column[:, 2 - 2 * part : 3 - 2 * part] + sums * column[:, 3 - 2 * part : 4 - 2 * part]
        gain_sum = jnp.sum(weights * raw, axis=1, keepdims=True)
        bias_sum = jnp.sum(weights * sums, axis=1, keepdims=True)
        row = pl.ds(pl.multiple_of(chunk * 128, 128), 128)
        if part == 0:
            vectors[row, 0:1] = gain_sum
            vectors[row, 1:2] = bias_sum
        else:
            lane = lax.broadcasted_iota(jnp.int32, scaled.shape, 1)
            scaled = jnp.where(lane == 0, gain_sum, scaled)
            scaled = jnp.where(lane == 1, bias_sum, scaled)
            scaled = jnp.where(lane == 2, vectors[row, 0:1], scaled)
            scaled = jnp.where(lane == 3, vectors[row, 1:2], scaled)
        per = 128 // piece
        for at in range(per):
            grads[part, at % 2, chunk * (per // 2) + at // 2] = scaled[at * piece : (at + 1) * piece].astype(NARROW)

    sum_units = jnp.sum(g_sum[...], axis=0, keepdims=True)

    def settle_up(chunk, carry):
        lanes = pl.ds(pl.multiple_of(chunk * 128, 128), 128)
        weights = wup_all[lanes, :].astype(WIDE)
        settle(chunk, 0, g_up[:, lanes].T, weights, sum_units, prm_all[:, lanes].T)
        return carry

    lax.fori_loop(0, D // 128, settle_up, 0)
    send_grads[0].start()
    w_heads_back[0:HD, :] = jnp.zeros((HD, D), NARROW)
    w_heads_back[HD:, :] = wqkv_t[...]
    g_heads[...] = jnp.zeros_like(g_heads)
    g_wout[...] = jnp.zeros_like(g_wout)
    sum_heads[...] = jnp.zeros_like(sum_heads)

    for group in range(groups):
        lanes = slice(group * BLK, (group + 1) * BLK)
        starts = starts_of(lengths_ref, group)

        def bring(at, carry, group=group, lanes=lanes):
            for side in range(2):
                source = found[group, 2 * at + side]
                part = heads_in[source, :, lanes]
                to = slice(side * BLK, (side + 1) * BLK)
                queries = part[0:HD].astype(WIDE) * scale
                keys = part[HD : 2 * HD]
                grads_part = part[3 * HD : 4 * HD]
                wide[at, 0:HD, to] = queries.astype(NARROW)
                wide[at, HD : 2 * HD, to] = keys
                wide[at, 2 * HD : 3 * HD, to] = grads_part
                q_rows[at, to, :] = queries.T.astype(NARROW)
                k_rows[at, to, :] = keys.astype(WIDE).T.astype(NARROW)
                v_rows[at, to, :] = part[2 * HD : 3 * HD].astype(WIDE).T.astype(NARROW)
                g_rows[at, to, :] = grads_part.astype(WIDE).T.astype(NARROW)
            g_key[at] = jnp.zeros((span, HD), WIDE)
            g_value[at] = jnp.zeros((span, HD), WIDE)
            return carry

        lax.fori_loop(0, spans, bring, 0)
        chain(0, 2 * group)

        def one_span(at, carry, group=group, starts=starts):
            natural = at * span + lax.broadcasted_iota(jnp.int32, (1, span), 1)
            opening = opening_of(natural, starts)
            key_in = lax.broadcasted_iota(jnp.int32, (2 * span, span), 0)
            queries = wide[at, 0:HD, :]
            g_attended = wide[at, 2 * HD : 3 * HD, :]
            attended = jnp.concatenate(
                [attended_in[group, 2 * at], attended_in[group, 2 * at + 1]], axis=1
            )
            row_dot = jnp.sum(attended * g_attended.astype(WIDE), axis=0, keepdims=True)
            log_total = total_in[group, at, 0:1, :]

            def add(pair, so_far, allowed):
                two = pl.ds(2 * pair, 2)
                keys = k_rows[two].reshape(2 * span, HD)
                values = v_rows[two].reshape(2 * span, HD)
                scores = dot(keys, queries)
                probs = jnp.where(allowed, jnp.exp(scores - log_total), 0.0)
                g_scores = (probs * (dot(values, g_attended) - row_dot)).astype(NARROW)
                g_key[two] += dot(g_scores, q_rows[at]).reshape(2, span, HD)
                g_value[two] += dot(probs.astype(NARROW), g_rows[at]).reshape(2, span, HD)
                keys_t = jnp.concatenate(
                    [wide[2 * pair + side, HD : 2 * HD, :] for side in range(2)], axis=1
                )
                return so_far + dot(keys_t, g_scores)

            def earlier(pair, so_far):
                return add(pair, so_far, key_in >= opening - pair * (2 * span))

            last = at // 2
            so_far = lax.fori_loop(0, last, earlier, jnp.zeros((HD, span), WIDE))
            place = key_in + last * (2 * span)
            so_far = add(last, so_far, jnp.logical_and(place <= natural, place >= opening))
            cosine, sine = turning(natural - opening)
            turned = jnp.concatenate([attended, unturn(so_far * scale, cosine, sine)], axis=0)
            for side in range(2):
                part = turned[:, side * BLK : (side + 1) * BLK]
                turned_all[group, 2 * at + side, 0 : 2 * HD, :] = part.astype(NARROW)
            return carry

        lax.fori_loop(0, spans, one_span, 0)
        if group == 0:
            chain(0, 1)
        else:
            cross_over(0)

        def give(at, carry, group=group, starts=starts):
            natural = at * span + lax.broadcasted_iota(jnp.int32, (1, span), 1)
            cosine, sine = turning(natural - opening_of(natural, starts))
            keys = unturn(g_key[at].T, cosine, sine)
            turned = jnp.concatenate([keys, g_value[at].T], axis=0)
            for side in range(2):
                part = turned[:, side * BLK : (side + 1) * BLK]
                turned_all[group, 2 * at + side, 2 * HD : 4 * HD, :] = part.astype(NARROW)
                whole = turned_all[group, 2 * at + side].astype(WIDE)
                by_token[group, 2 * at + side] = whole.T.astype(NARROW)
            return carry

        lax.fori_loop(0, spans, give, 0)

    for copy in load(0):
        copy.start()

    def tokens_of(shard):
        blocks = [by_token[group, dealing_ref[group, shard]] for group in range(groups)]
        return jnp.concatenate(blocks, axis=0)

    def give_back(at, carry):
        shard = shard_of(at)
        g_hidden = units_in[shard, :, units : 2 * units]
        part = dot(tokens_of(shard), w_heads_back[...]) * prm_all[0:1, :] + dot(
            g_hidden, wup_all[...], NT
        ) * prm_all[2:3, :]
        pass_on(1, at, part)
        return carry

    lax.fori_loop(0, count, give_back, 0)

    def post(part, to_c):
        return pltpu.make_async_remote_copy(
            mail.at[part, to_c],
            inbox.at[part, c],
            mail_send.at[part, to_c],
            mail_recv.at[part, c],
            device_id=(to_c, x),
            device_id_type=MESH,
        )

    def collect(part, from_c):
        return pltpu.make_async_remote_copy(
            mail.at[part, from_c],
            inbox.at[part, from_c],
            mail_send.at[part, from_c],
            mail_recv.at[part, from_c],
            device_id=(from_c, x),
            device_id_type=MESH,
        )

    def mail_out(part):
        send_grads[part].wait_recv()

        def fold(to_c, carry):
            mail[part, to_c] = (
                grads[part, x, to_c].astype(WIDE) + grads_in[part, to_c].astype(WIDE)
            ).astype(NARROW)
            return carry

        lax.fori_loop(0, count, fold, 0)

        def start(offset, carry):
            post(part, lax.rem(c + offset, count)).start()
            return carry

        lax.fori_loop(1, count, start, 0)
        inbox[part, c] = mail[part, c]

    mail_out(0)

    def weigh(at, carry):
        shard, slot = shard_of(at), lax.rem(at, 2)

        @pl.when(at + 1 < count)
        def _():
            for copy in load(at + 1):
                copy.start()

        for copy in load(at):
            copy.wait()
        turned = jnp.concatenate(
            [turned_all[group, dealing_ref[group, shard]] for group in range(groups)], axis=1
        )
        g_wout[...] += dot(turned[0:HD], stream[1, slot])
        g_heads[HD:, :] += dot(turned[HD:], stream[0, slot])
        sum_heads[...] += jnp.sum(
            tokens_of(shard).astype(WIDE).reshape(rows // 8, 8, 4 * HD), axis=0
        )
        return carry

    inner = jnp.logical_and(here.has_above, here.has_below)
    outer = jnp.logical_not(inner)
    early, middle = count // 4, count * 5 // 8
    lax.fori_loop(0, early, weigh, 0)

    @pl.when(outer)
    def _():
        chain(1, 0)

    lax.fori_loop(early, middle, weigh, 0)

    @pl.when(outer)
    def _():
        chain(1, 1)

    @pl.when(inner)
    def _():
        chain(1, 0)

    lax.fori_loop(middle, count, weigh, 0)
    send_wout.start()
    sum_row = jnp.sum(sum_heads[...], axis=0, keepdims=True)

    def settle_qkv(chunk, carry):
        lanes = pl.ds(pl.multiple_of(chunk * 128, 128), 128)
        weights = w_heads_back[:, lanes].astype(WIDE).T
        settle(chunk, 1, g_heads[:, lanes].T, weights, sum_row, prm_all[:, lanes].T)
        return carry

    lax.fori_loop(0, D // 128, settle_qkv, 0)
    send_grads[1].start()

    @pl.when(inner)
    def _():
        chain(1, 1)

    mail_out(1)
    for at in range(2, depth - 1):
        chain(1, at)
    cross_over(1)


    sum_out[...] = gather_total(0)
    send_down.wait()
    down_ref[...] = g_down[pl.ds(x * half_down, half_down), :] + down_in[...]
    send_wout.wait()
    wout_ref[...] = g_wout[pl.ds(x * half_wout, half_wout), :] + wout_in[...]

    def close(offset, carry):
        other = lax.rem(c + offset, count)
        for part in range(2):
            collect(part, other).wait_recv()
            post(part, other).wait_send()
        return carry

    lax.fori_loop(1, count, close, 0)
    for part in range(2):
        send_grads[part].wait_send()
    together = jnp.zeros((piece, 128), WIDE)
    for from_c in range(count):
        together = together + inbox[1, from_c, :, 0:128].astype(WIDE)
    vec_ref[...] = together.T[0:8]
    sum_back[...] = gather_total(1)

    def finish(to_z, carry):
        to_twin(1, to_z).wait_send()
        to_twin(1, depth + to_z).wait_send()
        for what in range(2):
            for piece in range(2):
                to_beside(what, piece, to_z).wait_send()

            @pl.when(to_z > z)
            def _():
                to_above(what, 2, 0, to_z).wait_send()
                for piece in range(3):
                    to_above(what, piece, 1, to_z).wait_send()

            @pl.when(to_z < z)
            def _():
                to_below(what, 2, 0, to_z).wait_send()
                for piece in range(3):
                    to_below(what, piece, 1, to_z).wait_send()

        return carry

    lax.fori_loop(0, depth, finish, 0)
    for what in range(2):
        cross_last(what).wait_send()


def reduce_call(depth, scalars, small, large, rows):
    count = depth * 4
    groups = scalars[1].shape[0]
    spans, span = count // 2, 2 * BLK
    piece = D // (2 * count)
    units = large[5].shape[1]
    vmem = pl.BlockSpec(memory_space=pltpu.VMEM)
    smem = pl.BlockSpec(memory_space=pltpu.SMEM)
    any_spec = pl.BlockSpec(memory_space=pl.ANY)
    shape = jax.ShapeDtypeStruct
    message = (rows, D)
    row_form = pltpu.VMEM((spans, span, HD), NARROW)
    return pl.pallas_call(
        functools.partial(reduce_kernel, depth),
        out_shape=(
            shape((rows, D), WIDE),
            shape((rows, D), WIDE),
            shape((2, count, piece, 256), NARROW),
            shape((HD // 2, D), WIDE),
            shape((units // 2, D), WIDE),
            shape((8, piece), WIDE),
        ),
        in_specs=[smem] * 3 + [vmem] * 3 + [any_spec] * 11,
        out_specs=(vmem,) * 6,
        scratch_shapes=[pltpu.VMEM(array.shape, array.dtype) for array in large[:9]]
        + [
            pltpu.VMEM((4 * HD, D), NARROW),
            pltpu.VMEM((2 * depth,) + message, NARROW),
            pltpu.VMEM((2, 2 * depth) + message, NARROW),
            pltpu.VMEM((2, depth) + message, NARROW),
            pltpu.VMEM((2, depth + 1) + message, NARROW),
            pltpu.VMEM((2, depth + 1, max(ALONG), D), NARROW),
            pltpu.VMEM((spans, 3 * HD, span), NARROW),
            row_form,
            row_form,
            row_form,
            row_form,
            pltpu.VMEM((spans, span, HD), WIDE),
            pltpu.VMEM((spans, span, HD), WIDE),
            pltpu.VMEM((groups, count, 4 * HD, BLK), NARROW),
            pltpu.VMEM((groups, count, BLK, 4 * HD), NARROW),
            pltpu.VMEM((2, 2, rows, D), NARROW),
            pltpu.VMEM((4 * HD, D), WIDE),
            pltpu.VMEM((HD, D), WIDE),
            pltpu.VMEM((8, 4 * HD), WIDE),
            pltpu.VMEM((D, 128), WIDE),
            pltpu.VMEM((2, 2, count, piece, 256), NARROW),
            pltpu.VMEM((2, count, piece, 256), NARROW),
            pltpu.VMEM((2, count, piece, 256), NARROW),
            pltpu.VMEM((HD // 2, D), WIDE),
            pltpu.VMEM((units // 2, D), WIDE),
            pltpu.SemaphoreType.DMA((9,)),
            pltpu.SemaphoreType.DMA((2, 2 * depth)),
            pltpu.SemaphoreType.DMA((2, 2, depth)),
            pltpu.SemaphoreType.DMA((2, 2 * depth)),
            pltpu.SemaphoreType.DMA((2, 2, depth)),
            pltpu.SemaphoreType.DMA((2, 4, depth + 1)),
            pltpu.SemaphoreType.DMA((2, 4, depth)),
            pltpu.SemaphoreType.DMA((2,)),
            pltpu.SemaphoreType.DMA((2,)),
            pltpu.SemaphoreType.DMA((2, 2)),
            pltpu.SemaphoreType.DMA((4,)),
            pltpu.SemaphoreType.DMA((4,)),
            pltpu.SemaphoreType.DMA((2, count)),
            pltpu.SemaphoreType.DMA((2, count)),
        ],
        name="backward_and_reduce",
        compiler_params=pltpu.CompilerParams(
            collective_id=2, has_side_effects=True, vmem_limit_bytes=VMEM_LIMIT
        ),
    )(*scalars, *small, *large)


def last_kernel(
    tok_ref,
    cot_ref,
    sum_out,
    sum_back,
    inbox,
    wout_in,
    down_in,
    vec_in,
    out_ref,
    grad_ref,
    qkv_ref,
    wout_ref,
    up_ref,
    down_ref,
    vec_a,
    vec_b,
    vec_c,
    vec_d,
):
    tokens = tok_ref[...].astype(WIDE)
    out_ref[...] = (tokens + sum_out[...]).astype(NARROW)
    average = jnp.mean(tokens, axis=-1, keepdims=True)
    centred = tokens - average
    variance = jnp.mean(centred * centred, axis=-1, keepdims=True)
    rise = lax.rsqrt(variance + EPSILON)
    xhat = centred * rise
    g_xhat = sum_back[...]
    along = jnp.mean(g_xhat * xhat, axis=-1, keepdims=True)
    level = jnp.mean(g_xhat, axis=-1, keepdims=True)
    grad_ref[...] = cot_ref[...].astype(WIDE) + rise * (g_xhat - level - xhat * along)
    count = inbox.shape[1]
    units = up_ref.shape[1] // count
    for from_c in range(count):
        up_ref[:, from_c * units : (from_c + 1) * units] = inbox[0, from_c].astype(WIDE)
    for pair in range(count // 2):
        left = inbox[1, 2 * pair].astype(WIDE)
        right = inbox[1, 2 * pair + 1].astype(WIDE)
        for part in range(3):
            lanes = slice((part + 1) * HD, (part + 2) * HD)
            to = part * D + pair * 128
            qkv_ref[:, to : to + 128] = jnp.concatenate([left[:, lanes], right[:, lanes]], axis=1)
    wout_ref[...] = wout_in[...]
    down_ref[...] = down_in[...]
    for at, ref in enumerate((vec_a, vec_b, vec_c, vec_d)):
        ref[...] = vec_in[at]


def last_call(tok, cot, sum_out, sum_back, inbox, wout_in, down_in, vec_in):
    rows = tok.shape[0]
    _, count, piece, units = inbox.shape
    shape = jax.ShapeDtypeStruct
    steps = 2

    def cut(array_shape):
        return pl.BlockSpec((array_shape[0] // steps,) + array_shape[1:], lambda at: (at, 0))

    whole = pl.BlockSpec((8, piece), lambda at: (0, 0))
    vector = pl.BlockSpec((piece,), lambda at: (0,))
    letters = pl.BlockSpec((2, count, piece // steps, units), lambda at: (0, 0, at, 0))
    outs = (
        shape((rows, D), NARROW),
        shape((rows, D), WIDE),
        shape((piece, 3 * D), WIDE),
        shape(wout_in.shape, WIDE),
        shape((piece, count * units), WIDE),
        shape(down_in.shape, WIDE),
    )
    return pl.pallas_call(
        last_kernel,
        grid=(steps,),
        out_shape=outs + (shape((piece,), WIDE),) * 4,
        in_specs=[cut(array.shape) for array in (tok, cot, sum_out, sum_back)]
        + [letters, cut(wout_in.shape), cut(down_in.shape), whole],
        out_specs=tuple(cut(array.shape) for array in outs) + (vector,) * 4,
        name="last_rows",
        compiler_params=pltpu.CompilerParams(vmem_limit_bytes=VMEM_LIMIT),
    )(tok, cot, sum_out, sum_back, inbox, wout_in, down_in, vec_in)


def fast_shards(depth, *arguments):
    tokens, cotangent, lengths, dealing = arguments[:4]
    gains = arguments[4:8]
    rows = tokens.shape[0] * tokens.shape[1]
    tok = tokens.reshape(rows, D)
    cot = cotangent.reshape(rows, D)
    forward = gather_call(depth, lengths, dealing, tok, cot, gains, *arguments[8:])
    heads, units, xhat, cot_all, attended, total, g_up, g_down, g_sum = forward[:9]
    wqkv_t, wup_all, wdown_part, wout_part, prm_all, found = forward[9:]
    small = (total, prm_all, g_sum)
    large = (
        attended, wout_part, wdown_part, units, g_up, wup_all, wqkv_t, g_down, heads, xhat, cot_all
    )
    out, grad_tokens, qkv_part, out_part, up_part, down_part, *vectors = last_call(
        tok, cot, *reduce_call(depth, (lengths, dealing, found), small, large, rows)
    )
    return (
        out.reshape(tokens.shape),
        grad_tokens.reshape(tokens.shape),
        *vectors,
        qkv_part,
        out_part,
        up_part,
        down_part,
    )


def solution(mesh):
    placed = (
        P("wsh", "ctx", None),
        P("wsh", "ctx", None),
        P("wsh", None),
        P("wsh", None),
        P("wsh"),
        P("wsh"),
        P("wsh"),
        P("wsh"),
        P("wsh", None),
        P("wsh", None),
        P("wsh", None),
        P("wsh", None),
    )
    ctx_size = mesh.shape["ctx"]
    by_heads = ctx_size == H and mesh.shape["wsh"] == 2
    body = functools.partial(fast_shards, ctx_size // 4) if by_heads else shards
    return jax.shard_map(
        body,
        mesh=mesh,
        in_specs=placed,
        out_specs=(
            P("wsh", "ctx", None),
            P("wsh", "ctx", None),
            P(("ctx", "wsh")),
            P(("ctx", "wsh")),
            P(("ctx", "wsh")),
            P(("ctx", "wsh")),
            P(("ctx", "wsh"), None),
            P(("ctx", "wsh"), None),
            P(("ctx", "wsh"), None),
            P(("ctx", "wsh"), None),
        ),
        check_vma=False,
    )
```

```python
import functools

import jax
import jax.numpy as jnp
from jax import lax
from jax.experimental import pallas as pl
from jax.experimental.pallas import tpu as pltpu
from jax.sharding import PartitionSpec as P

D = 1024
H = 16
HD = 64
ROT = 16
BLK = 128


EPSILON = 1e-05
MASKED = -1e30
WIDE = jnp.float32
NARROW = jnp.bfloat16


def norm_layer(values_in, scale_by, shift_by):
    average = jnp.mean(values_in, axis=-1, keepdims=True)
    centred = values_in - average
    variance = jnp.mean(centred * centred, axis=-1, keepdims=True)
    return centred * lax.rsqrt(variance + EPSILON) * scale_by + shift_by


def rotate(values_in, places):
    split_at = ROT // 2
    frequency = 10000.0 ** (-2.0 * jnp.arange(split_at, dtype=WIDE) / ROT)
    angles = places.astype(WIDE)[:, None] * frequency[None, :]
    cosine_table = jnp.cos(angles)[:, None, :]
    sine_table = jnp.sin(angles)[:, None, :]
    first_half = values_in[..., :split_at]
    second_half = values_in[..., split_at:ROT]
    return jnp.concatenate(
        [
            first_half * cosine_table - second_half * sine_table,
            second_half * cosine_table + first_half * sine_table,
            values_in[..., ROT:],
        ],
        axis=-1,
    )


def natural_rows(dealing_row, offset_row, row_count):
    ordinal = offset_row + jnp.arange(row_count, dtype=jnp.int32)
    table_ids = jnp.arange(dealing_row.shape[0], dtype=jnp.int32)
    picked = jnp.sum(
        jnp.where((ordinal // BLK)[:, None] == table_ids[None, :], dealing_row[None, :], 0), axis=1
    )
    return picked * BLK + ordinal % BLK


def sequence_openings(natural, lengths_row):
    openings = jnp.cumsum(lengths_row) - lengths_row
    return jnp.max(jnp.where(openings[None, :] <= natural[:, None], openings[None, :], 0), axis=1)


def score_block(queries, block_keys, offset_row, natural_q, opening_q, dealing_row):
    row_count = block_keys.shape[0]
    key_natural = natural_rows(dealing_row, offset_row, row_count)
    scores = jnp.einsum(
        "qhd,khd->hqk", queries, block_keys.reshape(row_count, H, HD), preferred_element_type=WIDE
    ) * HD ** (-0.5)
    allowed = (key_natural[None, :] <= natural_q[:, None]) & (
        key_natural[None, :] >= opening_q[:, None]
    )
    return (scores, allowed[None])


def fold_blocks(step_fn, state_in, arrays):
    row_count = arrays[0].shape[0]
    block_width = 1024
    stacked = tuple(
        (
            member.reshape((row_count // block_width, block_width) + member.shape[1:])
            for member in arrays
        )
    )
    offsets = jnp.arange(row_count // block_width, dtype=jnp.int32) * block_width

    def inner_step(state_now, block_item):
        return (step_fn(state_now, block_item[0], block_item[1]), None)

    state_out, _ = lax.scan(inner_step, state_in, (stacked, offsets))
    return state_out


def project(tokens_f, weights, places):
    w_qkv, w_out, w_up, w_down, gain_one, bias_one, gain_two, bias_two = weights
    all_rows = tokens_f.shape[0]
    normed_one = norm_layer(tokens_f, gain_one.astype(WIDE), bias_one.astype(WIDE)).astype(NARROW)
    normed_two = norm_layer(tokens_f, gain_two.astype(WIDE), bias_two.astype(WIDE)).astype(NARROW)
    mixed = jnp.dot(normed_one, w_qkv, preferred_element_type=WIDE).reshape(all_rows, 3, H, HD)
    queries = rotate(mixed[:, 0], places).astype(NARROW)
    keys_here = rotate(mixed[:, 1], places).astype(NARROW).reshape(all_rows, D)
    values_here = mixed[:, 2].astype(NARROW).reshape(all_rows, D)
    hidden = jnp.dot(normed_two, w_up, preferred_element_type=WIDE)
    activated = jax.nn.gelu(hidden, approximate=False).astype(NARROW)
    return (normed_one, normed_two, queries, keys_here, values_here, hidden, activated)


def attend(queries, keys_here, values_here, natural_q, opening_q, dealing_row):
    local_rows = queries.shape[0]

    def max_step(state_in, block_arrays, offset_row):
        row_top, row_total = state_in
        scores, allowed = score_block(
            queries, block_arrays[0], offset_row, natural_q, opening_q, dealing_row
        )
        new_top = jnp.maximum(row_top, jnp.max(jnp.where(allowed, scores, MASKED), axis=-1))
        kept_terms = jnp.where(allowed, jnp.exp(scores - new_top[..., None]), 0.0)
        return (new_top, row_total * jnp.exp(row_top - new_top) + jnp.sum(kept_terms, axis=-1))

    start_state = (jnp.full((H, local_rows), MASKED, WIDE), jnp.zeros((H, local_rows), WIDE))
    row_top, row_total = fold_blocks(
        max_step, start_state, (lax.all_gather(keys_here, "ctx", axis=0, tiled=True),)
    )
    log_total = row_top + jnp.log(row_total)

    def value_step(state_in, block_arrays, offset_row):
        scores, allowed = score_block(
            queries, block_arrays[0], offset_row, natural_q, opening_q, dealing_row
        )
        soft_probs = jnp.where(allowed, jnp.exp(scores - log_total[..., None]), 0.0).astype(NARROW)
        row_count = block_arrays[1].shape[0]
        return state_in + jnp.einsum(
            "hqk,khd->qhd",
            soft_probs,
            block_arrays[1].reshape(row_count, H, HD),
            preferred_element_type=WIDE,
        )

    attended = fold_blocks(
        value_step,
        jnp.zeros((local_rows, H, HD), WIDE),
        (
            lax.all_gather(keys_here, "ctx", axis=0, tiled=True),
            lax.all_gather(values_here, "ctx", axis=0, tiled=True),
        ),
    )
    return (attended, log_total)


def attention_back(
    queries,
    keys_here,
    values_here,
    g_attended,
    row_dot,
    log_total,
    natural_q,
    opening_q,
    dealing_row,
):
    local_rows = queries.shape[0]
    scale_factor = HD ** (-0.5)
    gathered_keys, gathered_values = (
        lax.all_gather(keys_here, "ctx", axis=0, tiled=True),
        lax.all_gather(values_here, "ctx", axis=0, tiled=True),
    )
    group_rows = gathered_keys.shape[0]
    key_span = 1024

    def key_block(state_in, block_item):
        block_keys, block_values, offset_row = block_item
        scores, allowed = score_block(
            queries, block_keys, offset_row, natural_q, opening_q, dealing_row
        )
        soft_probs = jnp.where(allowed, jnp.exp(scores - log_total[..., None]), 0.0)
        g_probs = jnp.einsum(
            "qhd,khd->hqk",
            g_attended,
            block_values.reshape(key_span, H, HD),
            preferred_element_type=WIDE,
        )
        g_scores = (soft_probs * (g_probs - row_dot[..., None])).astype(NARROW)
        state_out = (
            state_in
            + jnp.einsum(
                "hqk,khd->qhd",
                g_scores,
                block_keys.reshape(key_span, H, HD),
                preferred_element_type=WIDE,
            )
            * scale_factor
        )
        key_terms = (
            jnp.einsum("hqk,qhd->khd", g_scores, queries, preferred_element_type=WIDE)
            * scale_factor
        )
        value_terms = jnp.einsum(
            "hqk,qhd->khd", soft_probs.astype(NARROW), g_attended, preferred_element_type=WIDE
        )
        return (
            state_out,
            jnp.concatenate(
                [key_terms.reshape(key_span, D), value_terms.reshape(key_span, D)], axis=1
            ),
        )

    block_total = group_rows // key_span
    block_starts = jnp.arange(block_total, dtype=jnp.int32) * key_span
    stacked_blocks = (
        gathered_keys.reshape(block_total, key_span, D),
        gathered_values.reshape(block_total, key_span, D),
        block_starts,
    )
    g_queries, stacked_terms = lax.scan(
        key_block, jnp.zeros((local_rows, H, HD), WIDE), stacked_blocks
    )
    g_pairs = lax.psum_scatter(
        stacked_terms.reshape(group_rows, 2 * D), "ctx", scatter_dimension=0, tiled=True
    )
    g_keys = g_pairs[:, :D].reshape(local_rows, H, HD)
    g_values = g_pairs[:, D:].reshape(local_rows, H, HD)
    return (g_queries, g_keys, g_values)


def shards(
    tokens,
    cotangent,
    lengths,
    dealing,
    gain_one,
    bias_one,
    gain_two,
    bias_two,
    w_qkv,
    w_out,
    w_up,
    w_down,
):
    group_count = tokens.shape[0]
    local_rows = tokens.shape[1]
    all_rows = group_count * local_rows
    tokens_f = tokens.reshape(all_rows, D).astype(WIDE)
    first_row = lax.axis_index("ctx") * local_rows
    natural_list = [
        natural_rows(dealing[member], first_row, local_rows) for member in range(group_count)
    ]
    opening_list = [
        sequence_openings(natural_list[member], lengths[member]) for member in range(group_count)
    ]
    places = jnp.concatenate(
        [natural_list[member] - opening_list[member] for member in range(group_count)], axis=0
    )

    def forward():
        weights = (
            lax.all_gather(w_qkv, "wsh", axis=0, tiled=True),
            lax.all_gather(w_out, "wsh", axis=0, tiled=True),
            lax.all_gather(w_up, "wsh", axis=0, tiled=True),
            lax.all_gather(w_down, "wsh", axis=0, tiled=True),
            lax.all_gather(gain_one, "wsh", axis=0, tiled=True),
            lax.all_gather(bias_one, "wsh", axis=0, tiled=True),
            lax.all_gather(gain_two, "wsh", axis=0, tiled=True),
            lax.all_gather(bias_two, "wsh", axis=0, tiled=True),
        )
        local_parts = project(tokens_f, weights, places)
        attended_list = []
        total_list = []
        for member in range(group_count):
            rows_from = member * local_rows
            attended_one, total_one = attend(
                local_parts[2][rows_from : rows_from + local_rows],
                local_parts[3][rows_from : rows_from + local_rows],
                local_parts[4][rows_from : rows_from + local_rows],
                natural_list[member],
                opening_list[member],
                dealing[member],
            )
            attended_list.append(attended_one)
            total_list.append(total_one)
        return (weights, local_parts, jnp.concatenate(attended_list, axis=0), total_list)

    weights, local_parts, attended, total_list = forward()
    attended_low = attended.reshape(all_rows, D).astype(NARROW)
    mixed_out = (
        tokens_f
        + jnp.dot(attended_low, weights[1], preferred_element_type=WIDE)
        + jnp.dot(local_parts[6], weights[3], preferred_element_type=WIDE)
    )
    out = mixed_out.astype(NARROW)
    weights, local_parts, attended, total_list = forward()
    attended_low = attended.reshape(all_rows, D).astype(NARROW)
    w_qkv_all, w_out_all, w_up_all, w_down_all = (weights[0], weights[1], weights[2], weights[3])
    normed_one, normed_two, queries, keys_here, values_here, hidden, activated = local_parts
    grad_rows = cotangent.reshape(all_rows, D)
    grad_f = grad_rows.astype(WIDE)
    g_down = jnp.einsum("tf,td->fd", activated, grad_rows, preferred_element_type=WIDE)
    g_activated = jnp.einsum("td,fd->tf", grad_rows, w_down_all, preferred_element_type=WIDE)
    _, gelu_back = jax.vjp(lambda pre_act: jax.nn.gelu(pre_act, approximate=False), hidden)
    g_hidden = gelu_back(g_activated)[0].astype(NARROW)
    g_up = jnp.einsum("td,tf->df", normed_two, g_hidden, preferred_element_type=WIDE)
    g_normed_two = jnp.einsum("tf,df->td", g_hidden, w_up_all, preferred_element_type=WIDE)
    g_weight_out = jnp.einsum("te,td->ed", attended_low, grad_rows, preferred_element_type=WIDE)
    g_attended = (
        jnp.einsum("td,ed->te", grad_rows, w_out_all, preferred_element_type=WIDE)
        .astype(NARROW)
        .reshape(all_rows, H, HD)
    )
    row_dot = jnp.einsum("qhd,qhd->hq", g_attended.astype(WIDE), attended)
    query_grads = []
    key_grads = []
    value_grads = []
    for member in range(group_count):
        rows_from = member * local_rows
        rows_to = rows_from + local_rows
        g_q, g_k, g_v = attention_back(
            queries[rows_from:rows_to],
            keys_here[rows_from:rows_to],
            values_here[rows_from:rows_to],
            g_attended[rows_from:rows_to],
            row_dot[:, rows_from:rows_to],
            total_list[member],
            natural_list[member],
            opening_list[member],
            dealing[member],
        )
        query_grads.append(g_q)
        key_grads.append(g_k)
        value_grads.append(g_v)
    g_queries = jnp.concatenate(query_grads, axis=0)
    g_keys = jnp.concatenate(key_grads, axis=0)
    g_values = jnp.concatenate(value_grads, axis=0)
    _, rotate_back = jax.vjp(
        lambda pre_rot: rotate(pre_rot, places), jnp.zeros((all_rows, H, HD), WIDE)
    )
    g_queries_pre = rotate_back(g_queries)[0]
    g_keys_pre = rotate_back(g_keys)[0]
    g_mixed = (
        jnp.stack([g_queries_pre, g_keys_pre, g_values], axis=1)
        .reshape(all_rows, 3 * D)
        .astype(NARROW)
    )
    g_qkv = jnp.einsum("td,te->de", normed_one, g_mixed, preferred_element_type=WIDE)
    g_normed_one = jnp.einsum("te,de->td", g_mixed, w_qkv_all, preferred_element_type=WIDE)

    def both_norms(tokens_in, scale_one, shift_one, scale_two, shift_two):
        return (
            norm_layer(tokens_in, scale_one, shift_one),
            norm_layer(tokens_in, scale_two, shift_two),
        )

    _, norm_back = jax.vjp(
        both_norms,
        tokens_f,
        weights[4].astype(WIDE),
        weights[5].astype(WIDE),
        weights[6].astype(WIDE),
        weights[7].astype(WIDE),
    )
    g_tokens, g_scale_one, g_shift_one, g_scale_two, g_shift_two = norm_back(
        (g_normed_one, g_normed_two)
    )
    grad_tokens = g_tokens + grad_f
    summed = (
        lax.psum_scatter(g_qkv, ("ctx", "wsh"), scatter_dimension=0, tiled=True),
        lax.psum_scatter(g_weight_out, ("ctx", "wsh"), scatter_dimension=0, tiled=True),
        lax.psum_scatter(g_up, ("ctx", "wsh"), scatter_dimension=0, tiled=True),
        lax.psum_scatter(g_down, ("ctx", "wsh"), scatter_dimension=0, tiled=True),
        lax.psum_scatter(g_scale_one, ("ctx", "wsh"), scatter_dimension=0, tiled=True),
        lax.psum_scatter(g_shift_one, ("ctx", "wsh"), scatter_dimension=0, tiled=True),
        lax.psum_scatter(g_scale_two, ("ctx", "wsh"), scatter_dimension=0, tiled=True),
        lax.psum_scatter(g_shift_two, ("ctx", "wsh"), scatter_dimension=0, tiled=True),
    )
    return (
        out.reshape(group_count, local_rows, D),
        grad_tokens.reshape(group_count, local_rows, D),
        summed[4],
        summed[5],
        summed[6],
        summed[7],
        summed[0],
        summed[1],
        summed[2],
        summed[3],
    )


MESH = pl.DeviceIdType.MESH
NT = (((1,), (1,)), ((), ()))
TN = (((0,), (0,)), ((), ()))
VMEM_LIMIT = 60 * 1024 * 1024


def dot(a, b, dims=(((1,), (0,)), ((), ()))):
    return lax.dot_general(a, b, dims, preferred_element_type=WIDE)


def pick(index, table):
    result = jnp.int32(table[0])
    for at in range(1, len(table)):
        result = jnp.where(index == at, jnp.int32(table[at]), result)
    return result


def near_first(depth):
    return [sorted(range(depth), key=lambda to, z=z: (abs(to - z), to)) for z in range(depth)]


def pick2(row, column, table):
    result = pick(column, table[0])
    for at in range(1, len(table)):
        result = jnp.where(row == at, pick(column, table[at]), result)
    return result


class Place:
    def __init__(self, depth):
        self.depth = depth
        self.c = lax.axis_index("ctx")
        self.x = lax.axis_index("wsh")
        self.core = lax.rem(self.c, 2)
        self.y = lax.rem(self.c // 2, 2)
        self.z = self.c // 4
        self.beside = (self.at(self.z, 1 - self.y, self.core), self.x)
        self.twin = (self.at(self.z, self.y, 1 - self.core), self.x)
        self.above = (self.at(self.z + 1, self.y, self.core), self.x)
        self.below = (self.at(self.z - 1, self.y, self.core), self.x)
        self.across = (self.c, 1 - self.x)
        self.has_above = self.z < depth - 1
        self.has_below = self.z > 0

    def at(self, z, y, core):
        return (z * 2 + y) * 2 + core

    def greet(self):
        barrier = pltpu.get_barrier_semaphore()

        def hail(device):
            pl.semaphore_signal(barrier, inc=1, device_id=device, device_id_type=MESH)

        hail(self.beside)
        hail(self.twin)
        hail(self.across)

        @pl.when(self.has_above)
        def _():
            hail(self.above)

        @pl.when(self.has_below)
        def _():
            hail(self.below)

        pl.semaphore_wait(
            barrier, 3 + self.has_above.astype(jnp.int32) + self.has_below.astype(jnp.int32)
        )


    def greet_all(self):
        barrier = pltpu.get_barrier_semaphore()
        count = 4 * self.depth
        pl.semaphore_signal(barrier, inc=1, device_id=self.across, device_id_type=MESH)

        def hail(offset, carry):
            device = (lax.rem(self.c + offset, count), self.x)
            pl.semaphore_signal(barrier, inc=1, device_id=device, device_id_type=MESH)
            return carry

        lax.fori_loop(1, count, hail, 0)
        pl.semaphore_wait(barrier, count)


FREQUENCY = tuple(10000.0 ** (-2.0 * i / ROT) for i in range(ROT // 2))


def turning(place):
    row = lax.broadcasted_iota(jnp.int32, (ROT // 2, 1), 0)
    frequency = jnp.full((ROT // 2, 1), FREQUENCY[0], WIDE)
    for at in range(1, ROT // 2):
        frequency = jnp.where(row == at, FREQUENCY[at], frequency)
    angles = place.astype(WIDE) * frequency
    return jnp.cos(angles), jnp.sin(angles)


ALONG = (16, 16)


def cut(rows, what, piece):
    rest = rows - ALONG[what]
    first = (rest // 2 + 15) // 16 * 16
    begin = (0, first, rest, rows)
    return pl.ds(begin[piece], begin[piece + 1] - begin[piece])


def starts_of(lengths_ref, group):
    starts = []
    so_far = jnp.int32(0)
    for piece in range(lengths_ref.shape[1] - 1):
        so_far = so_far + lengths_ref[group, piece]
        starts.append(so_far)
    return starts


def opening_of(natural, starts):
    opening = jnp.zeros(natural.shape, jnp.int32)
    for start in starts:
        opening = jnp.where(natural >= start, start, opening)
    return opening


def find_blocks(dealing_ref, found):
    groups, blocks = dealing_ref.shape
    for group in range(groups):

        def look(block, carry):
            where = jnp.int32(0)
            for at in range(blocks):
                where = jnp.where(dealing_ref[group, at] == block, jnp.int32(at), where)
            found[group, block] = where
            return carry

        lax.fori_loop(0, blocks, look, 0)


def gather_kernel(
    depth,
    lengths_ref,
    dealing_ref,
    tok_ref,
    cot_ref,
    gain_one_ref,
    bias_one_ref,
    gain_two_ref,
    bias_two_ref,
    wqkv_ref,
    wout_ref,
    wup_ref,
    wdown_ref,
    heads_out,
    units_out,
    xhat_out,
    cot_out,
    attended_out,
    total_out,
    g_up,
    g_down,
    g_sum,
    wqkv_t,
    wup_all,
    wdown_part,
    wout_part,
    prm_all,
    found,
    both,
    xhat_all,
    heads_buf,
    units_buf,
    slope_buf,
    wide,
    k_rows,
    wq_buf,
    prm_buf,
    in_sem,
    w_sem,
    wsend_sem,
    wrecv_sem,
    send_sem,
    recv_sem,
    out_sem,
):
    here = Place(depth)
    c, x, y, z, core = here.c, here.x, here.y, here.z, here.core
    count = depth * 4
    rows = tok_ref.shape[0]
    groups = dealing_ref.shape[0]
    units = wup_all.shape[1]
    half = prm_buf.shape[2]
    order = near_first(depth)

    own_in = (
        pltpu.make_async_copy(tok_ref, both.at[0, c], in_sem.at[0]),
        pltpu.make_async_copy(cot_ref, both.at[1, c], in_sem.at[1]),
    )
    for copy in own_in:
        copy.start()
    prm_rows = [
        ref[...].astype(WIDE).reshape(1, half) for ref in (gain_one_ref, bias_one_ref, gain_two_ref, bias_two_ref)
    ]
    prm_buf[x] = jnp.concatenate(prm_rows + prm_rows, axis=0)

    pair = c // 2
    per_half = count // 2
    owner = c // per_half
    inside = lax.rem(c, per_half)
    shared = []
    for part in range(3):
        shared.append(
            (
                wqkv_ref.at[:, pl.ds(pl.multiple_of(part * D + pair * 128, 128), 128)],
                wq_buf.at[x, part],
            )
        )
    shared.append(
        (
            wup_ref.at[:, pl.ds(pl.multiple_of(c * units, 128), units)],
            wup_all.at[pl.ds(pl.multiple_of(x * half, 128), half)],
        )
    )
    held = (
        (wdown_ref.at[pl.ds(pl.multiple_of(inside * units, 128), units)], wdown_part),
        (wout_ref.at[pl.ds(pl.multiple_of(inside * HD, HD), HD)], wout_part),
    )
    is_owner = owner == x
    for at, (source, place) in enumerate(shared):
        pltpu.make_async_copy(source, place, w_sem.at[at]).start()

    @pl.when(is_owner)
    def _():
        for at, (source, place) in enumerate(held):
            pltpu.make_async_copy(source, place, w_sem.at[5 + at]).start()

    here.greet()

    def remote(source, place, at):
        return pltpu.make_async_remote_copy(
            source,
            place,
            wsend_sem.at[at],
            wrecv_sem.at[at],
            device_id=here.across,
            device_id_type=MESH,
        )

    prm_copy = remote(prm_buf.at[x], prm_buf.at[x], 4)
    prm_copy.start()
    for at, (source, place) in enumerate(shared):
        remote(source, place, at).start()

    def passing(what, piece, shard, way):
        device = (here.beside, here.twin, here.above, here.below)[way]
        return pltpu.make_async_remote_copy(
            both.at[what, shard, cut(rows, what, piece)],
            both.at[what, shard, cut(rows, what, piece)],
            send_sem.at[what, piece, way, shard],
            recv_sem.at[what, piece, shard],
            device_id=device,
            device_id_type=MESH,
        )

    def onward(what, piece, shard, from_z, cross):
        if cross:
            passing(what, piece, shard, 0).start()

        @pl.when(jnp.logical_and(from_z <= z, here.has_above))
        def _():
            passing(what, piece, shard, 2).start()

        @pl.when(jnp.logical_and(from_z >= z, here.has_below))
        def _():
            passing(what, piece, shard, 3).start()

        passing(what, piece, shard, 1).start()

    def arrived(what, piece, shard):
        passing(what, piece, shard, 1).wait_recv()

    def relay(what, shard, from_z):
        for piece in range(3):
            arrived(what, piece, shard)
            onward(what, piece, shard, from_z, piece < 2)

    own_in[0].wait()
    for piece in range(3):
        onward(0, piece, c, z, True)
    own_in[1].wait()
    for piece in range(3):
        onward(1, piece, c, z, True)
    find_blocks(dealing_ref, found)

    for at, (source, place) in enumerate(shared):
        pltpu.make_async_copy(source, place, w_sem.at[at]).wait()
        remote(source, place, at).wait_recv()
    prm_copy.wait_recv()

    @pl.when(is_owner)
    def _():
        for at, (source, place) in enumerate(held):
            remote(source, place, 5 + at).start()

    odd = lax.rem(c, 2) == 1
    for side in range(2):
        prm_all[:, side * half : (side + 1) * half] = prm_buf[side]
        for part in range(3):
            turned = wq_buf[side, part].astype(WIDE).T
            chosen = jnp.where(odd, turned[HD:], turned[:HD])
            wqkv_t[part * HD : (part + 1) * HD, side * half : (side + 1) * half] = chosen.astype(
                NARROW
            )
    g_up[...] = jnp.zeros_like(g_up)
    g_down[...] = jnp.zeros_like(g_down)
    g_sum[...] = jnp.zeros_like(g_sum)

    kept = (
        (xhat_all, xhat_out),
        (both.at[1], cot_out),
        (heads_buf, heads_out),
        (units_buf, units_out),
    )

    def copy_out(at, shard):
        source, place = kept[at]
        return pltpu.make_async_copy(source.at[shard], place.at[shard], out_sem.at[at, shard])

    def ahead(shard):
        tokens = both[0, shard].astype(WIDE)
        average = jnp.mean(tokens, axis=-1, keepdims=True)
        centred = tokens - average
        variance = jnp.mean(centred * centred, axis=-1, keepdims=True)
        xhat = centred * lax.rsqrt(variance + EPSILON)
        xhat_all[shard] = xhat.astype(NARROW)
        n_one = (xhat * prm_all[0:1, :] + prm_all[1:2, :]).astype(NARROW)
        n_two = (xhat * prm_all[2:3, :] + prm_all[3:4, :]).astype(NARROW)
        mixed = dot(wqkv_t[...], n_one, NT)
        places = []
        for group in range(groups):
            natural = dealing_ref[group, shard] * BLK + lax.broadcasted_iota(jnp.int32, (1, BLK), 1)
            places.append(natural - opening_of(natural, starts_of(lengths_ref, group)))
        cosine, sine = turning(jnp.concatenate(places, axis=1))
        pieces = []
        for base in (0, HD):
            first, second = mixed[base : base + 8], mixed[base + 8 : base + 16]
            pieces += [
                first * cosine - second * sine,
                second * cosine + first * sine,
                mixed[base + 16 : base + HD],
            ]
        pieces.append(mixed[2 * HD : 3 * HD])
        heads_buf[shard, 0 : 3 * HD, :] = jnp.concatenate(pieces, axis=0).astype(NARROW)
        hidden = dot(n_two, wup_all[...])
        spread = 0.5 * (1.0 + lax.erf(hidden * (0.5**0.5)))
        units_buf[shard, :, 0:units] = (hidden * spread).astype(NARROW)
        slope_buf[shard] = spread + hidden * (jnp.exp(hidden * hidden * -0.5) * 0.3989422804014327)
        copy_out(0, shard).start()

    def behind(shard):
        cotangent = both[1, shard]
        heads_buf[shard, 3 * HD : 4 * HD, :] = dot(wout_part[...], cotangent, NT).astype(NARROW)
        g_hidden = (dot(cotangent, wdown_part[...], NT) * slope_buf[shard]).astype(NARROW)
        units_buf[shard, :, units : 2 * units] = g_hidden
        g_up[...] += dot(g_hidden, xhat_all[shard], TN)
        g_down[...] += dot(units_buf[shard, :, 0:units], cotangent, TN)
        g_sum[...] += jnp.sum(g_hidden.astype(WIDE).reshape(rows // 8, 8, units), axis=0)
        for at in (1, 2, 3):
            copy_out(at, shard).start()

    inner = jnp.logical_and(here.has_above, here.has_below)

    def sweep(what, work, beside_work, first=0):
        relays = what == 0

        def step(at, carry):
            turn_no = at // 4
            kind = lax.rem(at, 4)
            late = jnp.where(kind >= 2, turn_no - 1, turn_no)
            from_z = pick2(z, jnp.clip(late, 0, depth - 1), order)
            next_z = pick2(z, jnp.clip(turn_no + 1, 0, depth - 1), order)
            shard_y = jnp.where(kind >= 2, 1 - y, y)
            shard_core = jnp.where(lax.rem(kind, 2) == 1, 1 - core, core)
            shard = here.at(from_z, shard_y, shard_core)
            live = jnp.logical_and(late >= 0, late < depth)

            early = jnp.logical_and(inner, turn_no == 2)
            is_own = jnp.logical_and(kind == 0, turn_no == 0)
            done = jnp.logical_or(is_own, jnp.logical_and(kind == 0, early))

            @pl.when(jnp.logical_and(lax.rem(kind, 2) == 1, live))
            def _():
                for piece in range(3):
                    arrived(what, piece, shard)

            if relays:

                @pl.when(jnp.logical_and(jnp.logical_and(kind == 0, live), jnp.logical_not(done)))
                def _():
                    relay(what, shard, from_z)

            @pl.when(jnp.logical_and(kind == 2, live))
            def _():
                arrived(what, 2, shard)
                onward(what, 2, shard, from_z, False)
                for piece in range(2):
                    arrived(what, piece, shard)
                    passing(what, piece, shard, 1).start()

            if relays:

                @pl.when(jnp.logical_and(jnp.logical_and(kind == 1, turn_no == 1), inner))
                def _():
                    relay(what, here.at(next_z, y, core), next_z)

            beside_work(at)

            @pl.when(live)
            def _():
                work(shard)

            return carry

        lax.fori_loop(first, 4 * depth + 4, step, 0)

    def relay_next(at, wanted, index, which):
        @pl.when(jnp.logical_and(at == wanted, which))
        def _():
            from_z = pick2(z, jnp.int32(index), order)
            relay(1, here.at(from_z, y, core), from_z)

    outer = jnp.logical_not(inner)

    def late_weights():
        @pl.when(is_owner)
        def _():
            for at, (source, place) in enumerate(held):
                pltpu.make_async_copy(source, place, w_sem.at[5 + at]).wait()

        @pl.when(jnp.logical_not(is_owner))
        def _():
            for at, (source, place) in enumerate(held):
                remote(source, place, 5 + at).wait_recv()

    def cotangents_start(at):
        relay_next(at, 4 * depth, 1, at >= 0)
        relay_next(at, 4 * depth + 1, 2, inner)

        @pl.when(at == 4 * depth)
        def _():
            late_weights()
            behind(c)

        @pl.when(at == 4 * depth + 1)
        def _():
            twin = here.at(z, y, 1 - core)
            for piece in range(3):
                arrived(1, piece, twin)
            behind(twin)

    sweep(0, ahead, cotangents_start)

    spans = count // 2
    span = 2 * BLK

    def bring(at, carry):
        for group in range(groups):
            lanes = slice(group * BLK, (group + 1) * BLK)
            for side in range(2):
                source = found[group, 2 * at + side]
                part = heads_buf[source, 0 : 3 * HD, lanes]
                to = slice(side * BLK, (side + 1) * BLK)
                wide[group, at, 0:HD, to] = (part[0:HD].astype(WIDE) * HD ** (-0.5)).astype(NARROW)
                wide[group, at, HD : 2 * HD, to] = part[2 * HD : 3 * HD]
                k_rows[group, at, to, :] = part[HD : 2 * HD].astype(WIDE).T.astype(NARROW)
        return carry

    lax.fori_loop(0, spans, bring, 0)
    openings = [starts_of(lengths_ref, group) for group in range(groups)]

    def attend(at):
        group = lax.rem(at, groups)
        turn_no = at // groups
        mine = jnp.where(lax.rem(turn_no, 2) == 0, spans - 1 - turn_no // 2, turn_no // 2)
        natural = mine * span + lax.broadcasted_iota(jnp.int32, (1, span), 1)
        opening = opening_of(natural, [jnp.where(group == 0, *pair) for pair in zip(*openings)])
        queries = wide[group, mine, 0:HD, :]

        def add(first, width, state, diagonal):
            top, total, so_far = state
            keys = k_rows[group, pl.ds(first, width)].reshape(width * span, HD)
            place = lax.broadcasted_iota(jnp.int32, (width * span, span), 0)
            allowed = place >= opening - first * span
            if diagonal:
                allowed = jnp.logical_and(allowed, place <= natural - first * span)
            raw = jnp.where(allowed, dot(keys, queries), MASKED)
            new_top = jnp.maximum(top, jnp.max(raw, axis=0, keepdims=True))
            risen = jnp.exp(raw - new_top)
            fade = jnp.exp(top - new_top)
            total = total * fade + jnp.sum(risen, axis=0, keepdims=True)
            values = jnp.concatenate(
                [wide[group, first + side, HD : 2 * HD, :] for side in range(width)], axis=1
            )
            return new_top, total, so_far * fade + dot(values, risen.astype(NARROW))

        state = (
            jnp.full((1, span), MASKED, WIDE),
            jnp.zeros((1, span), WIDE),
            jnp.zeros((HD, span), WIDE),
        )
        last = mine // 2
        state = lax.cond(
            lax.rem(mine, 2) == 1,
            lambda state: add(mine - 1, 2, state, True),
            lambda state: add(mine, 1, state, True),
            state,
        )

        def earlier(back, state):
            return add(2 * (last - 1 - back), 2, state, False)

        top, total, so_far = lax.fori_loop(0, last, earlier, state)
        attended = so_far / total
        for side in range(2):
            attended_out[group, 2 * mine + side] = attended[:, side * BLK : (side + 1) * BLK]
        total_out[group, mine] = jnp.broadcast_to(top + jnp.log(total), (8, span))

    def attend_too(at):
        relay_next(at, 4, 2, outer)
        relay_next(at, 4, 3, inner)
        relay_next(at, 7, 3, outer)

        @pl.when(at < groups * spans + 4)
        def _():
            attend(at - 4)

    sweep(1, behind, attend_too, first=4)

    def finish(shard, carry):
        shard_z = shard // 4
        mine = lax.rem(shard, 2) == core
        column = lax.rem(shard // 2, 2) == y
        for what in range(2):

            @pl.when(mine)
            def _():
                for piece in range(3):
                    passing(what, piece, shard, 1).wait_send()

            for piece in range(3):
                along = mine if piece == 2 else jnp.logical_and(mine, column)

                @pl.when(jnp.logical_and(along, jnp.logical_and(shard_z <= z, here.has_above)))
                def _():
                    passing(what, piece, shard, 2).wait_send()

                @pl.when(jnp.logical_and(along, jnp.logical_and(shard_z >= z, here.has_below)))
                def _():
                    passing(what, piece, shard, 3).wait_send()

                crossed = shard == c if piece == 2 else jnp.logical_and(mine, column)

                @pl.when(crossed)
                def _():
                    passing(what, piece, shard, 0).wait_send()

        for at in range(4):
            copy_out(at, shard).wait()
        return carry

    lax.fori_loop(0, count, finish, 0)
    for at, (source, place) in enumerate(shared):
        remote(source, place, at).wait_send()
    prm_copy.wait_send()

    @pl.when(is_owner)
    def _():
        for at, (source, place) in enumerate(held):
            remote(source, place, 5 + at).wait_send()


def gather_call(depth, lengths, dealing, tok, cot, gains, w_qkv, w_out, w_up, w_down):
    count = depth * 4
    rows = tok.shape[0]
    groups = dealing.shape[0]
    spans, span = count // 2, 2 * BLK
    units = w_up.shape[1] // count
    any_spec = pl.BlockSpec(memory_space=pl.ANY)
    vmem = pl.BlockSpec(memory_space=pltpu.VMEM)
    smem = pl.BlockSpec(memory_space=pltpu.SMEM)
    shape = jax.ShapeDtypeStruct
    return pl.pallas_call(
        functools.partial(gather_kernel, depth),
        out_shape=(
            shape((count, 4 * HD, rows), NARROW),
            shape((count, rows, 2 * units), NARROW),
            shape((count, rows, D), NARROW),
            shape((count, rows, D), NARROW),
            shape((groups, count, HD, BLK), WIDE),
            shape((groups, spans, 8, span), WIDE),
            shape((units, D), WIDE),
            shape((units, D), WIDE),
            shape((8, units), WIDE),
            shape((3 * HD, D), NARROW),
            shape((D, units), NARROW),
            shape((units, D), NARROW),
            shape((HD, D), NARROW),
            shape((8, D), WIDE),
            shape((groups, count), jnp.int32),
        ),
        in_specs=[smem, smem, any_spec, any_spec] + [vmem] * 4 + [any_spec] * 4,
        out_specs=(any_spec,) * 4 + (vmem,) * 10 + (smem,),
        scratch_shapes=[
            pltpu.VMEM((2, count, rows, D), NARROW),
            pltpu.VMEM((count, rows, D), NARROW),
            pltpu.VMEM((count, 4 * HD, rows), NARROW),
            pltpu.VMEM((count, rows, 2 * units), NARROW),
            pltpu.VMEM((count, rows, units), WIDE),
            pltpu.VMEM((groups, spans, 2 * HD, span), NARROW),
            pltpu.VMEM((groups, spans, span, HD), NARROW),
            pltpu.VMEM((2, 3, D // 2, 128), NARROW),
            pltpu.VMEM((2, 8, D // 2), WIDE),
            pltpu.SemaphoreType.DMA((2,)),
            pltpu.SemaphoreType.DMA((7,)),
            pltpu.SemaphoreType.DMA((7,)),
            pltpu.SemaphoreType.DMA((7,)),
            pltpu.SemaphoreType.DMA((2, 3, 4, count)),
            pltpu.SemaphoreType.DMA((2, 3, count)),
            pltpu.SemaphoreType.DMA((4, count)),
        ],
        name="gather_and_forward",
        compiler_params=pltpu.CompilerParams(
            collective_id=1, has_side_effects=True, vmem_limit_bytes=VMEM_LIMIT
        ),
    )(lengths, dealing, tok, cot, *gains, w_qkv, w_out, w_up, w_down)


def far_first(depth):
    return [list(reversed(row)) for row in near_first(depth)]


def unturn(rows, cosine, sine):
    first, second = rows[0:8], rows[8:16]
    return jnp.concatenate(
        [first * cosine + second * sine, second * cosine - first * sine, rows[16:]], axis=0
    )


def reduce_kernel(
    depth,
    lengths_ref,
    dealing_ref,
    found,
    total_in,
    prm_all,
    g_sum,
    attended_hbm,
    wout_hbm,
    wdown_hbm,
    units_hbm,
    g_up_hbm,
    wup_hbm,
    wqkv_hbm,
    g_down_hbm,
    heads_hbm,
    xhat_in,
    cot_in,
    sum_out,
    sum_back,
    inbox,
    wout_ref,
    down_ref,
    vec_ref,
    attended_in,
    wout_part,
    wdown_part,
    units_in,
    g_up,
    wup_all,
    wqkv_t,
    g_down,
    heads_in,
    w_heads_back,
    give_buf,
    sum_buf,
    beside_buf,
    line_buf,
    other_line,
    wide,
    q_rows,
    k_rows,
    v_rows,
    g_rows,
    g_key,
    g_value,
    turned_all,
    by_token,
    stream,
    g_heads,
    g_wout,
    sum_heads,
    vectors,
    grads,
    grads_in,
    mail,
    wout_in,
    down_in,
    first_sem,
    send_twin,
    send_beside,
    recv_twin,
    recv_beside,
    recv_z,
    send_z,
    send_last,
    recv_last,
    stream_sem,
    across_send,
    across_recv,
    mail_send,
    mail_recv,
):
    here = Place(depth)
    c, x, y, z, core = here.c, here.x, here.y, here.z, here.core
    rows = sum_out.shape[0]
    units = wup_all.shape[1]
    groups = dealing_ref.shape[0]
    count = 4 * depth
    brought = [
        pltpu.make_async_copy(source, place, first_sem.at[at])
        for at, (source, place) in enumerate(
            (
                (attended_hbm, attended_in),
                (wout_hbm, wout_part),
                (wdown_hbm, wdown_part),
                (units_hbm, units_in),
                (g_up_hbm, g_up),
                (wup_hbm, wup_all),
                (wqkv_hbm, wqkv_t),
                (g_down_hbm, g_down),
                (heads_hbm, heads_in),
            )
        )
    ]
    for copy in brought:
        copy.start()
    spans, span = count // 2, 2 * BLK
    scale = HD ** (-0.5)
    piece = D // (2 * count)
    order = far_first(depth)

    def shard_of(at):
        kind = lax.rem(at, 4)
        to_y = jnp.where(lax.rem(kind, 2) == 1, y, 1 - y)
        to_core = jnp.where(kind < 2, 1 - core, core)
        return here.at(pick2(z, at // 4, order), to_y, to_core)

    def load(at):
        shard, slot = shard_of(at), lax.rem(at, 2)
        return (
            pltpu.make_async_copy(xhat_in.at[shard], stream.at[0, slot], stream_sem.at[0, slot]),
            pltpu.make_async_copy(cot_in.at[shard], stream.at[1, slot], stream_sem.at[1, slot]),
        )

    here.greet_all()

    def crossing(source, place, at):
        return pltpu.make_async_remote_copy(
            source,
            place,
            across_send.at[at],
            across_recv.at[at],
            device_id=here.across,
            device_id_type=MESH,
        )

    half_down = g_down.shape[0] // 2
    half_wout = HD // 2
    send_down = crossing(g_down.at[pl.ds((1 - x) * half_down, half_down)], down_in, 0)
    send_wout = crossing(g_wout.at[pl.ds((1 - x) * half_wout, half_wout)], wout_in, 1)
    send_grads = [crossing(grads.at[part, 1 - x], grads_in.at[part], 2 + part) for part in range(2)]

    def to_twin(what, slot):
        return pltpu.make_async_remote_copy(
            give_buf.at[slot],
            sum_buf.at[what, slot],
            send_twin.at[what, slot],
            recv_twin.at[what, slot],
            device_id=here.twin,
            device_id_type=MESH,
        )

    def to_beside(what, piece, to_z):
        return pltpu.make_async_remote_copy(
            sum_buf.at[what, to_z, cut(rows, what, piece)],
            beside_buf.at[what, to_z, cut(rows, what, piece)],
            send_beside.at[what, piece, to_z],
            recv_beside.at[what, piece, to_z],
            device_id=here.beside,
            device_id_type=MESH,
        )

    def over_slot(to_z, at_z):
        return jnp.where(to_z == at_z, depth, to_z)

    def along(what, piece, home, to_z, place, device):
        here_rows = cut(rows, what, piece)
        if piece == 2:
            target = other_line.at[what, place, pl.ds(0, ALONG[what])]
            if home == 1:
                target = line_buf.at[what, place, here_rows]
        else:
            target = line_buf.at[what, place, here_rows]
        lane = piece + (home if piece == 2 else 0)
        return pltpu.make_async_remote_copy(
            sum_buf.at[what, home * depth + to_z, here_rows],
            target,
            send_z.at[what, lane, to_z],
            recv_z.at[what, lane, place],
            device_id=device,
            device_id_type=MESH,
        )

    def to_above(what, piece, home, to_z):
        return along(what, piece, home, to_z, to_z, here.above)

    def to_below(what, piece, home, to_z):
        return along(what, piece, home, to_z, over_slot(to_z, z - 1), here.below)

    def from_above(what, piece, home, to_z):
        return along(what, piece, home, to_z, over_slot(to_z, z), here.above)

    def cross_last(what):
        here_rows = cut(rows, what, 2)
        return pltpu.make_async_remote_copy(
            sum_buf.at[what, z, here_rows],
            beside_buf.at[what, z, here_rows],
            send_last.at[what],
            recv_last.at[what],
            device_id=here.beside,
            device_id_type=MESH,
        )

    def pass_on(what, at, part):
        to_z = pick2(z, at // 4, order)
        kind = lax.rem(at, 4)
        slot = lax.rem(kind, 2) * depth + to_z

        @pl.when(kind < 2)
        def _():
            if what == 1:
                to_twin(0, slot).wait_send()
            give_buf[slot] = part.astype(NARROW)
            to_twin(what, slot).start()

        @pl.when(kind >= 2)
        def _():
            to_twin(what, slot).wait_recv()
            sum_buf[what, slot] = (part + sum_buf[what, slot].astype(WIDE)).astype(NARROW)

        @pl.when(kind == 2)
        def _():
            for piece in range(2):
                to_beside(what, piece, to_z).start()

    def chain_piece(what, at, piece, home):
        to_z = pick2(z, at, order)
        slot = home * depth + to_z
        here_rows = cut(rows, what, piece)
        if piece < 2:
            to_beside(what, piece, to_z).wait_recv()

        def add(incoming):
            total = sum_buf[what, slot, here_rows, :].astype(WIDE)
            if piece < 2:
                total = total + beside_buf[what, to_z, here_rows, :].astype(WIDE)
            if incoming:
                if piece == 2 and home == 0:
                    came = other_line[what, to_z, 0 : ALONG[what], :]
                else:
                    came = line_buf[what, to_z, here_rows, :]
                total = total + came.astype(WIDE)
            sum_buf[what, slot, here_rows, :] = total.astype(NARROW)

        @pl.when(to_z > z)
        def _():
            @pl.when(here.has_below)
            def _():
                to_above(what, piece, home, to_z).wait_recv()
                add(True)

            if piece < 2:

                @pl.when(jnp.logical_not(here.has_below))
                def _():
                    add(False)

            to_above(what, piece, home, to_z).start()

        @pl.when(to_z < z)
        def _():
            @pl.when(here.has_above)
            def _():
                from_above(what, piece, home, to_z).wait_recv()
                add(True)

            if piece < 2:

                @pl.when(jnp.logical_not(here.has_above))
                def _():
                    add(False)

            to_below(what, piece, home, to_z).start()

    def chain(what, at):
        for home in range(2):
            chain_piece(what, at, 2, home)
        for piece in range(2):
            chain_piece(what, at, piece, 1)

    def cross_over(what):
        here_rows = cut(rows, what, 2)
        came = slice(0, ALONG[what])

        @pl.when(here.has_below)
        def _():
            to_above(what, 2, 0, z).wait_recv()
            total = sum_buf[what, z, here_rows, :].astype(WIDE)
            total = total + other_line[what, z, came, :].astype(WIDE)
            sum_buf[what, z, here_rows, :] = total.astype(NARROW)

        @pl.when(here.has_above)
        def _():
            from_above(what, 2, 0, z).wait_recv()
            total = sum_buf[what, z, here_rows, :].astype(WIDE)
            total = total + other_line[what, depth, came, :].astype(WIDE)
            sum_buf[what, z, here_rows, :] = total.astype(NARROW)

        cross_last(what).start()

    def gather_total(what):
        for piece in range(2):
            to_beside(what, piece, z).wait_recv()
        cross_last(what).wait_recv()

        @pl.when(here.has_below)
        def _():
            for piece in range(3):
                to_above(what, piece, 1, z).wait_recv()

        @pl.when(jnp.logical_not(here.has_below))
        def _():
            line_buf[what, z] = jnp.zeros((rows, D), NARROW)

        @pl.when(here.has_above)
        def _():
            for piece in range(3):
                from_above(what, piece, 1, z).wait_recv()

        @pl.when(jnp.logical_not(here.has_above))
        def _():
            line_buf[what, depth] = jnp.zeros((rows, D), NARROW)

        return (
            sum_buf[what, depth + z].astype(WIDE)
            + beside_buf[what, z].astype(WIDE)
            + line_buf[what, z].astype(WIDE)
            + line_buf[what, depth].astype(WIDE)
        )

    def give_out(at, carry):
        shard = shard_of(at)
        parts = []
        for group in range(groups):
            attended = attended_in[group, dealing_ref[group, shard]].astype(NARROW)
            parts.append(dot(attended, wout_part[...], TN))
        part = jnp.concatenate(parts, axis=0) + dot(units_in[shard, :, 0:units], wdown_part[...])
        pass_on(0, at, part)
        return carry

    for copy in brought[:4]:
        copy.wait()
    lax.fori_loop(0, count, give_out, 0)
    for copy in brought[4:]:
        copy.wait()
    send_down.start()

    def settle(chunk, part, raw, weights, sums, column):
        scaled = raw * column[:, 2 - 2 * part : 3 - 2 * part] + sums * column[:, 3 - 2 * part : 4 - 2 * part]
        gain_sum = jnp.sum(weights * raw, axis=1, keepdims=True)
        bias_sum = jnp.sum(weights * sums, axis=1, keepdims=True)
        row = pl.ds(pl.multiple_of(chunk * 128, 128), 128)
        if part == 0:
            vectors[row, 0:1] = gain_sum
            vectors[row, 1:2] = bias_sum
        else:
            lane = lax.broadcasted_iota(jnp.int32, scaled.shape, 1)
            scaled = jnp.where(lane == 0, gain_sum, scaled)
            scaled = jnp.where(lane == 1, bias_sum, scaled)
            scaled = jnp.where(lane == 2, vectors[row, 0:1], scaled)
            scaled = jnp.where(lane == 3, vectors[row, 1:2], scaled)
        per = 128 // piece
        for at in range(per):
            grads[part, at % 2, chunk * (per // 2) + at // 2] = scaled[at * piece : (at + 1) * piece].astype(NARROW)

    sum_units = jnp.sum(g_sum[...], axis=0, keepdims=True)

    def settle_up(chunk, carry):
        lanes = pl.ds(pl.multiple_of(chunk * 128, 128), 128)
        weights = wup_all[lanes, :].astype(WIDE)
        settle(chunk, 0, g_up[:, lanes].T, weights, sum_units, prm_all[:, lanes].T)
        return carry

    lax.fori_loop(0, D // 128, settle_up, 0)
    send_grads[0].start()
    w_heads_back[0:HD, :] = jnp.zeros((HD, D), NARROW)
    w_heads_back[HD:, :] = wqkv_t[...]
    g_heads[...] = jnp.zeros_like(g_heads)
    g_wout[...] = jnp.zeros_like(g_wout)
    sum_heads[...] = jnp.zeros_like(sum_heads)

    for group in range(groups):
        lanes = slice(group * BLK, (group + 1) * BLK)
        starts = starts_of(lengths_ref, group)

        def bring(at, carry, group=group, lanes=lanes):
            for side in range(2):
                source = found[group, 2 * at + side]
                part = heads_in[source, :, lanes]
                to = slice(side * BLK, (side + 1) * BLK)
                queries = part[0:HD].astype(WIDE) * scale
                keys = part[HD : 2 * HD]
                grads_part = part[3 * HD : 4 * HD]
                wide[at, 0:HD, to] = queries.astype(NARROW)
                wide[at, HD : 2 * HD, to] = keys
                wide[at, 2 * HD : 3 * HD, to] = grads_part
                q_rows[at, to, :] = queries.T.astype(NARROW)
                k_rows[at, to, :] = keys.astype(WIDE).T.astype(NARROW)
                v_rows[at, to, :] = part[2 * HD : 3 * HD].astype(WIDE).T.astype(NARROW)
                g_rows[at, to, :] = grads_part.astype(WIDE).T.astype(NARROW)
            g_key[at] = jnp.zeros((span, HD), WIDE)
            g_value[at] = jnp.zeros((span, HD), WIDE)
            return carry

        lax.fori_loop(0, spans, bring, 0)
        chain(0, 2 * group)

        def one_span(at, carry, group=group, starts=starts):
            natural = at * span + lax.broadcasted_iota(jnp.int32, (1, span), 1)
            opening = opening_of(natural, starts)
            queries = wide[at, 0:HD, :]
            g_attended = wide[at, 2 * HD : 3 * HD, :]
            attended = jnp.concatenate(
                [attended_in[group, 2 * at], attended_in[group, 2 * at + 1]], axis=1
            )
            row_dot = jnp.sum(attended * g_attended.astype(WIDE), axis=0, keepdims=True)
            log_total = total_in[group, at, 0:1, :]

            def add(first, width, so_far, diagonal):
                some = pl.ds(first, width)
                keys = k_rows[some].reshape(width * span, HD)
                values = v_rows[some].reshape(width * span, HD)
                place = lax.broadcasted_iota(jnp.int32, (width * span, span), 0)
                allowed = place >= opening - first * span
                if diagonal:
                    allowed = jnp.logical_and(allowed, place <= natural - first * span)
                scores = dot(keys, queries)
                probs = jnp.where(allowed, jnp.exp(scores - log_total), 0.0)
                g_scores = (probs * (dot(values, g_attended) - row_dot)).astype(NARROW)
                g_key[some] += dot(g_scores, q_rows[at]).reshape(width, span, HD)
                g_value[some] += dot(probs.astype(NARROW), g_rows[at]).reshape(width, span, HD)
                keys_t = jnp.concatenate(
                    [wide[first + side, HD : 2 * HD, :] for side in range(width)], axis=1
                )
                return so_far + dot(keys_t, g_scores)

            def earlier(pair, so_far):
                return add(2 * pair, 2, so_far, False)

            so_far = lax.fori_loop(0, at // 2, earlier, jnp.zeros((HD, span), WIDE))
            so_far = lax.cond(
                lax.rem(at, 2) == 1,
                lambda so_far: add(at - 1, 2, so_far, True),
                lambda so_far: add(at, 1, so_far, True),
                so_far,
            )
            cosine, sine = turning(natural - opening)
            turned = jnp.concatenate([attended, unturn(so_far * scale, cosine, sine)], axis=0)
            for side in range(2):
                part = turned[:, side * BLK : (side + 1) * BLK]
                turned_all[group, 2 * at + side, 0 : 2 * HD, :] = part.astype(NARROW)
            return carry

        lax.fori_loop(0, spans, one_span, 0)
        if group == 0:
            chain(0, 1)
        else:
            cross_over(0)

        def give(at, carry, group=group, starts=starts):
            natural = at * span + lax.broadcasted_iota(jnp.int32, (1, span), 1)
            cosine, sine = turning(natural - opening_of(natural, starts))
            keys = unturn(g_key[at].T, cosine, sine)
            turned = jnp.concatenate([keys, g_value[at].T], axis=0)
            for side in range(2):
                part = turned[:, side * BLK : (side + 1) * BLK]
                turned_all[group, 2 * at + side, 2 * HD : 4 * HD, :] = part.astype(NARROW)
                whole = turned_all[group, 2 * at + side].astype(WIDE)
                by_token[group, 2 * at + side] = whole.T.astype(NARROW)
            return carry

        lax.fori_loop(0, spans, give, 0)

    for copy in load(0):
        copy.start()

    def tokens_of(shard):
        blocks = [by_token[group, dealing_ref[group, shard]] for group in range(groups)]
        return jnp.concatenate(blocks, axis=0)

    def give_back(at, carry):
        shard = shard_of(at)
        g_hidden = units_in[shard, :, units : 2 * units]
        part = dot(tokens_of(shard), w_heads_back[...]) * prm_all[0:1, :] + dot(
            g_hidden, wup_all[...], NT
        ) * prm_all[2:3, :]
        pass_on(1, at, part)
        return carry

    lax.fori_loop(0, count, give_back, 0)

    def post(part, to_c):
        return pltpu.make_async_remote_copy(
            mail.at[part, to_c],
            inbox.at[part, c],
            mail_send.at[part, to_c],
            mail_recv.at[part, c],
            device_id=(to_c, x),
            device_id_type=MESH,
        )

    def collect(part, from_c):
        return pltpu.make_async_remote_copy(
            mail.at[part, from_c],
            inbox.at[part, from_c],
            mail_send.at[part, from_c],
            mail_recv.at[part, from_c],
            device_id=(from_c, x),
            device_id_type=MESH,
        )

    def mail_out(part):
        send_grads[part].wait_recv()

        def fold(to_c, carry):
            mail[part, to_c] = (
                grads[part, x, to_c].astype(WIDE) + grads_in[part, to_c].astype(WIDE)
            ).astype(NARROW)
            return carry

        lax.fori_loop(0, count, fold, 0)

        def start(offset, carry):
            post(part, lax.rem(c + offset, count)).start()
            return carry

        lax.fori_loop(1, count, start, 0)
        inbox[part, c] = mail[part, c]

    mail_out(0)

    def weigh(at, carry):
        shard, slot = shard_of(at), lax.rem(at, 2)

        @pl.when(at + 1 < count)
        def _():
            for copy in load(at + 1):
                copy.start()

        for copy in load(at):
            copy.wait()
        turned = jnp.concatenate(
            [turned_all[group, dealing_ref[group, shard]] for group in range(groups)], axis=1
        )
        g_wout[...] += dot(turned[0:HD], stream[1, slot])
        g_heads[HD:, :] += dot(turned[HD:], stream[0, slot])
        sum_heads[...] += jnp.sum(
            tokens_of(shard).astype(WIDE).reshape(rows // 8, 8, 4 * HD), axis=0
        )
        return carry

    inner = jnp.logical_and(here.has_above, here.has_below)
    outer = jnp.logical_not(inner)
    early, middle = count // 4, count * 5 // 8
    lax.fori_loop(0, early, weigh, 0)

    @pl.when(outer)
    def _():
        chain(1, 0)

    lax.fori_loop(early, middle, weigh, 0)

    @pl.when(outer)
    def _():
        chain(1, 1)

    @pl.when(inner)
    def _():
        chain(1, 0)

    lax.fori_loop(middle, count, weigh, 0)
    send_wout.start()
    sum_row = jnp.sum(sum_heads[...], axis=0, keepdims=True)

    def settle_qkv(chunk, carry):
        lanes = pl.ds(pl.multiple_of(chunk * 128, 128), 128)
        weights = w_heads_back[:, lanes].astype(WIDE).T
        settle(chunk, 1, g_heads[:, lanes].T, weights, sum_row, prm_all[:, lanes].T)
        return carry

    lax.fori_loop(0, D // 128, settle_qkv, 0)
    send_grads[1].start()

    @pl.when(inner)
    def _():
        chain(1, 1)

    for at in range(2, depth - 1):
        chain(1, at)
    mail_out(1)
    cross_over(1)


    sum_out[...] = gather_total(0)
    send_down.wait()
    down_ref[...] = g_down[pl.ds(x * half_down, half_down), :] + down_in[...]
    send_wout.wait()
    wout_ref[...] = g_wout[pl.ds(x * half_wout, half_wout), :] + wout_in[...]

    def close(offset, carry):
        other = lax.rem(c + offset, count)
        for part in range(2):
            collect(part, other).wait_recv()
            post(part, other).wait_send()
        return carry

    lax.fori_loop(1, count, close, 0)
    for part in range(2):
        send_grads[part].wait_send()
    together = jnp.zeros((piece, 128), WIDE)
    for from_c in range(count):
        together = together + inbox[1, from_c, :, 0:128].astype(WIDE)
    vec_ref[...] = together.T[0:8]
    sum_back[...] = gather_total(1)

    def finish(to_z, carry):
        to_twin(1, to_z).wait_send()
        to_twin(1, depth + to_z).wait_send()
        for what in range(2):
            for piece in range(2):
                to_beside(what, piece, to_z).wait_send()

            @pl.when(to_z > z)
            def _():
                to_above(what, 2, 0, to_z).wait_send()
                for piece in range(3):
                    to_above(what, piece, 1, to_z).wait_send()

            @pl.when(to_z < z)
            def _():
                to_below(what, 2, 0, to_z).wait_send()
                for piece in range(3):
                    to_below(what, piece, 1, to_z).wait_send()

        return carry

    lax.fori_loop(0, depth, finish, 0)
    for what in range(2):
        cross_last(what).wait_send()


def reduce_call(depth, scalars, small, large, rows):
    count = depth * 4
    groups = scalars[1].shape[0]
    spans, span = count // 2, 2 * BLK
    piece = D // (2 * count)
    units = large[5].shape[1]
    vmem = pl.BlockSpec(memory_space=pltpu.VMEM)
    smem = pl.BlockSpec(memory_space=pltpu.SMEM)
    any_spec = pl.BlockSpec(memory_space=pl.ANY)
    shape = jax.ShapeDtypeStruct
    message = (rows, D)
    row_form = pltpu.VMEM((spans, span, HD), NARROW)
    return pl.pallas_call(
        functools.partial(reduce_kernel, depth),
        out_shape=(
            shape((rows, D), WIDE),
            shape((rows, D), WIDE),
            shape((2, count, piece, 256), NARROW),
            shape((HD // 2, D), WIDE),
            shape((units // 2, D), WIDE),
            shape((8, piece), WIDE),
        ),
        in_specs=[smem] * 3 + [vmem] * 3 + [any_spec] * 11,
        out_specs=(vmem,) * 6,
        scratch_shapes=[pltpu.VMEM(array.shape, array.dtype) for array in large[:9]]
        + [
            pltpu.VMEM((4 * HD, D), NARROW),
            pltpu.VMEM((2 * depth,) + message, NARROW),
            pltpu.VMEM((2, 2 * depth) + message, NARROW),
            pltpu.VMEM((2, depth) + message, NARROW),
            pltpu.VMEM((2, depth + 1) + message, NARROW),
            pltpu.VMEM((2, depth + 1, max(ALONG), D), NARROW),
            pltpu.VMEM((spans, 3 * HD, span), NARROW),
            row_form,
            row_form,
            row_form,
            row_form,
            pltpu.VMEM((spans, span, HD), WIDE),
            pltpu.VMEM((spans, span, HD), WIDE),
            pltpu.VMEM((groups, count, 4 * HD, BLK), NARROW),
            pltpu.VMEM((groups, count, BLK, 4 * HD), NARROW),
            pltpu.VMEM((2, 2, rows, D), NARROW),
            pltpu.VMEM((4 * HD, D), WIDE),
            pltpu.VMEM((HD, D), WIDE),
            pltpu.VMEM((8, 4 * HD), WIDE),
            pltpu.VMEM((D, 128), WIDE),
            pltpu.VMEM((2, 2, count, piece, 256), NARROW),
            pltpu.VMEM((2, count, piece, 256), NARROW),
            pltpu.VMEM((2, count, piece, 256), NARROW),
            pltpu.VMEM((HD // 2, D), WIDE),
            pltpu.VMEM((units // 2, D), WIDE),
            pltpu.SemaphoreType.DMA((9,)),
            pltpu.SemaphoreType.DMA((2, 2 * depth)),
            pltpu.SemaphoreType.DMA((2, 2, depth)),
            pltpu.SemaphoreType.DMA((2, 2 * depth)),
            pltpu.SemaphoreType.DMA((2, 2, depth)),
            pltpu.SemaphoreType.DMA((2, 4, depth + 1)),
            pltpu.SemaphoreType.DMA((2, 4, depth)),
            pltpu.SemaphoreType.DMA((2,)),
            pltpu.SemaphoreType.DMA((2,)),
            pltpu.SemaphoreType.DMA((2, 2)),
            pltpu.SemaphoreType.DMA((4,)),
            pltpu.SemaphoreType.DMA((4,)),
            pltpu.SemaphoreType.DMA((2, count)),
            pltpu.SemaphoreType.DMA((2, count)),
        ],
        name="backward_and_reduce",
        compiler_params=pltpu.CompilerParams(
            collective_id=2, has_side_effects=True, vmem_limit_bytes=VMEM_LIMIT
        ),
    )(*scalars, *small, *large)


def last_kernel(
    tok_ref,
    cot_ref,
    sum_out,
    sum_back,
    inbox,
    wout_in,
    down_in,
    vec_in,
    out_ref,
    grad_ref,
    qkv_ref,
    wout_ref,
    up_ref,
    down_ref,
    vec_a,
    vec_b,
    vec_c,
    vec_d,
):
    tokens = tok_ref[...].astype(WIDE)
    out_ref[...] = (tokens + sum_out[...]).astype(NARROW)
    average = jnp.mean(tokens, axis=-1, keepdims=True)
    centred = tokens - average
    variance = jnp.mean(centred * centred, axis=-1, keepdims=True)
    rise = lax.rsqrt(variance + EPSILON)
    xhat = centred * rise
    g_xhat = sum_back[...]
    along = jnp.mean(g_xhat * xhat, axis=-1, keepdims=True)
    level = jnp.mean(g_xhat, axis=-1, keepdims=True)
    grad_ref[...] = cot_ref[...].astype(WIDE) + rise * (g_xhat - level - xhat * along)
    count = inbox.shape[1]
    units = up_ref.shape[1] // count
    for from_c in range(count):
        up_ref[:, from_c * units : (from_c + 1) * units] = inbox[0, from_c].astype(WIDE)
    for pair in range(count // 2):
        left = inbox[1, 2 * pair].astype(WIDE)
        right = inbox[1, 2 * pair + 1].astype(WIDE)
        for part in range(3):
            lanes = slice((part + 1) * HD, (part + 2) * HD)
            to = part * D + pair * 128
            qkv_ref[:, to : to + 128] = jnp.concatenate([left[:, lanes], right[:, lanes]], axis=1)
    wout_ref[...] = wout_in[...]
    down_ref[...] = down_in[...]
    for at, ref in enumerate((vec_a, vec_b, vec_c, vec_d)):
        ref[...] = vec_in[at]


def last_call(tok, cot, sum_out, sum_back, inbox, wout_in, down_in, vec_in):
    rows = tok.shape[0]
    _, count, piece, units = inbox.shape
    shape = jax.ShapeDtypeStruct
    steps = 2

    def cut(array_shape):
        return pl.BlockSpec((array_shape[0] // steps,) + array_shape[1:], lambda at: (at, 0))

    whole = pl.BlockSpec((8, piece), lambda at: (0, 0))
    vector = pl.BlockSpec((piece,), lambda at: (0,))
    letters = pl.BlockSpec((2, count, piece // steps, units), lambda at: (0, 0, at, 0))
    outs = (
        shape((rows, D), NARROW),
        shape((rows, D), WIDE),
        shape((piece, 3 * D), WIDE),
        shape(wout_in.shape, WIDE),
        shape((piece, count * units), WIDE),
        shape(down_in.shape, WIDE),
    )
    return pl.pallas_call(
        last_kernel,
        grid=(steps,),
        out_shape=outs + (shape((piece,), WIDE),) * 4,
        in_specs=[cut(array.shape) for array in (tok, cot, sum_out, sum_back)]
        + [letters, cut(wout_in.shape), cut(down_in.shape), whole],
        out_specs=tuple(cut(array.shape) for array in outs) + (vector,) * 4,
        name="last_rows",
        compiler_params=pltpu.CompilerParams(vmem_limit_bytes=VMEM_LIMIT),
    )(tok, cot, sum_out, sum_back, inbox, wout_in, down_in, vec_in)


def fast_shards(depth, *arguments):
    tokens, cotangent, lengths, dealing = arguments[:4]
    gains = arguments[4:8]
    rows = tokens.shape[0] * tokens.shape[1]
    tok = tokens.reshape(rows, D)
    cot = cotangent.reshape(rows, D)
    forward = gather_call(depth, lengths, dealing, tok, cot, gains, *arguments[8:])
    heads, units, xhat, cot_all, attended, total, g_up, g_down, g_sum = forward[:9]
    wqkv_t, wup_all, wdown_part, wout_part, prm_all, found = forward[9:]
    small = (total, prm_all, g_sum)
    large = (
        attended, wout_part, wdown_part, units, g_up, wup_all, wqkv_t, g_down, heads, xhat, cot_all
    )
    out, grad_tokens, qkv_part, out_part, up_part, down_part, *vectors = last_call(
        tok, cot, *reduce_call(depth, (lengths, dealing, found), small, large, rows)
    )
    return (
        out.reshape(tokens.shape),
        grad_tokens.reshape(tokens.shape),
        *vectors,
        qkv_part,
        out_part,
        up_part,
        down_part,
    )


def solution(mesh):
    placed = (
        P("wsh", "ctx", None),
        P("wsh", "ctx", None),
        P("wsh", None),
        P("wsh", None),
        P("wsh"),
        P("wsh"),
        P("wsh"),
        P("wsh"),
        P("wsh", None),
        P("wsh", None),
        P("wsh", None),
        P("wsh", None),
    )
    ctx_size = mesh.shape["ctx"]
    by_heads = ctx_size == H and mesh.shape["wsh"] == 2
    body = functools.partial(fast_shards, ctx_size // 4) if by_heads else shards
    return jax.shard_map(
        body,
        mesh=mesh,
        in_specs=placed,
        out_specs=(
            P("wsh", "ctx", None),
            P("wsh", "ctx", None),
            P(("ctx", "wsh")),
            P(("ctx", "wsh")),
            P(("ctx", "wsh")),
            P(("ctx", "wsh")),
            P(("ctx", "wsh"), None),
            P(("ctx", "wsh"), None),
            P(("ctx", "wsh"), None),
            P(("ctx", "wsh"), None),
        ),
        check_vma=False,
    )
```

```python
import functools

import jax
import jax.numpy as jnp
from jax import lax
from jax.experimental import pallas as pl
from jax.experimental.pallas import tpu as pltpu
from jax.sharding import PartitionSpec as P

D = 1024
H = 16
HD = 64
ROT = 16
BLK = 128


EPSILON = 1e-05
MASKED = -1e30
WIDE = jnp.float32
NARROW = jnp.bfloat16


def norm_layer(values_in, scale_by, shift_by):
    average = jnp.mean(values_in, axis=-1, keepdims=True)
    centred = values_in - average
    variance = jnp.mean(centred * centred, axis=-1, keepdims=True)
    return centred * lax.rsqrt(variance + EPSILON) * scale_by + shift_by


def rotate(values_in, places):
    split_at = ROT // 2
    frequency = 10000.0 ** (-2.0 * jnp.arange(split_at, dtype=WIDE) / ROT)
    angles = places.astype(WIDE)[:, None] * frequency[None, :]
    cosine_table = jnp.cos(angles)[:, None, :]
    sine_table = jnp.sin(angles)[:, None, :]
    first_half = values_in[..., :split_at]
    second_half = values_in[..., split_at:ROT]
    return jnp.concatenate(
        [
            first_half * cosine_table - second_half * sine_table,
            second_half * cosine_table + first_half * sine_table,
            values_in[..., ROT:],
        ],
        axis=-1,
    )


def natural_rows(dealing_row, offset_row, row_count):
    ordinal = offset_row + jnp.arange(row_count, dtype=jnp.int32)
    table_ids = jnp.arange(dealing_row.shape[0], dtype=jnp.int32)
    picked = jnp.sum(
        jnp.where((ordinal // BLK)[:, None] == table_ids[None, :], dealing_row[None, :], 0), axis=1
    )
    return picked * BLK + ordinal % BLK


def sequence_openings(natural, lengths_row):
    openings = jnp.cumsum(lengths_row) - lengths_row
    return jnp.max(jnp.where(openings[None, :] <= natural[:, None], openings[None, :], 0), axis=1)


def score_block(queries, block_keys, offset_row, natural_q, opening_q, dealing_row):
    row_count = block_keys.shape[0]
    key_natural = natural_rows(dealing_row, offset_row, row_count)
    scores = jnp.einsum(
        "qhd,khd->hqk", queries, block_keys.reshape(row_count, H, HD), preferred_element_type=WIDE
    ) * HD ** (-0.5)
    allowed = (key_natural[None, :] <= natural_q[:, None]) & (
        key_natural[None, :] >= opening_q[:, None]
    )
    return (scores, allowed[None])


def fold_blocks(step_fn, state_in, arrays):
    row_count = arrays[0].shape[0]
    block_width = 1024
    stacked = tuple(
        (
            member.reshape((row_count // block_width, block_width) + member.shape[1:])
            for member in arrays
        )
    )
    offsets = jnp.arange(row_count // block_width, dtype=jnp.int32) * block_width

    def inner_step(state_now, block_item):
        return (step_fn(state_now, block_item[0], block_item[1]), None)

    state_out, _ = lax.scan(inner_step, state_in, (stacked, offsets))
    return state_out


def project(tokens_f, weights, places):
    w_qkv, w_out, w_up, w_down, gain_one, bias_one, gain_two, bias_two = weights
    all_rows = tokens_f.shape[0]
    normed_one = norm_layer(tokens_f, gain_one.astype(WIDE), bias_one.astype(WIDE)).astype(NARROW)
    normed_two = norm_layer(tokens_f, gain_two.astype(WIDE), bias_two.astype(WIDE)).astype(NARROW)
    mixed = jnp.dot(normed_one, w_qkv, preferred_element_type=WIDE).reshape(all_rows, 3, H, HD)
    queries = rotate(mixed[:, 0], places).astype(NARROW)
    keys_here = rotate(mixed[:, 1], places).astype(NARROW).reshape(all_rows, D)
    values_here = mixed[:, 2].astype(NARROW).reshape(all_rows, D)
    hidden = jnp.dot(normed_two, w_up, preferred_element_type=WIDE)
    activated = jax.nn.gelu(hidden, approximate=False).astype(NARROW)
    return (normed_one, normed_two, queries, keys_here, values_here, hidden, activated)


def attend(queries, keys_here, values_here, natural_q, opening_q, dealing_row):
    local_rows = queries.shape[0]

    def max_step(state_in, block_arrays, offset_row):
        row_top, row_total = state_in
        scores, allowed = score_block(
            queries, block_arrays[0], offset_row, natural_q, opening_q, dealing_row
        )
        new_top = jnp.maximum(row_top, jnp.max(jnp.where(allowed, scores, MASKED), axis=-1))
        kept_terms = jnp.where(allowed, jnp.exp(scores - new_top[..., None]), 0.0)
        return (new_top, row_total * jnp.exp(row_top - new_top) + jnp.sum(kept_terms, axis=-1))

    start_state = (jnp.full((H, local_rows), MASKED, WIDE), jnp.zeros((H, local_rows), WIDE))
    row_top, row_total = fold_blocks(
        max_step, start_state, (lax.all_gather(keys_here, "ctx", axis=0, tiled=True),)
    )
    log_total = row_top + jnp.log(row_total)

    def value_step(state_in, block_arrays, offset_row):
        scores, allowed = score_block(
            queries, block_arrays[0], offset_row, natural_q, opening_q, dealing_row
        )
        soft_probs = jnp.where(allowed, jnp.exp(scores - log_total[..., None]), 0.0).astype(NARROW)
        row_count = block_arrays[1].shape[0]
        return state_in + jnp.einsum(
            "hqk,khd->qhd",
            soft_probs,
            block_arrays[1].reshape(row_count, H, HD),
            preferred_element_type=WIDE,
        )

    attended = fold_blocks(
        value_step,
        jnp.zeros((local_rows, H, HD), WIDE),
        (
            lax.all_gather(keys_here, "ctx", axis=0, tiled=True),
            lax.all_gather(values_here, "ctx", axis=0, tiled=True),
        ),
    )
    return (attended, log_total)


def attention_back(
    queries,
    keys_here,
    values_here,
    g_attended,
    row_dot,
    log_total,
    natural_q,
    opening_q,
    dealing_row,
):
    local_rows = queries.shape[0]
    scale_factor = HD ** (-0.5)
    gathered_keys, gathered_values = (
        lax.all_gather(keys_here, "ctx", axis=0, tiled=True),
        lax.all_gather(values_here, "ctx", axis=0, tiled=True),
    )
    group_rows = gathered_keys.shape[0]
    key_span = 1024

    def key_block(state_in, block_item):
        block_keys, block_values, offset_row = block_item
        scores, allowed = score_block(
            queries, block_keys, offset_row, natural_q, opening_q, dealing_row
        )
        soft_probs = jnp.where(allowed, jnp.exp(scores - log_total[..., None]), 0.0)
        g_probs = jnp.einsum(
            "qhd,khd->hqk",
            g_attended,
            block_values.reshape(key_span, H, HD),
            preferred_element_type=WIDE,
        )
        g_scores = (soft_probs * (g_probs - row_dot[..., None])).astype(NARROW)
        state_out = (
            state_in
            + jnp.einsum(
                "hqk,khd->qhd",
                g_scores,
                block_keys.reshape(key_span, H, HD),
                preferred_element_type=WIDE,
            )
            * scale_factor
        )
        key_terms = (
            jnp.einsum("hqk,qhd->khd", g_scores, queries, preferred_element_type=WIDE)
            * scale_factor
        )
        value_terms = jnp.einsum(
            "hqk,qhd->khd", soft_probs.astype(NARROW), g_attended, preferred_element_type=WIDE
        )
        return (
            state_out,
            jnp.concatenate(
                [key_terms.reshape(key_span, D), value_terms.reshape(key_span, D)], axis=1
            ),
        )

    block_total = group_rows // key_span
    block_starts = jnp.arange(block_total, dtype=jnp.int32) * key_span
    stacked_blocks = (
        gathered_keys.reshape(block_total, key_span, D),
        gathered_values.reshape(block_total, key_span, D),
        block_starts,
    )
    g_queries, stacked_terms = lax.scan(
        key_block, jnp.zeros((local_rows, H, HD), WIDE), stacked_blocks
    )
    g_pairs = lax.psum_scatter(
        stacked_terms.reshape(group_rows, 2 * D), "ctx", scatter_dimension=0, tiled=True
    )
    g_keys = g_pairs[:, :D].reshape(local_rows, H, HD)
    g_values = g_pairs[:, D:].reshape(local_rows, H, HD)
    return (g_queries, g_keys, g_values)


def shards(
    tokens,
    cotangent,
    lengths,
    dealing,
    gain_one,
    bias_one,
    gain_two,
    bias_two,
    w_qkv,
    w_out,
    w_up,
    w_down,
):
    group_count = tokens.shape[0]
    local_rows = tokens.shape[1]
    all_rows = group_count * local_rows
    tokens_f = tokens.reshape(all_rows, D).astype(WIDE)
    first_row = lax.axis_index("ctx") * local_rows
    natural_list = [
        natural_rows(dealing[member], first_row, local_rows) for member in range(group_count)
    ]
    opening_list = [
        sequence_openings(natural_list[member], lengths[member]) for member in range(group_count)
    ]
    places = jnp.concatenate(
        [natural_list[member] - opening_list[member] for member in range(group_count)], axis=0
    )

    def forward():
        weights = (
            lax.all_gather(w_qkv, "wsh", axis=0, tiled=True),
            lax.all_gather(w_out, "wsh", axis=0, tiled=True),
            lax.all_gather(w_up, "wsh", axis=0, tiled=True),
            lax.all_gather(w_down, "wsh", axis=0, tiled=True),
            lax.all_gather(gain_one, "wsh", axis=0, tiled=True),
            lax.all_gather(bias_one, "wsh", axis=0, tiled=True),
            lax.all_gather(gain_two, "wsh", axis=0, tiled=True),
            lax.all_gather(bias_two, "wsh", axis=0, tiled=True),
        )
        local_parts = project(tokens_f, weights, places)
        attended_list = []
        total_list = []
        for member in range(group_count):
            rows_from = member * local_rows
            attended_one, total_one = attend(
                local_parts[2][rows_from : rows_from + local_rows],
                local_parts[3][rows_from : rows_from + local_rows],
                local_parts[4][rows_from : rows_from + local_rows],
                natural_list[member],
                opening_list[member],
                dealing[member],
            )
            attended_list.append(attended_one)
            total_list.append(total_one)
        return (weights, local_parts, jnp.concatenate(attended_list, axis=0), total_list)

    weights, local_parts, attended, total_list = forward()
    attended_low = attended.reshape(all_rows, D).astype(NARROW)
    mixed_out = (
        tokens_f
        + jnp.dot(attended_low, weights[1], preferred_element_type=WIDE)
        + jnp.dot(local_parts[6], weights[3], preferred_element_type=WIDE)
    )
    out = mixed_out.astype(NARROW)
    weights, local_parts, attended, total_list = forward()
    attended_low = attended.reshape(all_rows, D).astype(NARROW)
    w_qkv_all, w_out_all, w_up_all, w_down_all = (weights[0], weights[1], weights[2], weights[3])
    normed_one, normed_two, queries, keys_here, values_here, hidden, activated = local_parts
    grad_rows = cotangent.reshape(all_rows, D)
    grad_f = grad_rows.astype(WIDE)
    g_down = jnp.einsum("tf,td->fd", activated, grad_rows, preferred_element_type=WIDE)
    g_activated = jnp.einsum("td,fd->tf", grad_rows, w_down_all, preferred_element_type=WIDE)
    _, gelu_back = jax.vjp(lambda pre_act: jax.nn.gelu(pre_act, approximate=False), hidden)
    g_hidden = gelu_back(g_activated)[0].astype(NARROW)
    g_up = jnp.einsum("td,tf->df", normed_two, g_hidden, preferred_element_type=WIDE)
    g_normed_two = jnp.einsum("tf,df->td", g_hidden, w_up_all, preferred_element_type=WIDE)
    g_weight_out = jnp.einsum("te,td->ed", attended_low, grad_rows, preferred_element_type=WIDE)
    g_attended = (
        jnp.einsum("td,ed->te", grad_rows, w_out_all, preferred_element_type=WIDE)
        .astype(NARROW)
        .reshape(all_rows, H, HD)
    )
    row_dot = jnp.einsum("qhd,qhd->hq", g_attended.astype(WIDE), attended)
    query_grads = []
    key_grads = []
    value_grads = []
    for member in range(group_count):
        rows_from = member * local_rows
        rows_to = rows_from + local_rows
        g_q, g_k, g_v = attention_back(
            queries[rows_from:rows_to],
            keys_here[rows_from:rows_to],
            values_here[rows_from:rows_to],
            g_attended[rows_from:rows_to],
            row_dot[:, rows_from:rows_to],
            total_list[member],
            natural_list[member],
            opening_list[member],
            dealing[member],
        )
        query_grads.append(g_q)
        key_grads.append(g_k)
        value_grads.append(g_v)
    g_queries = jnp.concatenate(query_grads, axis=0)
    g_keys = jnp.concatenate(key_grads, axis=0)
    g_values = jnp.concatenate(value_grads, axis=0)
    _, rotate_back = jax.vjp(
        lambda pre_rot: rotate(pre_rot, places), jnp.zeros((all_rows, H, HD), WIDE)
    )
    g_queries_pre = rotate_back(g_queries)[0]
    g_keys_pre = rotate_back(g_keys)[0]
    g_mixed = (
        jnp.stack([g_queries_pre, g_keys_pre, g_values], axis=1)
        .reshape(all_rows, 3 * D)
        .astype(NARROW)
    )
    g_qkv = jnp.einsum("td,te->de", normed_one, g_mixed, preferred_element_type=WIDE)
    g_normed_one = jnp.einsum("te,de->td", g_mixed, w_qkv_all, preferred_element_type=WIDE)

    def both_norms(tokens_in, scale_one, shift_one, scale_two, shift_two):
        return (
            norm_layer(tokens_in, scale_one, shift_one),
            norm_layer(tokens_in, scale_two, shift_two),
        )

    _, norm_back = jax.vjp(
        both_norms,
        tokens_f,
        weights[4].astype(WIDE),
        weights[5].astype(WIDE),
        weights[6].astype(WIDE),
        weights[7].astype(WIDE),
    )
    g_tokens, g_scale_one, g_shift_one, g_scale_two, g_shift_two = norm_back(
        (g_normed_one, g_normed_two)
    )
    grad_tokens = g_tokens + grad_f
    summed = (
        lax.psum_scatter(g_qkv, ("ctx", "wsh"), scatter_dimension=0, tiled=True),
        lax.psum_scatter(g_weight_out, ("ctx", "wsh"), scatter_dimension=0, tiled=True),
        lax.psum_scatter(g_up, ("ctx", "wsh"), scatter_dimension=0, tiled=True),
        lax.psum_scatter(g_down, ("ctx", "wsh"), scatter_dimension=0, tiled=True),
        lax.psum_scatter(g_scale_one, ("ctx", "wsh"), scatter_dimension=0, tiled=True),
        lax.psum_scatter(g_shift_one, ("ctx", "wsh"), scatter_dimension=0, tiled=True),
        lax.psum_scatter(g_scale_two, ("ctx", "wsh"), scatter_dimension=0, tiled=True),
        lax.psum_scatter(g_shift_two, ("ctx", "wsh"), scatter_dimension=0, tiled=True),
    )
    return (
        out.reshape(group_count, local_rows, D),
        grad_tokens.reshape(group_count, local_rows, D),
        summed[4],
        summed[5],
        summed[6],
        summed[7],
        summed[0],
        summed[1],
        summed[2],
        summed[3],
    )


MESH = pl.DeviceIdType.MESH
NT = (((1,), (1,)), ((), ()))
TN = (((0,), (0,)), ((), ()))
VMEM_LIMIT = 60 * 1024 * 1024


def dot(a, b, dims=(((1,), (0,)), ((), ()))):
    return lax.dot_general(a, b, dims, preferred_element_type=WIDE)


def pick(index, table):
    result = jnp.int32(table[0])
    for at in range(1, len(table)):
        result = jnp.where(index == at, jnp.int32(table[at]), result)
    return result


def near_first(depth):
    return [sorted(range(depth), key=lambda to, z=z: (abs(to - z), to)) for z in range(depth)]


def pick2(row, column, table):
    result = pick(column, table[0])
    for at in range(1, len(table)):
        result = jnp.where(row == at, pick(column, table[at]), result)
    return result


class Place:
    def __init__(self, depth):
        self.depth = depth
        self.c = lax.axis_index("ctx")
        self.x = lax.axis_index("wsh")
        self.core = lax.rem(self.c, 2)
        self.y = lax.rem(self.c // 2, 2)
        self.z = self.c // 4
        self.beside = (self.at(self.z, 1 - self.y, self.core), self.x)
        self.twin = (self.at(self.z, self.y, 1 - self.core), self.x)
        self.above = (self.at(self.z + 1, self.y, self.core), self.x)
        self.below = (self.at(self.z - 1, self.y, self.core), self.x)
        self.across = (self.c, 1 - self.x)
        self.has_above = self.z < depth - 1
        self.has_below = self.z > 0

    def at(self, z, y, core):
        return (z * 2 + y) * 2 + core

    def greet(self):
        barrier = pltpu.get_barrier_semaphore()

        def hail(device):
            pl.semaphore_signal(barrier, inc=1, device_id=device, device_id_type=MESH)

        hail(self.beside)
        hail(self.twin)
        hail(self.across)

        @pl.when(self.has_above)
        def _():
            hail(self.above)

        @pl.when(self.has_below)
        def _():
            hail(self.below)

        pl.semaphore_wait(
            barrier, 3 + self.has_above.astype(jnp.int32) + self.has_below.astype(jnp.int32)
        )


    def greet_all(self):
        barrier = pltpu.get_barrier_semaphore()
        count = 4 * self.depth
        pl.semaphore_signal(barrier, inc=1, device_id=self.across, device_id_type=MESH)

        def hail(offset, carry):
            device = (lax.rem(self.c + offset, count), self.x)
            pl.semaphore_signal(barrier, inc=1, device_id=device, device_id_type=MESH)
            return carry

        lax.fori_loop(1, count, hail, 0)
        pl.semaphore_wait(barrier, count)


FREQUENCY = tuple(10000.0 ** (-2.0 * i / ROT) for i in range(ROT // 2))


def turning(place):
    row = lax.broadcasted_iota(jnp.int32, (ROT // 2, 1), 0)
    frequency = jnp.full((ROT // 2, 1), FREQUENCY[0], WIDE)
    for at in range(1, ROT // 2):
        frequency = jnp.where(row == at, FREQUENCY[at], frequency)
    angles = place.astype(WIDE) * frequency
    return jnp.cos(angles), jnp.sin(angles)


ALONG = (16, 16)


def cut(rows, what, piece):
    rest = rows - ALONG[what]
    first = (rest // 2 + 15) // 16 * 16
    begin = (0, first, rest, rows)
    return pl.ds(begin[piece], begin[piece + 1] - begin[piece])


def starts_of(lengths_ref, group):
    starts = []
    so_far = jnp.int32(0)
    for piece in range(lengths_ref.shape[1] - 1):
        so_far = so_far + lengths_ref[group, piece]
        starts.append(so_far)
    return starts


def opening_of(natural, starts):
    opening = jnp.zeros(natural.shape, jnp.int32)
    for start in starts:
        opening = jnp.where(natural >= start, start, opening)
    return opening


def find_blocks(dealing_ref, found):
    groups, blocks = dealing_ref.shape
    for group in range(groups):

        def look(block, carry):
            where = jnp.int32(0)
            for at in range(blocks):
                where = jnp.where(dealing_ref[group, at] == block, jnp.int32(at), where)
            found[group, block] = where
            return carry

        lax.fori_loop(0, blocks, look, 0)


def gather_kernel(
    depth,
    lengths_ref,
    dealing_ref,
    tok_ref,
    cot_ref,
    gain_one_ref,
    bias_one_ref,
    gain_two_ref,
    bias_two_ref,
    wqkv_ref,
    wout_ref,
    wup_ref,
    wdown_ref,
    heads_out,
    units_out,
    xhat_out,
    cot_out,
    attended_out,
    total_out,
    g_up,
    g_down,
    g_sum,
    wqkv_t,
    wup_all,
    wdown_part,
    wout_part,
    prm_all,
    found,
    both,
    xhat_all,
    heads_buf,
    units_buf,
    slope_buf,
    wide,
    k_rows,
    wq_buf,
    prm_buf,
    in_sem,
    w_sem,
    wsend_sem,
    wrecv_sem,
    send_sem,
    recv_sem,
    out_sem,
):
    here = Place(depth)
    c, x, y, z, core = here.c, here.x, here.y, here.z, here.core
    count = depth * 4
    rows = tok_ref.shape[0]
    groups = dealing_ref.shape[0]
    units = wup_all.shape[1]
    half = prm_buf.shape[2]
    order = near_first(depth)

    own_in = (
        pltpu.make_async_copy(tok_ref, both.at[0, c], in_sem.at[0]),
        pltpu.make_async_copy(cot_ref, both.at[1, c], in_sem.at[1]),
    )
    for copy in own_in:
        copy.start()
    prm_rows = [
        ref[...].astype(WIDE).reshape(1, half) for ref in (gain_one_ref, bias_one_ref, gain_two_ref, bias_two_ref)
    ]
    prm_buf[x] = jnp.concatenate(prm_rows + prm_rows, axis=0)

    pair = c // 2
    per_half = count // 2
    owner = c // per_half
    inside = lax.rem(c, per_half)
    shared = []
    for part in range(3):
        shared.append(
            (
                wqkv_ref.at[:, pl.ds(pl.multiple_of(part * D + pair * 128, 128), 128)],
                wq_buf.at[x, part],
            )
        )
    shared.append(
        (
            wup_ref.at[:, pl.ds(pl.multiple_of(c * units, 128), units)],
            wup_all.at[pl.ds(pl.multiple_of(x * half, 128), half)],
        )
    )
    held = (
        (wdown_ref.at[pl.ds(pl.multiple_of(inside * units, 128), units)], wdown_part),
        (wout_ref.at[pl.ds(pl.multiple_of(inside * HD, HD), HD)], wout_part),
    )
    is_owner = owner == x
    for at, (source, place) in enumerate(shared):
        pltpu.make_async_copy(source, place, w_sem.at[at]).start()

    @pl.when(is_owner)
    def _():
        for at, (source, place) in enumerate(held):
            pltpu.make_async_copy(source, place, w_sem.at[5 + at]).start()

    here.greet()

    def remote(source, place, at):
        return pltpu.make_async_remote_copy(
            source,
            place,
            wsend_sem.at[at],
            wrecv_sem.at[at],
            device_id=here.across,
            device_id_type=MESH,
        )

    prm_copy = remote(prm_buf.at[x], prm_buf.at[x], 4)
    prm_copy.start()
    for at, (source, place) in enumerate(shared):
        remote(source, place, at).start()

    def passing(what, piece, shard, way):
        device = (here.beside, here.twin, here.above, here.below)[way]
        return pltpu.make_async_remote_copy(
            both.at[what, shard, cut(rows, what, piece)],
            both.at[what, shard, cut(rows, what, piece)],
            send_sem.at[what, piece, way, shard],
            recv_sem.at[what, piece, shard],
            device_id=device,
            device_id_type=MESH,
        )

    def onward(what, piece, shard, from_z, cross):
        if cross:
            passing(what, piece, shard, 0).start()

        @pl.when(jnp.logical_and(from_z <= z, here.has_above))
        def _():
            passing(what, piece, shard, 2).start()

        @pl.when(jnp.logical_and(from_z >= z, here.has_below))
        def _():
            passing(what, piece, shard, 3).start()

        passing(what, piece, shard, 1).start()

    def arrived(what, piece, shard):
        passing(what, piece, shard, 1).wait_recv()

    def relay(what, shard, from_z):
        for piece in range(3):
            arrived(what, piece, shard)
            onward(what, piece, shard, from_z, piece < 2)

    own_in[0].wait()
    for piece in range(3):
        onward(0, piece, c, z, True)
    own_in[1].wait()
    for piece in range(3):
        onward(1, piece, c, z, True)
    find_blocks(dealing_ref, found)

    for at, (source, place) in enumerate(shared):
        pltpu.make_async_copy(source, place, w_sem.at[at]).wait()
        remote(source, place, at).wait_recv()
    prm_copy.wait_recv()

    @pl.when(is_owner)
    def _():
        for at, (source, place) in enumerate(held):
            remote(source, place, 5 + at).start()

    odd = lax.rem(c, 2) == 1
    for side in range(2):
        prm_all[:, side * half : (side + 1) * half] = prm_buf[side]
        for part in range(3):
            turned = wq_buf[side, part].astype(WIDE).T
            chosen = jnp.where(odd, turned[HD:], turned[:HD])
            wqkv_t[part * HD : (part + 1) * HD, side * half : (side + 1) * half] = chosen.astype(
                NARROW
            )
    g_up[...] = jnp.zeros_like(g_up)
    g_down[...] = jnp.zeros_like(g_down)
    g_sum[...] = jnp.zeros_like(g_sum)

    kept = (
        (xhat_all, xhat_out),
        (both.at[1], cot_out),
        (heads_buf, heads_out),
        (units_buf, units_out),
    )

    def copy_out(at, shard):
        source, place = kept[at]
        return pltpu.make_async_copy(source.at[shard], place.at[shard], out_sem.at[at, shard])

    def ahead(shard):
        tokens = both[0, shard].astype(WIDE)
        average = jnp.mean(tokens, axis=-1, keepdims=True)
        centred = tokens - average
        variance = jnp.mean(centred * centred, axis=-1, keepdims=True)
        xhat = centred * lax.rsqrt(variance + EPSILON)
        xhat_all[shard] = xhat.astype(NARROW)
        n_one = (xhat * prm_all[0:1, :] + prm_all[1:2, :]).astype(NARROW)
        n_two = (xhat * prm_all[2:3, :] + prm_all[3:4, :]).astype(NARROW)
        mixed = dot(wqkv_t[...], n_one, NT)
        places = []
        for group in range(groups):
            natural = dealing_ref[group, shard] * BLK + lax.broadcasted_iota(jnp.int32, (1, BLK), 1)
            places.append(natural - opening_of(natural, starts_of(lengths_ref, group)))
        cosine, sine = turning(jnp.concatenate(places, axis=1))
        pieces = []
        for base in (0, HD):
            first, second = mixed[base : base + 8], mixed[base + 8 : base + 16]
            pieces += [
                first * cosine - second * sine,
                second * cosine + first * sine,
                mixed[base + 16 : base + HD],
            ]
        pieces.append(mixed[2 * HD : 3 * HD])
        heads_buf[shard, 0 : 3 * HD, :] = jnp.concatenate(pieces, axis=0).astype(NARROW)
        hidden = dot(n_two, wup_all[...])
        spread = 0.5 * (1.0 + lax.erf(hidden * (0.5**0.5)))
        units_buf[shard, :, 0:units] = (hidden * spread).astype(NARROW)
        slope_buf[shard] = spread + hidden * (jnp.exp(hidden * hidden * -0.5) * 0.3989422804014327)
        copy_out(0, shard).start()

    def behind(shard):
        cotangent = both[1, shard]
        heads_buf[shard, 3 * HD : 4 * HD, :] = dot(wout_part[...], cotangent, NT).astype(NARROW)
        g_hidden = (dot(cotangent, wdown_part[...], NT) * slope_buf[shard]).astype(NARROW)
        units_buf[shard, :, units : 2 * units] = g_hidden
        g_up[...] += dot(g_hidden, xhat_all[shard], TN)
        g_down[...] += dot(units_buf[shard, :, 0:units], cotangent, TN)
        g_sum[...] += jnp.sum(g_hidden.astype(WIDE).reshape(rows // 8, 8, units), axis=0)
        for at in (1, 2, 3):
            copy_out(at, shard).start()

    inner = jnp.logical_and(here.has_above, here.has_below)

    def sweep(what, work, beside_work, first=0):
        relays = what == 0

        def step(at, carry):
            turn_no = at // 4
            kind = lax.rem(at, 4)
            late = jnp.where(kind >= 2, turn_no - 1, turn_no)
            from_z = pick2(z, jnp.clip(late, 0, depth - 1), order)
            next_z = pick2(z, jnp.clip(turn_no + 1, 0, depth - 1), order)
            shard_y = jnp.where(kind >= 2, 1 - y, y)
            shard_core = jnp.where(lax.rem(kind, 2) == 1, 1 - core, core)
            shard = here.at(from_z, shard_y, shard_core)
            live = jnp.logical_and(late >= 0, late < depth)

            early = jnp.logical_and(inner, turn_no == 2)
            is_own = jnp.logical_and(kind == 0, turn_no == 0)
            done = jnp.logical_or(is_own, jnp.logical_and(kind == 0, early))

            @pl.when(jnp.logical_and(lax.rem(kind, 2) == 1, live))
            def _():
                for piece in range(3):
                    arrived(what, piece, shard)

            if relays:

                @pl.when(jnp.logical_and(jnp.logical_and(kind == 0, live), jnp.logical_not(done)))
                def _():
                    relay(what, shard, from_z)

            @pl.when(jnp.logical_and(kind == 2, live))
            def _():
                arrived(what, 2, shard)
                onward(what, 2, shard, from_z, False)
                for piece in range(2):
                    arrived(what, piece, shard)
                    passing(what, piece, shard, 1).start()

            if relays:

                @pl.when(jnp.logical_and(jnp.logical_and(kind == 1, turn_no == 1), inner))
                def _():
                    relay(what, here.at(next_z, y, core), next_z)

            beside_work(at)

            @pl.when(live)
            def _():
                work(shard)

            return carry

        lax.fori_loop(first, 4 * depth + 4, step, 0)

    def relay_next(at, wanted, index, which):
        @pl.when(jnp.logical_and(at == wanted, which))
        def _():
            from_z = pick2(z, jnp.int32(index), order)
            relay(1, here.at(from_z, y, core), from_z)

    outer = jnp.logical_not(inner)

    def late_weights():
        @pl.when(is_owner)
        def _():
            for at, (source, place) in enumerate(held):
                pltpu.make_async_copy(source, place, w_sem.at[5 + at]).wait()

        @pl.when(jnp.logical_not(is_owner))
        def _():
            for at, (source, place) in enumerate(held):
                remote(source, place, 5 + at).wait_recv()

    def cotangents_start(at):
        relay_next(at, 4 * depth, 1, at >= 0)
        relay_next(at, 4 * depth + 1, 2, inner)

        @pl.when(at == 4 * depth)
        def _():
            late_weights()
            behind(c)

        @pl.when(at == 4 * depth + 1)
        def _():
            twin = here.at(z, y, 1 - core)
            for piece in range(3):
                arrived(1, piece, twin)
            behind(twin)

    sweep(0, ahead, cotangents_start)

    spans = count // 2
    span = 2 * BLK

    def bring(at, carry):
        for group in range(groups):
            lanes = slice(group * BLK, (group + 1) * BLK)
            for side in range(2):
                source = found[group, 2 * at + side]
                part = heads_buf[source, 0 : 3 * HD, lanes]
                to = slice(side * BLK, (side + 1) * BLK)
                wide[group, at, 0:HD, to] = (part[0:HD].astype(WIDE) * HD ** (-0.5)).astype(NARROW)
                wide[group, at, HD : 2 * HD, to] = part[2 * HD : 3 * HD]
                k_rows[group, at, to, :] = part[HD : 2 * HD].astype(WIDE).T.astype(NARROW)
        return carry

    lax.fori_loop(0, spans, bring, 0)
    openings = [starts_of(lengths_ref, group) for group in range(groups)]

    def attend(at):
        group = lax.rem(at, groups)
        turn_no = at // groups
        mine = jnp.where(lax.rem(turn_no, 2) == 0, spans - 1 - turn_no // 2, turn_no // 2)
        natural = mine * span + lax.broadcasted_iota(jnp.int32, (1, span), 1)
        opening = opening_of(natural, [jnp.where(group == 0, *pair) for pair in zip(*openings)])
        queries = wide[group, mine, 0:HD, :]

        def add(first, width, state, diagonal):
            top, total, so_far = state
            keys = k_rows[group, pl.ds(first, width)].reshape(width * span, HD)
            place = lax.broadcasted_iota(jnp.int32, (width * span, span), 0)
            allowed = place >= opening - first * span
            if diagonal:
                allowed = jnp.logical_and(allowed, place <= natural - first * span)
            raw = jnp.where(allowed, dot(keys, queries), MASKED)
            new_top = jnp.maximum(top, jnp.max(raw, axis=0, keepdims=True))
            risen = jnp.exp(raw - new_top)
            fade = jnp.exp(top - new_top)
            total = total * fade + jnp.sum(risen, axis=0, keepdims=True)
            values = jnp.concatenate(
                [wide[group, first + side, HD : 2 * HD, :] for side in range(width)], axis=1
            )
            return new_top, total, so_far * fade + dot(values, risen.astype(NARROW))

        state = (
            jnp.full((1, span), MASKED, WIDE),
            jnp.zeros((1, span), WIDE),
            jnp.zeros((HD, span), WIDE),
        )
        last = mine // 2
        state = lax.cond(
            lax.rem(mine, 2) == 1,
            lambda state: add(mine - 1, 2, state, True),
            lambda state: add(mine, 1, state, True),
            state,
        )

        def earlier(back, state):
            return add(2 * (last - 1 - back), 2, state, False)

        top, total, so_far = lax.fori_loop(0, last, earlier, state)
        attended = so_far / total
        for side in range(2):
            attended_out[group, 2 * mine + side] = attended[:, side * BLK : (side + 1) * BLK]
        total_out[group, mine] = jnp.broadcast_to(top + jnp.log(total), (8, span))

    def attend_too(at):
        relay_next(at, 4, 2, outer)
        relay_next(at, 4, 3, inner)
        relay_next(at, 7, 3, outer)

        @pl.when(at < groups * spans + 4)
        def _():
            attend(at - 4)

    sweep(1, behind, attend_too, first=4)

    def finish(shard, carry):
        shard_z = shard // 4
        mine = lax.rem(shard, 2) == core
        column = lax.rem(shard // 2, 2) == y
        for what in range(2):

            @pl.when(mine)
            def _():
                for piece in range(3):
                    passing(what, piece, shard, 1).wait_send()

            for piece in range(3):
                along = mine if piece == 2 else jnp.logical_and(mine, column)

                @pl.when(jnp.logical_and(along, jnp.logical_and(shard_z <= z, here.has_above)))
                def _():
                    passing(what, piece, shard, 2).wait_send()

                @pl.when(jnp.logical_and(along, jnp.logical_and(shard_z >= z, here.has_below)))
                def _():
                    passing(what, piece, shard, 3).wait_send()

                crossed = shard == c if piece == 2 else jnp.logical_and(mine, column)

                @pl.when(crossed)
                def _():
                    passing(what, piece, shard, 0).wait_send()

        for at in range(4):
            copy_out(at, shard).wait()
        return carry

    lax.fori_loop(0, count, finish, 0)
    for at, (source, place) in enumerate(shared):
        remote(source, place, at).wait_send()
    prm_copy.wait_send()

    @pl.when(is_owner)
    def _():
        for at, (source, place) in enumerate(held):
            remote(source, place, 5 + at).wait_send()


def gather_call(depth, lengths, dealing, tok, cot, gains, w_qkv, w_out, w_up, w_down):
    count = depth * 4
    rows = tok.shape[0]
    groups = dealing.shape[0]
    spans, span = count // 2, 2 * BLK
    units = w_up.shape[1] // count
    any_spec = pl.BlockSpec(memory_space=pl.ANY)
    vmem = pl.BlockSpec(memory_space=pltpu.VMEM)
    smem = pl.BlockSpec(memory_space=pltpu.SMEM)
    shape = jax.ShapeDtypeStruct
    return pl.pallas_call(
        functools.partial(gather_kernel, depth),
        out_shape=(
            shape((count, 4 * HD, rows), NARROW),
            shape((count, rows, 2 * units), NARROW),
            shape((count, rows, D), NARROW),
            shape((count, rows, D), NARROW),
            shape((groups, count, HD, BLK), WIDE),
            shape((groups, spans, 8, span), WIDE),
            shape((units, D), WIDE),
            shape((units, D), WIDE),
            shape((8, units), WIDE),
            shape((3 * HD, D), NARROW),
            shape((D, units), NARROW),
            shape((units, D), NARROW),
            shape((HD, D), NARROW),
            shape((8, D), WIDE),
            shape((groups, count), jnp.int32),
        ),
        in_specs=[smem, smem, any_spec, any_spec] + [vmem] * 4 + [any_spec] * 4,
        out_specs=(any_spec,) * 4 + (vmem,) * 10 + (smem,),
        scratch_shapes=[
            pltpu.VMEM((2, count, rows, D), NARROW),
            pltpu.VMEM((count, rows, D), NARROW),
            pltpu.VMEM((count, 4 * HD, rows), NARROW),
            pltpu.VMEM((count, rows, 2 * units), NARROW),
            pltpu.VMEM((count, rows, units), WIDE),
            pltpu.VMEM((groups, spans, 2 * HD, span), NARROW),
            pltpu.VMEM((groups, spans, span, HD), NARROW),
            pltpu.VMEM((2, 3, D // 2, 128), NARROW),
            pltpu.VMEM((2, 8, D // 2), WIDE),
            pltpu.SemaphoreType.DMA((2,)),
            pltpu.SemaphoreType.DMA((7,)),
            pltpu.SemaphoreType.DMA((7,)),
            pltpu.SemaphoreType.DMA((7,)),
            pltpu.SemaphoreType.DMA((2, 3, 4, count)),
            pltpu.SemaphoreType.DMA((2, 3, count)),
            pltpu.SemaphoreType.DMA((4, count)),
        ],
        name="gather_and_forward",
        compiler_params=pltpu.CompilerParams(
            collective_id=1, has_side_effects=True, vmem_limit_bytes=VMEM_LIMIT
        ),
    )(lengths, dealing, tok, cot, *gains, w_qkv, w_out, w_up, w_down)


def far_first(depth):
    return [list(reversed(row)) for row in near_first(depth)]


def unturn(rows, cosine, sine):
    first, second = rows[0:8], rows[8:16]
    return jnp.concatenate(
        [first * cosine + second * sine, second * cosine - first * sine, rows[16:]], axis=0
    )


def reduce_kernel(
    depth,
    lengths_ref,
    dealing_ref,
    found,
    total_in,
    prm_all,
    g_sum,
    attended_hbm,
    wout_hbm,
    wdown_hbm,
    units_hbm,
    g_up_hbm,
    wup_hbm,
    wqkv_hbm,
    g_down_hbm,
    heads_hbm,
    xhat_in,
    cot_in,
    sum_out,
    sum_back,
    inbox,
    wout_ref,
    down_ref,
    vec_ref,
    attended_in,
    wout_part,
    wdown_part,
    units_in,
    g_up,
    wup_all,
    wqkv_t,
    g_down,
    heads_in,
    w_heads_back,
    give_buf,
    sum_buf,
    beside_buf,
    line_buf,
    other_line,
    wide,
    q_rows,
    k_rows,
    v_rows,
    g_rows,
    g_key,
    g_value,
    turned_all,
    by_token,
    stream,
    g_heads,
    g_wout,
    sum_heads,
    vectors,
    grads,
    grads_in,
    mail,
    wout_in,
    down_in,
    first_sem,
    send_twin,
    send_beside,
    recv_twin,
    recv_beside,
    recv_z,
    send_z,
    send_last,
    recv_last,
    stream_sem,
    across_send,
    across_recv,
    mail_send,
    mail_recv,
):
    here = Place(depth)
    c, x, y, z, core = here.c, here.x, here.y, here.z, here.core
    rows = sum_out.shape[0]
    units = wup_all.shape[1]
    groups = dealing_ref.shape[0]
    count = 4 * depth
    brought = [
        pltpu.make_async_copy(source, place, first_sem.at[at])
        for at, (source, place) in enumerate(
            (
                (attended_hbm, attended_in),
                (wout_hbm, wout_part),
                (wdown_hbm, wdown_part),
                (units_hbm, units_in),
                (g_up_hbm, g_up),
                (wup_hbm, wup_all),
                (wqkv_hbm, wqkv_t),
                (g_down_hbm, g_down),
                (heads_hbm, heads_in),
            )
        )
    ]
    for copy in brought:
        copy.start()
    spans, span = count // 2, 2 * BLK
    scale = HD ** (-0.5)
    piece = D // (2 * count)
    order = far_first(depth)

    def shard_of(at):
        kind = lax.rem(at, 4)
        to_y = jnp.where(lax.rem(kind, 2) == 1, y, 1 - y)
        to_core = jnp.where(kind < 2, 1 - core, core)
        return here.at(pick2(z, at // 4, order), to_y, to_core)

    def load(at):
        shard, slot = shard_of(at), lax.rem(at, 2)
        return (
            pltpu.make_async_copy(xhat_in.at[shard], stream.at[0, slot], stream_sem.at[0, slot]),
            pltpu.make_async_copy(cot_in.at[shard], stream.at[1, slot], stream_sem.at[1, slot]),
        )

    here.greet_all()

    def crossing(source, place, at):
        return pltpu.make_async_remote_copy(
            source,
            place,
            across_send.at[at],
            across_recv.at[at],
            device_id=here.across,
            device_id_type=MESH,
        )

    half_down = g_down.shape[0] // 2
    half_wout = HD // 2
    send_down = crossing(g_down.at[pl.ds((1 - x) * half_down, half_down)], down_in, 0)
    send_wout = crossing(g_wout.at[pl.ds((1 - x) * half_wout, half_wout)], wout_in, 1)
    send_grads = [crossing(grads.at[part, 1 - x], grads_in.at[part], 2 + part) for part in range(2)]

    def to_twin(what, slot):
        return pltpu.make_async_remote_copy(
            give_buf.at[slot],
            sum_buf.at[what, slot],
            send_twin.at[what, slot],
            recv_twin.at[what, slot],
            device_id=here.twin,
            device_id_type=MESH,
        )

    def to_beside(what, piece, to_z):
        return pltpu.make_async_remote_copy(
            sum_buf.at[what, to_z, cut(rows, what, piece)],
            beside_buf.at[what, to_z, cut(rows, what, piece)],
            send_beside.at[what, piece, to_z],
            recv_beside.at[what, piece, to_z],
            device_id=here.beside,
            device_id_type=MESH,
        )

    def over_slot(to_z, at_z):
        return jnp.where(to_z == at_z, depth, to_z)

    def along(what, piece, home, to_z, place, device):
        here_rows = cut(rows, what, piece)
        if piece == 2:
            target = other_line.at[what, place, pl.ds(0, ALONG[what])]
            if home == 1:
                target = line_buf.at[what, place, here_rows]
        else:
            target = line_buf.at[what, place, here_rows]
        lane = piece + (home if piece == 2 else 0)
        return pltpu.make_async_remote_copy(
            sum_buf.at[what, home * depth + to_z, here_rows],
            target,
            send_z.at[what, lane, to_z],
            recv_z.at[what, lane, place],
            device_id=device,
            device_id_type=MESH,
        )

    def to_above(what, piece, home, to_z):
        return along(what, piece, home, to_z, to_z, here.above)

    def to_below(what, piece, home, to_z):
        return along(what, piece, home, to_z, over_slot(to_z, z - 1), here.below)

    def from_above(what, piece, home, to_z):
        return along(what, piece, home, to_z, over_slot(to_z, z), here.above)

    def cross_last(what):
        here_rows = cut(rows, what, 2)
        return pltpu.make_async_remote_copy(
            sum_buf.at[what, z, here_rows],
            beside_buf.at[what, z, here_rows],
            send_last.at[what],
            recv_last.at[what],
            device_id=here.beside,
            device_id_type=MESH,
        )

    def pass_on(what, at, part):
        to_z = pick2(z, at // 4, order)
        kind = lax.rem(at, 4)
        slot = lax.rem(kind, 2) * depth + to_z

        @pl.when(kind < 2)
        def _():
            if what == 1:
                to_twin(0, slot).wait_send()
            give_buf[slot] = part.astype(NARROW)
            to_twin(what, slot).start()

        @pl.when(kind >= 2)
        def _():
            to_twin(what, slot).wait_recv()
            sum_buf[what, slot] = (part + sum_buf[what, slot].astype(WIDE)).astype(NARROW)

        @pl.when(kind == 2)
        def _():
            for piece in range(2):
                to_beside(what, piece, to_z).start()

    def chain_piece(what, at, piece, home):
        to_z = pick2(z, at, order)
        slot = home * depth + to_z
        here_rows = cut(rows, what, piece)
        if piece < 2:
            to_beside(what, piece, to_z).wait_recv()

        def add(incoming):
            total = sum_buf[what, slot, here_rows, :].astype(WIDE)
            if piece < 2:
                total = total + beside_buf[what, to_z, here_rows, :].astype(WIDE)
            if incoming:
                if piece == 2 and home == 0:
                    came = other_line[what, to_z, 0 : ALONG[what], :]
                else:
                    came = line_buf[what, to_z, here_rows, :]
                total = total + came.astype(WIDE)
            sum_buf[what, slot, here_rows, :] = total.astype(NARROW)

        @pl.when(to_z > z)
        def _():
            @pl.when(here.has_below)
            def _():
                to_above(what, piece, home, to_z).wait_recv()
                add(True)

            if piece < 2:

                @pl.when(jnp.logical_not(here.has_below))
                def _():
                    add(False)

            to_above(what, piece, home, to_z).start()

        @pl.when(to_z < z)
        def _():
            @pl.when(here.has_above)
            def _():
                from_above(what, piece, home, to_z).wait_recv()
                add(True)

            if piece < 2:

                @pl.when(jnp.logical_not(here.has_above))
                def _():
                    add(False)

            to_below(what, piece, home, to_z).start()

    def chain(what, at):
        for home in range(2):
            chain_piece(what, at, 2, home)
        for piece in range(2):
            chain_piece(what, at, piece, 1)

    def cross_over(what):
        here_rows = cut(rows, what, 2)
        came = slice(0, ALONG[what])

        @pl.when(here.has_below)
        def _():
            to_above(what, 2, 0, z).wait_recv()
            total = sum_buf[what, z, here_rows, :].astype(WIDE)
            total = total + other_line[what, z, came, :].astype(WIDE)
            sum_buf[what, z, here_rows, :] = total.astype(NARROW)

        @pl.when(here.has_above)
        def _():
            from_above(what, 2, 0, z).wait_recv()
            total = sum_buf[what, z, here_rows, :].astype(WIDE)
            total = total + other_line[what, depth, came, :].astype(WIDE)
            sum_buf[what, z, here_rows, :] = total.astype(NARROW)

        cross_last(what).start()

    def gather_total(what):
        for piece in range(2):
            to_beside(what, piece, z).wait_recv()
        cross_last(what).wait_recv()

        @pl.when(here.has_below)
        def _():
            for piece in range(3):
                to_above(what, piece, 1, z).wait_recv()

        @pl.when(jnp.logical_not(here.has_below))
        def _():
            line_buf[what, z] = jnp.zeros((rows, D), NARROW)

        @pl.when(here.has_above)
        def _():
            for piece in range(3):
                from_above(what, piece, 1, z).wait_recv()

        @pl.when(jnp.logical_not(here.has_above))
        def _():
            line_buf[what, depth] = jnp.zeros((rows, D), NARROW)

        return (
            sum_buf[what, depth + z].astype(WIDE)
            + beside_buf[what, z].astype(WIDE)
            + line_buf[what, z].astype(WIDE)
            + line_buf[what, depth].astype(WIDE)
        )

    def give_out(at, carry):
        shard = shard_of(at)
        parts = []
        for group in range(groups):
            attended = attended_in[group, dealing_ref[group, shard]].astype(NARROW)
            parts.append(dot(attended, wout_part[...], TN))
        part = jnp.concatenate(parts, axis=0) + dot(units_in[shard, :, 0:units], wdown_part[...])
        pass_on(0, at, part)
        return carry

    for copy in brought[:4]:
        copy.wait()
    lax.fori_loop(0, count, give_out, 0)
    for copy in brought[4:]:
        copy.wait()
    send_down.start()

    def settle(chunk, part, raw, weights, sums, column):
        scaled = raw * column[:, 2 - 2 * part : 3 - 2 * part] + sums * column[:, 3 - 2 * part : 4 - 2 * part]
        gain_sum = jnp.sum(weights * raw, axis=1, keepdims=True)
        bias_sum = jnp.sum(weights * sums, axis=1, keepdims=True)
        row = pl.ds(pl.multiple_of(chunk * 128, 128), 128)
        if part == 0:
            vectors[row, 0:1] = gain_sum
            vectors[row, 1:2] = bias_sum
        else:
            lane = lax.broadcasted_iota(jnp.int32, scaled.shape, 1)
            scaled = jnp.where(lane == 0, gain_sum, scaled)
            scaled = jnp.where(lane == 1, bias_sum, scaled)
            scaled = jnp.where(lane == 2, vectors[row, 0:1], scaled)
            scaled = jnp.where(lane == 3, vectors[row, 1:2], scaled)
        per = 128 // piece
        for at in range(per):
            grads[part, at % 2, chunk * (per // 2) + at // 2] = scaled[at * piece : (at + 1) * piece].astype(NARROW)

    sum_units = jnp.sum(g_sum[...], axis=0, keepdims=True)

    def settle_up(chunk, carry):
        lanes = pl.ds(pl.multiple_of(chunk * 128, 128), 128)
        weights = wup_all[lanes, :].astype(WIDE)
        settle(chunk, 0, g_up[:, lanes].T, weights, sum_units, prm_all[:, lanes].T)
        return carry

    lax.fori_loop(0, D // 128, settle_up, 0)
    send_grads[0].start()
    w_heads_back[0:HD, :] = jnp.zeros((HD, D), NARROW)
    w_heads_back[HD:, :] = wqkv_t[...]
    g_heads[...] = jnp.zeros_like(g_heads)
    g_wout[...] = jnp.zeros_like(g_wout)
    sum_heads[...] = jnp.zeros_like(sum_heads)

    for group in range(groups):
        lanes = slice(group * BLK, (group + 1) * BLK)
        starts = starts_of(lengths_ref, group)

        def bring(at, carry, group=group, lanes=lanes):
            for side in range(2):
                source = found[group, 2 * at + side]
                part = heads_in[source, :, lanes]
                to = slice(side * BLK, (side + 1) * BLK)
                queries = part[0:HD].astype(WIDE) * scale
                keys = part[HD : 2 * HD]
                grads_part = part[3 * HD : 4 * HD]
                wide[at, 0:HD, to] = queries.astype(NARROW)
                wide[at, HD : 2 * HD, to] = keys
                wide[at, 2 * HD : 3 * HD, to] = grads_part
                q_rows[at, to, :] = queries.T.astype(NARROW)
                k_rows[at, to, :] = keys.astype(WIDE).T.astype(NARROW)
                v_rows[at, to, :] = part[2 * HD : 3 * HD].astype(WIDE).T.astype(NARROW)
                g_rows[at, to, :] = grads_part.astype(WIDE).T.astype(NARROW)
            g_key[at] = jnp.zeros((span, HD), WIDE)
            g_value[at] = jnp.zeros((span, HD), WIDE)
            return carry

        lax.fori_loop(0, spans, bring, 0)
        chain(0, 2 * group)

        def one_span(at, carry, group=group, starts=starts):
            natural = at * span + lax.broadcasted_iota(jnp.int32, (1, span), 1)
            opening = opening_of(natural, starts)
            queries = wide[at, 0:HD, :]
            g_attended = wide[at, 2 * HD : 3 * HD, :]
            attended = jnp.concatenate(
                [attended_in[group, 2 * at], attended_in[group, 2 * at + 1]], axis=1
            )
            row_dot = jnp.sum(attended * g_attended.astype(WIDE), axis=0, keepdims=True)
            log_total = total_in[group, at, 0:1, :]

            def add(first, width, so_far, diagonal):
                some = pl.ds(first, width)
                keys = k_rows[some].reshape(width * span, HD)
                values = v_rows[some].reshape(width * span, HD)
                place = lax.broadcasted_iota(jnp.int32, (width * span, span), 0)
                allowed = place >= opening - first * span
                if diagonal:
                    allowed = jnp.logical_and(allowed, place <= natural - first * span)
                scores = dot(keys, queries)
                probs = jnp.where(allowed, jnp.exp(scores - log_total), 0.0)
                g_scores = (probs * (dot(values, g_attended) - row_dot)).astype(NARROW)
                g_key[some] += dot(g_scores, q_rows[at]).reshape(width, span, HD)
                g_value[some] += dot(probs.astype(NARROW), g_rows[at]).reshape(width, span, HD)
                keys_t = jnp.concatenate(
                    [wide[first + side, HD : 2 * HD, :] for side in range(width)], axis=1
                )
                return so_far + dot(keys_t, g_scores)

            def earlier(pair, so_far):
                return add(2 * pair, 2, so_far, False)

            so_far = lax.fori_loop(0, at // 2, earlier, jnp.zeros((HD, span), WIDE))
            so_far = lax.cond(
                lax.rem(at, 2) == 1,
                lambda so_far: add(at - 1, 2, so_far, True),
                lambda so_far: add(at, 1, so_far, True),
                so_far,
            )
            cosine, sine = turning(natural - opening)
            turned = jnp.concatenate([attended, unturn(so_far * scale, cosine, sine)], axis=0)
            for side in range(2):
                part = turned[:, side * BLK : (side + 1) * BLK]
                turned_all[group, 2 * at + side, 0 : 2 * HD, :] = part.astype(NARROW)
            return carry

        lax.fori_loop(0, spans, one_span, 0)
        if group == 0:
            chain(0, 1)
        else:
            cross_over(0)

        def give(at, carry, group=group, starts=starts):
            natural = at * span + lax.broadcasted_iota(jnp.int32, (1, span), 1)
            cosine, sine = turning(natural - opening_of(natural, starts))
            keys = unturn(g_key[at].T, cosine, sine)
            turned = jnp.concatenate([keys, g_value[at].T], axis=0)
            for side in range(2):
                part = turned[:, side * BLK : (side + 1) * BLK]
                turned_all[group, 2 * at + side, 2 * HD : 4 * HD, :] = part.astype(NARROW)
                whole = turned_all[group, 2 * at + side].astype(WIDE)
                by_token[group, 2 * at + side] = whole.T.astype(NARROW)
            return carry

        lax.fori_loop(0, spans, give, 0)

    for copy in load(0):
        copy.start()

    def tokens_of(shard):
        blocks = [by_token[group, dealing_ref[group, shard]] for group in range(groups)]
        return jnp.concatenate(blocks, axis=0)

    def give_back(at, carry):
        shard = shard_of(at)
        g_hidden = units_in[shard, :, units : 2 * units]
        part = dot(tokens_of(shard), w_heads_back[...]) * prm_all[0:1, :] + dot(
            g_hidden, wup_all[...], NT
        ) * prm_all[2:3, :]
        pass_on(1, at, part)
        return carry

    lax.fori_loop(0, count, give_back, 0)

    def post(part, to_c):
        return pltpu.make_async_remote_copy(
            mail.at[part, to_c],
            inbox.at[part, c],
            mail_send.at[part, to_c],
            mail_recv.at[part, c],
            device_id=(to_c, x),
            device_id_type=MESH,
        )

    def collect(part, from_c):
        return pltpu.make_async_remote_copy(
            mail.at[part, from_c],
            inbox.at[part, from_c],
            mail_send.at[part, from_c],
            mail_recv.at[part, from_c],
            device_id=(from_c, x),
            device_id_type=MESH,
        )

    def mail_out(part):
        send_grads[part].wait_recv()

        def fold(to_c, carry):
            mail[part, to_c] = (
                grads[part, x, to_c].astype(WIDE) + grads_in[part, to_c].astype(WIDE)
            ).astype(NARROW)
            return carry

        lax.fori_loop(0, count, fold, 0)

        def start(offset, carry):
            post(part, lax.rem(c + offset, count)).start()
            return carry

        lax.fori_loop(1, count, start, 0)
        inbox[part, c] = mail[part, c]

    mail_out(0)

    def weigh(at, carry):
        shard, slot = shard_of(at), lax.rem(at, 2)

        @pl.when(at + 1 < count)
        def _():
            for copy in load(at + 1):
                copy.start()

        for copy in load(at):
            copy.wait()
        turned = jnp.concatenate(
            [turned_all[group, dealing_ref[group, shard]] for group in range(groups)], axis=1
        )
        g_wout[...] += dot(turned[0:HD], stream[1, slot])
        g_heads[HD:, :] += dot(turned[HD:], stream[0, slot])
        sum_heads[...] += jnp.sum(
            tokens_of(shard).astype(WIDE).reshape(rows // 8, 8, 4 * HD), axis=0
        )
        return carry

    inner = jnp.logical_and(here.has_above, here.has_below)
    outer = jnp.logical_not(inner)
    early, middle = count // 4, count * 5 // 8
    lax.fori_loop(0, early, weigh, 0)

    @pl.when(outer)
    def _():
        chain(1, 0)

    lax.fori_loop(early, middle, weigh, 0)

    @pl.when(outer)
    def _():
        chain(1, 1)

    @pl.when(inner)
    def _():
        chain(1, 0)

    lax.fori_loop(middle, count, weigh, 0)
    send_wout.start()
    sum_row = jnp.sum(sum_heads[...], axis=0, keepdims=True)

    def settle_qkv(chunk, carry):
        lanes = pl.ds(pl.multiple_of(chunk * 128, 128), 128)
        weights = w_heads_back[:, lanes].astype(WIDE).T
        settle(chunk, 1, g_heads[:, lanes].T, weights, sum_row, prm_all[:, lanes].T)
        return carry

    lax.fori_loop(0, D // 128, settle_qkv, 0)
    send_grads[1].start()

    @pl.when(inner)
    def _():
        chain(1, 1)

    for at in range(2, depth - 1):
        chain(1, at)
    cross_over(1)
    mail_out(1)


    sum_out[...] = gather_total(0)
    send_down.wait()
    down_ref[...] = g_down[pl.ds(x * half_down, half_down), :] + down_in[...]
    send_wout.wait()
    wout_ref[...] = g_wout[pl.ds(x * half_wout, half_wout), :] + wout_in[...]

    def close(offset, carry):
        other = lax.rem(c + offset, count)
        for part in range(2):
            collect(part, other).wait_recv()
            post(part, other).wait_send()
        return carry

    lax.fori_loop(1, count, close, 0)
    for part in range(2):
        send_grads[part].wait_send()
    together = jnp.zeros((piece, 128), WIDE)
    for from_c in range(count):
        together = together + inbox[1, from_c, :, 0:128].astype(WIDE)
    vec_ref[...] = together.T[0:8]
    sum_back[...] = gather_total(1)

    def finish(to_z, carry):
        to_twin(1, to_z).wait_send()
        to_twin(1, depth + to_z).wait_send()
        for what in range(2):
            for piece in range(2):
                to_beside(what, piece, to_z).wait_send()

            @pl.when(to_z > z)
            def _():
                to_above(what, 2, 0, to_z).wait_send()
                for piece in range(3):
                    to_above(what, piece, 1, to_z).wait_send()

            @pl.when(to_z < z)
            def _():
                to_below(what, 2, 0, to_z).wait_send()
                for piece in range(3):
                    to_below(what, piece, 1, to_z).wait_send()

        return carry

    lax.fori_loop(0, depth, finish, 0)
    for what in range(2):
        cross_last(what).wait_send()


def reduce_call(depth, scalars, small, large, rows):
    count = depth * 4
    groups = scalars[1].shape[0]
    spans, span = count // 2, 2 * BLK
    piece = D // (2 * count)
    units = large[5].shape[1]
    vmem = pl.BlockSpec(memory_space=pltpu.VMEM)
    smem = pl.BlockSpec(memory_space=pltpu.SMEM)
    any_spec = pl.BlockSpec(memory_space=pl.ANY)
    shape = jax.ShapeDtypeStruct
    message = (rows, D)
    row_form = pltpu.VMEM((spans, span, HD), NARROW)
    return pl.pallas_call(
        functools.partial(reduce_kernel, depth),
        out_shape=(
            shape((rows, D), WIDE),
            shape((rows, D), WIDE),
            shape((2, count, piece, 256), NARROW),
            shape((HD // 2, D), WIDE),
            shape((units // 2, D), WIDE),
            shape((8, piece), WIDE),
        ),
        in_specs=[smem] * 3 + [vmem] * 3 + [any_spec] * 11,
        out_specs=(vmem,) * 6,
        scratch_shapes=[pltpu.VMEM(array.shape, array.dtype) for array in large[:9]]
        + [
            pltpu.VMEM((4 * HD, D), NARROW),
            pltpu.VMEM((2 * depth,) + message, NARROW),
            pltpu.VMEM((2, 2 * depth) + message, NARROW),
            pltpu.VMEM((2, depth) + message, NARROW),
            pltpu.VMEM((2, depth + 1) + message, NARROW),
            pltpu.VMEM((2, depth + 1, max(ALONG), D), NARROW),
            pltpu.VMEM((spans, 3 * HD, span), NARROW),
            row_form,
            row_form,
            row_form,
            row_form,
            pltpu.VMEM((spans, span, HD), WIDE),
            pltpu.VMEM((spans, span, HD), WIDE),
            pltpu.VMEM((groups, count, 4 * HD, BLK), NARROW),
            pltpu.VMEM((groups, count, BLK, 4 * HD), NARROW),
            pltpu.VMEM((2, 2, rows, D), NARROW),
            pltpu.VMEM((4 * HD, D), WIDE),
            pltpu.VMEM((HD, D), WIDE),
            pltpu.VMEM((8, 4 * HD), WIDE),
            pltpu.VMEM((D, 128), WIDE),
            pltpu.VMEM((2, 2, count, piece, 256), NARROW),
            pltpu.VMEM((2, count, piece, 256), NARROW),
            pltpu.VMEM((2, count, piece, 256), NARROW),
            pltpu.VMEM((HD // 2, D), WIDE),
            pltpu.VMEM((units // 2, D), WIDE),
            pltpu.SemaphoreType.DMA((9,)),
            pltpu.SemaphoreType.DMA((2, 2 * depth)),
            pltpu.SemaphoreType.DMA((2, 2, depth)),
            pltpu.SemaphoreType.DMA((2, 2 * depth)),
            pltpu.SemaphoreType.DMA((2, 2, depth)),
            pltpu.SemaphoreType.DMA((2, 4, depth + 1)),
            pltpu.SemaphoreType.DMA((2, 4, depth)),
            pltpu.SemaphoreType.DMA((2,)),
            pltpu.SemaphoreType.DMA((2,)),
            pltpu.SemaphoreType.DMA((2, 2)),
            pltpu.SemaphoreType.DMA((4,)),
            pltpu.SemaphoreType.DMA((4,)),
            pltpu.SemaphoreType.DMA((2, count)),
            pltpu.SemaphoreType.DMA((2, count)),
        ],
        name="backward_and_reduce",
        compiler_params=pltpu.CompilerParams(
            collective_id=2, has_side_effects=True, vmem_limit_bytes=VMEM_LIMIT
        ),
    )(*scalars, *small, *large)


def last_kernel(
    tok_ref,
    cot_ref,
    sum_out,
    sum_back,
    inbox,
    wout_in,
    down_in,
    vec_in,
    out_ref,
    grad_ref,
    qkv_ref,
    wout_ref,
    up_ref,
    down_ref,
    vec_a,
    vec_b,
    vec_c,
    vec_d,
):
    tokens = tok_ref[...].astype(WIDE)
    out_ref[...] = (tokens + sum_out[...]).astype(NARROW)
    average = jnp.mean(tokens, axis=-1, keepdims=True)
    centred = tokens - average
    variance = jnp.mean(centred * centred, axis=-1, keepdims=True)
    rise = lax.rsqrt(variance + EPSILON)
    xhat = centred * rise
    g_xhat = sum_back[...]
    along = jnp.mean(g_xhat * xhat, axis=-1, keepdims=True)
    level = jnp.mean(g_xhat, axis=-1, keepdims=True)
    grad_ref[...] = cot_ref[...].astype(WIDE) + rise * (g_xhat - level - xhat * along)
    count = inbox.shape[1]
    units = up_ref.shape[1] // count
    for from_c in range(count):
        up_ref[:, from_c * units : (from_c + 1) * units] = inbox[0, from_c].astype(WIDE)
    for pair in range(count // 2):
        left = inbox[1, 2 * pair].astype(WIDE)
        right = inbox[1, 2 * pair + 1].astype(WIDE)
        for part in range(3):
            lanes = slice((part + 1) * HD, (part + 2) * HD)
            to = part * D + pair * 128
            qkv_ref[:, to : to + 128] = jnp.concatenate([left[:, lanes], right[:, lanes]], axis=1)
    wout_ref[...] = wout_in[...]
    down_ref[...] = down_in[...]
    for at, ref in enumerate((vec_a, vec_b, vec_c, vec_d)):
        ref[...] = vec_in[at]


def last_call(tok, cot, sum_out, sum_back, inbox, wout_in, down_in, vec_in):
    rows = tok.shape[0]
    _, count, piece, units = inbox.shape
    shape = jax.ShapeDtypeStruct
    steps = 2

    def cut(array_shape):
        return pl.BlockSpec((array_shape[0] // steps,) + array_shape[1:], lambda at: (at, 0))

    whole = pl.BlockSpec((8, piece), lambda at: (0, 0))
    vector = pl.BlockSpec((piece,), lambda at: (0,))
    letters = pl.BlockSpec((2, count, piece // steps, units), lambda at: (0, 0, at, 0))
    outs = (
        shape((rows, D), NARROW),
        shape((rows, D), WIDE),
        shape((piece, 3 * D), WIDE),
        shape(wout_in.shape, WIDE),
        shape((piece, count * units), WIDE),
        shape(down_in.shape, WIDE),
    )
    return pl.pallas_call(
        last_kernel,
        grid=(steps,),
        out_shape=outs + (shape((piece,), WIDE),) * 4,
        in_specs=[cut(array.shape) for array in (tok, cot, sum_out, sum_back)]
        + [letters, cut(wout_in.shape), cut(down_in.shape), whole],
        out_specs=tuple(cut(array.shape) for array in outs) + (vector,) * 4,
        name="last_rows",
        compiler_params=pltpu.CompilerParams(vmem_limit_bytes=VMEM_LIMIT),
    )(tok, cot, sum_out, sum_back, inbox, wout_in, down_in, vec_in)


def fast_shards(depth, *arguments):
    tokens, cotangent, lengths, dealing = arguments[:4]
    gains = arguments[4:8]
    rows = tokens.shape[0] * tokens.shape[1]
    tok = tokens.reshape(rows, D)
    cot = cotangent.reshape(rows, D)
    forward = gather_call(depth, lengths, dealing, tok, cot, gains, *arguments[8:])
    heads, units, xhat, cot_all, attended, total, g_up, g_down, g_sum = forward[:9]
    wqkv_t, wup_all, wdown_part, wout_part, prm_all, found = forward[9:]
    small = (total, prm_all, g_sum)
    large = (
        attended, wout_part, wdown_part, units, g_up, wup_all, wqkv_t, g_down, heads, xhat, cot_all
    )
    out, grad_tokens, qkv_part, out_part, up_part, down_part, *vectors = last_call(
        tok, cot, *reduce_call(depth, (lengths, dealing, found), small, large, rows)
    )
    return (
        out.reshape(tokens.shape),
        grad_tokens.reshape(tokens.shape),
        *vectors,
        qkv_part,
        out_part,
        up_part,
        down_part,
    )


def solution(mesh):
    placed = (
        P("wsh", "ctx", None),
        P("wsh", "ctx", None),
        P("wsh", None),
        P("wsh", None),
        P("wsh"),
        P("wsh"),
        P("wsh"),
        P("wsh"),
        P("wsh", None),
        P("wsh", None),
        P("wsh", None),
        P("wsh", None),
    )
    ctx_size = mesh.shape["ctx"]
    by_heads = ctx_size == H and mesh.shape["wsh"] == 2
    body = functools.partial(fast_shards, ctx_size // 4) if by_heads else shards
    return jax.shard_map(
        body,
        mesh=mesh,
        in_specs=placed,
        out_specs=(
            P("wsh", "ctx", None),
            P("wsh", "ctx", None),
            P(("ctx", "wsh")),
            P(("ctx", "wsh")),
            P(("ctx", "wsh")),
            P(("ctx", "wsh")),
            P(("ctx", "wsh"), None),
            P(("ctx", "wsh"), None),
            P(("ctx", "wsh"), None),
            P(("ctx", "wsh"), None),
        ),
        check_vma=False,
    )
```
